32 devices in a mesh: parts: 2 (over y), dap: 4 (over z), sub: 4 (over x, core).
Axes of the slice: x: 2, y: 2, z: 4, core: 2. Of those that a mesh axis runs over, the one named last changes fastest.
Arguments:
- alignment: bfloat16 [512, 64, 256], P('parts', 'dap'), parts along dimension 0, may hold values from -6 to 6
- alignment_mask: int32 [512, 64], P('parts'), parts along dimension 0, may hold values from 0 to 1, as said below
- pair_input: bfloat16 [128, 64, 128], P(('parts', 'dap'), 'sub'), parts along dimension 0, may hold values from -6 to 6
- residue_mask: int32 [128], P('parts'), parts along dimension 0, may hold values from 0 to 1, as said below
- chain_index: int32 [128], P('parts'), parts along dimension 0, may hold values from 0 to 3, as said below
- outer_left: bfloat16 [256, 32], replicated, may hold values from -0.375 to 0.375
- outer_right: bfloat16 [256, 32], replicated, may hold values from -0.375 to 0.375
- outer_proj: float32 [32, 32, 128], replicated, may hold values from -1 to 1
- triangle_left: bfloat16 [128, 256], replicated, may hold values from -0.5 to 0.5
- triangle_right: bfloat16 [128, 256], replicated, may hold values from -0.5 to 0.5
- triangle_gate: bfloat16 [128, 128], replicated, may hold values from -0.5 to 0.5
- triangle_out: bfloat16 [128, 128], replicated, may hold values from -0.5 to 0.5
- relative_table: bfloat16 [66, 128], replicated, may hold values from -5 to 5
- transition_up: bfloat16 [128, 512], replicated, may hold values from -0.5 to 0.5
- transition_down: bfloat16 [512, 128], replicated, may hold values from -0.25 to 0.25
Outputs:
- pair_output: bfloat16 [128, 64, 128], P(('parts', 'dap'), 'sub'), parts along dimension 0
The draws below stay inside these ranges and needn't reach their ends.
There are 2 independent parts, one for each index of `parts`. The reference program is written for one: setup_inputs(seed, part) draws one part's arguments, and reference() takes and returns one part's arrays. A program takes and returns all parts, laid end to end along the dimension named above; an argument that names none is the same for every part. Nothing has to cross between parts.
Inputs may be any that keep to these rules, and one draw needn't show every extreme that they name: `residue_mask`: the first residue is live and the last residue is padding. `chain_index`: never falls along the residues; the first residue is in chain 0 and the last in chain 3. `alignment_mask`: for each chain, a leading run of alignment rows, at least 32 long, is 1 at that chain's live residues; every other entry is 0.
All inputs are finite; a program needn't handle non-finite values.
Results may differ from the reference program's by a relative error of at most 0.012.
Values may be sent and summed in bfloat16 or wider, within the bound.
No kernel may reach another device: no remote copies, remote signals or barrier semaphores. Data moves between devices by JAX's collectives and lax.ppermute only.
A program may use at most 64 MiB of HBM per device.

```python
import math
import jax
import jax.numpy as jnp
from jax import lax

S = 256
CM = 256
CZ = 128
CO = 32
CT = 128
FT = 512
REL_CLIP = 32
RELBINS = 66
N = 64


def chain_layout(key):
    live_key = jax.random.fold_in(key, 101)
    cut_key = jax.random.fold_in(key, 102)
    positions = jnp.arange(N, dtype=jnp.int32)
    coins = jax.random.randint(live_key, (N,), 0, 2)
    alive = jnp.where(positions == 0, 1, jnp.where(positions == N - 1, 0, coins)).astype(jnp.int32)
    cuts = jax.random.randint(cut_key, (3,), 1, N)
    chains = jnp.sum((positions[:, None] >= cuts[None, :]).astype(jnp.int32), axis=1)
    return (alive, chains.astype(jnp.int32))


def draw_residue_mask(key, part):
    alive, chains = chain_layout(key)
    return alive


def draw_chain_index(key, part):
    alive, chains = chain_layout(key)
    return chains


def draw_alignment_mask(key, part):
    alive, chains = chain_layout(key)
    key = jax.random.fold_in(key, 7)
    depths = jax.random.randint(key, (4,), S // 8, S + 1)
    sequence = jnp.arange(S, dtype=jnp.int32)
    per_residue = depths[chains]
    inside = (sequence[:, None] < per_residue[None, :]) & (alive[None, :] == 1)
    return inside.astype(jnp.int32)


def shard_levels(stream_key, extent, pieces, low, top_value):
    level, own = 1.0, jax.random.fold_in(stream_key, 6)
    for dim, shards_of in pieces:
        heights = jnp.exp(jax.random.uniform(jax.random.fold_in(own, dim), (shards_of,), jnp.float32, low / len(pieces), top_value / len(pieces)))
        level = level * jnp.repeat(heights, extent[dim] // shards_of).reshape([-1 if axis == dim else 1 for axis in range(len(extent))])
    return level


def noise(own_key, dims, width, limit, pieces=(), kind=jnp.bfloat16):
    array = width * jax.random.normal(own_key, dims, jnp.float32)
    if pieces:
        array = array * shard_levels(own_key, dims, pieces, -0.22, 0.18)
    return jnp.clip(array, -limit, limit).astype(kind)


def setup_inputs(seed: int = 0, part: int = 0) -> dict:
    key_of = jax.random.split(jax.random.key(seed), 16)
    own_keys = jax.random.split(jax.random.fold_in(key_of[15], part), 16)
    return {
        "alignment": noise(own_keys[0], (S, N, CM), 1.0, 6.0, ((1, 4),)),
        "alignment_mask": draw_alignment_mask(jax.random.fold_in(jax.random.fold_in(key_of[15], part), 71), part),
        "pair_input": noise(own_keys[2], (N, N, CZ), 1.0, 6.0, ((0, 4), (1, 4))),
        "residue_mask": draw_residue_mask(jax.random.fold_in(jax.random.fold_in(key_of[15], part), 71), part),
        "chain_index": draw_chain_index(jax.random.fold_in(jax.random.fold_in(key_of[15], part), 71), part),
        "outer_left": noise(key_of[5], (CM, CO), CM ** -0.5, 0.375),
        "outer_right": noise(key_of[6], (CM, CO), CM ** -0.5, 0.375),
        "outer_proj": noise(key_of[7], (CO, CO, CZ), CO ** -0.5, 1.0, (), jnp.float32),
        "triangle_left": noise(key_of[8], (CZ, 2 * CT), CZ ** -0.5, 0.5),
        "triangle_right": noise(key_of[9], (CZ, 2 * CT), CZ ** -0.5, 0.5),
        "triangle_gate": noise(key_of[10], (CZ, CZ), CZ ** -0.5, 0.5),
        "triangle_out": noise(key_of[11], (CT, CZ), CT ** -0.5, 0.5),
        "relative_table": noise(key_of[12], (RELBINS, CZ), 1.0, 5.0),
        "transition_up": noise(key_of[13], (CZ, FT), CZ ** -0.5, 0.5),
        "transition_down": noise(key_of[14], (FT, CZ), FT ** -0.5, 0.25),
    }


epsilon = 1e-05

def layer_norm(values, along):
    average = lax.optimization_barrier(jnp.mean(values, axis=along, keepdims=True))
    centered = values - average
    spread = lax.optimization_barrier(jnp.mean(centered * centered, axis=along, keepdims=True))
    return centered * lax.rsqrt(spread + epsilon)

def relative_bias(row_ids, col_ids, row_chain, col_chain, relative_table):
    offset = jnp.clip(row_ids[:, None] - col_ids[None, :] + REL_CLIP, 0, 2 * REL_CLIP)
    bucket = jnp.where(row_chain[:, None] == col_chain[None, :], offset, 2 * REL_CLIP + 1)
    classes = jnp.arange(RELBINS, dtype=jnp.int32)
    onehot = (bucket[:, :, None] == classes[None, None, :]).astype(jnp.bfloat16)
    return jnp.dot(onehot, relative_table, preferred_element_type=jnp.float32)

def reference(alignment, alignment_mask, pair_input, residue_mask, chain_index, outer_left, outer_right, outer_proj, triangle_left, triangle_right, triangle_gate, triangle_out, relative_table, transition_up, transition_down):
    highest = lax.Precision.HIGHEST
    aligned = layer_norm(alignment.astype(jnp.float32), -1).astype(jnp.bfloat16)
    seq_mask = alignment_mask.astype(jnp.float32)
    left_factor = (jnp.dot(aligned, outer_left, preferred_element_type=jnp.float32) * seq_mask[:, :, None]).astype(jnp.bfloat16)
    right_factor = (jnp.dot(aligned, outer_right, preferred_element_type=jnp.float32) * seq_mask[:, :, None]).astype(jnp.bfloat16)
    counts = jnp.dot(seq_mask.T, seq_mask, precision=highest)
    right_wide = right_factor.astype(jnp.float32)
    block_rows = math.gcd(N, 16)
    starts = (jnp.arange(N // block_rows, dtype=jnp.int32) * block_rows).astype(jnp.int32)

    def outer_block(start):
        left_part = lax.dynamic_slice_in_dim(left_factor, start, block_rows, 1).astype(jnp.float32)
        outer = jnp.einsum('sic,sje->icej', left_part, right_wide, precision=highest)
        return jnp.einsum('icej,ced->ijd', outer, outer_proj, precision=highest)
    projected = lax.map(outer_block, starts).reshape(N, N, CZ)
    outer_mean = projected / jnp.maximum(counts, 1.0)[:, :, None]
    positions = jnp.arange(N, dtype=jnp.int32)
    chains = chain_index.astype(jnp.int32)
    relative = relative_bias(positions, positions, chains, chains, relative_table)
    pair_one = (pair_input.astype(jnp.float32) + relative + outer_mean).astype(jnp.bfloat16)
    tri_norm = layer_norm(pair_one.astype(jnp.float32), -1).astype(jnp.bfloat16)
    live = residue_mask.astype(jnp.float32)
    pair_mask = live[:, None] * live[None, :]

    def gated(weight):
        both = jnp.dot(tri_norm, weight, preferred_element_type=jnp.float32)
        return (jax.nn.sigmoid(both[:, :, :CT]) * both[:, :, CT:] * pair_mask[:, :, None]).astype(jnp.bfloat16)
    left_tri = gated(triangle_left)
    right_tri = gated(triangle_right)
    tri_sum = jnp.einsum('ikc,jkc->ijc', left_tri.astype(jnp.float32), right_tri.astype(jnp.float32), precision=highest).astype(jnp.bfloat16)
    tri_hidden = layer_norm(tri_sum.astype(jnp.float32), -1).astype(jnp.bfloat16)
    gate = jax.nn.sigmoid(jnp.dot(tri_norm, triangle_gate, preferred_element_type=jnp.float32))
    update = jnp.dot(tri_hidden, triangle_out, preferred_element_type=jnp.float32)
    pair_two = (pair_one.astype(jnp.float32) + gate * update).astype(jnp.bfloat16)
    trans_norm = layer_norm(pair_two.astype(jnp.float32), -1).astype(jnp.bfloat16)
    trans_hidden = jax.nn.relu(jnp.dot(trans_norm, transition_up, preferred_element_type=jnp.float32)).astype(jnp.bfloat16)
    result = pair_two.astype(jnp.float32) + jnp.dot(trans_hidden, transition_down, preferred_element_type=jnp.float32)
    return result.astype(jnp.bfloat16)
```

```python
import functools

import jax
import jax.numpy as jnp
from jax import lax
from jax.experimental import pallas as pl
from jax.experimental.pallas import tpu as pltpu
from jax.sharding import PartitionSpec as P

REL_CLIP = 32
LANES = 128
EPSILON = 1e-05
BF16 = jnp.bfloat16
F32 = jnp.float32
NT = (((1,), (1,)), ((), ()))


def layer_norm(values):
    average = jnp.mean(values, axis=-1, keepdims=True)
    centered = values - average
    spread = jnp.mean(centered * centered, axis=-1, keepdims=True)
    return centered * lax.rsqrt(spread + EPSILON)


def dot(left, right):
    return jnp.dot(left, right, preferred_element_type=F32)


def dot_nt(left, right):
    return lax.dot_general(left, right, NT, preferred_element_type=F32)


def iota(shape, dim):
    return lax.broadcasted_iota(jnp.int32, shape, dim)


def vmem():
    return pl.BlockSpec(memory_space=pltpu.VMEM)


def factor_kernel(x_ref, mask_ref, wl_ref, wr_ref, zl_ref, zr_ref, w_scr, yl_scr, yr_scr):
    seqs, rows, channels = x_ref.shape
    hidden = wl_ref.shape[1]
    rep = LANES // hidden
    residues = mask_ref.shape[1]
    start = lax.axis_index("dap") * rows

    @pl.when(pl.program_id(0) == 0)
    def _():
        wl, wr = wl_ref[...], wr_ref[...]
        w_scr[:, :LANES] = jnp.concatenate([wl] * rep, axis=1)
        w_scr[:, LANES : 2 * LANES] = jnp.concatenate([wr] * rep, axis=1)
        w_scr[:, 2 * LANES :] = jnp.ones((channels, LANES), BF16)

    x = x_ref[...].reshape(seqs * rows, channels)
    w = w_scr[...]
    sums = dot(jnp.ones((8, channels), BF16), w)[:1]
    y = dot(x, w)
    mean = y[:, 2 * LANES :] * (1.0 / channels)
    xf = x.astype(F32)
    square = jnp.zeros_like(mean)
    for part in range(channels // LANES):
        centered = xf[:, part * LANES : (part + 1) * LANES] - mean
        square = square + centered * centered
    ones = jnp.ones((LANES, LANES), BF16)
    scale = lax.rsqrt(dot(square.astype(BF16), ones) * (1.0 / channels) + EPSILON)
    yl_scr[...] = (y[:, :LANES] - mean * sums[:, :LANES]) * scale
    yr_scr[...] = (y[:, LANES : 2 * LANES] - mean * sums[:, LANES : 2 * LANES]) * scale
    width = rows * hidden
    spread = (iota((residues, width), 0) == start + iota((residues, width), 1) // hidden).astype(BF16)
    live = dot(mask_ref[...].astype(BF16), spread)
    block = iota((seqs, LANES), 1) // hidden
    for scr, out in ((yr_scr, zr_ref), (yl_scr, zl_ref)):
        for group in range(rows // rep):
            z = scr[pl.ds(group * rep, seqs, stride=rows), :]
            for k in range(1, rep):
                z = jnp.where(block == k, scr[pl.ds(group * rep + k, seqs, stride=rows), :], z)
            lanes = slice(group * LANES, (group + 1) * LANES)
            out[:, lanes] = (z * live[:, lanes]).astype(BF16)


def factors(alignment, alignment_mask, outer_left, outer_right):
    seqs, rows, channels = alignment.shape
    residues = alignment_mask.shape[1]
    hidden = outer_left.shape[1]
    step = seqs // 4
    width = rows * hidden
    out = jax.ShapeDtypeStruct((seqs, width), BF16)
    return pl.pallas_call(
        factor_kernel,
        out_shape=(out, out),
        grid=(seqs // step,),
        in_specs=[
            pl.BlockSpec((step, rows, channels), lambda s: (s, 0, 0)),
            pl.BlockSpec((step, residues), lambda s: (s, 0)),
            pl.BlockSpec((channels, hidden), lambda s: (0, 0)),
            pl.BlockSpec((channels, hidden), lambda s: (0, 0)),
        ],
        out_specs=[pl.BlockSpec((step, width), lambda s: (s, 0))] * 2,
        scratch_shapes=[
            pltpu.VMEM((channels, 3 * LANES), BF16),
            pltpu.VMEM((step * rows, LANES), F32),
            pltpu.VMEM((step * rows, LANES), F32),
        ],
        compiler_params=pltpu.CompilerParams(vmem_limit_bytes=24 << 20),
        cost_estimate=pl.CostEstimate(
            flops=2 * seqs * rows * channels * 512, bytes_accessed=4 << 20, transcendentals=0
        ),
    )(alignment, alignment_mask, outer_left, outer_right)


def prepare_kernel(
    zl_ref, mask_ref, pair_ref, live_ref, chain_ref, table_ref, proj_ref,
    zlt_ref, base_ref, inverse_ref, live_out_ref, proj_out_ref, pair_scr, table_scr,
):
    rows, cols, _ = pair_ref.shape
    pairs = rows * cols
    residues = mask_ref.shape[1]
    classes = table_ref.shape[0]
    row_start = lax.axis_index("dap") * rows
    col_start = lax.axis_index("sub") * cols
    zlt_ref[...] = zl_ref[...].T
    proj_out_ref[...] = proj_ref[...].reshape(proj_out_ref.shape).astype(BF16)
    which = iota((pairs, residues), 0)
    place = iota((pairs, residues), 1)
    pick_row = (place == row_start + which % rows).astype(BF16)
    pick_col = (place == col_start + which // rows).astype(BF16)
    mask = mask_ref[...].astype(BF16)
    both = (dot_nt(pick_row, mask) * dot_nt(pick_col, mask)).astype(BF16)
    counts = dot(both, jnp.ones((mask.shape[0], LANES), BF16))
    inverse_ref[...] = 1.0 / jnp.maximum(counts, 1.0)
    live = jnp.broadcast_to(live_ref[...].astype(F32), (LANES, residues)).astype(BF16)
    chain = jnp.broadcast_to(chain_ref[...].astype(F32), (LANES, residues)).astype(BF16)
    live_out_ref[...] = dot_nt(pick_row, live) * dot_nt(pick_col, live)
    same = dot_nt(pick_row, chain) == dot_nt(pick_col, chain)
    pair = iota((pairs, LANES), 0)
    offset = (row_start + pair % rows) - (col_start + pair // rows) + REL_CLIP
    bucket = jnp.where(same, jnp.clip(offset, 0, 2 * REL_CLIP), 2 * REL_CLIP + 1)
    table_scr[...] = jnp.zeros_like(table_scr)
    table_scr[pl.ds(0, classes), :] = table_ref[...].astype(F32)
    onehot = (bucket == iota((pairs, LANES), 1)).astype(BF16)
    relative = dot(onehot, table_scr[...].astype(BF16))
    pair_scr[...] = pair_ref[...].reshape(pairs, LANES).astype(F32)
    for col in range(cols):
        here = slice(col * rows, (col + 1) * rows)
        base_ref[here, :] = relative[here] + pair_scr[pl.ds(col, rows, stride=cols), :]


def prepare(zl, alignment_mask, pair_input, residue_mask, chain_index, table, proj):
    rows, cols, channels = pair_input.shape
    pairs = rows * cols
    shape = jax.ShapeDtypeStruct((pairs, channels), F32)
    depth = proj.shape[0] * proj.shape[1]
    return pl.pallas_call(
        prepare_kernel,
        out_shape=(
            jax.ShapeDtypeStruct(zl.shape[::-1], BF16),
            shape,
            shape,
            shape,
            jax.ShapeDtypeStruct((depth, channels), BF16),
        ),
        in_specs=[vmem()] * 7,
        out_specs=[vmem()] * 5,
        scratch_shapes=[pltpu.VMEM((pairs, channels), F32), pltpu.VMEM((LANES, channels), F32)],
        compiler_params=pltpu.CompilerParams(vmem_limit_bytes=24 << 20),
        cost_estimate=pl.CostEstimate(
            flops=2 * pairs * 256 * 1024, bytes_accessed=2 << 20, transcendentals=0
        ),
    )(zl, alignment_mask, pair_input, residue_mask[None, :], chain_index[None, :], table, proj)


def pair_kernel(ratio, hidden, zlt_ref, *refs):
    zr_refs, refs = refs[:ratio], refs[ratio:]
    (base_ref, inverse_ref, live_ref, proj_ref, tl_ref, tr_ref,
     left_ref, right_ref, one_ref, outer_scr, flat_scr, one_scr) = refs
    pairs, channels = base_ref.shape
    rows = zlt_ref.shape[0] // hidden
    rep = LANES // hidden
    me = lax.axis_index("dap")
    lane = iota((rows, LANES), 1)
    odd = (lane // hidden) % 2 == 1
    upper = lane // (2 * hidden) == 1
    half = 2 * hidden
    for step in range(ratio):
        block = lax.rem(me + step, ratio)
        outer = dot(zlt_ref[...], zr_refs[step][...])
        for group in range(rows // rep):
            outer_scr[group] = outer[:, group * LANES : (group + 1) * LANES]
        for group in range(rows // rep):
            for quad in range(hidden // rep):
                s0, s1, s2, s3 = (
                    outer_scr[group, pl.ds(quad * rep + k, rows, stride=hidden), :] for k in range(rep)
                )
                t0 = jnp.where(upper, pltpu.roll(s2, half, 1), s0)
                t1 = jnp.where(upper, pltpu.roll(s3, half, 1), s1)
                t2 = jnp.where(upper, s2, pltpu.roll(s0, half, 1))
                t3 = jnp.where(upper, s3, pltpu.roll(s1, half, 1))
                back = LANES - hidden
                found = (
                    jnp.where(odd, pltpu.roll(t1, hidden, 1), t0),
                    jnp.where(odd, t1, pltpu.roll(t0, back, 1)),
                    jnp.where(odd, pltpu.roll(t3, hidden, 1), t2),
                    jnp.where(odd, t3, pltpu.roll(t2, back, 1)),
                )
                for k in range(rep):
                    first = block * rows * rows + (group * rep + k) * rows
                    if ratio == 1:
                        first = (group * rep + k) * rows
                    else:
                        first = pl.multiple_of(first, rows)
                    flat_scr[pl.ds(first, rows), quad * LANES : (quad + 1) * LANES] = found[k].astype(BF16)
    outer_mean = dot(flat_scr[...], proj_ref[...]) * inverse_ref[...]
    one = (base_ref[...] + outer_mean).astype(BF16).astype(F32)
    one_scr[...] = one
    norm = layer_norm(one).astype(BF16)
    for weight, out in ((tl_ref, left_ref), (tr_ref, right_ref)):
        both = dot(norm, weight[...])
        out[...] = (jax.nn.sigmoid(both[:, :channels]) * both[:, channels:] * live_ref[...]).astype(BF16)
    cols = pairs // rows
    for row in range(rows):
        one_ref[row * cols : (row + 1) * cols, :] = one_scr[pl.ds(row, cols, stride=rows), :].astype(BF16)


def pair_update(hidden, zlt, zrs, base, inverse, live, proj, triangle_left, triangle_right):
    pairs, channels = base.shape
    ratio = len(zrs)
    shape = jax.ShapeDtypeStruct((pairs, channels), BF16)
    return pl.pallas_call(
        functools.partial(pair_kernel, ratio, hidden),
        out_shape=(shape, shape, shape),
        in_specs=[vmem()] * (7 + ratio),
        out_specs=[vmem()] * 3,
        scratch_shapes=[
            pltpu.VMEM((zrs[0].shape[1] // LANES, zlt.shape[0], LANES), F32),
            pltpu.VMEM((pairs, proj.shape[0]), BF16),
            pltpu.VMEM((pairs, channels), F32),
        ],
        compiler_params=pltpu.CompilerParams(vmem_limit_bytes=32 << 20),
        cost_estimate=pl.CostEstimate(
            flops=2 * pairs * 1024 * 512, bytes_accessed=2 << 20, transcendentals=pairs * 256
        ),
    )(zlt, *zrs, base, inverse, live, proj, triangle_left, triangle_right)


def triangle_kernel(subs, ratio, cols, *refs):
    lefts, refs = refs[:subs], refs[subs:]
    rights, refs = refs[: subs * ratio], refs[subs * ratio :]
    (one_ref, gate_ref, out_ref, up_ref, down_ref, result_ref, left_scr, right_scr, sum_scr) = refs
    pairs, channels = one_ref.shape
    rows = pairs // cols
    here, there = lax.axis_index("dap"), lax.axis_index("sub")
    for step in range(subs):
        left_scr[lax.rem(there + step, subs)] = lefts[step][...].astype(F32)
    for turn in range(ratio):
        block = lax.rem(here + turn, ratio)
        for step in range(subs):
            slot = block * subs + lax.rem(here // ratio + step, subs)
            right_scr[slot] = rights[turn * subs + step][...].astype(F32)
    for block in range(ratio):
        totals = tuple(jnp.zeros((rows, channels), F32) for _ in range(rows))
        for sub in range(subs):

            def body(k, totals, sub=sub, block=block):
                first = pl.multiple_of(k * rows, rows)
                right = right_scr[block * subs + sub, pl.ds(first, rows), :]
                return tuple(
                    totals[i] + left_scr[sub, pl.ds(first + i, 1), :] * right for i in range(rows)
                )

            totals = lax.fori_loop(0, cols, body, totals, unroll=4)
        for i in range(rows):
            sum_scr[i * cols + block * rows : i * cols + (block + 1) * rows, :] = totals[i]
    one = one_ref[...].astype(F32)
    norm = layer_norm(one).astype(BF16)
    gate = jax.nn.sigmoid(dot(norm, gate_ref[...]))
    hidden = layer_norm(sum_scr[...].astype(BF16).astype(F32)).astype(BF16)
    two = (one + gate * dot(hidden, out_ref[...])).astype(BF16).astype(F32)
    wide = jnp.maximum(dot(layer_norm(two).astype(BF16), up_ref[...]), 0.0).astype(BF16)
    result = (two + dot(wide, down_ref[...])).astype(BF16)
    result_ref[...] = result.reshape(result_ref.shape)


def triangle_update(lefts, rights, one, cols, gate, out, up, down):
    pairs, channels = one.shape
    rows = pairs // cols
    subs = len(lefts)
    ratio = len(rights) // subs
    return pl.pallas_call(
        functools.partial(triangle_kernel, subs, ratio, cols),
        out_shape=jax.ShapeDtypeStruct((rows, cols, channels), BF16),
        in_specs=[vmem()] * (subs + subs * ratio + 5),
        out_specs=vmem(),
        scratch_shapes=[
            pltpu.VMEM((subs, pairs, channels), F32),
            pltpu.VMEM((subs * ratio, pairs, channels), F32),
            pltpu.VMEM((pairs, channels), F32),
        ],
        compiler_params=pltpu.CompilerParams(vmem_limit_bytes=(16 << 20) if ratio == 1 else (50 << 20)),
        cost_estimate=pl.CostEstimate(
            flops=2 * pairs * channels * 2048, bytes_accessed=2 << 20, transcendentals=pairs * 128
        ),
    )(*lefts, *rights, one, gate, out, up, down)


def per_device(
    alignment,
    alignment_mask,
    pair_input,
    residue_mask,
    chain_index,
    outer_left,
    outer_right,
    outer_proj,
    triangle_left,
    triangle_right,
    triangle_gate,
    triangle_out,
    relative_table,
    transition_up,
    transition_down,
):
    daps, subs = lax.axis_size("dap"), lax.axis_size("sub")
    ratio = daps // subs
    cols = pair_input.shape[1]

    def fetch(values, source):
        perm = []
        for a in range(daps):
            for b in range(subs):
                dap, sub = source(a, b)
                perm.append((dap * subs + sub, a * subs + b))
        return lax.ppermute(values, ("dap", "sub"), perm)

    def owner(a, b, turn):
        return ratio * b + (a + turn) % ratio

    zl, zr = factors(alignment, alignment_mask, outer_left, outer_right)
    zrs = [
        fetch(zr, lambda a, b, turn=turn: (owner(a, b, turn), a // ratio)) for turn in range(ratio)
    ]
    zlt, base, inverse, live, proj = prepare(
        zl, alignment_mask, pair_input, residue_mask, chain_index, relative_table, outer_proj
    )
    left, right, one = pair_update(
        outer_left.shape[1], zlt, zrs, base, inverse, live, proj, triangle_left, triangle_right
    )
    rights = [
        fetch(right, lambda a, b, t=turn, m=step: (owner(a, b, t), (a // ratio + m) % subs))
        for turn in range(ratio)
        for step in range(subs)
    ]
    lefts = [left] + [
        fetch(left, lambda a, b, m=step: (a, (b + m) % subs)) for step in range(1, subs)
    ]
    return triangle_update(
        lefts, rights, one, cols, triangle_gate, triangle_out, transition_up, transition_down
    )


def solution(mesh):
    in_specs = (
        P("parts", "dap", None),
        P("parts", None),
        P(("parts", "dap"), "sub", None),
        P("parts"),
        P("parts"),
        P(),
        P(),
        P(),
        P(),
        P(),
        P(),
        P(),
        P(),
        P(),
        P(),
    )
    out_specs = P(("parts", "dap"), "sub", None)
    return jax.shard_map(
        per_device, mesh=mesh, in_specs=in_specs, out_specs=out_specs, check_vma=False
    )
```

```python
import functools

import jax
import jax.numpy as jnp
from jax import lax
from jax.experimental import pallas as pl
from jax.experimental.pallas import tpu as pltpu
from jax.sharding import PartitionSpec as P

REL_CLIP = 32
LANES = 128
EPSILON = 1e-05
BF16 = jnp.bfloat16
F32 = jnp.float32
NT = (((1,), (1,)), ((), ()))
TN = (((0,), (0,)), ((), ()))


def layer_norm(values):
    average = jnp.mean(values, axis=-1, keepdims=True)
    centered = values - average
    spread = jnp.mean(centered * centered, axis=-1, keepdims=True)
    return centered * lax.rsqrt(spread + EPSILON)


def dot(left, right):
    return jnp.dot(left, right, preferred_element_type=F32)


def dot_nt(left, right):
    return lax.dot_general(left, right, NT, preferred_element_type=F32)


def dot_tn(left, right):
    return lax.dot_general(left, right, TN, preferred_element_type=F32)


def iota(shape, dim):
    return lax.broadcasted_iota(jnp.int32, shape, dim)


def vmem():
    return pl.BlockSpec(memory_space=pltpu.VMEM)


def factor_kernel(x_ref, mask_ref, wl_ref, wr_ref, zl_ref, zr_ref, w_scr, live_scr, yl_scr, yr_scr):
    seqs, rows, channels = x_ref.shape
    hidden = wl_ref.shape[0]
    rep = LANES // hidden
    residues = mask_ref.shape[0]
    width = rows * hidden
    step = pl.program_id(0)

    @pl.when(step == 0)
    def _():
        for k in range(rep):
            w_scr[k * hidden : (k + 1) * hidden, :] = wl_ref[...]
            w_scr[LANES + k * hidden : LANES + (k + 1) * hidden, :] = wr_ref[...]
        w_scr[2 * LANES :, :] = jnp.ones((LANES, channels), BF16)
        start = lax.axis_index("dap") * rows
        spread = iota((residues, width), 0) == start + iota((residues, width), 1) // hidden
        live_scr[...] = dot_tn(mask_ref[...].astype(BF16), spread.astype(BF16))

    x = x_ref[...].reshape(seqs * rows, channels)
    w = w_scr[...]
    sums = dot_nt(jnp.ones((8, channels), BF16), w)[:1]
    y = dot_nt(x, w)
    mean = y[:, 2 * LANES :] * (1.0 / channels)
    xf = x.astype(F32)
    square = jnp.zeros_like(mean)
    for part in range(channels // LANES):
        centered = xf[:, part * LANES : (part + 1) * LANES] - mean
        square = square + centered * centered
    ones = jnp.ones((LANES, LANES), BF16)
    scale = lax.rsqrt(dot(square.astype(BF16), ones) * (1.0 / channels) + EPSILON)
    yl_scr[...] = (y[:, :LANES] - mean * sums[:, :LANES]) * scale
    yr_scr[...] = (y[:, LANES : 2 * LANES] - mean * sums[:, LANES : 2 * LANES]) * scale
    block = iota((seqs, LANES), 1) // hidden
    here = pl.ds(pl.multiple_of(step * seqs, seqs), seqs)
    for group in range(rows // rep):
        lanes = slice(group * LANES, (group + 1) * LANES)
        live = live_scr[here, lanes]
        for scr, out in ((yr_scr, zr_ref), (yl_scr, zl_ref)):
            z = scr[pl.ds(group * rep, seqs, stride=rows), :]
            for k in range(1, rep):
                z = jnp.where(block == k, scr[pl.ds(group * rep + k, seqs, stride=rows), :], z)
            out[:, lanes] = (z * live).astype(BF16)


def factors(alignment, mask, outer_left, outer_right):
    seqs, rows, channels = alignment.shape
    residues = mask.shape[0]
    hidden = outer_left.shape[0]
    step = seqs // 4
    width = rows * hidden
    out = jax.ShapeDtypeStruct((seqs, width), BF16)
    return pl.pallas_call(
        factor_kernel,
        out_shape=(out, out),
        grid=(seqs // step,),
        in_specs=[
            pl.BlockSpec((step, rows, channels), lambda s: (s, 0, 0)),
            pl.BlockSpec((residues, seqs), lambda s: (0, 0)),
            pl.BlockSpec((hidden, channels), lambda s: (0, 0)),
            pl.BlockSpec((hidden, channels), lambda s: (0, 0)),
        ],
        out_specs=[pl.BlockSpec((step, width), lambda s: (s, 0))] * 2,
        scratch_shapes=[
            pltpu.VMEM((3 * LANES, channels), BF16),
            pltpu.VMEM((seqs, width), F32),
            pltpu.VMEM((step * rows, LANES), F32),
            pltpu.VMEM((step * rows, LANES), F32),
        ],
        compiler_params=pltpu.CompilerParams(vmem_limit_bytes=119 << 19),
        cost_estimate=pl.CostEstimate(
            flops=2 * seqs * rows * channels * 512, bytes_accessed=4 << 20, transcendentals=0
        ),
    )(alignment, mask, outer_left, outer_right)


def prepare_kernel(
    zl_ref, mask_ref, pair_ref, live_ref, chain_ref, table_ref, proj_ref,
    zlt_ref, base_ref, inverse_ref, live_out_ref, proj_out_ref, pair_scr, table_scr,
):
    rows, cols, _ = pair_ref.shape
    pairs = rows * cols
    residues = mask_ref.shape[0]
    classes = table_ref.shape[0]
    row_start = lax.axis_index("dap") * rows
    col_start = lax.axis_index("sub") * cols
    zlt_ref[...] = zl_ref[...].T
    proj_out_ref[...] = proj_ref[...].reshape(proj_out_ref.shape).astype(BF16)
    which = iota((pairs, residues), 0)
    place = iota((pairs, residues), 1)
    pick_row = (place == row_start + which % rows).astype(BF16)
    pick_col = (place == col_start + which // rows).astype(BF16)
    mask = mask_ref[...].astype(BF16)
    both = (dot(pick_row, mask) * dot(pick_col, mask)).astype(BF16)
    counts = dot(both, jnp.ones((mask.shape[1], LANES), BF16))
    inverse_ref[...] = 1.0 / jnp.maximum(counts, 1.0)
    live = jnp.broadcast_to(live_ref[...].astype(F32), (LANES, residues)).astype(BF16)
    chain = jnp.broadcast_to(chain_ref[...].astype(F32), (LANES, residues)).astype(BF16)
    live_out_ref[...] = dot_nt(pick_row, live) * dot_nt(pick_col, live)
    same = dot_nt(pick_row, chain) == dot_nt(pick_col, chain)
    pair = iota((pairs, LANES), 0)
    offset = (row_start + pair % rows) - (col_start + pair // rows) + REL_CLIP
    bucket = jnp.where(same, jnp.clip(offset, 0, 2 * REL_CLIP), 2 * REL_CLIP + 1)
    table_scr[...] = jnp.zeros_like(table_scr)
    table_scr[pl.ds(0, classes), :] = table_ref[...].astype(F32)
    onehot = (bucket == iota((pairs, LANES), 1)).astype(BF16)
    relative = dot(onehot, table_scr[...].astype(BF16))
    pair_scr[...] = pair_ref[...].reshape(pairs, LANES).astype(F32)
    for col in range(cols):
        here = slice(col * rows, (col + 1) * rows)
        base_ref[here, :] = relative[here] + pair_scr[pl.ds(col, rows, stride=cols), :]


def prepare(zl, mask, pair_input, residue_mask, chain_index, table, proj):
    rows, cols, channels = pair_input.shape
    pairs = rows * cols
    shape = jax.ShapeDtypeStruct((pairs, channels), F32)
    depth = proj.shape[0] * proj.shape[1]
    return pl.pallas_call(
        prepare_kernel,
        out_shape=(
            jax.ShapeDtypeStruct(zl.shape[::-1], BF16),
            shape,
            shape,
            shape,
            jax.ShapeDtypeStruct((depth, channels), BF16),
        ),
        in_specs=[vmem()] * 7,
        out_specs=[vmem()] * 5,
        scratch_shapes=[pltpu.VMEM((pairs, channels), F32), pltpu.VMEM((LANES, channels), F32)],
        compiler_params=pltpu.CompilerParams(vmem_limit_bytes=24 << 20),
        cost_estimate=pl.CostEstimate(
            flops=2 * pairs * 256 * 1024, bytes_accessed=2 << 20, transcendentals=0
        ),
    )(zl, mask, pair_input, residue_mask[None, :], chain_index[None, :], table, proj)


def pair_kernel(ratio, hidden, zlt_ref, *refs):
    zr_refs, refs = refs[:ratio], refs[ratio:]
    (base_ref, inverse_ref, live_ref, proj_ref, tl_ref, tr_ref,
     left_ref, right_ref, one_ref, outer_scr, flat_scr, one_scr) = refs
    pairs, channels = base_ref.shape
    rows = zlt_ref.shape[0] // hidden
    rep = LANES // hidden
    me = lax.axis_index("dap")
    lane = iota((rows, LANES), 1)
    odd = (lane // hidden) % 2 == 1
    upper = lane // (2 * hidden) == 1
    half = 2 * hidden
    for step in range(ratio):
        block = lax.rem(me + step, ratio)
        outer = dot(zlt_ref[...], zr_refs[step][...])
        for group in range(rows // rep):
            outer_scr[group] = outer[:, group * LANES : (group + 1) * LANES]
        for group in range(rows // rep):
            for quad in range(hidden // rep):
                s0, s1, s2, s3 = (
                    outer_scr[group, pl.ds(quad * rep + k, rows, stride=hidden), :] for k in range(rep)
                )
                t0 = jnp.where(upper, pltpu.roll(s2, half, 1), s0)
                t1 = jnp.where(upper, pltpu.roll(s3, half, 1), s1)
                t2 = jnp.where(upper, s2, pltpu.roll(s0, half, 1))
                t3 = jnp.where(upper, s3, pltpu.roll(s1, half, 1))
                back = LANES - hidden
                found = (
                    jnp.where(odd, pltpu.roll(t1, hidden, 1), t0),
                    jnp.where(odd, t1, pltpu.roll(t0, back, 1)),
                    jnp.where(odd, pltpu.roll(t3, hidden, 1), t2),
                    jnp.where(odd, t3, pltpu.roll(t2, back, 1)),
                )
                for k in range(rep):
                    first = block * rows * rows + (group * rep + k) * rows
                    if ratio == 1:
                        first = (group * rep + k) * rows
                    else:
                        first = pl.multiple_of(first, rows)
                    flat_scr[pl.ds(first, rows), quad * LANES : (quad + 1) * LANES] = found[k].astype(BF16)
    outer_mean = dot(flat_scr[...], proj_ref[...]) * inverse_ref[...]
    one = (base_ref[...] + outer_mean).astype(BF16).astype(F32)
    one_scr[...] = one
    norm = layer_norm(one).astype(BF16)
    for weight, out in ((tl_ref, left_ref), (tr_ref, right_ref)):
        both = dot(norm, weight[...])
        out[...] = (jax.nn.sigmoid(both[:, :channels]) * both[:, channels:] * live_ref[...]).astype(BF16)
    cols = pairs // rows
    for row in range(rows):
        one_ref[row * cols : (row + 1) * cols, :] = one_scr[pl.ds(row, cols, stride=rows), :].astype(BF16)


def pair_update(hidden, zlt, zrs, base, inverse, live, proj, triangle_left, triangle_right):
    pairs, channels = base.shape
    ratio = len(zrs)
    shape = jax.ShapeDtypeStruct((pairs, channels), BF16)
    return pl.pallas_call(
        functools.partial(pair_kernel, ratio, hidden),
        out_shape=(shape, shape, shape),
        in_specs=[vmem()] * (7 + ratio),
        out_specs=[vmem()] * 3,
        scratch_shapes=[
            pltpu.VMEM((zrs[0].shape[1] // LANES, zlt.shape[0], LANES), F32),
            pltpu.VMEM((pairs, proj.shape[0]), BF16),
            pltpu.VMEM((pairs, channels), F32),
        ],
        compiler_params=pltpu.CompilerParams(vmem_limit_bytes=32 << 20),
        cost_estimate=pl.CostEstimate(
            flops=2 * pairs * 1024 * 512, bytes_accessed=2 << 20, transcendentals=pairs * 256
        ),
    )(zlt, *zrs, base, inverse, live, proj, triangle_left, triangle_right)


def triangle_kernel(subs, ratio, cols, *refs):
    lefts, refs = refs[:subs], refs[subs:]
    rights, refs = refs[: subs * ratio], refs[subs * ratio :]
    (one_ref, gate_ref, out_ref, up_ref, down_ref, result_ref, left_scr, right_scr, sum_scr) = refs
    pairs, channels = one_ref.shape
    rows = pairs // cols
    here, there = lax.axis_index("dap"), lax.axis_index("sub")
    for step in range(subs):
        left_scr[lax.rem(there + step, subs)] = lefts[step][...].astype(F32)
    for turn in range(ratio):
        block = lax.rem(here + turn, ratio)
        for step in range(subs):
            slot = block * subs + lax.rem(here // ratio + step, subs)
            right_scr[slot] = rights[turn * subs + step][...].astype(F32)
    for block in range(ratio):
        totals = tuple(jnp.zeros((rows, channels), F32) for _ in range(rows))
        for sub in range(subs):

            def body(k, totals, sub=sub, block=block):
                first = pl.multiple_of(k * rows, rows)
                right = right_scr[block * subs + sub, pl.ds(first, rows), :]
                return tuple(
                    totals[i] + left_scr[sub, pl.ds(first + i, 1), :] * right for i in range(rows)
                )

            totals = lax.fori_loop(0, cols, body, totals, unroll=4)
        for i in range(rows):
            sum_scr[i * cols + block * rows : i * cols + (block + 1) * rows, :] = totals[i]
    one = one_ref[...].astype(F32)
    norm = layer_norm(one).astype(BF16)
    gate = jax.nn.sigmoid(dot(norm, gate_ref[...]))
    hidden = layer_norm(sum_scr[...].astype(BF16).astype(F32)).astype(BF16)
    two = (one + gate * dot(hidden, out_ref[...])).astype(BF16).astype(F32)
    wide = jnp.maximum(dot(layer_norm(two).astype(BF16), up_ref[...]), 0.0).astype(BF16)
    result = (two + dot(wide, down_ref[...])).astype(BF16)
    result_ref[...] = result.reshape(result_ref.shape)


def triangle_update(lefts, rights, one, cols, gate, out, up, down):
    pairs, channels = one.shape
    rows = pairs // cols
    subs = len(lefts)
    ratio = len(rights) // subs
    return pl.pallas_call(
        functools.partial(triangle_kernel, subs, ratio, cols),
        out_shape=jax.ShapeDtypeStruct((rows, cols, channels), BF16),
        in_specs=[vmem()] * (subs + subs * ratio + 5),
        out_specs=vmem(),
        scratch_shapes=[
            pltpu.VMEM((subs, pairs, channels), F32),
            pltpu.VMEM((subs * ratio, pairs, channels), F32),
            pltpu.VMEM((pairs, channels), F32),
        ],
        compiler_params=pltpu.CompilerParams(vmem_limit_bytes=(16 << 20) if ratio == 1 else (50 << 20)),
        cost_estimate=pl.CostEstimate(
            flops=2 * pairs * channels * 2048, bytes_accessed=2 << 20, transcendentals=pairs * 128
        ),
    )(*lefts, *rights, one, gate, out, up, down)


def per_device(
    alignment,
    alignment_mask,
    pair_input,
    residue_mask,
    chain_index,
    outer_left,
    outer_right,
    outer_proj,
    triangle_left,
    triangle_right,
    triangle_gate,
    triangle_out,
    relative_table,
    transition_up,
    transition_down,
):
    daps, subs = lax.axis_size("dap"), lax.axis_size("sub")
    ratio = daps // subs
    cols = pair_input.shape[1]

    def fetch(values, source):
        perm = []
        for a in range(daps):
            for b in range(subs):
                dap, sub = source(a, b)
                perm.append((dap * subs + sub, a * subs + b))
        return lax.ppermute(values, ("dap", "sub"), perm)

    def owner(a, b, turn):
        return ratio * b + (a + turn) % ratio

    def spread(sub):
        half = subs // 2
        return (sub % half) * 2 + sub // half

    mask = alignment_mask.T
    zl, zr = factors(alignment, mask, outer_left.T, outer_right.T)
    zrs = [
        fetch(zr, lambda a, b, turn=turn: (owner(a, b, turn), spread(a // ratio)))
        for turn in range(ratio)
    ]
    zlt, base, inverse, live, proj = prepare(
        zl, mask, pair_input, residue_mask, chain_index, relative_table, outer_proj
    )
    left, right, one = pair_update(
        outer_left.shape[1], zlt, zrs, base, inverse, live, proj, triangle_left, triangle_right
    )
    rights = [
        fetch(right, lambda a, b, t=turn, m=step: (owner(a, b, t), (a // ratio + m) % subs))
        for turn in range(ratio)
        for step in range(subs)
    ]
    lefts = [left] + [
        fetch(left, lambda a, b, m=step: (a, (b + m) % subs)) for step in range(1, subs)
    ]
    return triangle_update(
        lefts, rights, one, cols, triangle_gate, triangle_out, transition_up, transition_down
    )


def solution(mesh):
    in_specs = (
        P("parts", "dap", None),
        P("parts", None),
        P(("parts", "dap"), "sub", None),
        P("parts"),
        P("parts"),
        P(),
        P(),
        P(),
        P(),
        P(),
        P(),
        P(),
        P(),
        P(),
        P(),
    )
    out_specs = P(("parts", "dap"), "sub", None)
    return jax.shard_map(
        per_device, mesh=mesh, in_specs=in_specs, out_specs=out_specs, check_vma=False
    )
```

```python
import functools

import jax
import jax.numpy as jnp
from jax import lax
from jax.experimental import pallas as pl
from jax.experimental.pallas import tpu as pltpu
from jax.sharding import PartitionSpec as P

REL_CLIP = 32
LANES = 128
PIECE = 16
EPSILON = 1e-05
BF16 = jnp.bfloat16
F32 = jnp.float32
NT = (((1,), (1,)), ((), ()))
TN = (((0,), (0,)), ((), ()))


def layer_norm(values):
    average = jnp.mean(values, axis=-1, keepdims=True)
    centered = values - average
    spread = jnp.mean(centered * centered, axis=-1, keepdims=True)
    return centered * lax.rsqrt(spread + EPSILON)


def dot(left, right):
    return jnp.dot(left, right, preferred_element_type=F32)


def dot_nt(left, right):
    return lax.dot_general(left, right, NT, preferred_element_type=F32)


def dot_tn(left, right):
    return lax.dot_general(left, right, TN, preferred_element_type=F32)


def iota(shape, dim):
    return lax.broadcasted_iota(jnp.int32, shape, dim)


def vmem():
    return pl.BlockSpec(memory_space=pltpu.VMEM)


def factor_kernel(x_ref, mask_ref, wl_ref, wr_ref, zl_ref, zr_ref, w_scr, live_scr, gather_scr):
    seqs, rows, channels = x_ref.shape
    hidden = wl_ref.shape[0]
    rep = LANES // hidden
    groups = rows // rep
    residues = mask_ref.shape[0]
    width = rows * hidden
    step = pl.program_id(0)

    @pl.when(step == 0)
    def _():
        for k in range(rep):
            w_scr[k * hidden : (k + 1) * hidden, :] = wl_ref[...]
            w_scr[LANES + k * hidden : LANES + (k + 1) * hidden, :] = wr_ref[...]
        w_scr[2 * LANES :, :] = jnp.ones((LANES, channels), BF16)
        start = lax.axis_index("dap") * rows
        spread = iota((residues, width), 0) == start + iota((residues, width), 1) // hidden
        live_scr[...] = dot_tn(mask_ref[...].astype(BF16), spread.astype(BF16))
        to, at = iota(gather_scr.shape, 0), iota(gather_scr.shape, 1)
        same = (to % PIECE == at // rows) & (to // PIECE == (at % rows) // rep)
        gather_scr[...] = same.astype(BF16)

    w = w_scr[...]
    sums = dot_nt(jnp.ones((8, channels), BF16), w)[:1]
    ones = jnp.ones((LANES, LANES), BF16)
    piece_rows = PIECE * rows
    own = iota((piece_rows, LANES), 1) // hidden == iota((piece_rows, LANES), 0) % rep
    own = own.astype(F32)
    for piece in range(seqs // PIECE):
        x = x_ref[piece * PIECE : (piece + 1) * PIECE].reshape(piece_rows, channels)
        y = dot_nt(x, w)
        mean = y[:, 2 * LANES :] * (1.0 / channels)
        xf = x.astype(F32)
        square = jnp.zeros_like(mean)
        for part in range(channels // LANES):
            centered = xf[:, part * LANES : (part + 1) * LANES] - mean
            square = square + centered * centered
        scale = lax.rsqrt(dot(square.astype(BF16), ones) * (1.0 / channels) + EPSILON) * own
        left = ((y[:, :LANES] - mean * sums[:, :LANES]) * scale).astype(BF16)
        right = ((y[:, LANES : 2 * LANES] - mean * sums[:, LANES : 2 * LANES]) * scale).astype(BF16)
        z = dot(gather_scr[...], jnp.concatenate([left, right], axis=1))
        here = slice(piece * PIECE, (piece + 1) * PIECE)
        whole = pl.ds(pl.multiple_of(step * seqs + piece * PIECE, PIECE), PIECE)
        for group in range(groups):
            lanes = slice(group * LANES, (group + 1) * LANES)
            both = z[group * PIECE : (group + 1) * PIECE]
            live = live_scr[whole, lanes]
            zl_ref[here, lanes] = (both[:, :LANES] * live).astype(BF16)
            zr_ref[here, lanes] = (both[:, LANES:] * live).astype(BF16)


def factors(alignment, mask, outer_left, outer_right):
    seqs, rows, channels = alignment.shape
    residues = mask.shape[0]
    hidden = outer_left.shape[0]
    step = seqs // 4
    width = rows * hidden
    out = jax.ShapeDtypeStruct((seqs, width), BF16)
    return pl.pallas_call(
        factor_kernel,
        out_shape=(out, out),
        grid=(seqs // step,),
        in_specs=[
            pl.BlockSpec((step, rows, channels), lambda s: (s, 0, 0)),
            pl.BlockSpec((residues, seqs), lambda s: (0, 0)),
            pl.BlockSpec((hidden, channels), lambda s: (0, 0)),
            pl.BlockSpec((hidden, channels), lambda s: (0, 0)),
        ],
        out_specs=[pl.BlockSpec((step, width), lambda s: (s, 0))] * 2,
        scratch_shapes=[
            pltpu.VMEM((3 * LANES, channels), BF16),
            pltpu.VMEM((seqs, width), F32),
            pltpu.VMEM((rows * hidden // LANES * PIECE, PIECE * rows), BF16),
        ],
        compiler_params=pltpu.CompilerParams(vmem_limit_bytes=119 << 19),
        cost_estimate=pl.CostEstimate(
            flops=2 * seqs * rows * channels * 512, bytes_accessed=4 << 20, transcendentals=0
        ),
    )(alignment, mask, outer_left, outer_right)


def prepare_kernel(
    zl_ref, mask_ref, pair_ref, live_ref, chain_ref, table_ref, proj_ref,
    zlt_ref, base_ref, inverse_ref, live_out_ref, proj_out_ref, pair_scr, table_scr,
):
    rows, cols, _ = pair_ref.shape
    pairs = rows * cols
    residues = mask_ref.shape[0]
    classes = table_ref.shape[0]
    row_start = lax.axis_index("dap") * rows
    col_start = lax.axis_index("sub") * cols
    zlt_ref[...] = zl_ref[...].T
    proj_out_ref[...] = proj_ref[...].reshape(proj_out_ref.shape).astype(BF16)
    which = iota((pairs, residues), 0)
    place = iota((pairs, residues), 1)
    pick_row = (place == row_start + which % rows).astype(BF16)
    pick_col = (place == col_start + which // rows).astype(BF16)
    mask = mask_ref[...].astype(BF16)
    both = (dot(pick_row, mask) * dot(pick_col, mask)).astype(BF16)
    counts = dot(both, jnp.ones((mask.shape[1], LANES), BF16))
    inverse_ref[...] = 1.0 / jnp.maximum(counts, 1.0)
    live = jnp.broadcast_to(live_ref[...].astype(F32), (LANES, residues)).astype(BF16)
    chain = jnp.broadcast_to(chain_ref[...].astype(F32), (LANES, residues)).astype(BF16)
    live_out_ref[...] = dot_nt(pick_row, live) * dot_nt(pick_col, live)
    same = dot_nt(pick_row, chain) == dot_nt(pick_col, chain)
    pair = iota((pairs, LANES), 0)
    offset = (row_start + pair % rows) - (col_start + pair // rows) + REL_CLIP
    bucket = jnp.where(same, jnp.clip(offset, 0, 2 * REL_CLIP), 2 * REL_CLIP + 1)
    table_scr[...] = jnp.zeros_like(table_scr)
    table_scr[pl.ds(0, classes), :] = table_ref[...].astype(F32)
    onehot = (bucket == iota((pairs, LANES), 1)).astype(BF16)
    relative = dot(onehot, table_scr[...].astype(BF16))
    pair_scr[...] = pair_ref[...].reshape(pairs, LANES).astype(F32)
    for col in range(cols):
        here = slice(col * rows, (col + 1) * rows)
        base_ref[here, :] = relative[here] + pair_scr[pl.ds(col, rows, stride=cols), :]


def prepare(zl, mask, pair_input, residue_mask, chain_index, table, proj):
    rows, cols, channels = pair_input.shape
    pairs = rows * cols
    shape = jax.ShapeDtypeStruct((pairs, channels), F32)
    depth = proj.shape[0] * proj.shape[1]
    return pl.pallas_call(
        prepare_kernel,
        out_shape=(
            jax.ShapeDtypeStruct(zl.shape[::-1], BF16),
            shape,
            shape,
            shape,
            jax.ShapeDtypeStruct((depth, channels), BF16),
        ),
        in_specs=[vmem()] * 7,
        out_specs=[vmem()] * 5,
        scratch_shapes=[pltpu.VMEM((pairs, channels), F32), pltpu.VMEM((LANES, channels), F32)],
        compiler_params=pltpu.CompilerParams(vmem_limit_bytes=24 << 20),
        cost_estimate=pl.CostEstimate(
            flops=2 * pairs * 256 * 1024, bytes_accessed=2 << 20, transcendentals=0
        ),
    )(zl, mask, pair_input, residue_mask[None, :], chain_index[None, :], table, proj)


def pair_kernel(ratio, hidden, zlt_ref, *refs):
    zr_refs, refs = refs[:ratio], refs[ratio:]
    (base_ref, inverse_ref, live_ref, proj_ref, tl_ref, tr_ref,
     both_ref, one_ref, outer_scr, flat_scr, one_scr) = refs
    pairs, channels = base_ref.shape
    rows = zlt_ref.shape[0] // hidden
    rep = LANES // hidden
    me = lax.axis_index("dap")
    lane = iota((rows, LANES), 1)
    odd = (lane // hidden) % 2 == 1
    upper = lane // (2 * hidden) == 1
    half = 2 * hidden
    for step in range(ratio):
        block = lax.rem(me + step, ratio)
        outer = dot(zlt_ref[...], zr_refs[step][...])
        for group in range(rows // rep):
            outer_scr[group] = outer[:, group * LANES : (group + 1) * LANES]
        for group in range(rows // rep):
            for quad in range(hidden // rep):
                s0, s1, s2, s3 = (
                    outer_scr[group, pl.ds(quad * rep + k, rows, stride=hidden), :] for k in range(rep)
                )
                t0 = jnp.where(upper, pltpu.roll(s2, half, 1), s0)
                t1 = jnp.where(upper, pltpu.roll(s3, half, 1), s1)
                t2 = jnp.where(upper, s2, pltpu.roll(s0, half, 1))
                t3 = jnp.where(upper, s3, pltpu.roll(s1, half, 1))
                back = LANES - hidden
                found = (
                    jnp.where(odd, pltpu.roll(t1, hidden, 1), t0),
                    jnp.where(odd, t1, pltpu.roll(t0, back, 1)),
                    jnp.where(odd, pltpu.roll(t3, hidden, 1), t2),
                    jnp.where(odd, t3, pltpu.roll(t2, back, 1)),
                )
                for k in range(rep):
                    first = block * rows * rows + (group * rep + k) * rows
                    if ratio == 1:
                        first = (group * rep + k) * rows
                    else:
                        first = pl.multiple_of(first, rows)
                    flat_scr[pl.ds(first, rows), quad * LANES : (quad + 1) * LANES] = found[k].astype(BF16)
    outer_mean = dot(flat_scr[...], proj_ref[...]) * inverse_ref[...]
    one = (base_ref[...] + outer_mean).astype(BF16).astype(F32)
    one_scr[...] = one
    norm = layer_norm(one).astype(BF16)
    for side, weight in enumerate((tl_ref, tr_ref)):
        both = dot(norm, weight[...])
        factor = jax.nn.sigmoid(both[:, :channels]) * both[:, channels:] * live_ref[...]
        both_ref[side] = factor.astype(BF16)
    cols = pairs // rows
    for row in range(rows):
        one_ref[row * cols : (row + 1) * cols, :] = one_scr[pl.ds(row, cols, stride=rows), :].astype(BF16)


def pair_update(hidden, zlt, zrs, base, inverse, live, proj, triangle_left, triangle_right):
    pairs, channels = base.shape
    ratio = len(zrs)
    shape = jax.ShapeDtypeStruct((pairs, channels), BF16)
    return pl.pallas_call(
        functools.partial(pair_kernel, ratio, hidden),
        out_shape=(jax.ShapeDtypeStruct((2, pairs, channels), BF16), shape),
        in_specs=[vmem()] * (7 + ratio),
        out_specs=[vmem()] * 2,
        scratch_shapes=[
            pltpu.VMEM((zrs[0].shape[1] // LANES, zlt.shape[0], LANES), F32),
            pltpu.VMEM((pairs, proj.shape[0]), BF16),
            pltpu.VMEM((pairs, channels), F32),
        ],
        compiler_params=pltpu.CompilerParams(vmem_limit_bytes=32 << 20),
        cost_estimate=pl.CostEstimate(
            flops=2 * pairs * 1024 * 512, bytes_accessed=2 << 20, transcendentals=pairs * 256
        ),
    )(zlt, *zrs, base, inverse, live, proj, triangle_left, triangle_right)


def other(sub):
    return sub + 1 - 2 * (sub % 2)


def triangle_kernel(subs, ratio, cols, *refs):
    twos = subs // 2
    lefts, refs = refs[:twos], refs[twos:]
    rights, refs = refs[: twos * ratio], refs[twos * ratio :]
    (one_ref, gate_ref, out_ref, up_ref, down_ref, result_ref, left_scr, right_scr, sum_scr) = refs
    pairs, channels = one_ref.shape
    rows = pairs // cols
    here, there = lax.axis_index("dap"), lax.axis_index("sub")
    for step in range(twos):
        sub = lax.rem(there + 2 * step, subs)
        left_scr[sub] = lefts[step][0].astype(F32)
        left_scr[other(sub)] = lefts[step][1].astype(F32)
    for turn in range(ratio):
        block = lax.rem(here + turn, ratio)
        for step in range(twos):
            sub = lax.rem(here // ratio + 2 * step, subs)
            right_scr[block * subs + sub] = rights[turn * twos + step][0].astype(F32)
            right_scr[block * subs + other(sub)] = rights[turn * twos + step][1].astype(F32)
    for block in range(ratio):
        totals = tuple(jnp.zeros((rows, channels), F32) for _ in range(rows))
        for sub in range(subs):

            def body(k, totals, sub=sub, block=block):
                first = pl.multiple_of(k * rows, rows)
                right = right_scr[block * subs + sub, pl.ds(first, rows), :]
                return tuple(
                    totals[i] + left_scr[sub, pl.ds(first + i, 1), :] * right for i in range(rows)
                )

            totals = lax.fori_loop(0, cols, body, totals, unroll=4)
        for i in range(rows):
            sum_scr[i * cols + block * rows : i * cols + (block + 1) * rows, :] = totals[i]
    one = one_ref[...].astype(F32)
    norm = layer_norm(one).astype(BF16)
    gate = jax.nn.sigmoid(dot(norm, gate_ref[...]))
    hidden = layer_norm(sum_scr[...].astype(BF16).astype(F32)).astype(BF16)
    two = (one + gate * dot(hidden, out_ref[...])).astype(BF16).astype(F32)
    wide = jnp.maximum(dot(layer_norm(two).astype(BF16), up_ref[...]), 0.0).astype(BF16)
    result = (two + dot(wide, down_ref[...])).astype(BF16)
    result_ref[...] = result.reshape(result_ref.shape)


def triangle_update(lefts, rights, one, cols, gate, out, up, down):
    pairs, channels = one.shape
    rows = pairs // cols
    subs = 2 * len(lefts)
    ratio = len(rights) // len(lefts)
    return pl.pallas_call(
        functools.partial(triangle_kernel, subs, ratio, cols),
        out_shape=jax.ShapeDtypeStruct((rows, cols, channels), BF16),
        in_specs=[vmem()] * (len(lefts) + len(rights) + 5),
        out_specs=vmem(),
        scratch_shapes=[
            pltpu.VMEM((subs, pairs, channels), F32),
            pltpu.VMEM((subs * ratio, pairs, channels), F32),
            pltpu.VMEM((pairs, channels), F32),
        ],
        compiler_params=pltpu.CompilerParams(vmem_limit_bytes=(16 << 20) if ratio == 1 else (50 << 20)),
        cost_estimate=pl.CostEstimate(
            flops=2 * pairs * channels * 2048, bytes_accessed=2 << 20, transcendentals=pairs * 128
        ),
    )(*lefts, *rights, one, gate, out, up, down)


def per_device(
    alignment,
    alignment_mask,
    pair_input,
    residue_mask,
    chain_index,
    outer_left,
    outer_right,
    outer_proj,
    triangle_left,
    triangle_right,
    triangle_gate,
    triangle_out,
    relative_table,
    transition_up,
    transition_down,
):
    daps, subs = lax.axis_size("dap"), lax.axis_size("sub")
    ratio = daps // subs
    cols = pair_input.shape[1]

    def fetch(values, source):
        perm = []
        for a in range(daps):
            for b in range(subs):
                dap, sub = source(a, b)
                perm.append((dap * subs + sub, a * subs + b))
        return lax.ppermute(values, ("dap", "sub"), perm)

    def owner(a, b, turn):
        return ratio * b + (a + turn) % ratio

    def sender(a, b):
        if (daps, subs) == (4, 4):
            return ((0, 2, 1, 3), (2, 1, 3, 0), (3, 1, 2, 0), (1, 2, 0, 3))[b][a]
        return a // ratio

    mask = alignment_mask.T
    zl, zr = factors(alignment, mask, outer_left.T, outer_right.T)
    zrs = [
        fetch(zr, lambda a, b, turn=turn: (owner(a, b, turn), sender(a, b)))
        for turn in range(ratio)
    ]
    zlt, base, inverse, live, proj = prepare(
        zl, mask, pair_input, residue_mask, chain_index, relative_table, outer_proj
    )
    own, one = pair_update(
        outer_left.shape[1], zlt, zrs, base, inverse, live, proj, triangle_left, triangle_right
    )
    near = fetch(own, lambda a, b: (a, other(b)))
    left = jnp.stack([own[0], near[0]])
    right = jnp.stack([own[1], near[1]])
    rights = [
        fetch(right, lambda a, b, t=turn, m=step: (owner(a, b, t), (a // ratio + 2 * m) % subs))
        for turn in range(ratio)
        for step in range(subs // 2)
    ]
    lefts = [left] + [
        fetch(left, lambda a, b, m=step: (a, (b + 2 * m) % subs)) for step in range(1, subs // 2)
    ]
    return triangle_update(
        lefts, rights, one, cols, triangle_gate, triangle_out, transition_up, transition_down
    )


def solution(mesh):
    in_specs = (
        P("parts", "dap", None),
        P("parts", None),
        P(("parts", "dap"), "sub", None),
        P("parts"),
        P("parts"),
        P(),
        P(),
        P(),
        P(),
        P(),
        P(),
        P(),
        P(),
        P(),
        P(),
    )
    out_specs = P(("parts", "dap"), "sub", None)
    return jax.shard_map(
        per_device, mesh=mesh, in_specs=in_specs, out_specs=out_specs, check_vma=False
    )
```

```python
import functools

import jax
import jax.numpy as jnp
from jax import lax
from jax.experimental import pallas as pl
from jax.experimental.pallas import tpu as pltpu
from jax.sharding import PartitionSpec as P

REL_CLIP = 32
LANES = 128
PIECE = 16
EPSILON = 1e-05
BF16 = jnp.bfloat16
F32 = jnp.float32
NT = (((1,), (1,)), ((), ()))
TN = (((0,), (0,)), ((), ()))


def layer_norm(values):
    average = jnp.mean(values, axis=-1, keepdims=True)
    centered = values - average
    spread = jnp.mean(centered * centered, axis=-1, keepdims=True)
    return centered * lax.rsqrt(spread + EPSILON)


def dot(left, right):
    return jnp.dot(left, right, preferred_element_type=F32)


def dot_nt(left, right):
    return lax.dot_general(left, right, NT, preferred_element_type=F32)


def dot_tn(left, right):
    return lax.dot_general(left, right, TN, preferred_element_type=F32)


def iota(shape, dim):
    return lax.broadcasted_iota(jnp.int32, shape, dim)


def vmem():
    return pl.BlockSpec(memory_space=pltpu.VMEM)


def factor_kernel(x_ref, mask_ref, wl_ref, wr_ref, zl_ref, zr_ref, w_scr, live_scr, gather_scr):
    seqs, rows, channels = x_ref.shape
    hidden = wl_ref.shape[0]
    rep = LANES // hidden
    groups = rows // rep
    residues = mask_ref.shape[0]
    width = rows * hidden
    step = pl.program_id(0)

    @pl.when(step == 0)
    def _():
        turned = jnp.concatenate([wl_ref[...]] * rep + [wr_ref[...]] * rep, axis=0)
        w_scr[:, : 2 * LANES] = turned.T
        w_scr[:, 2 * LANES :] = jnp.ones((channels, LANES), BF16)
        start = lax.axis_index("dap") * rows
        spread = iota((residues, width), 0) == start + iota((residues, width), 1) // hidden
        live_scr[...] = dot_tn(mask_ref[...].astype(BF16), spread.astype(BF16))
        to, at = iota(gather_scr.shape, 0), iota(gather_scr.shape, 1)
        same = (to % PIECE == at // rows) & (to // PIECE == (at % rows) // rep)
        gather_scr[...] = same.astype(BF16)

    w = w_scr[...]
    sums = dot(jnp.ones((8, channels), BF16), w)[:1]
    ones = jnp.ones((LANES, LANES), BF16)
    piece_rows = PIECE * rows
    own = iota((piece_rows, LANES), 1) // hidden == iota((piece_rows, LANES), 0) % rep
    own = own.astype(F32)
    for piece in range(seqs // PIECE):
        x = x_ref[piece * PIECE : (piece + 1) * PIECE].reshape(piece_rows, channels)
        y = dot(x, w)
        mean = y[:, 2 * LANES :] * (1.0 / channels)
        xf = x.astype(F32)
        square = jnp.zeros_like(mean)
        for part in range(channels // LANES):
            centered = xf[:, part * LANES : (part + 1) * LANES] - mean
            square = square + centered * centered
        scale = lax.rsqrt(dot(square.astype(BF16), ones) * (1.0 / channels) + EPSILON) * own
        left = ((y[:, :LANES] - mean * sums[:, :LANES]) * scale).astype(BF16)
        right = ((y[:, LANES : 2 * LANES] - mean * sums[:, LANES : 2 * LANES]) * scale).astype(BF16)
        z = dot(gather_scr[...], jnp.concatenate([left, right], axis=1))
        here = slice(piece * PIECE, (piece + 1) * PIECE)
        whole = pl.ds(pl.multiple_of(step * seqs + piece * PIECE, PIECE), PIECE)
        for group in range(groups):
            lanes = slice(group * LANES, (group + 1) * LANES)
            both = z[group * PIECE : (group + 1) * PIECE]
            live = live_scr[whole, lanes]
            zl_ref[here, lanes] = (both[:, :LANES] * live).astype(BF16)
            zr_ref[here, lanes] = (both[:, LANES:] * live).astype(BF16)


def factors(alignment, mask, outer_left, outer_right):
    seqs, rows, channels = alignment.shape
    residues = mask.shape[0]
    hidden = outer_left.shape[0]
    step = seqs // 4
    width = rows * hidden
    out = jax.ShapeDtypeStruct((seqs, width), BF16)
    return pl.pallas_call(
        factor_kernel,
        out_shape=(out, out),
        grid=(seqs // step,),
        in_specs=[
            pl.BlockSpec((step, rows, channels), lambda s: (s, 0, 0)),
            pl.BlockSpec((residues, seqs), lambda s: (0, 0)),
            pl.BlockSpec((hidden, channels), lambda s: (0, 0)),
            pl.BlockSpec((hidden, channels), lambda s: (0, 0)),
        ],
        out_specs=[pl.BlockSpec((step, width), lambda s: (s, 0))] * 2,
        scratch_shapes=[
            pltpu.VMEM((channels, 3 * LANES), BF16),
            pltpu.VMEM((seqs, width), F32),
            pltpu.VMEM((rows * hidden // LANES * PIECE, PIECE * rows), BF16),
        ],
        compiler_params=pltpu.CompilerParams(vmem_limit_bytes=119 << 19),
        cost_estimate=pl.CostEstimate(
            flops=2 * seqs * rows * channels * 512, bytes_accessed=4 << 20, transcendentals=0
        ),
    )(alignment, mask, outer_left, outer_right)


def prepare_kernel(
    zl_ref, mask_ref, pair_ref, live_ref, chain_ref, table_ref, proj_ref,
    zlt_ref, base_ref, inverse_ref, live_out_ref, proj_out_ref, pair_scr, table_scr,
):
    rows, cols, _ = pair_ref.shape
    pairs = rows * cols
    residues = mask_ref.shape[0]
    classes = table_ref.shape[0]
    row_start = lax.axis_index("dap") * rows
    col_start = lax.axis_index("sub") * cols
    zlt_ref[...] = zl_ref[...].T
    proj_out_ref[...] = proj_ref[...].reshape(proj_out_ref.shape).astype(BF16)
    which = iota((pairs, residues), 0)
    place = iota((pairs, residues), 1)
    pick_row = (place == row_start + which % rows).astype(BF16)
    pick_col = (place == col_start + which // rows).astype(BF16)
    mask = mask_ref[...].astype(BF16)
    both = (dot(pick_row, mask) * dot(pick_col, mask)).astype(BF16)
    counts = dot(both, jnp.ones((mask.shape[1], LANES), BF16))
    inverse_ref[...] = 1.0 / jnp.maximum(counts, 1.0)
    live = jnp.broadcast_to(live_ref[...].astype(F32), (LANES, residues)).astype(BF16)
    chain = jnp.broadcast_to(chain_ref[...].astype(F32), (LANES, residues)).astype(BF16)
    live_out_ref[...] = dot_nt(pick_row, live) * dot_nt(pick_col, live)
    same = dot_nt(pick_row, chain) == dot_nt(pick_col, chain)
    pair = iota((pairs, LANES), 0)
    offset = (row_start + pair % rows) - (col_start + pair // rows) + REL_CLIP
    bucket = jnp.where(same, jnp.clip(offset, 0, 2 * REL_CLIP), 2 * REL_CLIP + 1)
    table_scr[...] = jnp.zeros_like(table_scr)
    table_scr[pl.ds(0, classes), :] = table_ref[...].astype(F32)
    onehot = (bucket == iota((pairs, LANES), 1)).astype(BF16)
    relative = dot(onehot, table_scr[...].astype(BF16))
    pair_scr[...] = pair_ref[...].reshape(pairs, LANES).astype(F32)
    for col in range(cols):
        here = slice(col * rows, (col + 1) * rows)
        base_ref[here, :] = relative[here] + pair_scr[pl.ds(col, rows, stride=cols), :]


def prepare(zl, mask, pair_input, residue_mask, chain_index, table, proj):
    rows, cols, channels = pair_input.shape
    pairs = rows * cols
    shape = jax.ShapeDtypeStruct((pairs, channels), F32)
    depth = proj.shape[0] * proj.shape[1]
    return pl.pallas_call(
        prepare_kernel,
        out_shape=(
            jax.ShapeDtypeStruct(zl.shape[::-1], BF16),
            shape,
            shape,
            shape,
            jax.ShapeDtypeStruct((depth, channels), BF16),
        ),
        in_specs=[vmem()] * 7,
        out_specs=[vmem()] * 5,
        scratch_shapes=[pltpu.VMEM((pairs, channels), F32), pltpu.VMEM((LANES, channels), F32)],
        compiler_params=pltpu.CompilerParams(vmem_limit_bytes=24 << 20),
        cost_estimate=pl.CostEstimate(
            flops=2 * pairs * 256 * 1024, bytes_accessed=2 << 20, transcendentals=0
        ),
    )(zl, mask, pair_input, residue_mask[None, :], chain_index[None, :], table, proj)


def pair_kernel(ratio, hidden, zlt_ref, *refs):
    zr_refs, refs = refs[:ratio], refs[ratio:]
    (base_ref, inverse_ref, live_ref, proj_ref, tl_ref, tr_ref,
     both_ref, one_ref, outer_scr, flat_scr, one_scr) = refs
    pairs, channels = base_ref.shape
    rows = zlt_ref.shape[0] // hidden
    rep = LANES // hidden
    me = lax.axis_index("dap")
    lane = iota((rows, LANES), 1)
    odd = (lane // hidden) % 2 == 1
    upper = lane // (2 * hidden) == 1
    half = 2 * hidden
    for step in range(ratio):
        block = lax.rem(me + step, ratio)
        outer = dot(zlt_ref[...], zr_refs[step][...])
        for group in range(rows // rep):
            outer_scr[group] = outer[:, group * LANES : (group + 1) * LANES]
        for group in range(rows // rep):
            for quad in range(hidden // rep):
                s0, s1, s2, s3 = (
                    outer_scr[group, pl.ds(quad * rep + k, rows, stride=hidden), :] for k in range(rep)
                )
                t0 = jnp.where(upper, pltpu.roll(s2, half, 1), s0)
                t1 = jnp.where(upper, pltpu.roll(s3, half, 1), s1)
                t2 = jnp.where(upper, s2, pltpu.roll(s0, half, 1))
                t3 = jnp.where(upper, s3, pltpu.roll(s1, half, 1))
                back = LANES - hidden
                found = (
                    jnp.where(odd, pltpu.roll(t1, hidden, 1), t0),
                    jnp.where(odd, t1, pltpu.roll(t0, back, 1)),
                    jnp.where(odd, pltpu.roll(t3, hidden, 1), t2),
                    jnp.where(odd, t3, pltpu.roll(t2, back, 1)),
                )
                for k in range(rep):
                    first = block * rows * rows + (group * rep + k) * rows
                    if ratio == 1:
                        first = (group * rep + k) * rows
                    else:
                        first = pl.multiple_of(first, rows)
                    flat_scr[pl.ds(first, rows), quad * LANES : (quad + 1) * LANES] = found[k].astype(BF16)
    outer_mean = dot(flat_scr[...], proj_ref[...]) * inverse_ref[...]
    one = (base_ref[...] + outer_mean).astype(BF16).astype(F32)
    one_scr[...] = one
    norm = layer_norm(one).astype(BF16)
    for side, weight in enumerate((tl_ref, tr_ref)):
        both = dot(norm, weight[...])
        factor = jax.nn.sigmoid(both[:, :channels]) * both[:, channels:] * live_ref[...]
        both_ref[side] = factor.astype(BF16)
    cols = pairs // rows
    for row in range(rows):
        one_ref[row * cols : (row + 1) * cols, :] = one_scr[pl.ds(row, cols, stride=rows), :].astype(BF16)


def pair_update(hidden, zlt, zrs, base, inverse, live, proj, triangle_left, triangle_right):
    pairs, channels = base.shape
    ratio = len(zrs)
    shape = jax.ShapeDtypeStruct((pairs, channels), BF16)
    return pl.pallas_call(
        functools.partial(pair_kernel, ratio, hidden),
        out_shape=(jax.ShapeDtypeStruct((2, pairs, channels), BF16), shape),
        in_specs=[vmem()] * (7 + ratio),
        out_specs=[vmem()] * 2,
        scratch_shapes=[
            pltpu.VMEM((zrs[0].shape[1] // LANES, zlt.shape[0], LANES), F32),
            pltpu.VMEM((pairs, proj.shape[0]), BF16),
            pltpu.VMEM((pairs, channels), F32),
        ],
        compiler_params=pltpu.CompilerParams(vmem_limit_bytes=32 << 20),
        cost_estimate=pl.CostEstimate(
            flops=2 * pairs * 1024 * 512, bytes_accessed=2 << 20, transcendentals=pairs * 256
        ),
    )(zlt, *zrs, base, inverse, live, proj, triangle_left, triangle_right)


def other(sub):
    return sub + 1 - 2 * (sub % 2)


SENDERS = ((0, 2, 1, 3), (2, 1, 3, 0), (3, 1, 2, 0), (1, 2, 0, 3))


def sender(a, b, subs, ratio):
    if (subs, ratio) == (4, 1):
        return SENDERS[b][a]
    return a // ratio


def sender_index(a, b, subs, ratio):
    if (subs, ratio) != (4, 1):
        return a // ratio
    found = 0
    for col, places in enumerate(SENDERS):
        for row, place in enumerate(places):
            found = jnp.where((a == row) & (b == col), place, found)
    return found


def triangle_kernel(subs, ratio, cols, *refs):
    twos = subs // 2
    rights, refs = refs[: twos * ratio], refs[twos * ratio :]
    lefts, refs = refs[:twos], refs[twos:]
    (one_ref, gate_ref, out_ref, up_ref, down_ref, result_ref, left_scr, right_scr, sum_scr) = refs
    pairs, channels = one_ref.shape
    rows = pairs // cols
    here, there = lax.axis_index("dap"), lax.axis_index("sub")
    first_sub = sender_index(here, there, subs, ratio)
    for step in range(twos):
        sub = lax.rem(there + 2 * step, subs)
        left_scr[sub] = lefts[step][0].astype(F32)
        left_scr[other(sub)] = lefts[step][1].astype(F32)
    for turn in range(ratio):
        block = lax.rem(here + turn, ratio)
        for step in range(twos):
            sub = lax.rem(first_sub + 2 * step, subs)
            right_scr[block * subs + sub] = rights[turn * twos + step][0].astype(F32)
            right_scr[block * subs + other(sub)] = rights[turn * twos + step][1].astype(F32)
    for block in range(ratio):
        totals = tuple(jnp.zeros((rows, channels), F32) for _ in range(rows))
        for sub in range(subs):

            def body(k, totals, sub=sub, block=block):
                first = pl.multiple_of(k * rows, rows)
                right = right_scr[block * subs + sub, pl.ds(first, rows), :]
                return tuple(
                    totals[i] + left_scr[sub, pl.ds(first + i, 1), :] * right for i in range(rows)
                )

            totals = lax.fori_loop(0, cols, body, totals, unroll=4)
        for i in range(rows):
            sum_scr[i * cols + block * rows : i * cols + (block + 1) * rows, :] = totals[i]
    one = one_ref[...].astype(F32)
    norm = layer_norm(one).astype(BF16)
    gate = jax.nn.sigmoid(dot(norm, gate_ref[...]))
    hidden = layer_norm(sum_scr[...].astype(BF16).astype(F32)).astype(BF16)
    two = (one + gate * dot(hidden, out_ref[...])).astype(BF16).astype(F32)
    wide = jnp.maximum(dot(layer_norm(two).astype(BF16), up_ref[...]), 0.0).astype(BF16)
    result = (two + dot(wide, down_ref[...])).astype(BF16)
    result_ref[...] = result.reshape(result_ref.shape)


def triangle_update(lefts, rights, one, cols, gate, out, up, down):
    pairs, channels = one.shape
    rows = pairs // cols
    subs = 2 * len(lefts)
    ratio = len(rights) // len(lefts)
    return pl.pallas_call(
        functools.partial(triangle_kernel, subs, ratio, cols),
        out_shape=jax.ShapeDtypeStruct((rows, cols, channels), BF16),
        in_specs=[vmem()] * (len(lefts) + len(rights) + 5),
        out_specs=vmem(),
        scratch_shapes=[
            pltpu.VMEM((subs, pairs, channels), F32),
            pltpu.VMEM((subs * ratio, pairs, channels), F32),
            pltpu.VMEM((pairs, channels), F32),
        ],
        compiler_params=pltpu.CompilerParams(vmem_limit_bytes=(16 << 20) if ratio == 1 else (50 << 20)),
        cost_estimate=pl.CostEstimate(
            flops=2 * pairs * channels * 2048, bytes_accessed=2 << 20, transcendentals=pairs * 128
        ),
    )(*rights, *lefts, one, gate, out, up, down)


def per_device(
    alignment,
    alignment_mask,
    pair_input,
    residue_mask,
    chain_index,
    outer_left,
    outer_right,
    outer_proj,
    triangle_left,
    triangle_right,
    triangle_gate,
    triangle_out,
    relative_table,
    transition_up,
    transition_down,
):
    daps, subs = lax.axis_size("dap"), lax.axis_size("sub")
    ratio = daps // subs
    cols = pair_input.shape[1]

    def fetch(values, source):
        perm = []
        for a in range(daps):
            for b in range(subs):
                dap, sub = source(a, b)
                perm.append((dap * subs + sub, a * subs + b))
        return lax.ppermute(values, ("dap", "sub"), perm)

    def owner(a, b, turn):
        return ratio * b + (a + turn) % ratio

    mask = alignment_mask.T
    zl, zr = factors(alignment, mask, outer_left.T, outer_right.T)
    zrs = [
        fetch(zr, lambda a, b, turn=turn: (owner(a, b, turn), sender(a, b, subs, ratio)))
        for turn in range(ratio)
    ]
    zlt, base, inverse, live, proj = prepare(
        zl, mask, pair_input, residue_mask, chain_index, relative_table, outer_proj
    )
    own, one = pair_update(
        outer_left.shape[1], zlt, zrs, base, inverse, live, proj, triangle_left, triangle_right
    )
    near = fetch(own, lambda a, b: (a, other(b)))
    left = jnp.stack([own[0], near[0]])
    right = jnp.stack([own[1], near[1]])
    rights = [
        fetch(
            right,
            lambda a, b, t=turn, m=step: (
                owner(a, b, t), (sender(a, b, subs, ratio) + 2 * m) % subs
            ),
        )
        for turn in range(ratio)
        for step in range(subs // 2)
    ]
    lefts = [left] + [
        fetch(left, lambda a, b, m=step: (a, (b + 2 * m) % subs)) for step in range(1, subs // 2)
    ]
    return triangle_update(
        lefts, rights, one, cols, triangle_gate, triangle_out, transition_up, transition_down
    )


def solution(mesh):
    in_specs = (
        P("parts", "dap", None),
        P("parts", None),
        P(("parts", "dap"), "sub", None),
        P("parts"),
        P("parts"),
        P(),
        P(),
        P(),
        P(),
        P(),
        P(),
        P(),
        P(),
        P(),
        P(),
    )
    out_specs = P(("parts", "dap"), "sub", None)
    return jax.shard_map(
        per_device, mesh=mesh, in_specs=in_specs, out_specs=out_specs, check_vma=False
    )
```

```python
import functools

import jax
import jax.numpy as jnp
from jax import lax
from jax.experimental import pallas as pl
from jax.experimental.pallas import tpu as pltpu
from jax.sharding import PartitionSpec as P

REL_CLIP = 32
LANES = 128
PIECE = 16
EPSILON = 1e-05
BF16 = jnp.bfloat16
F32 = jnp.float32
NT = (((1,), (1,)), ((), ()))
TN = (((0,), (0,)), ((), ()))


def layer_norm(values):
    average = jnp.mean(values, axis=-1, keepdims=True)
    centered = values - average
    spread = jnp.mean(centered * centered, axis=-1, keepdims=True)
    return centered * lax.rsqrt(spread + EPSILON)


def dot(left, right):
    return jnp.dot(left, right, preferred_element_type=F32)


def dot_nt(left, right):
    return lax.dot_general(left, right, NT, preferred_element_type=F32)


def dot_tn(left, right):
    return lax.dot_general(left, right, TN, preferred_element_type=F32)


def iota(shape, dim):
    return lax.broadcasted_iota(jnp.int32, shape, dim)


def vmem():
    return pl.BlockSpec(memory_space=pltpu.VMEM)


def factor_kernel(x_ref, mask_ref, weight_ref, z_ref, w_scr, live_scr, gather_scr, y_scr):
    seqs, rows, channels = x_ref.shape
    hidden = weight_ref.shape[0]
    rep = LANES // hidden
    groups = rows // rep
    residues = mask_ref.shape[0]
    width = rows * hidden
    step = pl.program_id(0)

    @pl.when(step == 0)
    def _():
        w_scr[:, :LANES] = jnp.concatenate([weight_ref[...]] * rep, axis=0).T
        w_scr[:, LANES:] = jnp.ones((channels, LANES), BF16)
        start = lax.axis_index("dap") * rows
        spread = iota((residues, width), 0) == start + iota((residues, width), 1) // hidden
        live_scr[...] = dot_tn(mask_ref[...].astype(BF16), spread.astype(BF16))
        to, at = iota(gather_scr.shape, 0), iota(gather_scr.shape, 1)
        same = (to % PIECE == at // rows) & (to // PIECE == (at % rows) // rep)
        gather_scr[...] = same.astype(BF16)

    w = w_scr[...]
    sums = dot(jnp.ones((8, channels), BF16), w)[:1, :LANES]
    x = x_ref[...].reshape(seqs * rows, channels)
    y = dot(x, w)
    mean = y[:, LANES:] * (1.0 / channels)
    xf = x.astype(F32)
    square = jnp.zeros_like(mean)
    for part in range(channels // LANES):
        centered = xf[:, part * LANES : (part + 1) * LANES] - mean
        square = square + centered * centered
    spread = dot(square.astype(BF16), jnp.ones((LANES, LANES), BF16))
    own = (iota(mean.shape, 1) // hidden == iota(mean.shape, 0) % rep).astype(F32)
    scale = lax.rsqrt(spread * (1.0 / channels) + EPSILON) * own
    y_scr[...] = ((y[:, :LANES] - mean * sums) * scale).astype(BF16)
    for piece in range(seqs // PIECE):
        z = dot(gather_scr[...], y_scr[piece * PIECE * rows : (piece + 1) * PIECE * rows, :])
        here = slice(piece * PIECE, (piece + 1) * PIECE)
        whole = pl.ds(pl.multiple_of(step * seqs + piece * PIECE, PIECE), PIECE)
        for group in range(groups):
            lanes = slice(group * LANES, (group + 1) * LANES)
            part = z[group * PIECE : (group + 1) * PIECE]
            z_ref[here, lanes] = (part * live_scr[whole, lanes]).astype(BF16)


def factor(alignment, mask, weight):
    seqs, rows, channels = alignment.shape
    residues = mask.shape[0]
    hidden = weight.shape[0]
    step = seqs // 4
    width = rows * hidden
    return pl.pallas_call(
        factor_kernel,
        out_shape=jax.ShapeDtypeStruct((seqs, width), BF16),
        grid=(seqs // step,),
        in_specs=[
            pl.BlockSpec((step, rows, channels), lambda s: (s, 0, 0)),
            pl.BlockSpec((residues, seqs), lambda s: (0, 0)),
            pl.BlockSpec((hidden, channels), lambda s: (0, 0)),
        ],
        out_specs=pl.BlockSpec((step, width), lambda s: (s, 0)),
        scratch_shapes=[
            pltpu.VMEM((channels, 2 * LANES), BF16),
            pltpu.VMEM((seqs, width), F32),
            pltpu.VMEM((rows * hidden // LANES * PIECE, PIECE * rows), BF16),
            pltpu.VMEM((step * rows, LANES), BF16),
        ],
        compiler_params=pltpu.CompilerParams(vmem_limit_bytes=119 << 19),
        cost_estimate=pl.CostEstimate(
            flops=2 * seqs * rows * channels * 512, bytes_accessed=4 << 20, transcendentals=0
        ),
    )(alignment, mask, weight)


def prepare_kernel(
    zl_ref, mask_ref, pair_ref, live_ref, chain_ref, table_ref, proj_ref,
    zlt_ref, base_ref, inverse_ref, live_out_ref, proj_out_ref, pair_scr, table_scr,
):
    rows, cols, _ = pair_ref.shape
    pairs = rows * cols
    residues = mask_ref.shape[0]
    classes = table_ref.shape[0]
    row_start = lax.axis_index("dap") * rows
    col_start = lax.axis_index("sub") * cols
    zlt_ref[...] = zl_ref[...].T
    proj_out_ref[...] = proj_ref[...].reshape(proj_out_ref.shape).astype(BF16)
    which = iota((pairs, residues), 0)
    place = iota((pairs, residues), 1)
    pick_row = (place == row_start + which % rows).astype(BF16)
    pick_col = (place == col_start + which // rows).astype(BF16)
    mask = mask_ref[...].astype(BF16)
    both = (dot(pick_row, mask) * dot(pick_col, mask)).astype(BF16)
    counts = dot(both, jnp.ones((mask.shape[1], LANES), BF16))
    inverse_ref[...] = 1.0 / jnp.maximum(counts, 1.0)
    live = jnp.broadcast_to(live_ref[...].astype(F32), (LANES, residues)).astype(BF16)
    chain = jnp.broadcast_to(chain_ref[...].astype(F32), (LANES, residues)).astype(BF16)
    live_out_ref[...] = dot_nt(pick_row, live) * dot_nt(pick_col, live)
    same = dot_nt(pick_row, chain) == dot_nt(pick_col, chain)
    pair = iota((pairs, LANES), 0)
    offset = (row_start + pair % rows) - (col_start + pair // rows) + REL_CLIP
    bucket = jnp.where(same, jnp.clip(offset, 0, 2 * REL_CLIP), 2 * REL_CLIP + 1)
    table_scr[...] = jnp.zeros_like(table_scr)
    table_scr[pl.ds(0, classes), :] = table_ref[...].astype(F32)
    onehot = (bucket == iota((pairs, LANES), 1)).astype(BF16)
    relative = dot(onehot, table_scr[...].astype(BF16))
    pair_scr[...] = pair_ref[...].reshape(pairs, LANES).astype(F32)
    for col in range(cols):
        here = slice(col * rows, (col + 1) * rows)
        base_ref[here, :] = relative[here] + pair_scr[pl.ds(col, rows, stride=cols), :]


def prepare(zl, mask, pair_input, residue_mask, chain_index, table, proj):
    rows, cols, channels = pair_input.shape
    pairs = rows * cols
    shape = jax.ShapeDtypeStruct((pairs, channels), F32)
    depth = proj.shape[0] * proj.shape[1]
    return pl.pallas_call(
        prepare_kernel,
        out_shape=(
            jax.ShapeDtypeStruct(zl.shape[::-1], BF16),
            shape,
            shape,
            shape,
            jax.ShapeDtypeStruct((depth, channels), BF16),
        ),
        in_specs=[vmem()] * 7,
        out_specs=[vmem()] * 5,
        scratch_shapes=[pltpu.VMEM((pairs, channels), F32), pltpu.VMEM((LANES, channels), F32)],
        compiler_params=pltpu.CompilerParams(vmem_limit_bytes=24 << 20),
        cost_estimate=pl.CostEstimate(
            flops=2 * pairs * 256 * 1024, bytes_accessed=2 << 20, transcendentals=0
        ),
    )(zl, mask, pair_input, residue_mask[None, :], chain_index[None, :], table, proj)


def pair_kernel(ratio, hidden, zlt_ref, *refs):
    zr_refs, refs = refs[:ratio], refs[ratio:]
    (base_ref, inverse_ref, live_ref, proj_ref, tl_ref, tr_ref,
     both_ref, one_ref, outer_scr, flat_scr, one_scr) = refs
    pairs, channels = base_ref.shape
    rows = zlt_ref.shape[0] // hidden
    rep = LANES // hidden
    me = lax.axis_index("dap")
    lane = iota((rows, LANES), 1)
    odd = (lane // hidden) % 2 == 1
    upper = lane // (2 * hidden) == 1
    half = 2 * hidden
    for step in range(ratio):
        block = lax.rem(me + step, ratio)
        outer = dot(zlt_ref[...], zr_refs[step][...])
        for group in range(rows // rep):
            outer_scr[group] = outer[:, group * LANES : (group + 1) * LANES]
        for group in range(rows // rep):
            for quad in range(hidden // rep):
                s0, s1, s2, s3 = (
                    outer_scr[group, pl.ds(quad * rep + k, rows, stride=hidden), :] for k in range(rep)
                )
                t0 = jnp.where(upper, pltpu.roll(s2, half, 1), s0)
                t1 = jnp.where(upper, pltpu.roll(s3, half, 1), s1)
                t2 = jnp.where(upper, s2, pltpu.roll(s0, half, 1))
                t3 = jnp.where(upper, s3, pltpu.roll(s1, half, 1))
                back = LANES - hidden
                found = (
                    jnp.where(odd, pltpu.roll(t1, hidden, 1), t0),
                    jnp.where(odd, t1, pltpu.roll(t0, back, 1)),
                    jnp.where(odd, pltpu.roll(t3, hidden, 1), t2),
                    jnp.where(odd, t3, pltpu.roll(t2, back, 1)),
                )
                for k in range(rep):
                    first = block * rows * rows + (group * rep + k) * rows
                    if ratio == 1:
                        first = (group * rep + k) * rows
                    else:
                        first = pl.multiple_of(first, rows)
                    flat_scr[pl.ds(first, rows), quad * LANES : (quad + 1) * LANES] = found[k].astype(BF16)
    outer_mean = dot(flat_scr[...], proj_ref[...]) * inverse_ref[...]
    one = (base_ref[...] + outer_mean).astype(BF16).astype(F32)
    one_scr[...] = one
    norm = layer_norm(one).astype(BF16)
    for side, weight in enumerate((tl_ref, tr_ref)):
        both = dot(norm, weight[...])
        factor = jax.nn.sigmoid(both[:, :channels]) * both[:, channels:] * live_ref[...]
        both_ref[side] = factor.astype(BF16)
    cols = pairs // rows
    for row in range(rows):
        one_ref[row * cols : (row + 1) * cols, :] = one_scr[pl.ds(row, cols, stride=rows), :].astype(BF16)


def pair_update(hidden, zlt, zrs, base, inverse, live, proj, triangle_left, triangle_right):
    pairs, channels = base.shape
    ratio = len(zrs)
    shape = jax.ShapeDtypeStruct((pairs, channels), BF16)
    return pl.pallas_call(
        functools.partial(pair_kernel, ratio, hidden),
        out_shape=(jax.ShapeDtypeStruct((2, pairs, channels), BF16), shape),
        in_specs=[vmem()] * (7 + ratio),
        out_specs=[vmem()] * 2,
        scratch_shapes=[
            pltpu.VMEM((zrs[0].shape[1] // LANES, zlt.shape[0], LANES), F32),
            pltpu.VMEM((pairs, proj.shape[0]), BF16),
            pltpu.VMEM((pairs, channels), F32),
        ],
        compiler_params=pltpu.CompilerParams(vmem_limit_bytes=32 << 20),
        cost_estimate=pl.CostEstimate(
            flops=2 * pairs * 1024 * 512, bytes_accessed=2 << 20, transcendentals=pairs * 256
        ),
    )(zlt, *zrs, base, inverse, live, proj, triangle_left, triangle_right)


def other(sub):
    return sub + 1 - 2 * (sub % 2)


def gate_kernel(one_ref, weight_ref, gate_ref):
    norm = layer_norm(one_ref[...].astype(F32)).astype(BF16)
    gate_ref[...] = jax.nn.sigmoid(dot(norm, weight_ref[...]))


def output_gate(one, weight):
    return pl.pallas_call(
        gate_kernel,
        out_shape=jax.ShapeDtypeStruct(one.shape, F32),
        in_specs=[vmem()] * 2,
        out_specs=vmem(),
        cost_estimate=pl.CostEstimate(
            flops=2 * one.size * LANES, bytes_accessed=1 << 18, transcendentals=one.size
        ),
    )(one, weight)


SENDERS = ((0, 2, 1, 3), (2, 1, 3, 0), (3, 1, 2, 0), (1, 2, 0, 3))


def sender(a, b, subs, ratio):
    if (subs, ratio) == (4, 1):
        return SENDERS[b][a]
    return a // ratio


def sender_index(a, b, subs, ratio):
    if (subs, ratio) != (4, 1):
        return a // ratio
    found = 0
    for col, places in enumerate(SENDERS):
        for row, place in enumerate(places):
            found = jnp.where((a == row) & (b == col), place, found)
    return found


def triangle_kernel(subs, ratio, cols, *refs):
    twos = subs // 2
    lefts, refs = refs[:twos], refs[twos:]
    rights, refs = refs[: twos * ratio], refs[twos * ratio :]
    (one_ref, gate_ref, out_ref, up_ref, down_ref, result_ref, left_scr, right_scr, sum_scr) = refs
    pairs, channels = one_ref.shape
    rows = pairs // cols
    here, there = lax.axis_index("dap"), lax.axis_index("sub")
    first_sub = sender_index(here, there, subs, ratio)
    for step in range(twos):
        sub = lax.rem(there + 2 * step, subs)
        left_scr[sub] = lefts[step][0].astype(F32)
        left_scr[other(sub)] = lefts[step][1].astype(F32)
    for turn in range(ratio):
        block = lax.rem(here + turn, ratio)
        for step in range(twos):
            sub = lax.rem(first_sub + 2 * step, subs)
            right_scr[block * subs + sub] = rights[turn * twos + step][0].astype(F32)
            right_scr[block * subs + other(sub)] = rights[turn * twos + step][1].astype(F32)
    for block in range(ratio):
        totals = tuple(jnp.zeros((rows, channels), F32) for _ in range(rows))
        for sub in range(subs):

            def body(k, totals, sub=sub, block=block):
                first = pl.multiple_of(k * rows, rows)
                right = right_scr[block * subs + sub, pl.ds(first, rows), :]
                return tuple(
                    totals[i] + left_scr[sub, pl.ds(first + i, 1), :] * right for i in range(rows)
                )

            totals = lax.fori_loop(0, cols, body, totals, unroll=4)
        for i in range(rows):
            sum_scr[i * cols + block * rows : i * cols + (block + 1) * rows, :] = totals[i]
    one = one_ref[...].astype(F32)
    hidden = layer_norm(sum_scr[...].astype(BF16).astype(F32)).astype(BF16)
    two = (one + gate_ref[...] * dot(hidden, out_ref[...])).astype(BF16).astype(F32)
    wide = jnp.maximum(dot(layer_norm(two).astype(BF16), up_ref[...]), 0.0).astype(BF16)
    result = (two + dot(wide, down_ref[...])).astype(BF16)
    result_ref[...] = result.reshape(result_ref.shape)


def triangle_update(lefts, rights, one, cols, gate, out, up, down):
    pairs, channels = one.shape
    rows = pairs // cols
    subs = 2 * len(lefts)
    ratio = len(rights) // len(lefts)
    return pl.pallas_call(
        functools.partial(triangle_kernel, subs, ratio, cols),
        out_shape=jax.ShapeDtypeStruct((rows, cols, channels), BF16),
        in_specs=[vmem()] * (len(lefts) + len(rights) + 5),
        out_specs=vmem(),
        scratch_shapes=[
            pltpu.VMEM((subs, pairs, channels), F32),
            pltpu.VMEM((subs * ratio, pairs, channels), F32),
            pltpu.VMEM((pairs, channels), F32),
        ],
        compiler_params=pltpu.CompilerParams(vmem_limit_bytes=(16 << 20) if ratio == 1 else (50 << 20)),
        cost_estimate=pl.CostEstimate(
            flops=2 * pairs * channels * 2048, bytes_accessed=2 << 20, transcendentals=pairs * 128
        ),
    )(*lefts, *rights, one, gate, out, up, down)


def per_device(
    alignment,
    alignment_mask,
    pair_input,
    residue_mask,
    chain_index,
    outer_left,
    outer_right,
    outer_proj,
    triangle_left,
    triangle_right,
    triangle_gate,
    triangle_out,
    relative_table,
    transition_up,
    transition_down,
):
    daps, subs = lax.axis_size("dap"), lax.axis_size("sub")
    ratio = daps // subs
    cols = pair_input.shape[1]

    def fetch(values, source):
        perm = []
        for a in range(daps):
            for b in range(subs):
                dap, sub = source(a, b)
                perm.append((dap * subs + sub, a * subs + b))
        return lax.ppermute(values, ("dap", "sub"), perm)

    def owner(a, b, turn):
        return ratio * b + (a + turn) % ratio

    mask = alignment_mask.T
    zr = factor(alignment, mask, outer_right.T)
    zrs = [
        fetch(zr, lambda a, b, turn=turn: (owner(a, b, turn), sender(a, b, subs, ratio)))
        for turn in range(ratio)
    ]
    zl = factor(alignment, mask, outer_left.T)
    zlt, base, inverse, live, proj = prepare(
        zl, mask, pair_input, residue_mask, chain_index, relative_table, outer_proj
    )
    own, one = pair_update(
        outer_left.shape[1], zlt, zrs, base, inverse, live, proj, triangle_left, triangle_right
    )
    near = fetch(own, lambda a, b: (a, other(b)))
    left = jnp.stack([own[0], near[0]])
    right = jnp.stack([own[1], near[1]])
    rights = [
        fetch(
            right,
            lambda a, b, t=turn, m=step: (
                owner(a, b, t), (sender(a, b, subs, ratio) + 2 * m) % subs
            ),
        )
        for turn in range(ratio)
        for step in range(subs // 2)
    ]
    lefts = [left] + [
        fetch(left, lambda a, b, m=step: (a, (b + 2 * m) % subs)) for step in range(1, subs // 2)
    ]
    gate = output_gate(one, triangle_gate)
    return triangle_update(
        lefts, rights, one, cols, gate, triangle_out, transition_up, transition_down
    )


def solution(mesh):
    in_specs = (
        P("parts", "dap", None),
        P("parts", None),
        P(("parts", "dap"), "sub", None),
        P("parts"),
        P("parts"),
        P(),
        P(),
        P(),
        P(),
        P(),
        P(),
        P(),
        P(),
        P(),
        P(),
    )
    out_specs = P(("parts", "dap"), "sub", None)
    return jax.shard_map(
        per_device, mesh=mesh, in_specs=in_specs, out_specs=out_specs, check_vma=False
    )
```

```python
import functools

import jax
import jax.numpy as jnp
from jax import lax
from jax.experimental import pallas as pl
from jax.experimental.pallas import tpu as pltpu
from jax.sharding import PartitionSpec as P

REL_CLIP = 32
LANES = 128
PIECE = 16
STEPS = 4
EPSILON = 1e-05
BF16 = jnp.bfloat16
F32 = jnp.float32
NT = (((1,), (1,)), ((), ()))
TN = (((0,), (0,)), ((), ()))


def layer_norm(values):
    average = jnp.mean(values, axis=-1, keepdims=True)
    centered = values - average
    spread = jnp.mean(centered * centered, axis=-1, keepdims=True)
    return centered * lax.rsqrt(spread + EPSILON)


def dot(left, right):
    return jnp.dot(left, right, preferred_element_type=F32)


def dot_nt(left, right):
    return lax.dot_general(left, right, NT, preferred_element_type=F32)


def dot_tn(left, right):
    return lax.dot_general(left, right, TN, preferred_element_type=F32)


def iota(shape, dim):
    return lax.broadcasted_iota(jnp.int32, shape, dim)


def vmem():
    return pl.BlockSpec(memory_space=pltpu.VMEM)


def over(index, size):
    return lax.shift_right_logical(index, size.bit_length() - 1)


def within(index, size):
    return lax.bitwise_and(index, size - 1)


def factor_kernel(x_any, mask_ref, weight_ref, z_ref, x_scr, y_scr, sems):
    seqs, rows, channels = x_scr.shape
    hidden = weight_ref.shape[0]
    rep = LANES // hidden
    groups = rows // rep
    residues = mask_ref.shape[0]
    width = rows * hidden
    step = seqs // STEPS
    copies = []
    for turn in range(STEPS):
        part = pl.ds(turn * step, step)
        copies.append(pltpu.make_async_copy(x_any.at[part], x_scr.at[part], sems.at[turn]))
        copies[-1].start()
    weight = jnp.concatenate([weight_ref[...]] * rep, axis=0).T
    w = jnp.concatenate([weight, jnp.ones((channels, LANES), BF16)], axis=1)
    sums = dot(jnp.ones((8, channels), BF16), w)[:1, :LANES]
    start = lax.axis_index("dap") * rows
    spread = iota((residues, width), 0) == start + over(iota((residues, width), 1), hidden)
    live = dot_tn(mask_ref[...].astype(BF16), spread.astype(BF16))
    to, at = iota((groups * PIECE, PIECE * rows), 0), iota((groups * PIECE, PIECE * rows), 1)
    gather = within(to, PIECE) == over(at, rows)
    gather = (gather & (over(to, PIECE) == over(within(at, rows), rep))).astype(BF16)
    own = over(iota((8, LANES), 1), hidden) == within(iota((8, LANES), 0), rep)
    own = own.astype(F32)
    ones = jnp.ones((LANES, LANES), BF16)
    for turn in range(STEPS):
        copies[turn].wait()
        x = x_scr[turn * step : (turn + 1) * step].reshape(step * rows, channels)
        y = dot(x, w)
        mean = y[:, LANES:] * (1.0 / channels)
        xf = x.astype(F32)
        square = jnp.zeros_like(mean)
        for part in range(channels // LANES):
            centered = xf[:, part * LANES : (part + 1) * LANES] - mean
            square = square + centered * centered
        spread = dot(square.astype(BF16), ones)
        scale = lax.rsqrt(spread * (1.0 / channels) + EPSILON).reshape(-1, 8, LANES) * own[None]
        scaled = (y[:, :LANES] - mean * sums) * scale.reshape(mean.shape)
        y_scr[turn * step * rows : (turn + 1) * step * rows, :] = scaled.astype(BF16)
        for piece in range(turn * step // PIECE, (turn + 1) * step // PIECE):
            z = dot(gather, y_scr[piece * PIECE * rows : (piece + 1) * PIECE * rows, :])
            here = slice(piece * PIECE, (piece + 1) * PIECE)
            for group in range(groups):
                lanes = slice(group * LANES, (group + 1) * LANES)
                part = z[group * PIECE : (group + 1) * PIECE]
                z_ref[here, lanes] = (part * live[here, lanes]).astype(BF16)


def factor(alignment, mask, weight):
    seqs, rows, channels = alignment.shape
    hidden = weight.shape[0]
    return pl.pallas_call(
        factor_kernel,
        out_shape=jax.ShapeDtypeStruct((seqs, rows * hidden), BF16),
        in_specs=[pl.BlockSpec(memory_space=pl.ANY), vmem(), vmem()],
        out_specs=vmem(),
        scratch_shapes=[
            pltpu.VMEM(alignment.shape, BF16),
            pltpu.VMEM((seqs * rows, LANES), BF16),
            pltpu.SemaphoreType.DMA((STEPS,)),
        ],
        compiler_params=pltpu.CompilerParams(vmem_limit_bytes=119 << 19),
        cost_estimate=pl.CostEstimate(
            flops=2 * seqs * rows * channels * 512, bytes_accessed=4 << 20, transcendentals=0
        ),
    )(alignment, mask, weight)


def prepare_kernel(
    zl_ref, mask_ref, pair_ref, live_ref, chain_ref, table_ref, proj_ref,
    zlt_ref, base_ref, inverse_ref, live_out_ref, proj_out_ref, pair_scr, table_scr,
):
    rows, cols, _ = pair_ref.shape
    pairs = rows * cols
    residues = mask_ref.shape[0]
    classes = table_ref.shape[0]
    row_start = lax.axis_index("dap") * rows
    col_start = lax.axis_index("sub") * cols
    zlt_ref[...] = zl_ref[...].T
    proj_out_ref[...] = proj_ref[...].reshape(proj_out_ref.shape).astype(BF16)
    which = iota((pairs, residues), 0)
    place = iota((pairs, residues), 1)
    pick_row = (place == row_start + within(which, rows)).astype(BF16)
    pick_col = (place == col_start + over(which, rows)).astype(BF16)
    mask = mask_ref[...].astype(BF16)
    both = (dot(pick_row, mask) * dot(pick_col, mask)).astype(BF16)
    counts = dot(both, jnp.ones((mask.shape[1], LANES), BF16))
    inverse_ref[...] = 1.0 / jnp.maximum(counts, 1.0)
    live = jnp.broadcast_to(live_ref[...].astype(F32), (LANES, residues)).astype(BF16)
    chain = jnp.broadcast_to(chain_ref[...].astype(F32), (LANES, residues)).astype(BF16)
    live_out_ref[...] = dot_nt(pick_row, live) * dot_nt(pick_col, live)
    same = dot_nt(pick_row, chain) == dot_nt(pick_col, chain)
    pair = iota((pairs, LANES), 0)
    offset = (row_start + within(pair, rows)) - (col_start + over(pair, rows)) + REL_CLIP
    bucket = jnp.where(same, jnp.clip(offset, 0, 2 * REL_CLIP), 2 * REL_CLIP + 1)
    table_scr[...] = jnp.zeros_like(table_scr)
    table_scr[pl.ds(0, classes), :] = table_ref[...].astype(F32)
    onehot = (bucket == iota((pairs, LANES), 1)).astype(BF16)
    relative = dot(onehot, table_scr[...].astype(BF16))
    pair_scr[...] = pair_ref[...].reshape(pairs, LANES).astype(F32)
    for col in range(cols):
        here = slice(col * rows, (col + 1) * rows)
        base_ref[here, :] = relative[here] + pair_scr[pl.ds(col, rows, stride=cols), :]


def prepare(zl, mask, pair_input, residue_mask, chain_index, table, proj):
    rows, cols, channels = pair_input.shape
    pairs = rows * cols
    shape = jax.ShapeDtypeStruct((pairs, channels), F32)
    depth = proj.shape[0] * proj.shape[1]
    return pl.pallas_call(
        prepare_kernel,
        out_shape=(
            jax.ShapeDtypeStruct(zl.shape[::-1], BF16),
            shape,
            shape,
            shape,
            jax.ShapeDtypeStruct((depth, channels), BF16),
        ),
        in_specs=[vmem()] * 7,
        out_specs=[vmem()] * 5,
        scratch_shapes=[pltpu.VMEM((pairs, channels), F32), pltpu.VMEM((LANES, channels), F32)],
        compiler_params=pltpu.CompilerParams(vmem_limit_bytes=24 << 20),
        cost_estimate=pl.CostEstimate(
            flops=2 * pairs * 256 * 1024, bytes_accessed=2 << 20, transcendentals=0
        ),
    )(zl, mask, pair_input, residue_mask[None, :], chain_index[None, :], table, proj)


def pair_kernel(ratio, hidden, zlt_ref, *refs):
    zr_refs, refs = refs[:ratio], refs[ratio:]
    (base_ref, inverse_ref, live_ref, proj_ref, tl_ref, tr_ref,
     both_ref, one_ref, outer_scr, flat_scr, one_scr) = refs
    pairs, channels = base_ref.shape
    rows = zlt_ref.shape[0] // hidden
    rep = LANES // hidden
    me = lax.axis_index("dap")
    lane = iota((rows, LANES), 1)
    odd = (lane // hidden) % 2 == 1
    upper = lane // (2 * hidden) == 1
    half = 2 * hidden
    for step in range(ratio):
        block = lax.rem(me + step, ratio)
        outer = dot(zlt_ref[...], zr_refs[step][...])
        for group in range(rows // rep):
            outer_scr[group] = outer[:, group * LANES : (group + 1) * LANES]
        for group in range(rows // rep):
            for quad in range(hidden // rep):
                s0, s1, s2, s3 = (
                    outer_scr[group, pl.ds(quad * rep + k, rows, stride=hidden), :] for k in range(rep)
                )
                t0 = jnp.where(upper, pltpu.roll(s2, half, 1), s0)
                t1 = jnp.where(upper, pltpu.roll(s3, half, 1), s1)
                t2 = jnp.where(upper, s2, pltpu.roll(s0, half, 1))
                t3 = jnp.where(upper, s3, pltpu.roll(s1, half, 1))
                back = LANES - hidden
                found = (
                    jnp.where(odd, pltpu.roll(t1, hidden, 1), t0),
                    jnp.where(odd, t1, pltpu.roll(t0, back, 1)),
                    jnp.where(odd, pltpu.roll(t3, hidden, 1), t2),
                    jnp.where(odd, t3, pltpu.roll(t2, back, 1)),
                )
                for k in range(rep):
                    first = block * rows * rows + (group * rep + k) * rows
                    if ratio == 1:
                        first = (group * rep + k) * rows
                    else:
                        first = pl.multiple_of(first, rows)
                    flat_scr[pl.ds(first, rows), quad * LANES : (quad + 1) * LANES] = found[k].astype(BF16)
    outer_mean = dot(flat_scr[...], proj_ref[...]) * inverse_ref[...]
    one = (base_ref[...] + outer_mean).astype(BF16).astype(F32)
    one_scr[...] = one
    norm = layer_norm(one).astype(BF16)
    for side, weight in enumerate((tl_ref, tr_ref)):
        both = dot(norm, weight[...])
        factor = jax.nn.sigmoid(both[:, :channels]) * both[:, channels:] * live_ref[...]
        both_ref[side] = factor.astype(BF16)
    cols = pairs // rows
    for row in range(rows):
        one_ref[row * cols : (row + 1) * cols, :] = one_scr[pl.ds(row, cols, stride=rows), :].astype(BF16)


def pair_update(hidden, zlt, zrs, base, inverse, live, proj, triangle_left, triangle_right):
    pairs, channels = base.shape
    ratio = len(zrs)
    shape = jax.ShapeDtypeStruct((pairs, channels), BF16)
    return pl.pallas_call(
        functools.partial(pair_kernel, ratio, hidden),
        out_shape=(jax.ShapeDtypeStruct((2, pairs, channels), BF16), shape),
        in_specs=[vmem()] * (7 + ratio),
        out_specs=[vmem()] * 2,
        scratch_shapes=[
            pltpu.VMEM((zrs[0].shape[1] // LANES, zlt.shape[0], LANES), F32),
            pltpu.VMEM((pairs, proj.shape[0]), BF16),
            pltpu.VMEM((pairs, channels), F32),
        ],
        compiler_params=pltpu.CompilerParams(vmem_limit_bytes=32 << 20),
        cost_estimate=pl.CostEstimate(
            flops=2 * pairs * 1024 * 512, bytes_accessed=2 << 20, transcendentals=pairs * 256
        ),
    )(zlt, *zrs, base, inverse, live, proj, triangle_left, triangle_right)


def other(sub):
    return sub + 1 - 2 * (sub % 2)


def gate_kernel(one_ref, weight_ref, gate_ref):
    norm = layer_norm(one_ref[...].astype(F32)).astype(BF16)
    gate_ref[...] = jax.nn.sigmoid(dot(norm, weight_ref[...]))


def output_gate(one, weight):
    return pl.pallas_call(
        gate_kernel,
        out_shape=jax.ShapeDtypeStruct(one.shape, F32),
        in_specs=[vmem()] * 2,
        out_specs=vmem(),
        compiler_params=pltpu.CompilerParams(vmem_limit_bytes=4 << 20),
        cost_estimate=pl.CostEstimate(
            flops=2 * one.size * LANES, bytes_accessed=1 << 18, transcendentals=one.size
        ),
    )(one, weight)


SENDERS = ((0, 2, 1, 3), (2, 1, 3, 0), (3, 1, 2, 0), (1, 2, 0, 3))


def sender(a, b, subs, ratio):
    if (subs, ratio) == (4, 1):
        return SENDERS[b][a]
    return a // ratio


def sender_index(a, b, subs, ratio):
    if (subs, ratio) != (4, 1):
        return a // ratio
    found = 0
    for col, places in enumerate(SENDERS):
        for row, place in enumerate(places):
            found = jnp.where((a == row) & (b == col), place, found)
    return found


def triangle_kernel(subs, ratio, cols, *refs):
    twos = subs // 2
    lefts, refs = refs[:twos], refs[twos:]
    rights, refs = refs[: twos * ratio], refs[twos * ratio :]
    (one_ref, gate_ref, out_ref, up_ref, down_ref, result_ref, left_scr, right_scr, sum_scr) = refs
    pairs, channels = one_ref.shape
    rows = pairs // cols
    here, there = lax.axis_index("dap"), lax.axis_index("sub")
    first_sub = sender_index(here, there, subs, ratio)
    for step in range(twos):
        sub = lax.rem(there + 2 * step, subs)
        left_scr[sub] = lefts[step][0].astype(F32)
        left_scr[other(sub)] = lefts[step][1].astype(F32)
    for turn in range(ratio):
        block = lax.rem(here + turn, ratio)
        for step in range(twos):
            sub = lax.rem(first_sub + 2 * step, subs)
            right_scr[block * subs + sub] = rights[turn * twos + step][0].astype(F32)
            right_scr[block * subs + other(sub)] = rights[turn * twos + step][1].astype(F32)
    for block in range(ratio):
        totals = tuple(jnp.zeros((rows, channels), F32) for _ in range(rows))
        for sub in range(subs):

            def body(k, totals, sub=sub, block=block):
                first = pl.multiple_of(k * rows, rows)
                right = right_scr[block * subs + sub, pl.ds(first, rows), :]
                return tuple(
                    totals[i] + left_scr[sub, pl.ds(first + i, 1), :] * right for i in range(rows)
                )

            totals = lax.fori_loop(0, cols, body, totals, unroll=4)
        for i in range(rows):
            sum_scr[i * cols + block * rows : i * cols + (block + 1) * rows, :] = totals[i]
    one = one_ref[...].astype(F32)
    hidden = layer_norm(sum_scr[...].astype(BF16).astype(F32)).astype(BF16)
    two = (one + gate_ref[...] * dot(hidden, out_ref[...])).astype(BF16).astype(F32)
    wide = jnp.maximum(dot(layer_norm(two).astype(BF16), up_ref[...]), 0.0).astype(BF16)
    result = (two + dot(wide, down_ref[...])).astype(BF16)
    result_ref[...] = result.reshape(result_ref.shape)


def triangle_update(lefts, rights, one, cols, gate, out, up, down):
    pairs, channels = one.shape
    rows = pairs // cols
    subs = 2 * len(lefts)
    ratio = len(rights) // len(lefts)
    return pl.pallas_call(
        functools.partial(triangle_kernel, subs, ratio, cols),
        out_shape=jax.ShapeDtypeStruct((rows, cols, channels), BF16),
        in_specs=[vmem()] * (len(lefts) + len(rights) + 5),
        out_specs=vmem(),
        scratch_shapes=[
            pltpu.VMEM((subs, pairs, channels), F32),
            pltpu.VMEM((subs * ratio, pairs, channels), F32),
            pltpu.VMEM((pairs, channels), F32),
        ],
        compiler_params=pltpu.CompilerParams(vmem_limit_bytes=(16 << 20) if ratio == 1 else (50 << 20)),
        cost_estimate=pl.CostEstimate(
            flops=2 * pairs * channels * 2048, bytes_accessed=2 << 20, transcendentals=pairs * 128
        ),
    )(*lefts, *rights, one, gate, out, up, down)


def per_device(
    alignment,
    alignment_mask,
    pair_input,
    residue_mask,
    chain_index,
    outer_left,
    outer_right,
    outer_proj,
    triangle_left,
    triangle_right,
    triangle_gate,
    triangle_out,
    relative_table,
    transition_up,
    transition_down,
):
    daps, subs = lax.axis_size("dap"), lax.axis_size("sub")
    ratio = daps // subs
    cols = pair_input.shape[1]

    def fetch(values, source):
        perm = []
        for a in range(daps):
            for b in range(subs):
                dap, sub = source(a, b)
                perm.append((dap * subs + sub, a * subs + b))
        return lax.ppermute(values, ("dap", "sub"), perm)

    def owner(a, b, turn):
        return ratio * b + (a + turn) % ratio

    mask = alignment_mask.T
    zr = factor(alignment, mask, outer_right.T)
    zrs = [
        fetch(zr, lambda a, b, turn=turn: (owner(a, b, turn), sender(a, b, subs, ratio)))
        for turn in range(ratio)
    ]
    zl = factor(alignment, mask, outer_left.T)
    zlt, base, inverse, live, proj = prepare(
        zl, mask, pair_input, residue_mask, chain_index, relative_table, outer_proj
    )
    own, one = pair_update(
        outer_left.shape[1], zlt, zrs, base, inverse, live, proj, triangle_left, triangle_right
    )
    near = fetch(own, lambda a, b: (a, other(b)))
    left = jnp.stack([own[0], near[0]])
    right = jnp.stack([own[1], near[1]])
    rights = [
        fetch(
            right,
            lambda a, b, t=turn, m=step: (
                owner(a, b, t), (sender(a, b, subs, ratio) + 2 * m) % subs
            ),
        )
        for turn in range(ratio)
        for step in range(subs // 2)
    ]
    lefts = [left] + [
        fetch(left, lambda a, b, m=step: (a, (b + 2 * m) % subs)) for step in range(1, subs // 2)
    ]
    gate = output_gate(one, triangle_gate)
    return triangle_update(
        lefts, rights, one, cols, gate, triangle_out, transition_up, transition_down
    )


def solution(mesh):
    in_specs = (
        P("parts", "dap", None),
        P("parts", None),
        P(("parts", "dap"), "sub", None),
        P("parts"),
        P("parts"),
        P(),
        P(),
        P(),
        P(),
        P(),
        P(),
        P(),
        P(),
        P(),
        P(),
    )
    out_specs = P(("parts", "dap"), "sub", None)
    return jax.shard_map(
        per_device, mesh=mesh, in_specs=in_specs, out_specs=out_specs, check_vma=False
    )
```

```python
import functools

import jax
import jax.numpy as jnp
from jax import lax
from jax.experimental import pallas as pl
from jax.experimental.pallas import tpu as pltpu
from jax.sharding import PartitionSpec as P

REL_CLIP = 32
LANES = 128
PIECE = 16
STEPS = 4
EPSILON = 1e-05
BF16 = jnp.bfloat16
F32 = jnp.float32
NT = (((1,), (1,)), ((), ()))
TN = (((0,), (0,)), ((), ()))


def layer_norm(values):
    average = jnp.mean(values, axis=-1, keepdims=True)
    centered = values - average
    spread = jnp.mean(centered * centered, axis=-1, keepdims=True)
    return centered * lax.rsqrt(spread + EPSILON)


def dot(left, right):
    return jnp.dot(left, right, preferred_element_type=F32)


def dot_nt(left, right):
    return lax.dot_general(left, right, NT, preferred_element_type=F32)


def dot_tn(left, right):
    return lax.dot_general(left, right, TN, preferred_element_type=F32)


def iota(shape, dim):
    return lax.broadcasted_iota(jnp.int32, shape, dim)


def vmem():
    return pl.BlockSpec(memory_space=pltpu.VMEM)


def over(index, size):
    return lax.shift_right_logical(index, size.bit_length() - 1)


def within(index, size):
    return lax.bitwise_and(index, size - 1)


def factor_kernel(x_any, mask_ref, weight_ref, z_ref, x_scr, y_scr, sems):
    halves, seqs, rows, _ = x_scr.shape
    hidden, channels = weight_ref.shape
    rep = LANES // hidden
    groups = rows // rep
    residues = mask_ref.shape[0]
    width = rows * hidden
    step = seqs // STEPS
    copies = []
    for turn in range(STEPS):
        part = pl.ds(turn * step, step)
        for half in range(halves):
            source = x_any.at[part, :, pl.ds(half * LANES, LANES)]
            copies.append(pltpu.make_async_copy(source, x_scr.at[half, part], sems.at[turn, half]))
            copies[-1].start()
    weight = jnp.concatenate([weight_ref[...]] * rep, axis=0).T
    w = jnp.concatenate([weight, jnp.ones((channels, LANES), BF16)], axis=1)
    sums = dot(jnp.ones((8, channels), BF16), w)[:1, :LANES]
    start = lax.axis_index("dap") * rows
    spread = iota((residues, width), 0) == start + over(iota((residues, width), 1), hidden)
    live = dot_tn(mask_ref[...].astype(BF16), spread.astype(BF16))
    to, at = iota((groups * PIECE, PIECE * rows), 0), iota((groups * PIECE, PIECE * rows), 1)
    gather = within(to, PIECE) == over(at, rows)
    gather = (gather & (over(to, PIECE) == over(within(at, rows), rep))).astype(BF16)
    own = over(iota((8, LANES), 1), hidden) == within(iota((8, LANES), 0), rep)
    own = own.astype(F32)
    ones = jnp.ones((LANES, LANES), BF16)
    for turn in range(STEPS):
        x = []
        for half in range(halves):
            copies[turn * halves + half].wait()
            x.append(x_scr[half, turn * step : (turn + 1) * step].reshape(step * rows, LANES))
        y = dot(jnp.concatenate(x, axis=1), w)
        mean = y[:, LANES:] * (1.0 / channels)
        square = jnp.zeros_like(mean)
        for half in range(halves):
            centered = x[half].astype(F32) - mean
            square = square + centered * centered
        spread = dot(square.astype(BF16), ones)
        scale = lax.rsqrt(spread * (1.0 / channels) + EPSILON).reshape(-1, 8, LANES) * own[None]
        scaled = (y[:, :LANES] - mean * sums) * scale.reshape(mean.shape)
        y_scr[turn * step * rows : (turn + 1) * step * rows, :] = scaled.astype(BF16)
        for piece in range(turn * step // PIECE, (turn + 1) * step // PIECE):
            z = dot(gather, y_scr[piece * PIECE * rows : (piece + 1) * PIECE * rows, :])
            here = slice(piece * PIECE, (piece + 1) * PIECE)
            for group in range(groups):
                lanes = slice(group * LANES, (group + 1) * LANES)
                part = z[group * PIECE : (group + 1) * PIECE]
                z_ref[group, here, :] = (part * live[here, lanes]).astype(BF16)


def factor(alignment, mask, weight):
    seqs, rows, channels = alignment.shape
    hidden = weight.shape[0]
    return pl.pallas_call(
        factor_kernel,
        out_shape=jax.ShapeDtypeStruct((rows * hidden // LANES, seqs, LANES), BF16),
        in_specs=[pl.BlockSpec(memory_space=pl.ANY), vmem(), vmem()],
        out_specs=vmem(),
        scratch_shapes=[
            pltpu.VMEM((channels // LANES, seqs, rows, LANES), BF16),
            pltpu.VMEM((seqs * rows, LANES), BF16),
            pltpu.SemaphoreType.DMA((STEPS, channels // LANES)),
        ],
        compiler_params=pltpu.CompilerParams(vmem_limit_bytes=119 << 19),
        cost_estimate=pl.CostEstimate(
            flops=2 * seqs * rows * channels * 512, bytes_accessed=4 << 20, transcendentals=0
        ),
    )(alignment, mask, weight)


def prepare_kernel(
    zl_ref, mask_ref, pair_ref, live_ref, chain_ref, table_ref, proj_ref,
    zlt_ref, base_ref, inverse_ref, live_out_ref, proj_out_ref, pair_scr, table_scr,
):
    rows, cols, _ = pair_ref.shape
    pairs = rows * cols
    residues = mask_ref.shape[0]
    classes = table_ref.shape[0]
    row_start = lax.axis_index("dap") * rows
    col_start = lax.axis_index("sub") * cols
    for group in range(zl_ref.shape[0]):
        turned = zl_ref[group].T
        for half in range(zlt_ref.shape[0]):
            lanes = slice(half * LANES, (half + 1) * LANES)
            zlt_ref[half, group * LANES : (group + 1) * LANES, :] = turned[:, lanes]
    proj_out_ref[...] = proj_ref[...].reshape(proj_out_ref.shape).astype(BF16)
    which = iota((pairs, residues), 0)
    place = iota((pairs, residues), 1)
    pick_row = (place == row_start + within(which, rows)).astype(BF16)
    pick_col = (place == col_start + over(which, rows)).astype(BF16)
    mask = mask_ref[...].astype(BF16)
    both = (dot(pick_row, mask) * dot(pick_col, mask)).astype(BF16)
    counts = dot(both, jnp.ones((mask.shape[1], LANES), BF16))
    inverse_ref[...] = 1.0 / jnp.maximum(counts, 1.0)
    live = jnp.broadcast_to(live_ref[...].astype(F32), (LANES, residues)).astype(BF16)
    chain = jnp.broadcast_to(chain_ref[...].astype(F32), (LANES, residues)).astype(BF16)
    live_out_ref[...] = dot_nt(pick_row, live) * dot_nt(pick_col, live)
    same = dot_nt(pick_row, chain) == dot_nt(pick_col, chain)
    pair = iota((pairs, LANES), 0)
    offset = (row_start + within(pair, rows)) - (col_start + over(pair, rows)) + REL_CLIP
    bucket = jnp.where(same, jnp.clip(offset, 0, 2 * REL_CLIP), 2 * REL_CLIP + 1)
    table_scr[...] = jnp.zeros_like(table_scr)
    table_scr[pl.ds(0, classes), :] = table_ref[...].astype(F32)
    onehot = (bucket == iota((pairs, LANES), 1)).astype(BF16)
    relative = dot(onehot, table_scr[...].astype(BF16))
    pair_scr[...] = pair_ref[...].reshape(pairs, LANES).astype(F32)
    for col in range(cols):
        here = slice(col * rows, (col + 1) * rows)
        base_ref[here, :] = relative[here] + pair_scr[pl.ds(col, rows, stride=cols), :]


def prepare(zl, mask, pair_input, residue_mask, chain_index, table, proj):
    rows, cols, channels = pair_input.shape
    pairs = rows * cols
    shape = jax.ShapeDtypeStruct((pairs, channels), F32)
    depth = proj.shape[0] * proj.shape[1]
    return pl.pallas_call(
        prepare_kernel,
        out_shape=(
            jax.ShapeDtypeStruct((zl.shape[1] // LANES, zl.shape[0] * LANES, LANES), BF16),
            shape,
            shape,
            shape,
            jax.ShapeDtypeStruct((depth, channels), BF16),
        ),
        in_specs=[vmem()] * 7,
        out_specs=[vmem()] * 5,
        scratch_shapes=[pltpu.VMEM((pairs, channels), F32), pltpu.VMEM((LANES, channels), F32)],
        compiler_params=pltpu.CompilerParams(vmem_limit_bytes=24 << 20),
        cost_estimate=pl.CostEstimate(
            flops=2 * pairs * 256 * 1024, bytes_accessed=2 << 20, transcendentals=0
        ),
    )(zl, mask, pair_input, residue_mask[None, :], chain_index[None, :], table, proj)


def pair_kernel(ratio, hidden, zlt_ref, *refs):
    zr_refs, refs = refs[:ratio], refs[ratio:]
    (base_ref, inverse_ref, live_ref, proj_ref, tl_ref, tr_ref,
     both_ref, one_ref, outer_scr, flat_scr, one_scr) = refs
    pairs, channels = base_ref.shape
    rows = zlt_ref.shape[1] // hidden
    rep = LANES // hidden
    me = lax.axis_index("dap")
    lane = iota((rows, LANES), 1)
    odd = (lane // hidden) % 2 == 1
    upper = lane // (2 * hidden) == 1
    half = 2 * hidden
    left = jnp.concatenate([zlt_ref[part] for part in range(zlt_ref.shape[0])], axis=1)
    for step in range(ratio):
        block = lax.rem(me + step, ratio)
        right = [zr_refs[step][group] for group in range(rows // rep)]
        outer = dot(left, jnp.concatenate(right, axis=1))
        for group in range(rows // rep):
            outer_scr[group] = outer[:, group * LANES : (group + 1) * LANES]
        for group in range(rows // rep):
            for quad in range(hidden // rep):
                s0, s1, s2, s3 = (
                    outer_scr[group, pl.ds(quad * rep + k, rows, stride=hidden), :] for k in range(rep)
                )
                t0 = jnp.where(upper, pltpu.roll(s2, half, 1), s0)
                t1 = jnp.where(upper, pltpu.roll(s3, half, 1), s1)
                t2 = jnp.where(upper, s2, pltpu.roll(s0, half, 1))
                t3 = jnp.where(upper, s3, pltpu.roll(s1, half, 1))
                back = LANES - hidden
                found = (
                    jnp.where(odd, pltpu.roll(t1, hidden, 1), t0),
                    jnp.where(odd, t1, pltpu.roll(t0, back, 1)),
                    jnp.where(odd, pltpu.roll(t3, hidden, 1), t2),
                    jnp.where(odd, t3, pltpu.roll(t2, back, 1)),
                )
                for k in range(rep):
                    first = block * rows * rows + (group * rep + k) * rows
                    if ratio == 1:
                        first = (group * rep + k) * rows
                    else:
                        first = pl.multiple_of(first, rows)
                    flat_scr[quad, pl.ds(first, rows), :] = found[k].astype(BF16)
    flat = jnp.concatenate([flat_scr[quad] for quad in range(flat_scr.shape[0])], axis=1)
    outer_mean = dot(flat, proj_ref[...]) * inverse_ref[...]
    one = (base_ref[...] + outer_mean).astype(BF16).astype(F32)
    one_scr[...] = one
    norm = layer_norm(one).astype(BF16)
    for side, weight in enumerate((tl_ref, tr_ref)):
        both = dot(norm, weight[...])
        factor = jax.nn.sigmoid(both[:, :channels]) * both[:, channels:] * live_ref[...]
        both_ref[side] = factor.astype(BF16)
    cols = pairs // rows
    for row in range(rows):
        one_ref[row * cols : (row + 1) * cols, :] = one_scr[pl.ds(row, cols, stride=rows), :].astype(BF16)


def pair_update(hidden, zlt, zrs, base, inverse, live, proj, triangle_left, triangle_right):
    pairs, channels = base.shape
    ratio = len(zrs)
    shape = jax.ShapeDtypeStruct((pairs, channels), BF16)
    return pl.pallas_call(
        functools.partial(pair_kernel, ratio, hidden),
        out_shape=(jax.ShapeDtypeStruct((2, pairs, channels), BF16), shape),
        in_specs=[vmem()] * (7 + ratio),
        out_specs=[vmem()] * 2,
        scratch_shapes=[
            pltpu.VMEM((zrs[0].shape[0], zlt.shape[1], LANES), F32),
            pltpu.VMEM((proj.shape[0] // LANES, pairs, LANES), BF16),
            pltpu.VMEM((pairs, channels), F32),
        ],
        compiler_params=pltpu.CompilerParams(vmem_limit_bytes=32 << 20),
        cost_estimate=pl.CostEstimate(
            flops=2 * pairs * 1024 * 512, bytes_accessed=2 << 20, transcendentals=pairs * 256
        ),
    )(zlt, *zrs, base, inverse, live, proj, triangle_left, triangle_right)


def other(sub):
    return sub + 1 - 2 * (sub % 2)


def gate_kernel(one_ref, weight_ref, gate_ref):
    norm = layer_norm(one_ref[...].astype(F32)).astype(BF16)
    gate_ref[...] = jax.nn.sigmoid(dot(norm, weight_ref[...]))


def output_gate(one, weight):
    return pl.pallas_call(
        gate_kernel,
        out_shape=jax.ShapeDtypeStruct(one.shape, F32),
        in_specs=[vmem()] * 2,
        out_specs=vmem(),
        compiler_params=pltpu.CompilerParams(vmem_limit_bytes=4 << 20),
        cost_estimate=pl.CostEstimate(
            flops=2 * one.size * LANES, bytes_accessed=1 << 18, transcendentals=one.size
        ),
    )(one, weight)


SENDERS = ((0, 2, 1, 3), (2, 1, 3, 0), (3, 1, 2, 0), (1, 2, 0, 3))


def sender(a, b, subs, ratio):
    if (subs, ratio) == (4, 1):
        return SENDERS[b][a]
    return a // ratio


def sender_index(a, b, subs, ratio):
    if (subs, ratio) != (4, 1):
        return a // ratio
    found = 0
    for col, places in enumerate(SENDERS):
        for row, place in enumerate(places):
            found = jnp.where((a == row) & (b == col), place, found)
    return found


def triangle_kernel(subs, ratio, cols, *refs):
    twos = subs // 2
    lefts, refs = refs[:twos], refs[twos:]
    rights, refs = refs[: twos * ratio], refs[twos * ratio :]
    (one_ref, gate_ref, out_ref, up_ref, down_ref, result_ref, left_scr, right_scr, sum_scr) = refs
    pairs, channels = one_ref.shape
    rows = pairs // cols
    here, there = lax.axis_index("dap"), lax.axis_index("sub")
    first_sub = sender_index(here, there, subs, ratio)
    for step in range(twos):
        sub = lax.rem(there + 2 * step, subs)
        left_scr[sub] = lefts[step][0].astype(F32)
        left_scr[other(sub)] = lefts[step][1].astype(F32)
    for turn in range(ratio):
        block = lax.rem(here + turn, ratio)
        for step in range(twos):
            sub = lax.rem(first_sub + 2 * step, subs)
            right_scr[block * subs + sub] = rights[turn * twos + step][0].astype(F32)
            right_scr[block * subs + other(sub)] = rights[turn * twos + step][1].astype(F32)
    for block in range(ratio):
        totals = tuple(jnp.zeros((rows, channels), F32) for _ in range(rows))
        for sub in range(subs):

            def body(k, totals, sub=sub, block=block):
                first = pl.multiple_of(k * rows, rows)
                right = right_scr[block * subs + sub, pl.ds(first, rows), :]
                return tuple(
                    totals[i] + left_scr[sub, pl.ds(first + i, 1), :] * right for i in range(rows)
                )

            totals = lax.fori_loop(0, cols, body, totals, unroll=4)
        for i in range(rows):
            sum_scr[i * cols + block * rows : i * cols + (block + 1) * rows, :] = totals[i]
    one = one_ref[...].astype(F32)
    hidden = layer_norm(sum_scr[...].astype(BF16).astype(F32)).astype(BF16)
    two = (one + gate_ref[...] * dot(hidden, out_ref[...])).astype(BF16).astype(F32)
    wide = jnp.maximum(dot(layer_norm(two).astype(BF16), up_ref[...]), 0.0).astype(BF16)
    result = (two + dot(wide, down_ref[...])).astype(BF16)
    result_ref[...] = result.reshape(result_ref.shape)


def triangle_update(lefts, rights, one, cols, gate, out, up, down):
    pairs, channels = one.shape
    rows = pairs // cols
    subs = 2 * len(lefts)
    ratio = len(rights) // len(lefts)
    return pl.pallas_call(
        functools.partial(triangle_kernel, subs, ratio, cols),
        out_shape=jax.ShapeDtypeStruct((rows, cols, channels), BF16),
        in_specs=[vmem()] * (len(lefts) + len(rights) + 5),
        out_specs=vmem(),
        scratch_shapes=[
            pltpu.VMEM((subs, pairs, channels), F32),
            pltpu.VMEM((subs * ratio, pairs, channels), F32),
            pltpu.VMEM((pairs, channels), F32),
        ],
        compiler_params=pltpu.CompilerParams(vmem_limit_bytes=(16 << 20) if ratio == 1 else (50 << 20)),
        cost_estimate=pl.CostEstimate(
            flops=2 * pairs * channels * 2048, bytes_accessed=2 << 20, transcendentals=pairs * 128
        ),
    )(*lefts, *rights, one, gate, out, up, down)


def per_device(
    alignment,
    alignment_mask,
    pair_input,
    residue_mask,
    chain_index,
    outer_left,
    outer_right,
    outer_proj,
    triangle_left,
    triangle_right,
    triangle_gate,
    triangle_out,
    relative_table,
    transition_up,
    transition_down,
):
    daps, subs = lax.axis_size("dap"), lax.axis_size("sub")
    ratio = daps // subs
    cols = pair_input.shape[1]

    def fetch(values, source):
        perm = []
        for a in range(daps):
            for b in range(subs):
                dap, sub = source(a, b)
                perm.append((dap * subs + sub, a * subs + b))
        return lax.ppermute(values, ("dap", "sub"), perm)

    def owner(a, b, turn):
        return ratio * b + (a + turn) % ratio

    mask = alignment_mask.T
    zr = factor(alignment, mask, outer_right.T)
    zrs = [
        fetch(zr, lambda a, b, turn=turn: (owner(a, b, turn), sender(a, b, subs, ratio)))
        for turn in range(ratio)
    ]
    zl = factor(alignment, mask, outer_left.T)
    zlt, base, inverse, live, proj = prepare(
        zl, mask, pair_input, residue_mask, chain_index, relative_table, outer_proj
    )
    own, one = pair_update(
        outer_left.shape[1], zlt, zrs, base, inverse, live, proj, triangle_left, triangle_right
    )
    near = fetch(own, lambda a, b: (a, other(b)))
    left = jnp.stack([own[0], near[0]])
    right = jnp.stack([own[1], near[1]])
    rights = [
        fetch(
            right,
            lambda a, b, t=turn, m=step: (
                owner(a, b, t), (sender(a, b, subs, ratio) + 2 * m) % subs
            ),
        )
        for turn in range(ratio)
        for step in range(subs // 2)
    ]
    lefts = [left] + [
        fetch(left, lambda a, b, m=step: (a, (b + 2 * m) % subs)) for step in range(1, subs // 2)
    ]
    gate = output_gate(one, triangle_gate)
    return triangle_update(
        lefts, rights, one, cols, gate, triangle_out, transition_up, transition_down
    )


def solution(mesh):
    in_specs = (
        P("parts", "dap", None),
        P("parts", None),
        P(("parts", "dap"), "sub", None),
        P("parts"),
        P("parts"),
        P(),
        P(),
        P(),
        P(),
        P(),
        P(),
        P(),
        P(),
        P(),
        P(),
    )
    out_specs = P(("parts", "dap"), "sub", None)
    return jax.shard_map(
        per_device, mesh=mesh, in_specs=in_specs, out_specs=out_specs, check_vma=False
    )
```

```python
import functools

import jax
import jax.numpy as jnp
from jax import lax
from jax.experimental import pallas as pl
from jax.experimental.pallas import tpu as pltpu
from jax.sharding import PartitionSpec as P

REL_CLIP = 32
LANES = 128
PIECE = 16
STEPS = 4
TILE = 64
EPSILON = 1e-05
BF16 = jnp.bfloat16
F32 = jnp.float32
NT = (((1,), (1,)), ((), ()))
TN = (((0,), (0,)), ((), ()))


def layer_norm(values):
    average = jnp.mean(values, axis=-1, keepdims=True)
    centered = values - average
    spread = jnp.mean(centered * centered, axis=-1, keepdims=True)
    return centered * lax.rsqrt(spread + EPSILON)


def dot(left, right):
    return jnp.dot(left, right, preferred_element_type=F32)


def dot_nt(left, right):
    return lax.dot_general(left, right, NT, preferred_element_type=F32)


def dot_tn(left, right):
    return lax.dot_general(left, right, TN, preferred_element_type=F32)


def iota(shape, dim):
    return lax.broadcasted_iota(jnp.int32, shape, dim)


def vmem():
    return pl.BlockSpec(memory_space=pltpu.VMEM)


def over(index, size):
    return lax.shift_right_logical(index, size.bit_length() - 1)


def within(index, size):
    return lax.bitwise_and(index, size - 1)


def factor_kernel(
    x_any, mask_ref, weight_ref, z_ref,
    x_scr, y_scr, mean_scr, square_scr, spread_scr, out_scr, live_scr, sems,
):
    halves, seqs, rows, _ = x_scr.shape
    hidden, channels = weight_ref.shape
    rep = LANES // hidden
    groups = rows // rep
    residues = mask_ref.shape[0]
    width = rows * hidden
    step = seqs // STEPS
    copies = []
    for turn in range(STEPS):
        part = pl.ds(turn * step, step)
        for half in range(halves):
            source = x_any.at[part, :, pl.ds(half * LANES, LANES)]
            copies.append(pltpu.make_async_copy(source, x_scr.at[half, part], sems.at[turn, half]))
            copies[-1].start()
    weight = jnp.concatenate([weight_ref[...]] * rep, axis=0).T
    w = jnp.concatenate([weight, jnp.ones((channels, LANES), BF16)], axis=1)
    sums = dot(jnp.ones((8, channels), BF16), w)[:1, :LANES]
    start = lax.axis_index("dap") * rows
    spread = iota((residues, width), 0) == start + over(iota((residues, width), 1), hidden)
    live_scr[...] = dot_tn(mask_ref[...].astype(BF16), spread.astype(BF16))
    to, at = iota((groups * PIECE, PIECE * rows), 0), iota((groups * PIECE, PIECE * rows), 1)
    gather = within(to, PIECE) == over(at, rows)
    gather = (gather & (over(to, PIECE) == over(within(at, rows), rep))).astype(BF16)
    own = over(iota((TILE, LANES), 1), hidden) == within(iota((TILE, LANES), 0), rep)
    own = own.astype(F32)
    ones = jnp.ones((LANES, LANES), BF16)

    def square(tile, _):
        here = pl.ds(pl.multiple_of(tile * TILE, TILE), TILE)
        mean = mean_scr[here, :] * (1.0 / channels)
        total = jnp.zeros_like(mean)
        for half in range(halves):
            part = x_scr[half, pl.ds(tile * (TILE // rows), TILE // rows)].reshape(TILE, LANES)
            centered = part.astype(F32) - mean
            total = total + centered * centered
        square_scr[here, :] = total.astype(BF16)
        return _

    def normalise(tile, _):
        here = pl.ds(pl.multiple_of(tile * TILE, TILE), TILE)
        scale = lax.rsqrt(spread_scr[here, :] * (1.0 / channels) + EPSILON) * own
        mean = mean_scr[here, :] * (1.0 / channels)
        out_scr[here, :] = ((y_scr[here, :] - mean * sums) * scale).astype(BF16)
        return _

    tiles = step * rows // TILE
    for turn in range(STEPS):
        x = []
        for half in range(halves):
            copies[turn * halves + half].wait()
            x.append(x_scr[half, turn * step : (turn + 1) * step].reshape(step * rows, LANES))
        y = dot(jnp.concatenate(x, axis=1), w)
        here = slice(turn * step * rows, (turn + 1) * step * rows)
        y_scr[here, :] = y[:, :LANES]
        mean_scr[here, :] = y[:, LANES:]
        lax.fori_loop(turn * tiles, (turn + 1) * tiles, square, None, unroll=4)
    for turn in range(STEPS):
        here = slice(turn * step * rows, (turn + 1) * step * rows)
        spread_scr[here, :] = dot(square_scr[here, :], ones)
    lax.fori_loop(0, STEPS * tiles, normalise, None, unroll=4)
    for piece in range(seqs // PIECE):
        z = dot(gather, out_scr[piece * PIECE * rows : (piece + 1) * PIECE * rows, :])
        here = slice(piece * PIECE, (piece + 1) * PIECE)
        for group in range(groups):
            lanes = slice(group * LANES, (group + 1) * LANES)
            part = z[group * PIECE : (group + 1) * PIECE]
            z_ref[group, here, :] = (part * live_scr[here, lanes]).astype(BF16)


def factor(alignment, mask, weight):
    seqs, rows, channels = alignment.shape
    hidden = weight.shape[0]
    return pl.pallas_call(
        factor_kernel,
        out_shape=jax.ShapeDtypeStruct((rows * hidden // LANES, seqs, LANES), BF16),
        in_specs=[pl.BlockSpec(memory_space=pl.ANY), vmem(), vmem()],
        out_specs=vmem(),
        scratch_shapes=[
            pltpu.VMEM((channels // LANES, seqs, rows, LANES), BF16),
            pltpu.VMEM((seqs * rows, LANES), F32),
            pltpu.VMEM((seqs * rows, LANES), F32),
            pltpu.VMEM((seqs * rows, LANES), BF16),
            pltpu.VMEM((seqs * rows, LANES), F32),
            pltpu.VMEM((seqs * rows, LANES), BF16),
            pltpu.VMEM((seqs, rows * hidden), F32),
            pltpu.SemaphoreType.DMA((STEPS, channels // LANES)),
        ],
        compiler_params=pltpu.CompilerParams(vmem_limit_bytes=119 << 19),
        cost_estimate=pl.CostEstimate(
            flops=2 * seqs * rows * channels * 512, bytes_accessed=4 << 20, transcendentals=0
        ),
    )(alignment, mask, weight)


def prepare_kernel(
    zl_ref, mask_ref, pair_ref, live_ref, chain_ref, table_ref, proj_ref,
    zlt_ref, base_ref, inverse_ref, live_out_ref, proj_out_ref, pair_scr, table_scr,
):
    rows, cols, _ = pair_ref.shape
    pairs = rows * cols
    residues = mask_ref.shape[0]
    classes = table_ref.shape[0]
    row_start = lax.axis_index("dap") * rows
    col_start = lax.axis_index("sub") * cols
    for group in range(zl_ref.shape[0]):
        turned = zl_ref[group].T
        for half in range(zlt_ref.shape[0]):
            lanes = slice(half * LANES, (half + 1) * LANES)
            zlt_ref[half, group * LANES : (group + 1) * LANES, :] = turned[:, lanes]
    proj_out_ref[...] = proj_ref[...].reshape(proj_out_ref.shape).astype(BF16)
    which = iota((pairs, residues), 0)
    place = iota((pairs, residues), 1)
    pick_row = (place == row_start + within(which, rows)).astype(BF16)
    pick_col = (place == col_start + over(which, rows)).astype(BF16)
    mask = mask_ref[...].astype(BF16)
    both = (dot(pick_row, mask) * dot(pick_col, mask)).astype(BF16)
    counts = dot(both, jnp.ones((mask.shape[1], LANES), BF16))
    inverse_ref[...] = 1.0 / jnp.maximum(counts, 1.0)
    live = jnp.broadcast_to(live_ref[...].astype(F32), (LANES, residues)).astype(BF16)
    chain = jnp.broadcast_to(chain_ref[...].astype(F32), (LANES, residues)).astype(BF16)
    live_out_ref[...] = dot_nt(pick_row, live) * dot_nt(pick_col, live)
    same = dot_nt(pick_row, chain) == dot_nt(pick_col, chain)
    pair = iota((pairs, LANES), 0)
    offset = (row_start + within(pair, rows)) - (col_start + over(pair, rows)) + REL_CLIP
    bucket = jnp.where(same, jnp.clip(offset, 0, 2 * REL_CLIP), 2 * REL_CLIP + 1)
    table_scr[...] = jnp.zeros_like(table_scr)
    table_scr[pl.ds(0, classes), :] = table_ref[...].astype(F32)
    onehot = (bucket == iota((pairs, LANES), 1)).astype(BF16)
    relative = dot(onehot, table_scr[...].astype(BF16))
    pair_scr[...] = pair_ref[...].reshape(pairs, LANES).astype(F32)
    for col in range(cols):
        here = slice(col * rows, (col + 1) * rows)
        base_ref[here, :] = relative[here] + pair_scr[pl.ds(col, rows, stride=cols), :]


def prepare(zl, mask, pair_input, residue_mask, chain_index, table, proj):
    rows, cols, channels = pair_input.shape
    pairs = rows * cols
    shape = jax.ShapeDtypeStruct((pairs, channels), F32)
    depth = proj.shape[0] * proj.shape[1]
    return pl.pallas_call(
        prepare_kernel,
        out_shape=(
            jax.ShapeDtypeStruct((zl.shape[1] // LANES, zl.shape[0] * LANES, LANES), BF16),
            shape,
            shape,
            shape,
            jax.ShapeDtypeStruct((depth, channels), BF16),
        ),
        in_specs=[vmem()] * 7,
        out_specs=[vmem()] * 5,
        scratch_shapes=[pltpu.VMEM((pairs, channels), F32), pltpu.VMEM((LANES, channels), F32)],
        compiler_params=pltpu.CompilerParams(vmem_limit_bytes=24 << 20),
        cost_estimate=pl.CostEstimate(
            flops=2 * pairs * 256 * 1024, bytes_accessed=2 << 20, transcendentals=0
        ),
    )(zl, mask, pair_input, residue_mask[None, :], chain_index[None, :], table, proj)


def pair_kernel(ratio, hidden, zlt_ref, *refs):
    zr_refs, refs = refs[:ratio], refs[ratio:]
    (base_ref, inverse_ref, live_ref, proj_ref, tl_ref, tr_ref,
     both_ref, one_ref, outer_scr, flat_scr, one_scr) = refs
    pairs, channels = base_ref.shape
    rows = zlt_ref.shape[1] // hidden
    rep = LANES // hidden
    me = lax.axis_index("dap")
    lane = iota((rows, LANES), 1)
    odd = (lane // hidden) % 2 == 1
    upper = lane // (2 * hidden) == 1
    half = 2 * hidden
    left = jnp.concatenate([zlt_ref[part] for part in range(zlt_ref.shape[0])], axis=1)
    for step in range(ratio):
        block = lax.rem(me + step, ratio)
        right = [zr_refs[step][group] for group in range(rows // rep)]
        outer = dot(left, jnp.concatenate(right, axis=1))
        for group in range(rows // rep):
            outer_scr[group] = outer[:, group * LANES : (group + 1) * LANES]
        for group in range(rows // rep):
            for quad in range(hidden // rep):
                s0, s1, s2, s3 = (
                    outer_scr[group, pl.ds(quad * rep + k, rows, stride=hidden), :] for k in range(rep)
                )
                t0 = jnp.where(upper, pltpu.roll(s2, half, 1), s0)
                t1 = jnp.where(upper, pltpu.roll(s3, half, 1), s1)
                t2 = jnp.where(upper, s2, pltpu.roll(s0, half, 1))
                t3 = jnp.where(upper, s3, pltpu.roll(s1, half, 1))
                back = LANES - hidden
                found = (
                    jnp.where(odd, pltpu.roll(t1, hidden, 1), t0),
                    jnp.where(odd, t1, pltpu.roll(t0, back, 1)),
                    jnp.where(odd, pltpu.roll(t3, hidden, 1), t2),
                    jnp.where(odd, t3, pltpu.roll(t2, back, 1)),
                )
                for k in range(rep):
                    first = block * rows * rows + (group * rep + k) * rows
                    if ratio == 1:
                        first = (group * rep + k) * rows
                    else:
                        first = pl.multiple_of(first, rows)
                    flat_scr[quad, pl.ds(first, rows), :] = found[k].astype(BF16)
    flat = jnp.concatenate([flat_scr[quad] for quad in range(flat_scr.shape[0])], axis=1)
    outer_mean = dot(flat, proj_ref[...]) * inverse_ref[...]
    one = (base_ref[...] + outer_mean).astype(BF16).astype(F32)
    one_scr[...] = one
    norm = layer_norm(one).astype(BF16)
    for side, weight in enumerate((tl_ref, tr_ref)):
        both = dot(norm, weight[...])
        factor = jax.nn.sigmoid(both[:, :channels]) * both[:, channels:] * live_ref[...]
        both_ref[side] = factor.astype(BF16)
    cols = pairs // rows
    for row in range(rows):
        one_ref[row * cols : (row + 1) * cols, :] = one_scr[pl.ds(row, cols, stride=rows), :].astype(BF16)


def pair_update(hidden, zlt, zrs, base, inverse, live, proj, triangle_left, triangle_right):
    pairs, channels = base.shape
    ratio = len(zrs)
    shape = jax.ShapeDtypeStruct((pairs, channels), BF16)
    return pl.pallas_call(
        functools.partial(pair_kernel, ratio, hidden),
        out_shape=(jax.ShapeDtypeStruct((2, pairs, channels), BF16), shape),
        in_specs=[vmem()] * (7 + ratio),
        out_specs=[vmem()] * 2,
        scratch_shapes=[
            pltpu.VMEM((zrs[0].shape[0], zlt.shape[1], LANES), F32),
            pltpu.VMEM((proj.shape[0] // LANES, pairs, LANES), BF16),
            pltpu.VMEM((pairs, channels), F32),
        ],
        compiler_params=pltpu.CompilerParams(vmem_limit_bytes=32 << 20),
        cost_estimate=pl.CostEstimate(
            flops=2 * pairs * 1024 * 512, bytes_accessed=2 << 20, transcendentals=pairs * 256
        ),
    )(zlt, *zrs, base, inverse, live, proj, triangle_left, triangle_right)


def other(sub):
    return sub + 1 - 2 * (sub % 2)


def gate_kernel(one_ref, weight_ref, gate_ref):
    norm = layer_norm(one_ref[...].astype(F32)).astype(BF16)
    gate_ref[...] = jax.nn.sigmoid(dot(norm, weight_ref[...]))


def output_gate(one, weight):
    return pl.pallas_call(
        gate_kernel,
        out_shape=jax.ShapeDtypeStruct(one.shape, F32),
        in_specs=[vmem()] * 2,
        out_specs=vmem(),
        compiler_params=pltpu.CompilerParams(vmem_limit_bytes=4 << 20),
        cost_estimate=pl.CostEstimate(
            flops=2 * one.size * LANES, bytes_accessed=1 << 18, transcendentals=one.size
        ),
    )(one, weight)


SENDERS = ((0, 2, 1, 3), (2, 1, 3, 0), (3, 1, 2, 0), (1, 2, 0, 3))


def sender(a, b, subs, ratio):
    if (subs, ratio) == (4, 1):
        return SENDERS[b][a]
    return a // ratio


def sender_index(a, b, subs, ratio):
    if (subs, ratio) != (4, 1):
        return a // ratio
    found = 0
    for col, places in enumerate(SENDERS):
        for row, place in enumerate(places):
            found = jnp.where((a == row) & (b == col), place, found)
    return found


def triangle_kernel(subs, ratio, cols, *refs):
    twos = subs // 2
    lefts, refs = refs[:twos], refs[twos:]
    rights, refs = refs[: twos * ratio], refs[twos * ratio :]
    (one_ref, gate_ref, out_ref, up_ref, down_ref, result_ref, left_scr, right_scr, sum_scr) = refs
    pairs, channels = one_ref.shape
    rows = pairs // cols
    here, there = lax.axis_index("dap"), lax.axis_index("sub")
    first_sub = sender_index(here, there, subs, ratio)
    for step in range(twos):
        sub = lax.rem(there + 2 * step, subs)
        left_scr[sub] = lefts[step][0].astype(F32)
        left_scr[other(sub)] = lefts[step][1].astype(F32)
    for turn in range(ratio):
        block = lax.rem(here + turn, ratio)
        for step in range(twos):
            sub = lax.rem(first_sub + 2 * step, subs)
            right_scr[block * subs + sub] = rights[turn * twos + step][0].astype(F32)
            right_scr[block * subs + other(sub)] = rights[turn * twos + step][1].astype(F32)
    for block in range(ratio):
        totals = tuple(jnp.zeros((rows, channels), F32) for _ in range(rows))
        for sub in range(subs):

            def body(k, totals, sub=sub, block=block):
                first = pl.multiple_of(k * rows, rows)
                right = right_scr[block * subs + sub, pl.ds(first, rows), :]
                return tuple(
                    totals[i] + left_scr[sub, pl.ds(first + i, 1), :] * right for i in range(rows)
                )

            totals = lax.fori_loop(0, cols, body, totals, unroll=4)
        for i in range(rows):
            sum_scr[i * cols + block * rows : i * cols + (block + 1) * rows, :] = totals[i]
    one = one_ref[...].astype(F32)
    hidden = layer_norm(sum_scr[...].astype(BF16).astype(F32)).astype(BF16)
    two = (one + gate_ref[...] * dot(hidden, out_ref[...])).astype(BF16).astype(F32)
    wide = jnp.maximum(dot(layer_norm(two).astype(BF16), up_ref[...]), 0.0).astype(BF16)
    result = (two + dot(wide, down_ref[...])).astype(BF16)
    result_ref[...] = result.reshape(result_ref.shape)


def triangle_update(lefts, rights, one, cols, gate, out, up, down):
    pairs, channels = one.shape
    rows = pairs // cols
    subs = 2 * len(lefts)
    ratio = len(rights) // len(lefts)
    return pl.pallas_call(
        functools.partial(triangle_kernel, subs, ratio, cols),
        out_shape=jax.ShapeDtypeStruct((rows, cols, channels), BF16),
        in_specs=[vmem()] * (len(lefts) + len(rights) + 5),
        out_specs=vmem(),
        scratch_shapes=[
            pltpu.VMEM((subs, pairs, channels), F32),
            pltpu.VMEM((subs * ratio, pairs, channels), F32),
            pltpu.VMEM((pairs, channels), F32),
        ],
        compiler_params=pltpu.CompilerParams(vmem_limit_bytes=(16 << 20) if ratio == 1 else (50 << 20)),
        cost_estimate=pl.CostEstimate(
            flops=2 * pairs * channels * 2048, bytes_accessed=2 << 20, transcendentals=pairs * 128
        ),
    )(*lefts, *rights, one, gate, out, up, down)


def per_device(
    alignment,
    alignment_mask,
    pair_input,
    residue_mask,
    chain_index,
    outer_left,
    outer_right,
    outer_proj,
    triangle_left,
    triangle_right,
    triangle_gate,
    triangle_out,
    relative_table,
    transition_up,
    transition_down,
):
    daps, subs = lax.axis_size("dap"), lax.axis_size("sub")
    ratio = daps // subs
    cols = pair_input.shape[1]

    def fetch(values, source):
        perm = []
        for a in range(daps):
            for b in range(subs):
                dap, sub = source(a, b)
                perm.append((dap * subs + sub, a * subs + b))
        return lax.ppermute(values, ("dap", "sub"), perm)

    def owner(a, b, turn):
        return ratio * b + (a + turn) % ratio

    mask = alignment_mask.T
    zr = factor(alignment, mask, outer_right.T)
    zrs = [
        fetch(zr, lambda a, b, turn=turn: (owner(a, b, turn), sender(a, b, subs, ratio)))
        for turn in range(ratio)
    ]
    zl = factor(alignment, mask, outer_left.T)
    zlt, base, inverse, live, proj = prepare(
        zl, mask, pair_input, residue_mask, chain_index, relative_table, outer_proj
    )
    own, one = pair_update(
        outer_left.shape[1], zlt, zrs, base, inverse, live, proj, triangle_left, triangle_right
    )
    near = fetch(own, lambda a, b: (a, other(b)))
    left = jnp.stack([own[0], near[0]])
    right = jnp.stack([own[1], near[1]])
    rights = [
        fetch(
            right,
            lambda a, b, t=turn, m=step: (
                owner(a, b, t), (sender(a, b, subs, ratio) + 2 * m) % subs
            ),
        )
        for turn in range(ratio)
        for step in range(subs // 2)
    ]
    lefts = [left] + [
        fetch(left, lambda a, b, m=step: (a, (b + 2 * m) % subs)) for step in range(1, subs // 2)
    ]
    gate = output_gate(one, triangle_gate)
    return triangle_update(
        lefts, rights, one, cols, gate, triangle_out, transition_up, transition_down
    )


def solution(mesh):
    in_specs = (
        P("parts", "dap", None),
        P("parts", None),
        P(("parts", "dap"), "sub", None),
        P("parts"),
        P("parts"),
        P(),
        P(),
        P(),
        P(),
        P(),
        P(),
        P(),
        P(),
        P(),
        P(),
    )
    out_specs = P(("parts", "dap"), "sub", None)
    return jax.shard_map(
        per_device, mesh=mesh, in_specs=in_specs, out_specs=out_specs, check_vma=False
    )
```

```python
import functools

import jax
import jax.numpy as jnp
from jax import lax
from jax.experimental import pallas as pl
from jax.experimental.pallas import tpu as pltpu
from jax.sharding import PartitionSpec as P

REL_CLIP = 32
LANES = 128
STEPS = 4
EPSILON = 1e-05
BF16 = jnp.bfloat16
F32 = jnp.float32
NT = (((1,), (1,)), ((), ()))
TN = (((0,), (0,)), ((), ()))


def layer_norm(values):
    average = jnp.mean(values, axis=-1, keepdims=True)
    centered = values - average
    spread = jnp.mean(centered * centered, axis=-1, keepdims=True)
    return centered * lax.rsqrt(spread + EPSILON)


def dot(left, right):
    return jnp.dot(left, right, preferred_element_type=F32)


def dot_nt(left, right):
    return lax.dot_general(left, right, NT, preferred_element_type=F32)


def dot_tn(left, right):
    return lax.dot_general(left, right, TN, preferred_element_type=F32)


def iota(shape, dim):
    return lax.broadcasted_iota(jnp.int32, shape, dim)


def vmem():
    return pl.BlockSpec(memory_space=pltpu.VMEM)


def over(index, size):
    return lax.shift_right_logical(index, size.bit_length() - 1)


def within(index, size):
    return lax.bitwise_and(index, size - 1)


def factor_kernel(x_any, mask_ref, weight_ref, z_ref, x_scr, y_scr, sems):
    halves, seqs, rows, _ = x_scr.shape
    hidden, channels = weight_ref.shape
    rep = LANES // hidden
    groups = rows // rep
    residues = mask_ref.shape[0]
    width = rows * hidden
    step = seqs // STEPS
    copies = []
    for turn in range(STEPS):
        part = pl.ds(turn * step, step)
        for half in range(halves):
            source = x_any.at[part, :, pl.ds(half * LANES, LANES)]
            copies.append(pltpu.make_async_copy(source, x_scr.at[half, part], sems.at[turn, half]))
            copies[-1].start()
    weight = jnp.concatenate([weight_ref[...]] * rep, axis=0).T
    w = jnp.concatenate([weight, jnp.ones((channels, LANES), BF16)], axis=1)
    sums = dot(jnp.ones((8, channels), BF16), w)[:1, :LANES]
    start = lax.axis_index("dap") * rows
    spread = iota((residues, width), 0) == start + over(iota((residues, width), 1), hidden)
    live = dot_tn(mask_ref[...].astype(BF16), spread.astype(BF16))
    block = over(iota((step, LANES), 1), hidden)
    ones = jnp.ones((LANES, LANES), BF16)
    for turn in range(STEPS):
        x = []
        for half in range(halves):
            copies[turn * halves + half].wait()
            x.append(x_scr[half, turn * step : (turn + 1) * step].reshape(step * rows, LANES))
        y = dot(jnp.concatenate(x, axis=1), w)
        mean = y[:, LANES:] * (1.0 / channels)
        square = jnp.zeros_like(mean)
        for half in range(halves):
            centered = x[half].astype(F32) - mean
            square = square + centered * centered
        spread = dot(square.astype(BF16), ones)
        scale = lax.rsqrt(spread * (1.0 / channels) + EPSILON)
        y_scr[turn] = (y[:, :LANES] - mean * sums) * scale
        here = slice(turn * step, (turn + 1) * step)
        for group in range(groups):
            z = y_scr[turn, pl.ds(group * rep, step, stride=rows), :]
            for k in range(1, rep):
                next_z = y_scr[turn, pl.ds(group * rep + k, step, stride=rows), :]
                z = jnp.where(block == k, next_z, z)
            lanes = slice(group * LANES, (group + 1) * LANES)
            z_ref[group, here, :] = (z * live[here, lanes]).astype(BF16)


def factor(alignment, mask, weight):
    seqs, rows, channels = alignment.shape
    hidden = weight.shape[0]
    return pl.pallas_call(
        factor_kernel,
        out_shape=jax.ShapeDtypeStruct((rows * hidden // LANES, seqs, LANES), BF16),
        in_specs=[pl.BlockSpec(memory_space=pl.ANY), vmem(), vmem()],
        out_specs=vmem(),
        scratch_shapes=[
            pltpu.VMEM((channels // LANES, seqs, rows, LANES), BF16),
            pltpu.VMEM((STEPS, seqs * rows // STEPS, LANES), F32),
            pltpu.SemaphoreType.DMA((STEPS, channels // LANES)),
        ],
        compiler_params=pltpu.CompilerParams(vmem_limit_bytes=119 << 19),
        cost_estimate=pl.CostEstimate(
            flops=2 * seqs * rows * channels * 512, bytes_accessed=4 << 20, transcendentals=0
        ),
    )(alignment, mask, weight)


def prepare_kernel(
    zl_ref, mask_ref, pair_ref, live_ref, chain_ref, table_ref, proj_ref,
    zlt_ref, base_ref, inverse_ref, live_out_ref, proj_out_ref, pair_scr, table_scr,
):
    rows, cols, _ = pair_ref.shape
    pairs = rows * cols
    residues = mask_ref.shape[0]
    classes = table_ref.shape[0]
    row_start = lax.axis_index("dap") * rows
    col_start = lax.axis_index("sub") * cols
    for group in range(zl_ref.shape[0]):
        turned = zl_ref[group].T
        for half in range(zlt_ref.shape[0]):
            lanes = slice(half * LANES, (half + 1) * LANES)
            zlt_ref[half, group * LANES : (group + 1) * LANES, :] = turned[:, lanes]
    proj_out_ref[...] = proj_ref[...].reshape(proj_out_ref.shape).astype(BF16)
    which = iota((pairs, residues), 0)
    place = iota((pairs, residues), 1)
    pick_row = (place == row_start + within(which, rows)).astype(BF16)
    pick_col = (place == col_start + over(which, rows)).astype(BF16)
    mask = mask_ref[...].astype(BF16)
    both = (dot(pick_row, mask) * dot(pick_col, mask)).astype(BF16)
    counts = dot(both, jnp.ones((mask.shape[1], LANES), BF16))
    inverse_ref[...] = 1.0 / jnp.maximum(counts, 1.0)
    live = jnp.broadcast_to(live_ref[...].astype(F32), (LANES, residues)).astype(BF16)
    chain = jnp.broadcast_to(chain_ref[...].astype(F32), (LANES, residues)).astype(BF16)
    live_out_ref[...] = dot_nt(pick_row, live) * dot_nt(pick_col, live)
    same = dot_nt(pick_row, chain) == dot_nt(pick_col, chain)
    pair = iota((pairs, LANES), 0)
    offset = (row_start + within(pair, rows)) - (col_start + over(pair, rows)) + REL_CLIP
    bucket = jnp.where(same, jnp.clip(offset, 0, 2 * REL_CLIP), 2 * REL_CLIP + 1)
    table_scr[...] = jnp.zeros_like(table_scr)
    table_scr[pl.ds(0, classes), :] = table_ref[...].astype(F32)
    onehot = (bucket == iota((pairs, LANES), 1)).astype(BF16)
    relative = dot(onehot, table_scr[...].astype(BF16))
    pair_scr[...] = pair_ref[...].reshape(pairs, LANES).astype(F32)
    for col in range(cols):
        here = slice(col * rows, (col + 1) * rows)
        base_ref[here, :] = relative[here] + pair_scr[pl.ds(col, rows, stride=cols), :]


def prepare(zl, mask, pair_input, residue_mask, chain_index, table, proj):
    rows, cols, channels = pair_input.shape
    pairs = rows * cols
    shape = jax.ShapeDtypeStruct((pairs, channels), F32)
    depth = proj.shape[0] * proj.shape[1]
    return pl.pallas_call(
        prepare_kernel,
        out_shape=(
            jax.ShapeDtypeStruct((zl.shape[1] // LANES, zl.shape[0] * LANES, LANES), BF16),
            shape,
            shape,
            shape,
            jax.ShapeDtypeStruct((depth, channels), BF16),
        ),
        in_specs=[vmem()] * 7,
        out_specs=[vmem()] * 5,
        scratch_shapes=[pltpu.VMEM((pairs, channels), F32), pltpu.VMEM((LANES, channels), F32)],
        compiler_params=pltpu.CompilerParams(vmem_limit_bytes=24 << 20),
        cost_estimate=pl.CostEstimate(
            flops=2 * pairs * 256 * 1024, bytes_accessed=2 << 20, transcendentals=0
        ),
    )(zl, mask, pair_input, residue_mask[None, :], chain_index[None, :], table, proj)


def pair_kernel(ratio, hidden, zlt_ref, *refs):
    zr_refs, refs = refs[:ratio], refs[ratio:]
    (base_ref, inverse_ref, live_ref, proj_ref, tl_ref, tr_ref,
     both_ref, one_ref, outer_scr, flat_scr, one_scr) = refs
    pairs, channels = base_ref.shape
    rows = zlt_ref.shape[1] // hidden
    rep = LANES // hidden
    me = lax.axis_index("dap")
    lane = iota((rows, LANES), 1)
    odd = (lane // hidden) % 2 == 1
    upper = lane // (2 * hidden) == 1
    half = 2 * hidden
    left = jnp.concatenate([zlt_ref[part] for part in range(zlt_ref.shape[0])], axis=1)
    for step in range(ratio):
        block = lax.rem(me + step, ratio)
        right = [zr_refs[step][group] for group in range(rows // rep)]
        outer = dot(left, jnp.concatenate(right, axis=1))
        for group in range(rows // rep):
            outer_scr[group] = outer[:, group * LANES : (group + 1) * LANES]
        for group in range(rows // rep):
            for quad in range(hidden // rep):
                s0, s1, s2, s3 = (
                    outer_scr[group, pl.ds(quad * rep + k, rows, stride=hidden), :] for k in range(rep)
                )
                t0 = jnp.where(upper, pltpu.roll(s2, half, 1), s0)
                t1 = jnp.where(upper, pltpu.roll(s3, half, 1), s1)
                t2 = jnp.where(upper, s2, pltpu.roll(s0, half, 1))
                t3 = jnp.where(upper, s3, pltpu.roll(s1, half, 1))
                back = LANES - hidden
                found = (
                    jnp.where(odd, pltpu.roll(t1, hidden, 1), t0),
                    jnp.where(odd, t1, pltpu.roll(t0, back, 1)),
                    jnp.where(odd, pltpu.roll(t3, hidden, 1), t2),
                    jnp.where(odd, t3, pltpu.roll(t2, back, 1)),
                )
                for k in range(rep):
                    first = block * rows * rows + (group * rep + k) * rows
                    if ratio == 1:
                        first = (group * rep + k) * rows
                    else:
                        first = pl.multiple_of(first, rows)
                    flat_scr[quad, pl.ds(first, rows), :] = found[k].astype(BF16)
    flat = jnp.concatenate([flat_scr[quad] for quad in range(flat_scr.shape[0])], axis=1)
    outer_mean = dot(flat, proj_ref[...]) * inverse_ref[...]
    one = (base_ref[...] + outer_mean).astype(BF16).astype(F32)
    one_scr[...] = one
    norm = layer_norm(one).astype(BF16)
    for side, weight in enumerate((tl_ref, tr_ref)):
        both = dot(norm, weight[...])
        factor = jax.nn.sigmoid(both[:, :channels]) * both[:, channels:] * live_ref[...]
        both_ref[side] = factor.astype(BF16)
    cols = pairs // rows
    for row in range(rows):
        one_ref[row * cols : (row + 1) * cols, :] = one_scr[pl.ds(row, cols, stride=rows), :].astype(BF16)


def pair_update(hidden, zlt, zrs, base, inverse, live, proj, triangle_left, triangle_right):
    pairs, channels = base.shape
    ratio = len(zrs)
    shape = jax.ShapeDtypeStruct((pairs, channels), BF16)
    return pl.pallas_call(
        functools.partial(pair_kernel, ratio, hidden),
        out_shape=(jax.ShapeDtypeStruct((2, pairs, channels), BF16), shape),
        in_specs=[vmem()] * (7 + ratio),
        out_specs=[vmem()] * 2,
        scratch_shapes=[
            pltpu.VMEM((zrs[0].shape[0], zlt.shape[1], LANES), F32),
            pltpu.VMEM((proj.shape[0] // LANES, pairs, LANES), BF16),
            pltpu.VMEM((pairs, channels), F32),
        ],
        compiler_params=pltpu.CompilerParams(vmem_limit_bytes=32 << 20),
        cost_estimate=pl.CostEstimate(
            flops=2 * pairs * 1024 * 512, bytes_accessed=2 << 20, transcendentals=pairs * 256
        ),
    )(zlt, *zrs, base, inverse, live, proj, triangle_left, triangle_right)


def other(sub):
    return sub + 1 - 2 * (sub % 2)


def gate_kernel(one_ref, weight_ref, gate_ref):
    norm = layer_norm(one_ref[...].astype(F32)).astype(BF16)
    gate_ref[...] = jax.nn.sigmoid(dot(norm, weight_ref[...]))


def output_gate(one, weight):
    return pl.pallas_call(
        gate_kernel,
        out_shape=jax.ShapeDtypeStruct(one.shape, F32),
        in_specs=[vmem()] * 2,
        out_specs=vmem(),
        compiler_params=pltpu.CompilerParams(vmem_limit_bytes=4 << 20),
        cost_estimate=pl.CostEstimate(
            flops=2 * one.size * LANES, bytes_accessed=1 << 18, transcendentals=one.size
        ),
    )(one, weight)


SENDERS = ((0, 2, 1, 3), (2, 1, 3, 0), (3, 1, 2, 0), (1, 2, 0, 3))


def sender(a, b, subs, ratio):
    if (subs, ratio) == (4, 1):
        return SENDERS[b][a]
    return a // ratio


def sender_index(a, b, subs, ratio):
    if (subs, ratio) != (4, 1):
        return a // ratio
    found = 0
    for col, places in enumerate(SENDERS):
        for row, place in enumerate(places):
            found = jnp.where((a == row) & (b == col), place, found)
    return found


def triangle_kernel(subs, ratio, cols, *refs):
    twos = subs // 2
    rights, refs = refs[: twos * ratio], refs[twos * ratio :]
    lefts, refs = refs[:twos], refs[twos:]
    (one_ref, gate_ref, out_ref, up_ref, down_ref, result_ref, left_scr, right_scr, sum_scr) = refs
    pairs, channels = one_ref.shape
    rows = pairs // cols
    here, there = lax.axis_index("dap"), lax.axis_index("sub")
    first_sub = sender_index(here, there, subs, ratio)
    for step in range(twos):
        sub = lax.rem(there + 2 * step, subs)
        left_scr[sub] = lefts[step][0].astype(F32)
        left_scr[other(sub)] = lefts[step][1].astype(F32)
    for turn in range(ratio):
        block = lax.rem(here + turn, ratio)
        for step in range(twos):
            sub = lax.rem(first_sub + 2 * step, subs)
            right_scr[block * subs + sub] = rights[turn * twos + step][0].astype(F32)
            right_scr[block * subs + other(sub)] = rights[turn * twos + step][1].astype(F32)
    for block in range(ratio):
        totals = tuple(jnp.zeros((rows, channels), F32) for _ in range(rows))
        for sub in range(subs):

            def body(k, totals, sub=sub, block=block):
                first = pl.multiple_of(k * rows, rows)
                right = right_scr[block * subs + sub, pl.ds(first, rows), :]
                return tuple(
                    totals[i] + left_scr[sub, pl.ds(first + i, 1), :] * right for i in range(rows)
                )

            totals = lax.fori_loop(0, cols, body, totals, unroll=4)
        for i in range(rows):
            sum_scr[i * cols + block * rows : i * cols + (block + 1) * rows, :] = totals[i]
    one = one_ref[...].astype(F32)
    hidden = layer_norm(sum_scr[...].astype(BF16).astype(F32)).astype(BF16)
    two = (one + gate_ref[...] * dot(hidden, out_ref[...])).astype(BF16).astype(F32)
    wide = jnp.maximum(dot(layer_norm(two).astype(BF16), up_ref[...]), 0.0).astype(BF16)
    result = (two + dot(wide, down_ref[...])).astype(BF16)
    result_ref[...] = result.reshape(result_ref.shape)


def triangle_update(lefts, rights, one, cols, gate, out, up, down):
    pairs, channels = one.shape
    rows = pairs // cols
    subs = 2 * len(lefts)
    ratio = len(rights) // len(lefts)
    return pl.pallas_call(
        functools.partial(triangle_kernel, subs, ratio, cols),
        out_shape=jax.ShapeDtypeStruct((rows, cols, channels), BF16),
        in_specs=[vmem()] * (len(lefts) + len(rights) + 5),
        out_specs=vmem(),
        scratch_shapes=[
            pltpu.VMEM((subs, pairs, channels), F32),
            pltpu.VMEM((subs * ratio, pairs, channels), F32),
            pltpu.VMEM((pairs, channels), F32),
        ],
        compiler_params=pltpu.CompilerParams(vmem_limit_bytes=(16 << 20) if ratio == 1 else (50 << 20)),
        cost_estimate=pl.CostEstimate(
            flops=2 * pairs * channels * 2048, bytes_accessed=2 << 20, transcendentals=pairs * 128
        ),
    )(*rights, *lefts, one, gate, out, up, down)


def per_device(
    alignment,
    alignment_mask,
    pair_input,
    residue_mask,
    chain_index,
    outer_left,
    outer_right,
    outer_proj,
    triangle_left,
    triangle_right,
    triangle_gate,
    triangle_out,
    relative_table,
    transition_up,
    transition_down,
):
    daps, subs = lax.axis_size("dap"), lax.axis_size("sub")
    ratio = daps // subs
    cols = pair_input.shape[1]

    def fetch(values, source):
        perm = []
        for a in range(daps):
            for b in range(subs):
                dap, sub = source(a, b)
                perm.append((dap * subs + sub, a * subs + b))
        return lax.ppermute(values, ("dap", "sub"), perm)

    def owner(a, b, turn):
        return ratio * b + (a + turn) % ratio

    mask = alignment_mask.T
    zr = factor(alignment, mask, outer_right.T)
    zrs = [
        fetch(zr, lambda a, b, turn=turn: (owner(a, b, turn), sender(a, b, subs, ratio)))
        for turn in range(ratio)
    ]
    zl = factor(alignment, mask, outer_left.T)
    zlt, base, inverse, live, proj = prepare(
        zl, mask, pair_input, residue_mask, chain_index, relative_table, outer_proj
    )
    own, one = pair_update(
        outer_left.shape[1], zlt, zrs, base, inverse, live, proj, triangle_left, triangle_right
    )
    near = fetch(own, lambda a, b: (a, other(b)))
    left = jnp.stack([own[0], near[0]])
    right = jnp.stack([own[1], near[1]])
    rights = [
        fetch(
            right,
            lambda a, b, t=turn, m=step: (
                owner(a, b, t), (sender(a, b, subs, ratio) + 2 * m) % subs
            ),
        )
        for turn in range(ratio)
        for step in range(subs // 2)
    ]
    lefts = [left] + [
        fetch(left, lambda a, b, m=step: (a, (b + 2 * m) % subs)) for step in range(1, subs // 2)
    ]
    gate = output_gate(one, triangle_gate)
    return triangle_update(
        lefts, rights, one, cols, gate, triangle_out, transition_up, transition_down
    )


def solution(mesh):
    in_specs = (
        P("parts", "dap", None),
        P("parts", None),
        P(("parts", "dap"), "sub", None),
        P("parts"),
        P("parts"),
        P(),
        P(),
        P(),
        P(),
        P(),
        P(),
        P(),
        P(),
        P(),
        P(),
    )
    out_specs = P(("parts", "dap"), "sub", None)
    return jax.shard_map(
        per_device, mesh=mesh, in_specs=in_specs, out_specs=out_specs, check_vma=False
    )
```

```python
import functools

import jax
import jax.numpy as jnp
from jax import lax
from jax.experimental import pallas as pl
from jax.experimental.pallas import tpu as pltpu
from jax.sharding import PartitionSpec as P

REL_CLIP = 32
LANES = 128
STEPS = 4
EPSILON = 1e-05
BF16 = jnp.bfloat16
F32 = jnp.float32
NT = (((1,), (1,)), ((), ()))
TN = (((0,), (0,)), ((), ()))


def layer_norm(values):
    average = jnp.mean(values, axis=-1, keepdims=True)
    centered = values - average
    spread = jnp.mean(centered * centered, axis=-1, keepdims=True)
    return centered * lax.rsqrt(spread + EPSILON)


def dot(left, right):
    return jnp.dot(left, right, preferred_element_type=F32)


def dot_nt(left, right):
    return lax.dot_general(left, right, NT, preferred_element_type=F32)


def dot_tn(left, right):
    return lax.dot_general(left, right, TN, preferred_element_type=F32)


def iota(shape, dim):
    return lax.broadcasted_iota(jnp.int32, shape, dim)


def vmem():
    return pl.BlockSpec(memory_space=pltpu.VMEM)


def over(index, size):
    return lax.shift_right_logical(index, size.bit_length() - 1)


def within(index, size):
    return lax.bitwise_and(index, size - 1)


def factor_kernel(x_ref, mask_ref, weight_ref, z_ref, y_scr):
    seqs, rows, channels = x_ref.shape
    hidden = weight_ref.shape[0]
    rep = LANES // hidden
    groups = rows // rep
    residues = mask_ref.shape[0]
    width = rows * hidden
    step = seqs // STEPS
    weight = jnp.concatenate([weight_ref[...]] * rep, axis=0).T
    w = jnp.concatenate([weight, jnp.ones((channels, LANES), BF16)], axis=1)
    sums = dot(jnp.ones((8, channels), BF16), w)[:1, :LANES]
    start = lax.axis_index("dap") * rows
    spread = iota((residues, width), 0) == start + over(iota((residues, width), 1), hidden)
    live = dot_tn(mask_ref[...].astype(BF16), spread.astype(BF16))
    block = over(iota((step, LANES), 1), hidden)
    ones = jnp.ones((LANES, LANES), BF16)
    for turn in range(STEPS):
        x = x_ref[turn * step : (turn + 1) * step].reshape(step * rows, channels)
        y = dot(x, w)
        mean = y[:, LANES:] * (1.0 / channels)
        square = jnp.zeros_like(mean)
        for half in range(channels // LANES):
            centered = x[:, half * LANES : (half + 1) * LANES].astype(F32) - mean
            square = square + centered * centered
        spread = dot(square.astype(BF16), ones)
        scale = lax.rsqrt(spread * (1.0 / channels) + EPSILON)
        y_scr[turn] = (y[:, :LANES] - mean * sums) * scale
        here = slice(turn * step, (turn + 1) * step)
        for group in range(groups):
            z = y_scr[turn, pl.ds(group * rep, step, stride=rows), :]
            for k in range(1, rep):
                next_z = y_scr[turn, pl.ds(group * rep + k, step, stride=rows), :]
                z = jnp.where(block == k, next_z, z)
            lanes = slice(group * LANES, (group + 1) * LANES)
            z_ref[group, here, :] = (z * live[here, lanes]).astype(BF16)


def factor(alignment, mask, weight):
    seqs, rows, channels = alignment.shape
    hidden = weight.shape[0]
    return pl.pallas_call(
        factor_kernel,
        out_shape=jax.ShapeDtypeStruct((rows * hidden // LANES, seqs, LANES), BF16),
        in_specs=[vmem()] * 3,
        out_specs=vmem(),
        scratch_shapes=[
            pltpu.VMEM((STEPS, seqs * rows // STEPS, LANES), F32),
        ],
        compiler_params=pltpu.CompilerParams(vmem_limit_bytes=24 << 20),
        cost_estimate=pl.CostEstimate(
            flops=2 * seqs * rows * channels * 512, bytes_accessed=4 << 20, transcendentals=0
        ),
    )(alignment, mask, weight)


def prepare_kernel(
    zl_ref, mask_ref, pair_ref, live_ref, chain_ref, table_ref, proj_ref,
    zlt_ref, base_ref, inverse_ref, live_out_ref, proj_out_ref, pair_scr, table_scr,
):
    rows, cols, _ = pair_ref.shape
    pairs = rows * cols
    residues = mask_ref.shape[0]
    classes = table_ref.shape[0]
    row_start = lax.axis_index("dap") * rows
    col_start = lax.axis_index("sub") * cols
    for group in range(zl_ref.shape[0]):
        turned = zl_ref[group].T
        for half in range(zlt_ref.shape[0]):
            lanes = slice(half * LANES, (half + 1) * LANES)
            zlt_ref[half, group * LANES : (group + 1) * LANES, :] = turned[:, lanes]
    proj_out_ref[...] = proj_ref[...].reshape(proj_out_ref.shape).astype(BF16)
    which = iota((pairs, residues), 0)
    place = iota((pairs, residues), 1)
    pick_row = (place == row_start + within(which, rows)).astype(BF16)
    pick_col = (place == col_start + over(which, rows)).astype(BF16)
    mask = mask_ref[...].astype(BF16)
    both = (dot(pick_row, mask) * dot(pick_col, mask)).astype(BF16)
    counts = dot(both, jnp.ones((mask.shape[1], LANES), BF16))
    inverse_ref[...] = 1.0 / jnp.maximum(counts, 1.0)
    live = jnp.broadcast_to(live_ref[...].astype(F32), (LANES, residues)).astype(BF16)
    chain = jnp.broadcast_to(chain_ref[...].astype(F32), (LANES, residues)).astype(BF16)
    live_out_ref[...] = dot_nt(pick_row, live) * dot_nt(pick_col, live)
    same = dot_nt(pick_row, chain) == dot_nt(pick_col, chain)
    pair = iota((pairs, LANES), 0)
    offset = (row_start + within(pair, rows)) - (col_start + over(pair, rows)) + REL_CLIP
    bucket = jnp.where(same, jnp.clip(offset, 0, 2 * REL_CLIP), 2 * REL_CLIP + 1)
    table_scr[...] = jnp.zeros_like(table_scr)
    table_scr[pl.ds(0, classes), :] = table_ref[...].astype(F32)
    onehot = (bucket == iota((pairs, LANES), 1)).astype(BF16)
    relative = dot(onehot, table_scr[...].astype(BF16))
    pair_scr[...] = pair_ref[...].reshape(pairs, LANES).astype(F32)
    for col in range(cols):
        here = slice(col * rows, (col + 1) * rows)
        base_ref[here, :] = relative[here] + pair_scr[pl.ds(col, rows, stride=cols), :]


def prepare(zl, mask, pair_input, residue_mask, chain_index, table, proj):
    rows, cols, channels = pair_input.shape
    pairs = rows * cols
    shape = jax.ShapeDtypeStruct((pairs, channels), F32)
    depth = proj.shape[0] * proj.shape[1]
    return pl.pallas_call(
        prepare_kernel,
        out_shape=(
            jax.ShapeDtypeStruct((zl.shape[1] // LANES, zl.shape[0] * LANES, LANES), BF16),
            shape,
            shape,
            shape,
            jax.ShapeDtypeStruct((depth, channels), BF16),
        ),
        in_specs=[vmem()] * 7,
        out_specs=[vmem()] * 5,
        scratch_shapes=[pltpu.VMEM((pairs, channels), F32), pltpu.VMEM((LANES, channels), F32)],
        compiler_params=pltpu.CompilerParams(vmem_limit_bytes=24 << 20),
        cost_estimate=pl.CostEstimate(
            flops=2 * pairs * 256 * 1024, bytes_accessed=2 << 20, transcendentals=0
        ),
    )(zl, mask, pair_input, residue_mask[None, :], chain_index[None, :], table, proj)


def pair_kernel(ratio, hidden, zlt_ref, *refs):
    zr_refs, refs = refs[:ratio], refs[ratio:]
    (base_ref, inverse_ref, live_ref, proj_ref, tl_ref, tr_ref,
     both_ref, one_ref, outer_scr, flat_scr, one_scr) = refs
    pairs, channels = base_ref.shape
    rows = zlt_ref.shape[1] // hidden
    rep = LANES // hidden
    me = lax.axis_index("dap")
    lane = iota((rows, LANES), 1)
    odd = (lane // hidden) % 2 == 1
    upper = lane // (2 * hidden) == 1
    half = 2 * hidden
    left = jnp.concatenate([zlt_ref[part] for part in range(zlt_ref.shape[0])], axis=1)
    for step in range(ratio):
        block = lax.rem(me + step, ratio)
        right = [zr_refs[step][group] for group in range(rows // rep)]
        outer = dot(left, jnp.concatenate(right, axis=1))
        for group in range(rows // rep):
            outer_scr[group] = outer[:, group * LANES : (group + 1) * LANES]
        for group in range(rows // rep):
            for quad in range(hidden // rep):
                s0, s1, s2, s3 = (
                    outer_scr[group, pl.ds(quad * rep + k, rows, stride=hidden), :] for k in range(rep)
                )
                t0 = jnp.where(upper, pltpu.roll(s2, half, 1), s0)
                t1 = jnp.where(upper, pltpu.roll(s3, half, 1), s1)
                t2 = jnp.where(upper, s2, pltpu.roll(s0, half, 1))
                t3 = jnp.where(upper, s3, pltpu.roll(s1, half, 1))
                back = LANES - hidden
                found = (
                    jnp.where(odd, pltpu.roll(t1, hidden, 1), t0),
                    jnp.where(odd, t1, pltpu.roll(t0, back, 1)),
                    jnp.where(odd, pltpu.roll(t3, hidden, 1), t2),
                    jnp.where(odd, t3, pltpu.roll(t2, back, 1)),
                )
                for k in range(rep):
                    first = block * rows * rows + (group * rep + k) * rows
                    if ratio == 1:
                        first = (group * rep + k) * rows
                    else:
                        first = pl.multiple_of(first, rows)
                    flat_scr[quad, pl.ds(first, rows), :] = found[k].astype(BF16)
    flat = jnp.concatenate([flat_scr[quad] for quad in range(flat_scr.shape[0])], axis=1)
    outer_mean = dot(flat, proj_ref[...]) * inverse_ref[...]
    one = (base_ref[...] + outer_mean).astype(BF16).astype(F32)
    one_scr[...] = one
    norm = layer_norm(one).astype(BF16)
    for side, weight in enumerate((tl_ref, tr_ref)):
        both = dot(norm, weight[...])
        factor = jax.nn.sigmoid(both[:, :channels]) * both[:, channels:] * live_ref[...]
        both_ref[side] = factor.astype(BF16)
    cols = pairs // rows
    for row in range(rows):
        one_ref[row * cols : (row + 1) * cols, :] = one_scr[pl.ds(row, cols, stride=rows), :].astype(BF16)


def pair_update(hidden, zlt, zrs, base, inverse, live, proj, triangle_left, triangle_right):
    pairs, channels = base.shape
    ratio = len(zrs)
    shape = jax.ShapeDtypeStruct((pairs, channels), BF16)
    return pl.pallas_call(
        functools.partial(pair_kernel, ratio, hidden),
        out_shape=(jax.ShapeDtypeStruct((2, pairs, channels), BF16), shape),
        in_specs=[vmem()] * (7 + ratio),
        out_specs=[vmem()] * 2,
        scratch_shapes=[
            pltpu.VMEM((zrs[0].shape[0], zlt.shape[1], LANES), F32),
            pltpu.VMEM((proj.shape[0] // LANES, pairs, LANES), BF16),
            pltpu.VMEM((pairs, channels), F32),
        ],
        compiler_params=pltpu.CompilerParams(vmem_limit_bytes=32 << 20),
        cost_estimate=pl.CostEstimate(
            flops=2 * pairs * 1024 * 512, bytes_accessed=2 << 20, transcendentals=pairs * 256
        ),
    )(zlt, *zrs, base, inverse, live, proj, triangle_left, triangle_right)


def other(sub):
    return sub + 1 - 2 * (sub % 2)


def gate_kernel(one_ref, weight_ref, gate_ref):
    norm = layer_norm(one_ref[...].astype(F32)).astype(BF16)
    gate_ref[...] = jax.nn.sigmoid(dot(norm, weight_ref[...]))


def output_gate(one, weight):
    return pl.pallas_call(
        gate_kernel,
        out_shape=jax.ShapeDtypeStruct(one.shape, F32),
        in_specs=[vmem()] * 2,
        out_specs=vmem(),
        compiler_params=pltpu.CompilerParams(vmem_limit_bytes=4 << 20),
        cost_estimate=pl.CostEstimate(
            flops=2 * one.size * LANES, bytes_accessed=1 << 18, transcendentals=one.size
        ),
    )(one, weight)


SENDERS = ((0, 2, 1, 3), (2, 1, 3, 0), (3, 1, 2, 0), (1, 2, 0, 3))


def sender(a, b, subs, ratio):
    if (subs, ratio) == (4, 1):
        return SENDERS[b][a]
    return a // ratio


def sender_index(a, b, subs, ratio):
    if (subs, ratio) != (4, 1):
        return a // ratio
    found = 0
    for col, places in enumerate(SENDERS):
        for row, place in enumerate(places):
            found = jnp.where((a == row) & (b == col), place, found)
    return found


def triangle_kernel(subs, ratio, cols, *refs):
    twos = subs // 2
    rights, refs = refs[: twos * ratio], refs[twos * ratio :]
    lefts, refs = refs[:twos], refs[twos:]
    (one_ref, gate_ref, out_ref, up_ref, down_ref, result_ref, left_scr, right_scr, sum_scr) = refs
    pairs, channels = one_ref.shape
    rows = pairs // cols
    here, there = lax.axis_index("dap"), lax.axis_index("sub")
    first_sub = sender_index(here, there, subs, ratio)
    for step in range(twos):
        sub = lax.rem(there + 2 * step, subs)
        left_scr[sub] = lefts[step][0].astype(F32)
        left_scr[other(sub)] = lefts[step][1].astype(F32)
    for turn in range(ratio):
        block = lax.rem(here + turn, ratio)
        for step in range(twos):
            sub = lax.rem(first_sub + 2 * step, subs)
            right_scr[block * subs + sub] = rights[turn * twos + step][0].astype(F32)
            right_scr[block * subs + other(sub)] = rights[turn * twos + step][1].astype(F32)
    for block in range(ratio):
        totals = tuple(jnp.zeros((rows, channels), F32) for _ in range(rows))
        for sub in range(subs):

            def body(k, totals, sub=sub, block=block):
                first = pl.multiple_of(k * rows, rows)
                right = right_scr[block * subs + sub, pl.ds(first, rows), :]
                return tuple(
                    totals[i] + left_scr[sub, pl.ds(first + i, 1), :] * right for i in range(rows)
                )

            totals = lax.fori_loop(0, cols, body, totals, unroll=4)
        for i in range(rows):
            sum_scr[i * cols + block * rows : i * cols + (block + 1) * rows, :] = totals[i]
    one = one_ref[...].astype(F32)
    hidden = layer_norm(sum_scr[...].astype(BF16).astype(F32)).astype(BF16)
    two = (one + gate_ref[...] * dot(hidden, out_ref[...])).astype(BF16).astype(F32)
    wide = jnp.maximum(dot(layer_norm(two).astype(BF16), up_ref[...]), 0.0).astype(BF16)
    result = (two + dot(wide, down_ref[...])).astype(BF16)
    result_ref[...] = result.reshape(result_ref.shape)


def triangle_update(lefts, rights, one, cols, gate, out, up, down):
    pairs, channels = one.shape
    rows = pairs // cols
    subs = 2 * len(lefts)
    ratio = len(rights) // len(lefts)
    return pl.pallas_call(
        functools.partial(triangle_kernel, subs, ratio, cols),
        out_shape=jax.ShapeDtypeStruct((rows, cols, channels), BF16),
        in_specs=[vmem()] * (len(lefts) + len(rights) + 5),
        out_specs=vmem(),
        scratch_shapes=[
            pltpu.VMEM((subs, pairs, channels), F32),
            pltpu.VMEM((subs * ratio, pairs, channels), F32),
            pltpu.VMEM((pairs, channels), F32),
        ],
        compiler_params=pltpu.CompilerParams(vmem_limit_bytes=(16 << 20) if ratio == 1 else (50 << 20)),
        cost_estimate=pl.CostEstimate(
            flops=2 * pairs * channels * 2048, bytes_accessed=2 << 20, transcendentals=pairs * 128
        ),
    )(*rights, *lefts, one, gate, out, up, down)


def per_device(
    alignment,
    alignment_mask,
    pair_input,
    residue_mask,
    chain_index,
    outer_left,
    outer_right,
    outer_proj,
    triangle_left,
    triangle_right,
    triangle_gate,
    triangle_out,
    relative_table,
    transition_up,
    transition_down,
):
    daps, subs = lax.axis_size("dap"), lax.axis_size("sub")
    ratio = daps // subs
    cols = pair_input.shape[1]

    def fetch(values, source):
        perm = []
        for a in range(daps):
            for b in range(subs):
                dap, sub = source(a, b)
                perm.append((dap * subs + sub, a * subs + b))
        return lax.ppermute(values, ("dap", "sub"), perm)

    def owner(a, b, turn):
        return ratio * b + (a + turn) % ratio

    mask = alignment_mask.T
    zr = factor(alignment, mask, outer_right.T)
    zrs = [
        fetch(zr, lambda a, b, turn=turn: (owner(a, b, turn), sender(a, b, subs, ratio)))
        for turn in range(ratio)
    ]
    zl = factor(alignment, mask, outer_left.T)
    zlt, base, inverse, live, proj = prepare(
        zl, mask, pair_input, residue_mask, chain_index, relative_table, outer_proj
    )
    own, one = pair_update(
        outer_left.shape[1], zlt, zrs, base, inverse, live, proj, triangle_left, triangle_right
    )
    near = fetch(own, lambda a, b: (a, other(b)))
    left = jnp.stack([own[0], near[0]])
    right = jnp.stack([own[1], near[1]])
    rights = [
        fetch(
            right,
            lambda a, b, t=turn, m=step: (
                owner(a, b, t), (sender(a, b, subs, ratio) + 2 * m) % subs
            ),
        )
        for turn in range(ratio)
        for step in range(subs // 2)
    ]
    lefts = [left] + [
        fetch(left, lambda a, b, m=step: (a, (b + 2 * m) % subs)) for step in range(1, subs // 2)
    ]
    gate = output_gate(one, triangle_gate)
    return triangle_update(
        lefts, rights, one, cols, gate, triangle_out, transition_up, transition_down
    )


def solution(mesh):
    in_specs = (
        P("parts", "dap", None),
        P("parts", None),
        P(("parts", "dap"), "sub", None),
        P("parts"),
        P("parts"),
        P(),
        P(),
        P(),
        P(),
        P(),
        P(),
        P(),
        P(),
        P(),
        P(),
    )
    out_specs = P(("parts", "dap"), "sub", None)
    return jax.shard_map(
        per_device, mesh=mesh, in_specs=in_specs, out_specs=out_specs, check_vma=False
    )
```

```python
import functools

import jax
import jax.numpy as jnp
from jax import lax
from jax.experimental import pallas as pl
from jax.experimental.pallas import tpu as pltpu
from jax.sharding import PartitionSpec as P

REL_CLIP = 32
LANES = 128
PARTS = 2
EPSILON = 1e-05
BF16 = jnp.bfloat16
F32 = jnp.float32
NT = (((1,), (1,)), ((), ()))
TN = (((0,), (0,)), ((), ()))


def layer_norm(values):
    average = jnp.mean(values, axis=-1, keepdims=True)
    centered = values - average
    spread = jnp.mean(centered * centered, axis=-1, keepdims=True)
    return centered * lax.rsqrt(spread + EPSILON)


def dot(left, right):
    return jnp.dot(left, right, preferred_element_type=F32)


def dot_nt(left, right):
    return lax.dot_general(left, right, NT, preferred_element_type=F32)


def dot_tn(left, right):
    return lax.dot_general(left, right, TN, preferred_element_type=F32)


def iota(shape, dim):
    return lax.broadcasted_iota(jnp.int32, shape, dim)


def vmem():
    return pl.BlockSpec(memory_space=pltpu.VMEM)


def over(index, size):
    return lax.shift_right_logical(index, size.bit_length() - 1)


def within(index, size):
    return lax.bitwise_and(index, size - 1)


def factor_kernel(first, hidden, x_ref, weight_ref, *refs):
    mask_ref = refs[0] if len(refs) == 3 else None
    z_ref, y_scr = refs[-2:]
    groups, seqs, _ = z_ref.shape
    _, rows, channels = x_ref.shape
    rep = LANES // hidden
    width = rows * hidden
    step = y_scr.shape[1] // rows
    w = jnp.concatenate([weight_ref[...].T, jnp.ones((channels, LANES), BF16)], axis=1)
    sums = dot(jnp.ones((8, channels), BF16), w)[:1, :LANES]
    if mask_ref is not None:
        residues = mask_ref.shape[0]
        start = lax.axis_index("dap") * rows
        spread = iota((residues, width), 0) == start + over(iota((residues, width), 1), hidden)
        live = dot_tn(mask_ref[...].astype(BF16), spread.astype(BF16))
    block = over(iota((step, LANES), 1), hidden)
    ones = jnp.ones((LANES, LANES), BF16)
    for turn in range(seqs // step):
        x = x_ref[first + turn * step : first + (turn + 1) * step].reshape(step * rows, channels)
        y = dot(x, w)
        mean = y[:, LANES:] * (1.0 / channels)
        square = jnp.zeros_like(mean)
        for half in range(channels // LANES):
            centered = x[:, half * LANES : (half + 1) * LANES].astype(F32) - mean
            square = square + centered * centered
        spread = dot(square.astype(BF16), ones)
        scale = lax.rsqrt(spread * (1.0 / channels) + EPSILON)
        y_scr[turn] = (y[:, :LANES] - mean * sums) * scale
        here = slice(turn * step, (turn + 1) * step)
        for group in range(groups):
            z = y_scr[turn, pl.ds(group * rep, step, stride=rows), :]
            for k in range(1, rep):
                next_z = y_scr[turn, pl.ds(group * rep + k, step, stride=rows), :]
                z = jnp.where(block == k, next_z, z)
            if mask_ref is not None:
                z = z * live[here, group * LANES : (group + 1) * LANES]
            z_ref[group, here, :] = z.astype(BF16)


def factor(alignment, weight, hidden, first, seqs, mask=None):
    _, rows, channels = alignment.shape
    step = seqs // 4 if mask is not None else seqs // 2
    operands = (alignment, weight) if mask is None else (alignment, weight, mask)
    return pl.pallas_call(
        functools.partial(factor_kernel, first, hidden),
        out_shape=jax.ShapeDtypeStruct((rows * hidden // LANES, seqs, LANES), BF16),
        in_specs=[vmem()] * len(operands),
        out_specs=vmem(),
        scratch_shapes=[pltpu.VMEM((seqs // step, step * rows, LANES), F32)],
        compiler_params=pltpu.CompilerParams(vmem_limit_bytes=24 << 20),
        cost_estimate=pl.CostEstimate(
            flops=2 * seqs * rows * channels * 512, bytes_accessed=seqs << 14, transcendentals=0
        ),
    )(*operands)


def prepare_kernel(
    zl_ref, mask_ref, pair_ref, live_ref, chain_ref, table_ref, proj_ref,
    zlt_ref, base_ref, inverse_ref, live_out_ref, proj_out_ref, seen_ref, pair_scr, table_scr,
):
    rows, cols, _ = pair_ref.shape
    pairs = rows * cols
    residues = mask_ref.shape[0]
    classes = table_ref.shape[0]
    row_start = lax.axis_index("dap") * rows
    col_start = lax.axis_index("sub") * cols
    for group in range(zl_ref.shape[0]):
        turned = zl_ref[group].T
        for half in range(zlt_ref.shape[0]):
            lanes = slice(half * LANES, (half + 1) * LANES)
            zlt_ref[half, group * LANES : (group + 1) * LANES, :] = turned[:, lanes]
    proj_out_ref[...] = proj_ref[...].reshape(proj_out_ref.shape).astype(BF16)
    groups = zl_ref.shape[0]
    width = groups * LANES
    hidden = width // rows
    for block in range(cols // rows):
        column = col_start + block * rows + over(iota((residues, width), 1), hidden)
        spread = (iota((residues, width), 0) == column).astype(BF16)
        seen = dot_tn(mask_ref[...].astype(BF16), spread).astype(BF16)
        for group in range(groups):
            seen_ref[block * groups + group] = seen[:, group * LANES : (group + 1) * LANES]
    which = iota((pairs, residues), 0)
    place = iota((pairs, residues), 1)
    pick_row = (place == row_start + within(which, rows)).astype(BF16)
    pick_col = (place == col_start + over(which, rows)).astype(BF16)
    mask = mask_ref[...].astype(BF16)
    both = (dot(pick_row, mask) * dot(pick_col, mask)).astype(BF16)
    counts = dot(both, jnp.ones((mask.shape[1], LANES), BF16))
    inverse_ref[...] = 1.0 / jnp.maximum(counts, 1.0)
    live = jnp.broadcast_to(live_ref[...].astype(F32), (LANES, residues)).astype(BF16)
    chain = jnp.broadcast_to(chain_ref[...].astype(F32), (LANES, residues)).astype(BF16)
    live_out_ref[...] = dot_nt(pick_row, live) * dot_nt(pick_col, live)
    same = dot_nt(pick_row, chain) == dot_nt(pick_col, chain)
    pair = iota((pairs, LANES), 0)
    offset = (row_start + within(pair, rows)) - (col_start + over(pair, rows)) + REL_CLIP
    bucket = jnp.where(same, jnp.clip(offset, 0, 2 * REL_CLIP), 2 * REL_CLIP + 1)
    table_scr[...] = jnp.zeros_like(table_scr)
    table_scr[pl.ds(0, classes), :] = table_ref[...].astype(F32)
    onehot = (bucket == iota((pairs, LANES), 1)).astype(BF16)
    relative = dot(onehot, table_scr[...].astype(BF16))
    pair_scr[...] = pair_ref[...].reshape(pairs, LANES).astype(F32)
    for col in range(cols):
        here = slice(col * rows, (col + 1) * rows)
        base_ref[here, :] = relative[here] + pair_scr[pl.ds(col, rows, stride=cols), :]


def prepare(zl, mask, pair_input, residue_mask, chain_index, table, proj):
    rows, cols, channels = pair_input.shape
    pairs = rows * cols
    shape = jax.ShapeDtypeStruct((pairs, channels), F32)
    depth = proj.shape[0] * proj.shape[1]
    return pl.pallas_call(
        prepare_kernel,
        out_shape=(
            jax.ShapeDtypeStruct((zl.shape[1] // LANES, zl.shape[0] * LANES, LANES), BF16),
            shape,
            shape,
            shape,
            jax.ShapeDtypeStruct((depth, channels), BF16),
            jax.ShapeDtypeStruct((cols // rows * zl.shape[0], *zl.shape[1:]), BF16),
        ),
        in_specs=[vmem()] * 7,
        out_specs=[vmem()] * 6,
        scratch_shapes=[pltpu.VMEM((pairs, channels), F32), pltpu.VMEM((LANES, channels), F32)],
        compiler_params=pltpu.CompilerParams(vmem_limit_bytes=24 << 20),
        cost_estimate=pl.CostEstimate(
            flops=2 * pairs * 256 * 1024, bytes_accessed=2 << 20, transcendentals=0
        ),
    )(zl, mask, pair_input, residue_mask[None, :], chain_index[None, :], table, proj)


def pair_kernel(ratio, hidden, zlt_ref, *refs):
    zr_refs, refs = refs[: ratio * PARTS], refs[ratio * PARTS :]
    (seen_ref, base_ref, inverse_ref, live_ref, proj_ref, tl_ref, tr_ref,
     both_ref, one_ref, outer_scr, flat_scr, one_scr) = refs
    pairs, channels = base_ref.shape
    rows = zlt_ref.shape[1] // hidden
    rep = LANES // hidden
    me = lax.axis_index("dap")
    lane = iota((rows, LANES), 1)
    odd = (lane // hidden) % 2 == 1
    upper = lane // (2 * hidden) == 1
    half = 2 * hidden
    left = jnp.concatenate([zlt_ref[part] for part in range(zlt_ref.shape[0])], axis=1)
    for step in range(ratio):
        block = lax.rem(me + step, ratio)
        right = []
        for group in range(rows // rep):
            parts = [zr_refs[step * PARTS + part][group] for part in range(PARTS)]
            right.append(jnp.concatenate(parts, axis=0) * seen_ref[block * (rows // rep) + group])
        outer = dot(left, jnp.concatenate(right, axis=1))
        for group in range(rows // rep):
            outer_scr[group] = outer[:, group * LANES : (group + 1) * LANES]
        for group in range(rows // rep):
            for quad in range(hidden // rep):
                s0, s1, s2, s3 = (
                    outer_scr[group, pl.ds(quad * rep + k, rows, stride=hidden), :] for k in range(rep)
                )
                t0 = jnp.where(upper, pltpu.roll(s2, half, 1), s0)
                t1 = jnp.where(upper, pltpu.roll(s3, half, 1), s1)
                t2 = jnp.where(upper, s2, pltpu.roll(s0, half, 1))
                t3 = jnp.where(upper, s3, pltpu.roll(s1, half, 1))
                back = LANES - hidden
                found = (
                    jnp.where(odd, pltpu.roll(t1, hidden, 1), t0),
                    jnp.where(odd, t1, pltpu.roll(t0, back, 1)),
                    jnp.where(odd, pltpu.roll(t3, hidden, 1), t2),
                    jnp.where(odd, t3, pltpu.roll(t2, back, 1)),
                )
                for k in range(rep):
                    first = block * rows * rows + (group * rep + k) * rows
                    if ratio == 1:
                        first = (group * rep + k) * rows
                    else:
                        first = pl.multiple_of(first, rows)
                    flat_scr[quad, pl.ds(first, rows), :] = found[k].astype(BF16)
    flat = jnp.concatenate([flat_scr[quad] for quad in range(flat_scr.shape[0])], axis=1)
    outer_mean = dot(flat, proj_ref[...]) * inverse_ref[...]
    one = (base_ref[...] + outer_mean).astype(BF16).astype(F32)
    one_scr[...] = one
    norm = layer_norm(one).astype(BF16)
    for side, weight in enumerate((tl_ref, tr_ref)):
        both = dot(norm, weight[...])
        factor = jax.nn.sigmoid(both[:, :channels]) * both[:, channels:] * live_ref[...]
        both_ref[side] = factor.astype(BF16)
    cols = pairs // rows
    for row in range(rows):
        one_ref[row * cols : (row + 1) * cols, :] = one_scr[pl.ds(row, cols, stride=rows), :].astype(BF16)


def pair_update(hidden, zlt, zrs, seen, base, inverse, live, proj, triangle_left, triangle_right):
    pairs, channels = base.shape
    ratio = len(zrs) // PARTS
    shape = jax.ShapeDtypeStruct((pairs, channels), BF16)
    return pl.pallas_call(
        functools.partial(pair_kernel, ratio, hidden),
        out_shape=(jax.ShapeDtypeStruct((2, pairs, channels), BF16), shape),
        in_specs=[vmem()] * (8 + len(zrs)),
        out_specs=[vmem()] * 2,
        scratch_shapes=[
            pltpu.VMEM((zrs[0].shape[0], zlt.shape[1], LANES), F32),
            pltpu.VMEM((proj.shape[0] // LANES, pairs, LANES), BF16),
            pltpu.VMEM((pairs, channels), F32),
        ],
        compiler_params=pltpu.CompilerParams(vmem_limit_bytes=32 << 20),
        cost_estimate=pl.CostEstimate(
            flops=2 * pairs * 1024 * 512, bytes_accessed=2 << 20, transcendentals=pairs * 256
        ),
    )(zlt, *zrs, seen, base, inverse, live, proj, triangle_left, triangle_right)


def other(sub):
    return sub + 1 - 2 * (sub % 2)


def gate_kernel(one_ref, weight_ref, gate_ref):
    norm = layer_norm(one_ref[...].astype(F32)).astype(BF16)
    gate_ref[...] = jax.nn.sigmoid(dot(norm, weight_ref[...]))


def output_gate(one, weight):
    return pl.pallas_call(
        gate_kernel,
        out_shape=jax.ShapeDtypeStruct(one.shape, F32),
        in_specs=[vmem()] * 2,
        out_specs=vmem(),
        compiler_params=pltpu.CompilerParams(vmem_limit_bytes=4 << 20),
        cost_estimate=pl.CostEstimate(
            flops=2 * one.size * LANES, bytes_accessed=1 << 18, transcendentals=one.size
        ),
    )(one, weight)


SENDERS = ((0, 2, 1, 3), (2, 1, 3, 0), (3, 1, 2, 0), (1, 2, 0, 3))


def sender(a, b, subs, ratio):
    if (subs, ratio) == (4, 1):
        return SENDERS[b][a]
    return a // ratio


def sender_index(a, b, subs, ratio):
    if (subs, ratio) != (4, 1):
        return a // ratio
    found = 0
    for col, places in enumerate(SENDERS):
        for row, place in enumerate(places):
            found = jnp.where((a == row) & (b == col), place, found)
    return found


def triangle_kernel(subs, ratio, cols, *refs):
    twos = subs // 2
    rights, refs = refs[: twos * ratio], refs[twos * ratio :]
    lefts, refs = refs[:twos], refs[twos:]
    (one_ref, gate_ref, out_ref, up_ref, down_ref, result_ref, left_scr, right_scr, sum_scr) = refs
    pairs, channels = one_ref.shape
    rows = pairs // cols
    here, there = lax.axis_index("dap"), lax.axis_index("sub")
    first_sub = sender_index(here, there, subs, ratio)
    for step in range(twos):
        sub = lax.rem(there + 2 * step, subs)
        left_scr[sub] = lefts[step][0].astype(F32)
        left_scr[other(sub)] = lefts[step][1].astype(F32)
    for turn in range(ratio):
        block = lax.rem(here + turn, ratio)
        for step in range(twos):
            sub = lax.rem(first_sub + 2 * step, subs)
            right_scr[block * subs + sub] = rights[turn * twos + step][0].astype(F32)
            right_scr[block * subs + other(sub)] = rights[turn * twos + step][1].astype(F32)
    for block in range(ratio):
        totals = tuple(jnp.zeros((rows, channels), F32) for _ in range(rows))
        for sub in range(subs):

            def body(k, totals, sub=sub, block=block):
                first = pl.multiple_of(k * rows, rows)
                right = right_scr[block * subs + sub, pl.ds(first, rows), :]
                return tuple(
                    totals[i] + left_scr[sub, pl.ds(first + i, 1), :] * right for i in range(rows)
                )

            totals = lax.fori_loop(0, cols, body, totals, unroll=4)
        for i in range(rows):
            sum_scr[i * cols + block * rows : i * cols + (block + 1) * rows, :] = totals[i]
    one = one_ref[...].astype(F32)
    hidden = layer_norm(sum_scr[...].astype(BF16).astype(F32)).astype(BF16)
    two = (one + gate_ref[...] * dot(hidden, out_ref[...])).astype(BF16).astype(F32)
    wide = jnp.maximum(dot(layer_norm(two).astype(BF16), up_ref[...]), 0.0).astype(BF16)
    result = (two + dot(wide, down_ref[...])).astype(BF16)
    result_ref[...] = result.reshape(result_ref.shape)


def triangle_update(lefts, rights, one, cols, gate, out, up, down):
    pairs, channels = one.shape
    rows = pairs // cols
    subs = 2 * len(lefts)
    ratio = len(rights) // len(lefts)
    return pl.pallas_call(
        functools.partial(triangle_kernel, subs, ratio, cols),
        out_shape=jax.ShapeDtypeStruct((rows, cols, channels), BF16),
        in_specs=[vmem()] * (len(lefts) + len(rights) + 5),
        out_specs=vmem(),
        scratch_shapes=[
            pltpu.VMEM((subs, pairs, channels), F32),
            pltpu.VMEM((subs * ratio, pairs, channels), F32),
            pltpu.VMEM((pairs, channels), F32),
        ],
        compiler_params=pltpu.CompilerParams(vmem_limit_bytes=(16 << 20) if ratio == 1 else (50 << 20)),
        cost_estimate=pl.CostEstimate(
            flops=2 * pairs * channels * 2048, bytes_accessed=2 << 20, transcendentals=pairs * 128
        ),
    )(*rights, *lefts, one, gate, out, up, down)


def per_device(
    alignment,
    alignment_mask,
    pair_input,
    residue_mask,
    chain_index,
    outer_left,
    outer_right,
    outer_proj,
    triangle_left,
    triangle_right,
    triangle_gate,
    triangle_out,
    relative_table,
    transition_up,
    transition_down,
):
    daps, subs = lax.axis_size("dap"), lax.axis_size("sub")
    ratio = daps // subs
    cols = pair_input.shape[1]

    def fetch(values, source):
        perm = []
        for a in range(daps):
            for b in range(subs):
                dap, sub = source(a, b)
                perm.append((dap * subs + sub, a * subs + b))
        return lax.ppermute(values, ("dap", "sub"), perm)

    def owner(a, b, turn):
        return ratio * b + (a + turn) % ratio

    hidden = outer_left.shape[1]
    seqs = alignment.shape[0]
    part_seqs = seqs // PARTS
    mask = alignment_mask.T
    wide_left, wide_right = (
        jnp.tile(weight.T, (LANES // hidden, 1)) for weight in (outer_left, outer_right)
    )
    zr_parts = [
        factor(alignment, wide_right, hidden, part * part_seqs, part_seqs) for part in range(PARTS)
    ]
    zrs = [
        fetch(zr, lambda a, b, turn=turn: (owner(a, b, turn), sender(a, b, subs, ratio)))
        for turn in range(ratio)
        for zr in zr_parts
    ]
    zl = factor(alignment, wide_left, hidden, 0, seqs, mask)
    zlt, base, inverse, live, proj, seen = prepare(
        zl, mask, pair_input, residue_mask, chain_index, relative_table, outer_proj
    )
    own, one = pair_update(
        hidden, zlt, zrs, seen, base, inverse, live, proj, triangle_left, triangle_right
    )
    near = fetch(own, lambda a, b: (a, other(b)))
    left = jnp.stack([own[0], near[0]])
    right = jnp.stack([own[1], near[1]])
    rights = [
        fetch(
            right,
            lambda a, b, t=turn, m=step: (
                owner(a, b, t), (sender(a, b, subs, ratio) + 2 * m) % subs
            ),
        )
        for turn in range(ratio)
        for step in range(subs // 2)
    ]
    lefts = [left] + [
        fetch(left, lambda a, b, m=step: (a, (b + 2 * m) % subs)) for step in range(1, subs // 2)
    ]
    gate = output_gate(one, triangle_gate)
    return triangle_update(
        lefts, rights, one, cols, gate, triangle_out, transition_up, transition_down
    )


def solution(mesh):
    in_specs = (
        P("parts", "dap", None),
        P("parts", None),
        P(("parts", "dap"), "sub", None),
        P("parts"),
        P("parts"),
        P(),
        P(),
        P(),
        P(),
        P(),
        P(),
        P(),
        P(),
        P(),
        P(),
    )
    out_specs = P(("parts", "dap"), "sub", None)
    return jax.shard_map(
        per_device, mesh=mesh, in_specs=in_specs, out_specs=out_specs, check_vma=False
    )
```

```python
import functools

import jax
import jax.numpy as jnp
from jax import lax
from jax.experimental import pallas as pl
from jax.experimental.pallas import tpu as pltpu
from jax.sharding import PartitionSpec as P

REL_CLIP = 32
LANES = 128
PARTS = 1
EPSILON = 1e-05
BF16 = jnp.bfloat16
F32 = jnp.float32
NT = (((1,), (1,)), ((), ()))
TN = (((0,), (0,)), ((), ()))


def layer_norm(values):
    average = jnp.mean(values, axis=-1, keepdims=True)
    centered = values - average
    spread = jnp.mean(centered * centered, axis=-1, keepdims=True)
    return centered * lax.rsqrt(spread + EPSILON)


def dot(left, right):
    return jnp.dot(left, right, preferred_element_type=F32)


def dot_nt(left, right):
    return lax.dot_general(left, right, NT, preferred_element_type=F32)


def dot_tn(left, right):
    return lax.dot_general(left, right, TN, preferred_element_type=F32)


def iota(shape, dim):
    return lax.broadcasted_iota(jnp.int32, shape, dim)


def vmem():
    return pl.BlockSpec(memory_space=pltpu.VMEM)


def over(index, size):
    return lax.shift_right_logical(index, size.bit_length() - 1)


def within(index, size):
    return lax.bitwise_and(index, size - 1)


def factor_kernel(first, hidden, x_ref, weight_ref, *refs):
    mask_ref = refs[0] if len(refs) == 3 else None
    z_ref, y_scr = refs[-2:]
    groups, seqs, _ = z_ref.shape
    _, rows, channels = x_ref.shape
    rep = LANES // hidden
    width = rows * hidden
    step = y_scr.shape[1] // rows
    w = jnp.concatenate([weight_ref[...].T, jnp.ones((channels, LANES), BF16)], axis=1)
    sums = dot(jnp.ones((8, channels), BF16), w)[:1, :LANES]
    if mask_ref is not None:
        residues = mask_ref.shape[0]
        start = lax.axis_index("dap") * rows
        spread = iota((residues, width), 0) == start + over(iota((residues, width), 1), hidden)
        live = dot_tn(mask_ref[...].astype(BF16), spread.astype(BF16))
    block = over(iota((step, LANES), 1), hidden)
    side = (2 * LANES, 2 * LANES)
    ones = (over(iota(side, 0), LANES) == over(iota(side, 1), LANES)).astype(BF16)
    for turn in range(seqs // step):
        x = x_ref[first + turn * step : first + (turn + 1) * step].reshape(step * rows, channels)
        y = dot(x, w)
        mean = y[:, LANES:] * (1.0 / channels)
        square = jnp.zeros_like(mean)
        for half in range(channels // LANES):
            centered = x[:, half * LANES : (half + 1) * LANES].astype(F32) - mean
            square = square + centered * centered
        tops = square.shape[0] // 2
        square = jnp.concatenate([square[:tops], square[tops:]], axis=1)
        spread = dot(square.astype(BF16), ones)
        spread = jnp.concatenate([spread[:, :LANES], spread[:, LANES:]], axis=0)
        scale = lax.rsqrt(spread * (1.0 / channels) + EPSILON)
        y_scr[turn] = (y[:, :LANES] - mean * sums) * scale
        here = slice(turn * step, (turn + 1) * step)
        for group in range(groups):
            z = y_scr[turn, pl.ds(group * rep, step, stride=rows), :]
            for k in range(1, rep):
                next_z = y_scr[turn, pl.ds(group * rep + k, step, stride=rows), :]
                z = jnp.where(block == k, next_z, z)
            if mask_ref is not None:
                z = z * live[here, group * LANES : (group + 1) * LANES]
            z_ref[group, here, :] = z.astype(BF16)


def factor(alignment, weight, hidden, first, seqs, mask=None):
    _, rows, channels = alignment.shape
    step = seqs // 4
    operands = (alignment, weight) if mask is None else (alignment, weight, mask)
    return pl.pallas_call(
        functools.partial(factor_kernel, first, hidden),
        out_shape=jax.ShapeDtypeStruct((rows * hidden // LANES, seqs, LANES), BF16),
        in_specs=[vmem()] * len(operands),
        out_specs=vmem(),
        scratch_shapes=[pltpu.VMEM((seqs // step, step * rows, LANES), F32)],
        compiler_params=pltpu.CompilerParams(vmem_limit_bytes=24 << 20),
        cost_estimate=pl.CostEstimate(
            flops=2 * seqs * rows * channels * 512, bytes_accessed=seqs << 14, transcendentals=0
        ),
    )(*operands)


def prepare_kernel(
    zl_ref, mask_ref, pair_ref, live_ref, chain_ref, table_ref, proj_ref,
    zlt_ref, base_ref, inverse_ref, live_out_ref, proj_out_ref, seen_ref, pair_scr, table_scr,
):
    rows, cols, _ = pair_ref.shape
    pairs = rows * cols
    residues = mask_ref.shape[0]
    classes = table_ref.shape[0]
    row_start = lax.axis_index("dap") * rows
    col_start = lax.axis_index("sub") * cols
    for group in range(zl_ref.shape[0]):
        turned = zl_ref[group].T
        for half in range(zlt_ref.shape[0]):
            lanes = slice(half * LANES, (half + 1) * LANES)
            zlt_ref[half, group * LANES : (group + 1) * LANES, :] = turned[:, lanes]
    proj_out_ref[...] = proj_ref[...].reshape(proj_out_ref.shape).astype(BF16)
    groups = zl_ref.shape[0]
    width = groups * LANES
    hidden = width // rows
    for block in range(cols // rows):
        column = col_start + block * rows + over(iota((residues, width), 1), hidden)
        spread = (iota((residues, width), 0) == column).astype(BF16)
        seen = dot_tn(mask_ref[...].astype(BF16), spread).astype(BF16)
        for group in range(groups):
            seen_ref[block * groups + group] = seen[:, group * LANES : (group + 1) * LANES]
    which = iota((pairs, residues), 0)
    place = iota((pairs, residues), 1)
    pick_row = (place == row_start + within(which, rows)).astype(BF16)
    pick_col = (place == col_start + over(which, rows)).astype(BF16)
    mask = mask_ref[...].astype(BF16)
    both = (dot(pick_row, mask) * dot(pick_col, mask)).astype(BF16)
    counts = dot(both, jnp.ones((mask.shape[1], LANES), BF16))
    inverse_ref[...] = 1.0 / jnp.maximum(counts, 1.0)
    live = jnp.broadcast_to(live_ref[...].astype(F32), (LANES, residues)).astype(BF16)
    chain = jnp.broadcast_to(chain_ref[...].astype(F32), (LANES, residues)).astype(BF16)
    live_out_ref[...] = dot_nt(pick_row, live) * dot_nt(pick_col, live)
    same = dot_nt(pick_row, chain) == dot_nt(pick_col, chain)
    pair = iota((pairs, LANES), 0)
    offset = (row_start + within(pair, rows)) - (col_start + over(pair, rows)) + REL_CLIP
    bucket = jnp.where(same, jnp.clip(offset, 0, 2 * REL_CLIP), 2 * REL_CLIP + 1)
    table_scr[...] = jnp.zeros_like(table_scr)
    table_scr[pl.ds(0, classes), :] = table_ref[...].astype(F32)
    onehot = (bucket == iota((pairs, LANES), 1)).astype(BF16)
    relative = dot(onehot, table_scr[...].astype(BF16))
    pair_scr[...] = pair_ref[...].reshape(pairs, LANES).astype(F32)
    for col in range(cols):
        here = slice(col * rows, (col + 1) * rows)
        base_ref[here, :] = relative[here] + pair_scr[pl.ds(col, rows, stride=cols), :]


def prepare(zl, mask, pair_input, residue_mask, chain_index, table, proj):
    rows, cols, channels = pair_input.shape
    pairs = rows * cols
    shape = jax.ShapeDtypeStruct((pairs, channels), F32)
    depth = proj.shape[0] * proj.shape[1]
    return pl.pallas_call(
        prepare_kernel,
        out_shape=(
            jax.ShapeDtypeStruct((zl.shape[1] // LANES, zl.shape[0] * LANES, LANES), BF16),
            shape,
            shape,
            shape,
            jax.ShapeDtypeStruct((depth, channels), BF16),
            jax.ShapeDtypeStruct((cols // rows * zl.shape[0], *zl.shape[1:]), BF16),
        ),
        in_specs=[vmem()] * 7,
        out_specs=[vmem()] * 6,
        scratch_shapes=[pltpu.VMEM((pairs, channels), F32), pltpu.VMEM((LANES, channels), F32)],
        compiler_params=pltpu.CompilerParams(vmem_limit_bytes=24 << 20),
        cost_estimate=pl.CostEstimate(
            flops=2 * pairs * 256 * 1024, bytes_accessed=2 << 20, transcendentals=0
        ),
    )(zl, mask, pair_input, residue_mask[None, :], chain_index[None, :], table, proj)


def pair_kernel(ratio, hidden, zlt_ref, *refs):
    zr_refs, refs = refs[: ratio * PARTS], refs[ratio * PARTS :]
    (seen_ref, base_ref, inverse_ref, live_ref, proj_ref, tl_ref, tr_ref,
     both_ref, one_ref, outer_scr, flat_scr, one_scr) = refs
    pairs, channels = base_ref.shape
    rows = zlt_ref.shape[1] // hidden
    rep = LANES // hidden
    me = lax.axis_index("dap")
    lane = iota((rows, LANES), 1)
    odd = (lane // hidden) % 2 == 1
    upper = lane // (2 * hidden) == 1
    half = 2 * hidden
    left = jnp.concatenate([zlt_ref[part] for part in range(zlt_ref.shape[0])], axis=1)
    for step in range(ratio):
        block = lax.rem(me + step, ratio)
        right = []
        for group in range(rows // rep):
            parts = [zr_refs[step * PARTS + part][group] for part in range(PARTS)]
            right.append(jnp.concatenate(parts, axis=0) * seen_ref[block * (rows // rep) + group])
        outer = dot(left, jnp.concatenate(right, axis=1))
        for group in range(rows // rep):
            outer_scr[group] = outer[:, group * LANES : (group + 1) * LANES]
        for group in range(rows // rep):
            for quad in range(hidden // rep):
                s0, s1, s2, s3 = (
                    outer_scr[group, pl.ds(quad * rep + k, rows, stride=hidden), :] for k in range(rep)
                )
                t0 = jnp.where(upper, pltpu.roll(s2, half, 1), s0)
                t1 = jnp.where(upper, pltpu.roll(s3, half, 1), s1)
                t2 = jnp.where(upper, s2, pltpu.roll(s0, half, 1))
                t3 = jnp.where(upper, s3, pltpu.roll(s1, half, 1))
                back = LANES - hidden
                found = (
                    jnp.where(odd, pltpu.roll(t1, hidden, 1), t0),
                    jnp.where(odd, t1, pltpu.roll(t0, back, 1)),
                    jnp.where(odd, pltpu.roll(t3, hidden, 1), t2),
                    jnp.where(odd, t3, pltpu.roll(t2, back, 1)),
                )
                for k in range(rep):
                    first = block * rows * rows + (group * rep + k) * rows
                    if ratio == 1:
                        first = (group * rep + k) * rows
                    else:
                        first = pl.multiple_of(first, rows)
                    flat_scr[quad, pl.ds(first, rows), :] = found[k].astype(BF16)
    flat = jnp.concatenate([flat_scr[quad] for quad in range(flat_scr.shape[0])], axis=1)
    outer_mean = dot(flat, proj_ref[...]) * inverse_ref[...]
    one = (base_ref[...] + outer_mean).astype(BF16).astype(F32)
    one_scr[...] = one
    norm = layer_norm(one).astype(BF16)
    for side, weight in enumerate((tl_ref, tr_ref)):
        both = dot(norm, weight[...])
        factor = jax.nn.sigmoid(both[:, :channels]) * both[:, channels:] * live_ref[...]
        both_ref[side] = factor.astype(BF16)
    cols = pairs // rows
    for row in range(rows):
        one_ref[row * cols : (row + 1) * cols, :] = one_scr[pl.ds(row, cols, stride=rows), :].astype(BF16)


def pair_update(hidden, zlt, zrs, seen, base, inverse, live, proj, triangle_left, triangle_right):
    pairs, channels = base.shape
    ratio = len(zrs) // PARTS
    shape = jax.ShapeDtypeStruct((pairs, channels), BF16)
    return pl.pallas_call(
        functools.partial(pair_kernel, ratio, hidden),
        out_shape=(jax.ShapeDtypeStruct((2, pairs, channels), BF16), shape),
        in_specs=[vmem()] * (8 + len(zrs)),
        out_specs=[vmem()] * 2,
        scratch_shapes=[
            pltpu.VMEM((zrs[0].shape[0], zlt.shape[1], LANES), F32),
            pltpu.VMEM((proj.shape[0] // LANES, pairs, LANES), BF16),
            pltpu.VMEM((pairs, channels), F32),
        ],
        compiler_params=pltpu.CompilerParams(vmem_limit_bytes=32 << 20),
        cost_estimate=pl.CostEstimate(
            flops=2 * pairs * 1024 * 512, bytes_accessed=2 << 20, transcendentals=pairs * 256
        ),
    )(zlt, *zrs, seen, base, inverse, live, proj, triangle_left, triangle_right)


def other(sub):
    return sub + 1 - 2 * (sub % 2)


def gate_kernel(one_ref, weight_ref, gate_ref):
    norm = layer_norm(one_ref[...].astype(F32)).astype(BF16)
    gate_ref[...] = jax.nn.sigmoid(dot(norm, weight_ref[...]))


def output_gate(one, weight):
    return pl.pallas_call(
        gate_kernel,
        out_shape=jax.ShapeDtypeStruct(one.shape, F32),
        in_specs=[vmem()] * 2,
        out_specs=vmem(),
        compiler_params=pltpu.CompilerParams(vmem_limit_bytes=4 << 20),
        cost_estimate=pl.CostEstimate(
            flops=2 * one.size * LANES, bytes_accessed=1 << 18, transcendentals=one.size
        ),
    )(one, weight)


SENDERS = ((0, 2, 3, 1), (2, 1, 0, 3), (0, 3, 2, 1), (2, 0, 1, 3))


def sender(a, b, subs, ratio):
    if (subs, ratio) == (4, 1):
        return SENDERS[b][a]
    return a // ratio


def sender_index(a, b, subs, ratio):
    if (subs, ratio) != (4, 1):
        return a // ratio
    found = 0
    for col, places in enumerate(SENDERS):
        for row, place in enumerate(places):
            found = jnp.where((a == row) & (b == col), place, found)
    return found


def triangle_kernel(subs, ratio, cols, *refs):
    twos = subs // 2
    rights, refs = refs[: twos * ratio], refs[twos * ratio :]
    lefts, refs = refs[:twos], refs[twos:]
    (one_ref, gate_ref, out_ref, up_ref, down_ref, result_ref, left_scr, right_scr, sum_scr) = refs
    pairs, channels = one_ref.shape
    rows = pairs // cols
    here, there = lax.axis_index("dap"), lax.axis_index("sub")
    first_sub = sender_index(here, there, subs, ratio)
    for step in range(twos):
        sub = lax.rem(there + 2 * step, subs)
        left_scr[sub] = lefts[step][0].astype(F32)
        left_scr[other(sub)] = lefts[step][1].astype(F32)
    for turn in range(ratio):
        block = lax.rem(here + turn, ratio)
        for step in range(twos):
            sub = lax.rem(first_sub + 2 * step, subs)
            right_scr[block * subs + sub] = rights[turn * twos + step][0].astype(F32)
            right_scr[block * subs + other(sub)] = rights[turn * twos + step][1].astype(F32)
    for block in range(ratio):
        totals = tuple(jnp.zeros((rows, channels), F32) for _ in range(rows))
        for sub in range(subs):

            def body(k, totals, sub=sub, block=block):
                first = pl.multiple_of(k * rows, rows)
                right = right_scr[block * subs + sub, pl.ds(first, rows), :]
                return tuple(
                    totals[i] + left_scr[sub, pl.ds(first + i, 1), :] * right for i in range(rows)
                )

            totals = lax.fori_loop(0, cols, body, totals, unroll=4)
        for i in range(rows):
            sum_scr[i * cols + block * rows : i * cols + (block + 1) * rows, :] = totals[i]
    one = one_ref[...].astype(F32)
    hidden = layer_norm(sum_scr[...].astype(BF16).astype(F32)).astype(BF16)
    two = (one + gate_ref[...] * dot(hidden, out_ref[...])).astype(BF16).astype(F32)
    wide = jnp.maximum(dot(layer_norm(two).astype(BF16), up_ref[...]), 0.0).astype(BF16)
    result = (two + dot(wide, down_ref[...])).astype(BF16)
    result_ref[...] = result.reshape(result_ref.shape)


def triangle_update(lefts, rights, one, cols, gate, out, up, down):
    pairs, channels = one.shape
    rows = pairs // cols
    subs = 2 * len(lefts)
    ratio = len(rights) // len(lefts)
    return pl.pallas_call(
        functools.partial(triangle_kernel, subs, ratio, cols),
        out_shape=jax.ShapeDtypeStruct((rows, cols, channels), BF16),
        in_specs=[vmem()] * (len(lefts) + len(rights) + 5),
        out_specs=vmem(),
        scratch_shapes=[
            pltpu.VMEM((subs, pairs, channels), F32),
            pltpu.VMEM((subs * ratio, pairs, channels), F32),
            pltpu.VMEM((pairs, channels), F32),
        ],
        compiler_params=pltpu.CompilerParams(vmem_limit_bytes=(16 << 20) if ratio == 1 else (50 << 20)),
        cost_estimate=pl.CostEstimate(
            flops=2 * pairs * channels * 2048, bytes_accessed=2 << 20, transcendentals=pairs * 128
        ),
    )(*rights, *lefts, one, gate, out, up, down)


def per_device(
    alignment,
    alignment_mask,
    pair_input,
    residue_mask,
    chain_index,
    outer_left,
    outer_right,
    outer_proj,
    triangle_left,
    triangle_right,
    triangle_gate,
    triangle_out,
    relative_table,
    transition_up,
    transition_down,
):
    daps, subs = lax.axis_size("dap"), lax.axis_size("sub")
    ratio = daps // subs
    cols = pair_input.shape[1]

    def fetch(values, source):
        perm = []
        for a in range(daps):
            for b in range(subs):
                dap, sub = source(a, b)
                perm.append((dap * subs + sub, a * subs + b))
        return lax.ppermute(values, ("dap", "sub"), perm)

    def owner(a, b, turn):
        return ratio * b + (a + turn) % ratio

    hidden = outer_left.shape[1]
    seqs = alignment.shape[0]
    part_seqs = seqs // PARTS
    mask = alignment_mask.T
    wide_left, wide_right = (
        jnp.tile(weight.T, (LANES // hidden, 1)) for weight in (outer_left, outer_right)
    )
    zr_parts = [
        factor(alignment, wide_right, hidden, part * part_seqs, part_seqs) for part in range(PARTS)
    ]
    zrs = [
        fetch(zr, lambda a, b, turn=turn: (owner(a, b, turn), sender(a, b, subs, ratio)))
        for turn in range(ratio)
        for zr in zr_parts
    ]
    zl = factor(alignment, wide_left, hidden, 0, seqs, mask)
    zlt, base, inverse, live, proj, seen = prepare(
        zl, mask, pair_input, residue_mask, chain_index, relative_table, outer_proj
    )
    own, one = pair_update(
        hidden, zlt, zrs, seen, base, inverse, live, proj, triangle_left, triangle_right
    )
    near = fetch(own, lambda a, b: (a, other(b)))
    left = jnp.stack([own[0], near[0]])
    right = jnp.stack([own[1], near[1]])
    rights = [
        fetch(
            right,
            lambda a, b, t=turn, m=step: (
                owner(a, b, t), (sender(a, b, subs, ratio) + 2 * m) % subs
            ),
        )
        for turn in range(ratio)
        for step in range(subs // 2)
    ]
    lefts = [left] + [
        fetch(left, lambda a, b, m=step: (a, (b + 2 * m) % subs)) for step in range(1, subs // 2)
    ]
    gate = output_gate(one, triangle_gate)
    return triangle_update(
        lefts, rights, one, cols, gate, triangle_out, transition_up, transition_down
    )


def solution(mesh):
    in_specs = (
        P("parts", "dap", None),
        P("parts", None),
        P(("parts", "dap"), "sub", None),
        P("parts"),
        P("parts"),
        P(),
        P(),
        P(),
        P(),
        P(),
        P(),
        P(),
        P(),
        P(),
        P(),
    )
    out_specs = P(("parts", "dap"), "sub", None)
    return jax.shard_map(
        per_device, mesh=mesh, in_specs=in_specs, out_specs=out_specs, check_vma=False
    )
```

```python
import functools

import jax
import jax.numpy as jnp
from jax import lax
from jax.experimental import pallas as pl
from jax.experimental.pallas import tpu as pltpu
from jax.sharding import PartitionSpec as P

REL_CLIP = 32
LANES = 128
EPSILON = 1e-05
BF16 = jnp.bfloat16
F32 = jnp.float32
NT = (((1,), (1,)), ((), ()))
TN = (((0,), (0,)), ((), ()))


def layer_norm(values):
    average = jnp.mean(values, axis=-1, keepdims=True)
    centered = values - average
    spread = jnp.mean(centered * centered, axis=-1, keepdims=True)
    return centered * lax.rsqrt(spread + EPSILON)


def dot(left, right):
    return jnp.dot(left, right, preferred_element_type=F32)


def dot_nt(left, right):
    return lax.dot_general(left, right, NT, preferred_element_type=F32)


def dot_tn(left, right):
    return lax.dot_general(left, right, TN, preferred_element_type=F32)


def iota(shape, dim):
    return lax.broadcasted_iota(jnp.int32, shape, dim)


def vmem():
    return pl.BlockSpec(memory_space=pltpu.VMEM)


def over(index, size):
    return lax.shift_right_logical(index, size.bit_length() - 1)


def within(index, size):
    return lax.bitwise_and(index, size - 1)


def repeat_kernel(weight_ref, out_ref):
    rep = LANES // weight_ref.shape[0]
    out_ref[...] = jnp.concatenate([weight_ref[...]] * rep, axis=0).T


def repeat_weight(weight):
    return pl.pallas_call(
        repeat_kernel,
        out_shape=jax.ShapeDtypeStruct((weight.shape[1], LANES), BF16),
        in_specs=[vmem()],
        out_specs=vmem(),
        compiler_params=pltpu.CompilerParams(vmem_limit_bytes=2 << 20),
        cost_estimate=pl.CostEstimate(flops=1 << 30, bytes_accessed=1 << 17, transcendentals=0),
    )(weight)


def factor_kernel(x_ref, weight_ref, *refs):
    mask_ref = refs[0] if len(refs) == 3 else None
    z_ref, y_scr = refs[-2:]
    groups, seqs, _ = z_ref.shape
    _, rows, channels = x_ref.shape
    rep = rows // groups
    hidden = LANES // rep
    width = rows * hidden
    step = y_scr.shape[1] // rows
    w = jnp.concatenate([weight_ref[...], jnp.ones((channels, LANES), BF16)], axis=1)
    ones = jnp.ones((LANES, LANES), BF16)
    sums = dot(jnp.ones((8, channels), BF16), weight_ref[...])[:1]
    block = over(iota((step, LANES), 1), hidden)
    if mask_ref is not None:
        residues = mask_ref.shape[0]
        column = lax.axis_index("dap") * rows + over(iota((residues, width), 1), hidden)
        lanes_of = (iota((residues, width), 0) == column).astype(BF16)
        live = dot_tn(mask_ref[...].astype(BF16), lanes_of)
    for turn in range(seqs // step):
        x = x_ref[turn * step : (turn + 1) * step].reshape(step * rows, channels)
        y = dot(x, w)
        mean = y[:, LANES:] * (1.0 / channels)
        square = jnp.zeros_like(mean)
        for half in range(channels // LANES):
            centered = x[:, half * LANES : (half + 1) * LANES].astype(F32) - mean
            square = square + centered * centered
        spread = dot(square.astype(BF16), ones)
        scale = lax.rsqrt(spread * (1.0 / channels) + EPSILON)
        y_scr[turn] = (y[:, :LANES] - mean * sums) * scale
        here = slice(turn * step, (turn + 1) * step)
        for group in range(groups):
            z = y_scr[turn, pl.ds(group * rep, step, stride=rows), :]
            for k in range(1, rep):
                next_z = y_scr[turn, pl.ds(group * rep + k, step, stride=rows), :]
                z = jnp.where(block == k, next_z, z)
            if mask_ref is not None:
                z = z * live[here, group * LANES : (group + 1) * LANES]
            z_ref[group, here, :] = z.astype(BF16)


def factor(alignment, weight, hidden, mask=None):
    seqs, rows, channels = alignment.shape
    step = seqs // 4
    operands = (alignment, weight) if mask is None else (alignment, weight, mask)
    return pl.pallas_call(
        factor_kernel,
        out_shape=jax.ShapeDtypeStruct((rows * hidden // LANES, seqs, LANES), BF16),
        in_specs=[vmem()] * len(operands),
        out_specs=vmem(),
        scratch_shapes=[pltpu.VMEM((seqs // step, step * rows, LANES), F32)],
        compiler_params=pltpu.CompilerParams(vmem_limit_bytes=24 << 20),
        cost_estimate=pl.CostEstimate(
            flops=2 * seqs * rows * channels * 512, bytes_accessed=seqs << 14, transcendentals=0
        ),
    )(*operands)


def prepare_kernel(
    zl_ref, mask_ref, pair_ref, live_ref, chain_ref, table_ref, proj_ref,
    zlt_ref, base_ref, inverse_ref, live_out_ref, proj_out_ref, seen_ref, pair_scr, table_scr,
):
    rows, cols, _ = pair_ref.shape
    pairs = rows * cols
    residues = mask_ref.shape[0]
    classes = table_ref.shape[0]
    row_start = lax.axis_index("dap") * rows
    col_start = lax.axis_index("sub") * cols
    for group in range(zl_ref.shape[0]):
        turned = zl_ref[group].T
        for half in range(zlt_ref.shape[0]):
            lanes = slice(half * LANES, (half + 1) * LANES)
            zlt_ref[half, group * LANES : (group + 1) * LANES, :] = turned[:, lanes]
    proj_out_ref[...] = proj_ref[...].reshape(proj_out_ref.shape).astype(BF16)
    groups = zl_ref.shape[0]
    width = groups * LANES
    hidden = width // rows
    for block in range(cols // rows):
        column = col_start + block * rows + over(iota((residues, width), 1), hidden)
        spread = (iota((residues, width), 0) == column).astype(BF16)
        seen = dot_tn(mask_ref[...].astype(BF16), spread).astype(BF16)
        for group in range(groups):
            seen_ref[block * groups + group] = seen[:, group * LANES : (group + 1) * LANES]
    which = iota((pairs, residues), 0)
    place = iota((pairs, residues), 1)
    pick_row = (place == row_start + within(which, rows)).astype(BF16)
    pick_col = (place == col_start + over(which, rows)).astype(BF16)
    mask = mask_ref[...].astype(BF16)
    both = (dot(pick_row, mask) * dot(pick_col, mask)).astype(BF16)
    counts = dot(both, jnp.ones((mask.shape[1], LANES), BF16))
    inverse_ref[...] = 1.0 / jnp.maximum(counts, 1.0)
    live = jnp.broadcast_to(live_ref[...].astype(F32), (LANES, residues)).astype(BF16)
    chain = jnp.broadcast_to(chain_ref[...].astype(F32), (LANES, residues)).astype(BF16)
    live_out_ref[...] = dot_nt(pick_row, live) * dot_nt(pick_col, live)
    same = dot_nt(pick_row, chain) == dot_nt(pick_col, chain)
    pair = iota((pairs, LANES), 0)
    offset = (row_start + within(pair, rows)) - (col_start + over(pair, rows)) + REL_CLIP
    bucket = jnp.where(same, jnp.clip(offset, 0, 2 * REL_CLIP), 2 * REL_CLIP + 1)
    table_scr[...] = jnp.zeros_like(table_scr)
    table_scr[pl.ds(0, classes), :] = table_ref[...].astype(F32)
    onehot = (bucket == iota((pairs, LANES), 1)).astype(BF16)
    relative = dot(onehot, table_scr[...].astype(BF16))
    pair_scr[...] = pair_ref[...].reshape(pairs, LANES).astype(F32)
    for col in range(cols):
        here = slice(col * rows, (col + 1) * rows)
        base_ref[here, :] = relative[here] + pair_scr[pl.ds(col, rows, stride=cols), :]


def prepare(zl, mask, pair_input, residue_mask, chain_index, table, proj):
    rows, cols, channels = pair_input.shape
    pairs = rows * cols
    shape = jax.ShapeDtypeStruct((pairs, channels), F32)
    depth = proj.shape[0] * proj.shape[1]
    return pl.pallas_call(
        prepare_kernel,
        out_shape=(
            jax.ShapeDtypeStruct((zl.shape[1] // LANES, zl.shape[0] * LANES, LANES), BF16),
            shape,
            shape,
            shape,
            jax.ShapeDtypeStruct((depth, channels), BF16),
            jax.ShapeDtypeStruct((cols // rows * zl.shape[0], *zl.shape[1:]), BF16),
        ),
        in_specs=[vmem()] * 7,
        out_specs=[vmem()] * 6,
        scratch_shapes=[pltpu.VMEM((pairs, channels), F32), pltpu.VMEM((LANES, channels), F32)],
        compiler_params=pltpu.CompilerParams(vmem_limit_bytes=24 << 20),
        cost_estimate=pl.CostEstimate(
            flops=2 * pairs * 256 * 1024, bytes_accessed=2 << 20, transcendentals=0
        ),
    )(zl, mask, pair_input, residue_mask[None, :], chain_index[None, :], table, proj)


def pair_kernel(ratio, hidden, zlt_ref, *refs):
    zr_refs, refs = refs[:ratio], refs[ratio:]
    (seen_ref, base_ref, inverse_ref, live_ref, proj_ref, tl_ref, tr_ref,
     both_ref, left_ref, one_ref, outer_scr, flat_scr, one_scr) = refs
    pairs, channels = base_ref.shape
    rows = zlt_ref.shape[1] // hidden
    rep = LANES // hidden
    me = lax.axis_index("dap")
    lane = iota((rows, LANES), 1)
    odd = (lane // hidden) % 2 == 1
    upper = lane // (2 * hidden) == 1
    half = 2 * hidden
    left = jnp.concatenate([zlt_ref[part] for part in range(zlt_ref.shape[0])], axis=1)
    for step in range(ratio):
        block = lax.rem(me + step, ratio)
        right = []
        for group in range(rows // rep):
            right.append(zr_refs[step][group] * seen_ref[block * (rows // rep) + group])
        outer = dot(left, jnp.concatenate(right, axis=1))
        for group in range(rows // rep):
            outer_scr[group] = outer[:, group * LANES : (group + 1) * LANES]
        for group in range(rows // rep):
            for quad in range(hidden // rep):
                s0, s1, s2, s3 = (
                    outer_scr[group, pl.ds(quad * rep + k, rows, stride=hidden), :] for k in range(rep)
                )
                t0 = jnp.where(upper, pltpu.roll(s2, half, 1), s0)
                t1 = jnp.where(upper, pltpu.roll(s3, half, 1), s1)
                t2 = jnp.where(upper, s2, pltpu.roll(s0, half, 1))
                t3 = jnp.where(upper, s3, pltpu.roll(s1, half, 1))
                back = LANES - hidden
                found = (
                    jnp.where(odd, pltpu.roll(t1, hidden, 1), t0),
                    jnp.where(odd, t1, pltpu.roll(t0, back, 1)),
                    jnp.where(odd, pltpu.roll(t3, hidden, 1), t2),
                    jnp.where(odd, t3, pltpu.roll(t2, back, 1)),
                )
                for k in range(rep):
                    first = block * rows * rows + (group * rep + k) * rows
                    if ratio == 1:
                        first = (group * rep + k) * rows
                    else:
                        first = pl.multiple_of(first, rows)
                    flat_scr[quad, pl.ds(first, rows), :] = found[k].astype(BF16)
    flat = jnp.concatenate([flat_scr[quad] for quad in range(flat_scr.shape[0])], axis=1)
    outer_mean = dot(flat, proj_ref[...]) * inverse_ref[...]
    one = (base_ref[...] + outer_mean).astype(BF16).astype(F32)
    one_scr[...] = one
    norm = layer_norm(one).astype(BF16)
    for side, weight in enumerate((tl_ref, tr_ref)):
        both = dot(norm, weight[...])
        factor = jax.nn.sigmoid(both[:, :channels]) * both[:, channels:] * live_ref[...]
        both_ref[side] = factor.astype(BF16)
        if side == 0:
            left_ref[...] = factor.astype(BF16)
    cols = pairs // rows
    for row in range(rows):
        one_ref[row * cols : (row + 1) * cols, :] = one_scr[pl.ds(row, cols, stride=rows), :].astype(BF16)


def pair_update(hidden, zlt, zrs, seen, base, inverse, live, proj, triangle_left, triangle_right):
    pairs, channels = base.shape
    ratio = len(zrs)
    shape = jax.ShapeDtypeStruct((pairs, channels), BF16)
    return pl.pallas_call(
        functools.partial(pair_kernel, ratio, hidden),
        out_shape=(jax.ShapeDtypeStruct((2, pairs, channels), BF16), shape, shape),
        in_specs=[vmem()] * (8 + len(zrs)),
        out_specs=[vmem()] * 3,
        scratch_shapes=[
            pltpu.VMEM((zrs[0].shape[0], zlt.shape[1], LANES), F32),
            pltpu.VMEM((proj.shape[0] // LANES, pairs, LANES), BF16),
            pltpu.VMEM((pairs, channels), F32),
        ],
        compiler_params=pltpu.CompilerParams(vmem_limit_bytes=32 << 20),
        cost_estimate=pl.CostEstimate(
            flops=2 * pairs * 1024 * 512, bytes_accessed=2 << 20, transcendentals=pairs * 256
        ),
    )(zlt, *zrs, seen, base, inverse, live, proj, triangle_left, triangle_right)


def other(sub):
    return sub + 1 - 2 * (sub % 2)


SENDERS = ((0, 2, 3, 1), (2, 1, 0, 3), (0, 3, 2, 1), (2, 0, 1, 3))


def sender(a, b, subs, ratio):
    if (subs, ratio) == (4, 1):
        return SENDERS[b][a]
    return a // ratio


def sender_index(a, b, subs, ratio):
    if (subs, ratio) != (4, 1):
        return a // ratio
    found = 0
    for col, places in enumerate(SENDERS):
        for row, place in enumerate(places):
            found = jnp.where((a == row) & (b == col), place, found)
    return found


def add_terms(sums, start, lefts, rights, steps, ratio, cols, left_scr):
    subs = left_scr.shape[0]
    _, channels = sums.shape
    rows = left_scr.shape[1] // cols
    here, there = lax.axis_index("dap"), lax.axis_index("sub")
    first_sub = sender_index(here, there, subs, ratio)
    own, near, across, beyond = lefts
    left_scr[there] = own[0].astype(F32)
    left_scr[other(there)] = near[0].astype(F32)
    for step in range(1, subs // 2):
        sub = lax.rem(there + 2 * step, subs)
        left_scr[sub] = across[step - 1][...].astype(F32)
        left_scr[other(sub)] = beyond[step - 1][...].astype(F32)
    for turn in range(ratio):
        block = lax.rem(here + turn, ratio) if ratio > 1 else 0
        places = [i * cols + block * rows for i in range(rows)]
        if ratio > 1:
            places = [pl.multiple_of(place, rows) for place in places]
        if start is None:
            totals = tuple(jnp.zeros((rows, channels), F32) for _ in range(rows))
        else:
            totals = tuple(start[pl.ds(place, rows), :] for place in places)
        for index, step in enumerate(steps):
            sub = lax.rem(first_sub + 2 * step, subs)
            pair = rights[turn * len(steps) + index]
            for member, slot in enumerate((sub, other(sub))):

                def body(k, totals, slot=slot, member=member, pair=pair):
                    first = pl.multiple_of(k * rows, rows)
                    right = pair[member, pl.ds(first, rows), :].astype(F32)
                    return tuple(
                        totals[i] + left_scr[slot, pl.ds(first + i, 1), :] * right
                        for i in range(rows)
                    )

                totals = lax.fori_loop(0, cols, body, totals, unroll=4)
        for place, total in zip(places, totals):
            sums[pl.ds(place, rows), :] = total


def split_lefts(refs, twos):
    count = twos - 1
    lefts = (refs[0], refs[1], refs[2 : 2 + count], refs[2 + count : 2 + 2 * count])
    return lefts, refs[2 + 2 * count :]


def first_kernel(steps, twos, ratio, cols, *refs):
    lefts, refs = split_lefts(refs, twos)
    rights, refs = refs[: ratio * len(steps)], refs[ratio * len(steps) :]
    one_ref, weight_ref, sums_ref, gate_ref, left_scr = refs
    add_terms(sums_ref, None, lefts, rights, steps, ratio, cols, left_scr)
    norm = layer_norm(one_ref[...].astype(F32)).astype(BF16)
    gate_ref[...] = jax.nn.sigmoid(dot(norm, weight_ref[...]))


def last_kernel(steps, twos, ratio, cols, *refs):
    lefts, refs = split_lefts(refs, twos)
    rights, refs = refs[: ratio * len(steps)], refs[ratio * len(steps) :]
    (start_ref, one_ref, gate_ref, out_ref, up_ref, down_ref, result_ref, left_scr, sum_scr) = refs
    add_terms(sum_scr, start_ref, lefts, rights, steps, ratio, cols, left_scr)
    one = one_ref[...].astype(F32)
    hidden = layer_norm(sum_scr[...].astype(BF16).astype(F32)).astype(BF16)
    two = (one + gate_ref[...] * dot(hidden, out_ref[...])).astype(BF16).astype(F32)
    wide = jnp.maximum(dot(layer_norm(two).astype(BF16), up_ref[...]), 0.0).astype(BF16)
    result = (two + dot(wide, down_ref[...])).astype(BF16)
    result_ref[...] = result.reshape(result_ref.shape)


def triangle_update(lefts, rights, one, cols, gate_weight, out, up, down):
    pairs, channels = one.shape
    rows = pairs // cols
    twos = len(lefts) // 2
    subs = 2 * twos
    ratio = len(rights) // twos
    late, early = range(twos // 2), range(twos // 2, twos)
    limit = (12 << 20) if ratio == 1 else (50 << 20)
    left_scr = pltpu.VMEM((subs, pairs, channels), F32)
    shape = jax.ShapeDtypeStruct((pairs, channels), F32)

    def chosen(steps):
        return [rights[turn * twos + step] for turn in range(ratio) for step in steps]

    sums, gate = pl.pallas_call(
        functools.partial(first_kernel, early, twos, ratio, cols),
        out_shape=(shape, shape),
        in_specs=[vmem()] * (len(lefts) + ratio * len(early) + 2),
        out_specs=[vmem()] * 2,
        scratch_shapes=[left_scr],
        compiler_params=pltpu.CompilerParams(vmem_limit_bytes=limit),
        cost_estimate=pl.CostEstimate(
            flops=2 * pairs * channels * 1024, bytes_accessed=1 << 20, transcendentals=pairs * 128
        ),
    )(*lefts, *chosen(early), one, gate_weight)
    return pl.pallas_call(
        functools.partial(last_kernel, late, twos, ratio, cols),
        out_shape=jax.ShapeDtypeStruct((rows, cols, channels), BF16),
        in_specs=[vmem()] * (len(lefts) + ratio * len(late) + 6),
        out_specs=vmem(),
        scratch_shapes=[left_scr, pltpu.VMEM((pairs, channels), F32)],
        compiler_params=pltpu.CompilerParams(vmem_limit_bytes=limit),
        cost_estimate=pl.CostEstimate(
            flops=2 * pairs * channels * 2048, bytes_accessed=2 << 20, transcendentals=pairs * 128
        ),
    )(*lefts, *chosen(late), sums, one, gate, out, up, down)


def per_device(
    alignment,
    alignment_mask,
    pair_input,
    residue_mask,
    chain_index,
    outer_left,
    outer_right,
    outer_proj,
    triangle_left,
    triangle_right,
    triangle_gate,
    triangle_out,
    relative_table,
    transition_up,
    transition_down,
):
    daps, subs = lax.axis_size("dap"), lax.axis_size("sub")
    ratio = daps // subs
    cols = pair_input.shape[1]

    def fetch(values, source):
        perm = []
        for a in range(daps):
            for b in range(subs):
                dap, sub = source(a, b)
                perm.append((dap * subs + sub, a * subs + b))
        return lax.ppermute(values, ("dap", "sub"), perm)

    def owner(a, b, turn):
        return ratio * b + (a + turn) % ratio

    hidden = outer_left.shape[1]
    mask = alignment_mask.T
    zr = factor(alignment, repeat_weight(outer_right.T), hidden)
    zrs = [
        fetch(zr, lambda a, b, turn=turn: (owner(a, b, turn), sender(a, b, subs, ratio)))
        for turn in range(ratio)
    ]
    zl = factor(alignment, repeat_weight(outer_left.T), hidden, mask)
    zlt, base, inverse, live, proj, seen = prepare(
        zl, mask, pair_input, residue_mask, chain_index, relative_table, outer_proj
    )
    own, left, one = pair_update(
        hidden, zlt, zrs, seen, base, inverse, live, proj, triangle_left, triangle_right
    )
    near = fetch(own, lambda a, b: (a, other(b)))
    across = [
        fetch(left, lambda a, b, m=step: (a, (b + 2 * m) % subs)) for step in range(1, subs // 2)
    ]
    beyond = [fetch(block, lambda a, b: (a, other(b))) for block in across]
    right = jnp.stack([own[1], near[1]])
    rights = [
        fetch(
            right,
            lambda a, b, t=turn, m=step: (
                owner(a, b, t), (sender(a, b, subs, ratio) + 2 * m) % subs
            ),
        )
        for turn in range(ratio)
        for step in range(subs // 2)
    ]
    return triangle_update(
        [own, near, *across, *beyond],
        rights,
        one,
        cols,
        triangle_gate,
        triangle_out,
        transition_up,
        transition_down,
    )


def solution(mesh):
    in_specs = (
        P("parts", "dap", None),
        P("parts", None),
        P(("parts", "dap"), "sub", None),
        P("parts"),
        P("parts"),
        P(),
        P(),
        P(),
        P(),
        P(),
        P(),
        P(),
        P(),
        P(),
        P(),
    )
    out_specs = P(("parts", "dap"), "sub", None)
    return jax.shard_map(
        per_device, mesh=mesh, in_specs=in_specs, out_specs=out_specs, check_vma=False
    )
```

```python
import functools

import jax
import jax.numpy as jnp
from jax import lax
from jax.experimental import pallas as pl
from jax.experimental.pallas import tpu as pltpu
from jax.sharding import PartitionSpec as P

REL_CLIP = 32
LANES = 128
HALVES = 2
EPSILON = 1e-05
BF16 = jnp.bfloat16
F32 = jnp.float32
NT = (((1,), (1,)), ((), ()))
TN = (((0,), (0,)), ((), ()))


def layer_norm(values):
    average = jnp.mean(values, axis=-1, keepdims=True)
    centered = values - average
    spread = jnp.mean(centered * centered, axis=-1, keepdims=True)
    return centered * lax.rsqrt(spread + EPSILON)


def dot(left, right):
    return jnp.dot(left, right, preferred_element_type=F32)


def dot_nt(left, right):
    return lax.dot_general(left, right, NT, preferred_element_type=F32)


def dot_tn(left, right):
    return lax.dot_general(left, right, TN, preferred_element_type=F32)


def iota(shape, dim):
    return lax.broadcasted_iota(jnp.int32, shape, dim)


def vmem():
    return pl.BlockSpec(memory_space=pltpu.VMEM)


def over(index, size):
    return lax.shift_right_logical(index, size.bit_length() - 1)


def within(index, size):
    return lax.bitwise_and(index, size - 1)


def repeat_kernel(weight_ref, out_ref):
    rep = LANES // weight_ref.shape[0]
    out_ref[...] = jnp.concatenate([weight_ref[...]] * rep, axis=0).T


def repeat_weight(weight):
    return pl.pallas_call(
        repeat_kernel,
        out_shape=jax.ShapeDtypeStruct((weight.shape[1], LANES), BF16),
        in_specs=[vmem()],
        out_specs=vmem(),
        compiler_params=pltpu.CompilerParams(vmem_limit_bytes=2 << 20),
        cost_estimate=pl.CostEstimate(flops=1 << 30, bytes_accessed=1 << 17, transcendentals=0),
    )(weight)


def factor_kernel(x_ref, weight_ref, *refs):
    mask_ref = refs[0] if len(refs) == 3 else None
    z_ref, y_scr = refs[-2:]
    groups, seqs, _ = z_ref.shape
    _, rows, channels = x_ref.shape
    rep = rows // groups
    hidden = LANES // rep
    width = rows * hidden
    step = y_scr.shape[1] // rows
    w = jnp.concatenate([weight_ref[...], jnp.ones((channels, LANES), BF16)], axis=1)
    ones = jnp.ones((LANES, LANES), BF16)
    sums = dot(jnp.ones((8, channels), BF16), weight_ref[...])[:1]
    block = over(iota((step, LANES), 1), hidden)
    if mask_ref is not None:
        residues = mask_ref.shape[0]
        column = lax.axis_index("dap") * rows + over(iota((residues, width), 1), hidden)
        lanes_of = (iota((residues, width), 0) == column).astype(BF16)
        live = dot_tn(mask_ref[...].astype(BF16), lanes_of)
    for turn in range(seqs // step):
        x = x_ref[turn * step : (turn + 1) * step].reshape(step * rows, channels)
        y = dot(x, w)
        mean = y[:, LANES:] * (1.0 / channels)
        square = jnp.zeros_like(mean)
        for half in range(channels // LANES):
            centered = x[:, half * LANES : (half + 1) * LANES].astype(F32) - mean
            square = square + centered * centered
        spread = dot(square.astype(BF16), ones)
        scale = lax.rsqrt(spread * (1.0 / channels) + EPSILON)
        y_scr[turn] = (y[:, :LANES] - mean * sums) * scale
        here = slice(turn * step, (turn + 1) * step)
        for group in range(groups):
            z = y_scr[turn, pl.ds(group * rep, step, stride=rows), :]
            for k in range(1, rep):
                next_z = y_scr[turn, pl.ds(group * rep + k, step, stride=rows), :]
                z = jnp.where(block == k, next_z, z)
            if mask_ref is not None:
                z = z * live[here, group * LANES : (group + 1) * LANES]
            z_ref[group, here, :] = z.astype(BF16)


def factor(alignment, weight, hidden, mask=None):
    seqs, rows, channels = alignment.shape
    step = seqs // 8
    operands = (alignment, weight) if mask is None else (alignment, weight, mask)
    return pl.pallas_call(
        factor_kernel,
        out_shape=jax.ShapeDtypeStruct((rows * hidden // LANES, seqs, LANES), BF16),
        in_specs=[vmem()] * len(operands),
        out_specs=vmem(),
        scratch_shapes=[pltpu.VMEM((seqs // step, step * rows, LANES), F32)],
        compiler_params=pltpu.CompilerParams(vmem_limit_bytes=24 << 20),
        cost_estimate=pl.CostEstimate(
            flops=2 * seqs * rows * channels * 512, bytes_accessed=seqs << 14, transcendentals=0
        ),
    )(*operands)


def prepare_kernel(
    zl_ref, mask_ref, pair_ref, live_ref, chain_ref, table_ref, proj_ref,
    zlt_ref, base_ref, inverse_ref, live_out_ref, proj_out_ref, seen_ref, pair_scr, table_scr,
):
    rows, cols, _ = pair_ref.shape
    pairs = rows * cols
    residues = mask_ref.shape[0]
    classes = table_ref.shape[0]
    row_start = lax.axis_index("dap") * rows
    col_start = lax.axis_index("sub") * cols
    for group in range(zl_ref.shape[0]):
        turned = zl_ref[group].T
        for half in range(zlt_ref.shape[0]):
            lanes = slice(half * LANES, (half + 1) * LANES)
            zlt_ref[half, group * LANES : (group + 1) * LANES, :] = turned[:, lanes]
    proj_out_ref[...] = proj_ref[...].reshape(proj_out_ref.shape).astype(BF16)
    groups = zl_ref.shape[0]
    width = groups * LANES
    hidden = width // rows
    for block in range(cols // rows):
        column = col_start + block * rows + over(iota((residues, width), 1), hidden)
        spread = (iota((residues, width), 0) == column).astype(BF16)
        seen = dot_tn(mask_ref[...].astype(BF16), spread).astype(BF16)
        for group in range(groups):
            seen_ref[block * groups + group] = seen[:, group * LANES : (group + 1) * LANES]
    which = iota((pairs, residues), 0)
    place = iota((pairs, residues), 1)
    pick_row = (place == row_start + within(which, rows)).astype(BF16)
    pick_col = (place == col_start + over(which, rows)).astype(BF16)
    mask = mask_ref[...].astype(BF16)
    both = (dot(pick_row, mask) * dot(pick_col, mask)).astype(BF16)
    counts = dot(both, jnp.ones((mask.shape[1], LANES), BF16))
    inverse_ref[...] = 1.0 / jnp.maximum(counts, 1.0)
    live = jnp.broadcast_to(live_ref[...].astype(F32), (LANES, residues)).astype(BF16)
    chain = jnp.broadcast_to(chain_ref[...].astype(F32), (LANES, residues)).astype(BF16)
    live_out_ref[...] = dot_nt(pick_row, live) * dot_nt(pick_col, live)
    same = dot_nt(pick_row, chain) == dot_nt(pick_col, chain)
    pair = iota((pairs, LANES), 0)
    offset = (row_start + within(pair, rows)) - (col_start + over(pair, rows)) + REL_CLIP
    bucket = jnp.where(same, jnp.clip(offset, 0, 2 * REL_CLIP), 2 * REL_CLIP + 1)
    table_scr[...] = jnp.zeros_like(table_scr)
    table_scr[pl.ds(0, classes), :] = table_ref[...].astype(F32)
    onehot = (bucket == iota((pairs, LANES), 1)).astype(BF16)
    relative = dot(onehot, table_scr[...].astype(BF16))
    pair_scr[...] = pair_ref[...].reshape(pairs, LANES).astype(F32)
    for col in range(cols):
        here = slice(col * rows, (col + 1) * rows)
        base_ref[here, :] = relative[here] + pair_scr[pl.ds(col, rows, stride=cols), :]


def prepare(zl, mask, pair_input, residue_mask, chain_index, table, proj):
    rows, cols, channels = pair_input.shape
    pairs = rows * cols
    shape = jax.ShapeDtypeStruct((pairs, channels), F32)
    depth = proj.shape[0] * proj.shape[1]
    return pl.pallas_call(
        prepare_kernel,
        out_shape=(
            jax.ShapeDtypeStruct((zl.shape[1] // LANES, zl.shape[0] * LANES, LANES), BF16),
            shape,
            shape,
            shape,
            jax.ShapeDtypeStruct((depth, channels), BF16),
            jax.ShapeDtypeStruct((cols // rows * zl.shape[0], *zl.shape[1:]), BF16),
        ),
        in_specs=[vmem()] * 7,
        out_specs=[vmem()] * 6,
        scratch_shapes=[pltpu.VMEM((pairs, channels), F32), pltpu.VMEM((LANES, channels), F32)],
        compiler_params=pltpu.CompilerParams(vmem_limit_bytes=24 << 20),
        cost_estimate=pl.CostEstimate(
            flops=2 * pairs * 256 * 1024, bytes_accessed=2 << 20, transcendentals=0
        ),
    )(zl, mask, pair_input, residue_mask[None, :], chain_index[None, :], table, proj)


def pair_kernel(ratio, hidden, zlt_ref, *refs):
    zr_refs, refs = refs[:ratio], refs[ratio:]
    (seen_ref, base_ref, inverse_ref, live_ref, proj_ref, tl_ref, tr_ref,
     both_ref, left_ref, one_ref, outer_scr, flat_scr, one_scr) = refs
    pairs, channels = base_ref.shape
    rows = zlt_ref.shape[1] // hidden
    rep = LANES // hidden
    me = lax.axis_index("dap")
    lane = iota((rows, LANES), 1)
    odd = (lane // hidden) % 2 == 1
    upper = lane // (2 * hidden) == 1
    half = 2 * hidden
    left = jnp.concatenate([zlt_ref[part] for part in range(zlt_ref.shape[0])], axis=1)
    groups = rows // rep
    for step in range(ratio):
        block = lax.rem(me + step, ratio) if ratio > 1 else 0
        right = [zr_refs[step][group] * seen_ref[block * groups + group] for group in range(groups)]
        outer = dot(left, jnp.concatenate(right, axis=1))
        for group in range(groups):
            outer_scr[group] = outer[:, group * LANES : (group + 1) * LANES]
        for part in range(HALVES):
            span = rows * rows // HALVES
            for group in range(part * groups // HALVES, (part + 1) * groups // HALVES):
                for quad in range(hidden // rep):
                    s0, s1, s2, s3 = (
                        outer_scr[group, pl.ds(quad * rep + k, rows, stride=hidden), :]
                        for k in range(rep)
                    )
                    t0 = jnp.where(upper, pltpu.roll(s2, half, 1), s0)
                    t1 = jnp.where(upper, pltpu.roll(s3, half, 1), s1)
                    t2 = jnp.where(upper, s2, pltpu.roll(s0, half, 1))
                    t3 = jnp.where(upper, s3, pltpu.roll(s1, half, 1))
                    back = LANES - hidden
                    found = (
                        jnp.where(odd, pltpu.roll(t1, hidden, 1), t0),
                        jnp.where(odd, t1, pltpu.roll(t0, back, 1)),
                        jnp.where(odd, pltpu.roll(t3, hidden, 1), t2),
                        jnp.where(odd, t3, pltpu.roll(t2, back, 1)),
                    )
                    for k in range(rep):
                        place = ((group * rep + k) * rows) % span
                        flat_scr[part, quad, place : place + rows, :] = found[k].astype(BF16)
            first = block * rows * rows + part * span
            if ratio > 1:
                first = pl.multiple_of(first, span)
            here = pl.ds(first, span)
            flat = [flat_scr[part, quad] for quad in range(hidden // rep)]
            projected = dot(jnp.concatenate(flat, axis=1), proj_ref[...])
            one = (base_ref[here, :] + projected * inverse_ref[here, :]).astype(BF16).astype(F32)
            one_scr[here, :] = one
            norm = layer_norm(one).astype(BF16)
            live = live_ref[here, :]
            for side, weight in enumerate((tl_ref, tr_ref)):
                both = dot(norm, weight[...])
                factor = jax.nn.sigmoid(both[:, :channels]) * both[:, channels:] * live
                both_ref[side, here, :] = factor.astype(BF16)
                if side == 0:
                    left_ref[here, :] = factor.astype(BF16)
    cols = pairs // rows
    for row in range(rows):
        one_ref[row * cols : (row + 1) * cols, :] = one_scr[pl.ds(row, cols, stride=rows), :].astype(BF16)


def pair_update(hidden, zlt, zrs, seen, base, inverse, live, proj, triangle_left, triangle_right):
    pairs, channels = base.shape
    ratio = len(zrs)
    rows = zlt.shape[1] // hidden
    shape = jax.ShapeDtypeStruct((pairs, channels), BF16)
    return pl.pallas_call(
        functools.partial(pair_kernel, ratio, hidden),
        out_shape=(jax.ShapeDtypeStruct((2, pairs, channels), BF16), shape, shape),
        in_specs=[vmem()] * (8 + len(zrs)),
        out_specs=[vmem()] * 3,
        scratch_shapes=[
            pltpu.VMEM((zrs[0].shape[0], zlt.shape[1], LANES), F32),
            pltpu.VMEM((HALVES, hidden * hidden // LANES, rows * rows // HALVES, LANES), BF16),
            pltpu.VMEM((pairs, channels), F32),
        ],
        compiler_params=pltpu.CompilerParams(vmem_limit_bytes=32 << 20),
        cost_estimate=pl.CostEstimate(
            flops=2 * pairs * 1024 * 512, bytes_accessed=2 << 20, transcendentals=pairs * 256
        ),
    )(zlt, *zrs, seen, base, inverse, live, proj, triangle_left, triangle_right)


def other(sub):
    return sub + 1 - 2 * (sub % 2)


SENDERS = ((0, 2, 3, 1), (2, 1, 0, 3), (0, 3, 2, 1), (2, 0, 1, 3))


def sender(a, b, subs, ratio):
    if (subs, ratio) == (4, 1):
        return SENDERS[b][a]
    return a // ratio


def sender_index(a, b, subs, ratio):
    if (subs, ratio) != (4, 1):
        return a // ratio
    found = 0
    for col, places in enumerate(SENDERS):
        for row, place in enumerate(places):
            found = jnp.where((a == row) & (b == col), place, found)
    return found


def widen(lefts, left_scr):
    subs = left_scr.shape[0]
    there = lax.axis_index("sub")
    own, near, across, beyond = lefts
    left_scr[there] = own[0].astype(F32)
    left_scr[other(there)] = near[0].astype(F32)
    for step in range(1, subs // 2):
        sub = lax.rem(there + 2 * step, subs)
        left_scr[sub] = across[step - 1][...].astype(F32)
        left_scr[other(sub)] = beyond[step - 1][...].astype(F32)


def add_terms(sums, start, rights, steps, ratio, cols, left_scr):
    subs = left_scr.shape[0]
    _, channels = sums.shape
    rows = left_scr.shape[1] // cols
    here, there = lax.axis_index("dap"), lax.axis_index("sub")
    first_sub = sender_index(here, there, subs, ratio)
    for turn in range(ratio):
        block = lax.rem(here + turn, ratio) if ratio > 1 else 0
        places = [i * cols + block * rows for i in range(rows)]
        if ratio > 1:
            places = [pl.multiple_of(place, rows) for place in places]
        if start is None:
            totals = tuple(jnp.zeros((rows, channels), F32) for _ in range(rows))
        else:
            totals = tuple(start[pl.ds(place, rows), :] for place in places)
        for index, step in enumerate(steps):
            sub = lax.rem(first_sub + 2 * step, subs)
            pair = rights[turn * len(steps) + index]
            for member, slot in enumerate((sub, other(sub))):

                def body(k, totals, slot=slot, member=member, pair=pair):
                    first = pl.multiple_of(k * rows, rows)
                    right = pair[member, pl.ds(first, rows), :].astype(F32)
                    return tuple(
                        totals[i] + left_scr[slot, pl.ds(first + i, 1), :] * right
                        for i in range(rows)
                    )

                totals = lax.fori_loop(0, cols, body, totals, unroll=4)
        for place, total in zip(places, totals):
            sums[pl.ds(place, rows), :] = total


def split_lefts(refs, twos):
    count = twos - 1
    lefts = (refs[0], refs[1], refs[2 : 2 + count], refs[2 + count : 2 + 2 * count])
    return lefts, refs[2 + 2 * count :]


def first_kernel(steps, twos, ratio, cols, *refs):
    lefts, refs = split_lefts(refs, twos)
    rights, refs = refs[: ratio * len(steps)], refs[ratio * len(steps) :]
    one_ref, weight_ref, left_ref, sums_ref, gate_ref = refs
    widen(lefts, left_ref)
    add_terms(sums_ref, None, rights, steps, ratio, cols, left_ref)
    norm = layer_norm(one_ref[...].astype(F32)).astype(BF16)
    gate_ref[...] = jax.nn.sigmoid(dot(norm, weight_ref[...]))


def last_kernel(steps, ratio, cols, left_ref, *refs):
    rights, refs = refs[: ratio * len(steps)], refs[ratio * len(steps) :]
    (start_ref, one_ref, gate_ref, out_ref, up_ref, down_ref, result_ref, sum_scr) = refs
    add_terms(sum_scr, start_ref, rights, steps, ratio, cols, left_ref)
    pairs, channels = one_ref.shape
    span = pairs // HALVES
    parts = [slice(part * span, (part + 1) * span) for part in range(HALVES)]
    hidden = [layer_norm(sum_scr[part, :].astype(BF16).astype(F32)).astype(BF16) for part in parts]
    update = [dot(value, out_ref[...]) for value in hidden]
    two = [
        (one_ref[part, :].astype(F32) + gate_ref[part, :] * value).astype(BF16).astype(F32)
        for part, value in zip(parts, update)
    ]
    norm = [layer_norm(value).astype(BF16) for value in two]
    wide = [jnp.maximum(dot(value, up_ref[...]), 0.0).astype(BF16) for value in norm]
    result = [value + dot(inner, down_ref[...]) for value, inner in zip(two, wide)]
    lines = span // cols
    for part, value in enumerate(result):
        value = value.astype(BF16).reshape(lines, cols, channels)
        result_ref[part * lines : (part + 1) * lines] = value


def triangle_update(lefts, rights, one, cols, gate_weight, out, up, down):
    pairs, channels = one.shape
    rows = pairs // cols
    twos = len(lefts) // 2
    subs = 2 * twos
    ratio = len(rights) // twos
    late, early = range(twos // 2), range(twos // 2, twos)
    limit = (12 << 20) if ratio == 1 else (50 << 20)
    shape = jax.ShapeDtypeStruct((pairs, channels), F32)

    def chosen(steps):
        return [rights[turn * twos + step] for turn in range(ratio) for step in steps]

    left, sums, gate = pl.pallas_call(
        functools.partial(first_kernel, early, twos, ratio, cols),
        out_shape=(jax.ShapeDtypeStruct((subs, pairs, channels), F32), shape, shape),
        in_specs=[vmem()] * (len(lefts) + ratio * len(early) + 2),
        out_specs=[vmem()] * 3,
        compiler_params=pltpu.CompilerParams(vmem_limit_bytes=limit),
        cost_estimate=pl.CostEstimate(
            flops=2 * pairs * channels * 1024, bytes_accessed=1 << 20, transcendentals=pairs * 128
        ),
    )(*lefts, *chosen(early), one, gate_weight)
    return pl.pallas_call(
        functools.partial(last_kernel, late, ratio, cols),
        out_shape=jax.ShapeDtypeStruct((rows, cols, channels), BF16),
        in_specs=[vmem()] * (1 + ratio * len(late) + 6),
        out_specs=vmem(),
        scratch_shapes=[pltpu.VMEM((pairs, channels), F32)],
        compiler_params=pltpu.CompilerParams(vmem_limit_bytes=limit),
        cost_estimate=pl.CostEstimate(
            flops=2 * pairs * channels * 2048, bytes_accessed=2 << 20, transcendentals=pairs * 128
        ),
    )(left, *chosen(late), sums, one, gate, out, up, down)


def per_device(
    alignment,
    alignment_mask,
    pair_input,
    residue_mask,
    chain_index,
    outer_left,
    outer_right,
    outer_proj,
    triangle_left,
    triangle_right,
    triangle_gate,
    triangle_out,
    relative_table,
    transition_up,
    transition_down,
):
    daps, subs = lax.axis_size("dap"), lax.axis_size("sub")
    ratio = daps // subs
    cols = pair_input.shape[1]

    def fetch(values, source):
        perm = []
        for a in range(daps):
            for b in range(subs):
                dap, sub = source(a, b)
                perm.append((dap * subs + sub, a * subs + b))
        return lax.ppermute(values, ("dap", "sub"), perm)

    def owner(a, b, turn):
        return ratio * b + (a + turn) % ratio

    hidden = outer_left.shape[1]
    mask = alignment_mask.T
    zr = factor(alignment, repeat_weight(outer_right.T), hidden)
    zrs = [
        fetch(zr, lambda a, b, turn=turn: (owner(a, b, turn), sender(a, b, subs, ratio)))
        for turn in range(ratio)
    ]
    zl = factor(alignment, repeat_weight(outer_left.T), hidden, mask)
    zlt, base, inverse, live, proj, seen = prepare(
        zl, mask, pair_input, residue_mask, chain_index, relative_table, outer_proj
    )
    own, left, one = pair_update(
        hidden, zlt, zrs, seen, base, inverse, live, proj, triangle_left, triangle_right
    )
    near = fetch(own, lambda a, b: (a, other(b)))
    across = [
        fetch(left, lambda a, b, m=step: (a, (b + 2 * m) % subs)) for step in range(1, subs // 2)
    ]
    beyond = [fetch(block, lambda a, b: (a, other(b))) for block in across]
    right = jnp.stack([own[1], near[1]])
    rights = [
        fetch(
            right,
            lambda a, b, t=turn, m=step: (
                owner(a, b, t), (sender(a, b, subs, ratio) + 2 * m) % subs
            ),
        )
        for turn in range(ratio)
        for step in range(subs // 2)
    ]
    return triangle_update(
        [own, near, *across, *beyond],
        rights,
        one,
        cols,
        triangle_gate,
        triangle_out,
        transition_up,
        transition_down,
    )


def solution(mesh):
    in_specs = (
        P("parts", "dap", None),
        P("parts", None),
        P(("parts", "dap"), "sub", None),
        P("parts"),
        P("parts"),
        P(),
        P(),
        P(),
        P(),
        P(),
        P(),
        P(),
        P(),
        P(),
        P(),
    )
    out_specs = P(("parts", "dap"), "sub", None)
    return jax.shard_map(
        per_device, mesh=mesh, in_specs=in_specs, out_specs=out_specs, check_vma=False
    )
```

```python
import functools

import jax
import jax.numpy as jnp
from jax import lax
from jax.experimental import pallas as pl
from jax.experimental.pallas import tpu as pltpu
from jax.sharding import PartitionSpec as P

REL_CLIP = 32
LANES = 128
PARTS = 2
EPSILON = 1e-05
BF16 = jnp.bfloat16
F32 = jnp.float32
NT = (((1,), (1,)), ((), ()))
TN = (((0,), (0,)), ((), ()))


def layer_norm(values):
    average = jnp.mean(values, axis=-1, keepdims=True)
    centered = values - average
    spread = jnp.mean(centered * centered, axis=-1, keepdims=True)
    return centered * lax.rsqrt(spread + EPSILON)


def dot(left, right):
    return jnp.dot(left, right, preferred_element_type=F32)


def dot_nt(left, right):
    return lax.dot_general(left, right, NT, preferred_element_type=F32)


def dot_tn(left, right):
    return lax.dot_general(left, right, TN, preferred_element_type=F32)


def iota(shape, dim):
    return lax.broadcasted_iota(jnp.int32, shape, dim)


def vmem():
    return pl.BlockSpec(memory_space=pltpu.VMEM)


def over(index, size):
    return lax.shift_right_logical(index, size.bit_length() - 1)


def within(index, size):
    return lax.bitwise_and(index, size - 1)


def repeat_kernel(weight_ref, out_ref):
    rep = LANES // weight_ref.shape[0]
    out_ref[...] = jnp.concatenate([weight_ref[...]] * rep, axis=0).T


def repeat_weight(weight):
    return pl.pallas_call(
        repeat_kernel,
        out_shape=jax.ShapeDtypeStruct((weight.shape[1], LANES), BF16),
        in_specs=[vmem()],
        out_specs=vmem(),
        compiler_params=pltpu.CompilerParams(vmem_limit_bytes=2 << 20),
        cost_estimate=pl.CostEstimate(flops=1 << 30, bytes_accessed=1 << 17, transcendentals=0),
    )(weight)


def factor_kernel(masked, hidden, x_ref, weight_ref, *refs):
    mask_ref = refs[0] if masked else None
    z_refs, y_scr = refs[masked:-1], refs[-1]
    each, seqs, _ = z_refs[0].shape
    groups = each * len(z_refs)
    _, rows, channels = x_ref.shape
    rep = rows // groups
    width = rows * hidden
    step = y_scr.shape[1] // rows
    w = jnp.concatenate([weight_ref[...], jnp.ones((channels, LANES), BF16)], axis=1)
    ones = jnp.ones((LANES, LANES), BF16)
    sums = dot(jnp.ones((8, channels), BF16), weight_ref[...])[:1]
    block = over(iota((step, LANES), 1), hidden)
    if mask_ref is not None:
        residues = mask_ref.shape[0]
        column = lax.axis_index("dap") * rows + over(iota((residues, width), 1), hidden)
        lanes_of = (iota((residues, width), 0) == column).astype(BF16)
        live = dot_tn(mask_ref[...].astype(BF16), lanes_of)
    for turn in range(seqs // step):
        x = x_ref[turn * step : (turn + 1) * step].reshape(step * rows, channels)
        y = dot(x, w)
        mean = y[:, LANES:] * (1.0 / channels)
        square = jnp.zeros_like(mean)
        for half in range(channels // LANES):
            centered = x[:, half * LANES : (half + 1) * LANES].astype(F32) - mean
            square = square + centered * centered
        spread = dot(square.astype(BF16), ones)
        scale = lax.rsqrt(spread * (1.0 / channels) + EPSILON)
        y_scr[turn] = (y[:, :LANES] - mean * sums) * scale
        here = slice(turn * step, (turn + 1) * step)
        for group in range(groups):
            z = y_scr[turn, pl.ds(group * rep, step, stride=rows), :]
            for k in range(1, rep):
                next_z = y_scr[turn, pl.ds(group * rep + k, step, stride=rows), :]
                z = jnp.where(block == k, next_z, z)
            if mask_ref is not None:
                z = z * live[here, group * LANES : (group + 1) * LANES]
            z_refs[group // each][group % each, here, :] = z.astype(BF16)


def factor(alignment, weight, hidden, parts, mask=None):
    seqs, rows, channels = alignment.shape
    step = seqs // 2
    operands = (alignment, weight) if mask is None else (alignment, weight, mask)
    shape = jax.ShapeDtypeStruct((rows * hidden // LANES // parts, seqs, LANES), BF16)
    return pl.pallas_call(
        functools.partial(factor_kernel, mask is not None, hidden),
        out_shape=(shape,) * parts,
        in_specs=[vmem()] * len(operands),
        out_specs=[vmem()] * parts,
        scratch_shapes=[pltpu.VMEM((seqs // step, step * rows, LANES), F32)],
        compiler_params=pltpu.CompilerParams(vmem_limit_bytes=24 << 20),
        cost_estimate=pl.CostEstimate(
            flops=2 * seqs * rows * channels * 512, bytes_accessed=seqs << 14, transcendentals=0
        ),
    )(*operands)


def prepare_kernel(
    zl_ref, mask_ref, pair_ref, live_ref, chain_ref, table_ref, proj_ref,
    zlt_ref, base_ref, inverse_ref, live_out_ref, proj_out_ref, seen_ref, pair_scr, table_scr,
):
    rows, cols, _ = pair_ref.shape
    pairs = rows * cols
    residues = mask_ref.shape[0]
    classes = table_ref.shape[0]
    row_start = lax.axis_index("dap") * rows
    col_start = lax.axis_index("sub") * cols
    for group in range(zl_ref.shape[0]):
        turned = zl_ref[group].T
        for half in range(zlt_ref.shape[0]):
            lanes = slice(half * LANES, (half + 1) * LANES)
            zlt_ref[half, group * LANES : (group + 1) * LANES, :] = turned[:, lanes]
    proj_out_ref[...] = proj_ref[...].reshape(proj_out_ref.shape).astype(BF16)
    groups = zl_ref.shape[0]
    width = groups * LANES
    hidden = width // rows
    for block in range(cols // rows):
        column = col_start + block * rows + over(iota((residues, width), 1), hidden)
        spread = (iota((residues, width), 0) == column).astype(BF16)
        seen = dot_tn(mask_ref[...].astype(BF16), spread).astype(BF16)
        for group in range(groups):
            seen_ref[block * groups + group] = seen[:, group * LANES : (group + 1) * LANES]
    which = iota((pairs, residues), 0)
    place = iota((pairs, residues), 1)
    pick_row = (place == row_start + within(which, rows)).astype(BF16)
    pick_col = (place == col_start + over(which, rows)).astype(BF16)
    mask = mask_ref[...].astype(BF16)
    both = (dot(pick_row, mask) * dot(pick_col, mask)).astype(BF16)
    counts = dot(both, jnp.ones((mask.shape[1], LANES), BF16))
    inverse_ref[...] = 1.0 / jnp.maximum(counts, 1.0)
    live = jnp.broadcast_to(live_ref[...].astype(F32), (LANES, residues)).astype(BF16)
    chain = jnp.broadcast_to(chain_ref[...].astype(F32), (LANES, residues)).astype(BF16)
    live_out_ref[...] = dot_nt(pick_row, live) * dot_nt(pick_col, live)
    same = dot_nt(pick_row, chain) == dot_nt(pick_col, chain)
    pair = iota((pairs, LANES), 0)
    offset = (row_start + within(pair, rows)) - (col_start + over(pair, rows)) + REL_CLIP
    bucket = jnp.where(same, jnp.clip(offset, 0, 2 * REL_CLIP), 2 * REL_CLIP + 1)
    table_scr[...] = jnp.zeros_like(table_scr)
    table_scr[pl.ds(0, classes), :] = table_ref[...].astype(F32)
    onehot = (bucket == iota((pairs, LANES), 1)).astype(BF16)
    relative = dot(onehot, table_scr[...].astype(BF16))
    pair_scr[...] = pair_ref[...].reshape(pairs, LANES).astype(F32)
    for col in range(cols):
        here = slice(col * rows, (col + 1) * rows)
        base_ref[here, :] = relative[here] + pair_scr[pl.ds(col, rows, stride=cols), :]


def prepare(zl, mask, pair_input, residue_mask, chain_index, table, proj):
    rows, cols, channels = pair_input.shape
    pairs = rows * cols
    shape = jax.ShapeDtypeStruct((pairs, channels), F32)
    depth = proj.shape[0] * proj.shape[1]
    return pl.pallas_call(
        prepare_kernel,
        out_shape=(
            jax.ShapeDtypeStruct((zl.shape[1] // LANES, zl.shape[0] * LANES, LANES), BF16),
            shape,
            shape,
            shape,
            jax.ShapeDtypeStruct((depth, channels), BF16),
            jax.ShapeDtypeStruct((cols // rows * zl.shape[0], *zl.shape[1:]), BF16),
        ),
        in_specs=[vmem()] * 7,
        out_specs=[vmem()] * 6,
        scratch_shapes=[pltpu.VMEM((pairs, channels), F32), pltpu.VMEM((LANES, channels), F32)],
        compiler_params=pltpu.CompilerParams(vmem_limit_bytes=24 << 20),
        cost_estimate=pl.CostEstimate(
            flops=2 * pairs * 256 * 1024, bytes_accessed=2 << 20, transcendentals=0
        ),
    )(zl, mask, pair_input, residue_mask[None, :], chain_index[None, :], table, proj)


def pair_kernel(ratio, hidden, zlt_ref, *refs):
    zr_refs, refs = refs[: ratio * PARTS], refs[ratio * PARTS :]
    (seen_ref, base_ref, inverse_ref, live_ref, proj_ref, tl_ref, tr_ref,
     both_ref, left_ref, one_ref, outer_scr, flat_scr, one_scr) = refs
    pairs, channels = base_ref.shape
    rows = zlt_ref.shape[1] // hidden
    rep = LANES // hidden
    me = lax.axis_index("dap")
    lane = iota((rows, LANES), 1)
    odd = (lane // hidden) % 2 == 1
    upper = lane // (2 * hidden) == 1
    half = 2 * hidden
    left = jnp.concatenate([zlt_ref[part] for part in range(zlt_ref.shape[0])], axis=1)
    for step in range(ratio):
        block = lax.rem(me + step, ratio)
        right = []
        for group in range(rows // rep):
            each = rows // rep // PARTS
            factor = zr_refs[step * PARTS + group // each][group % each]
            right.append(factor * seen_ref[block * (rows // rep) + group])
        outer = dot(left, jnp.concatenate(right, axis=1))
        for group in range(rows // rep):
            outer_scr[group] = outer[:, group * LANES : (group + 1) * LANES]
        for group in range(rows // rep):
            for quad in range(hidden // rep):
                s0, s1, s2, s3 = (
                    outer_scr[group, pl.ds(quad * rep + k, rows, stride=hidden), :] for k in range(rep)
                )
                t0 = jnp.where(upper, pltpu.roll(s2, half, 1), s0)
                t1 = jnp.where(upper, pltpu.roll(s3, half, 1), s1)
                t2 = jnp.where(upper, s2, pltpu.roll(s0, half, 1))
                t3 = jnp.where(upper, s3, pltpu.roll(s1, half, 1))
                back = LANES - hidden
                found = (
                    jnp.where(odd, pltpu.roll(t1, hidden, 1), t0),
                    jnp.where(odd, t1, pltpu.roll(t0, back, 1)),
                    jnp.where(odd, pltpu.roll(t3, hidden, 1), t2),
                    jnp.where(odd, t3, pltpu.roll(t2, back, 1)),
                )
                for k in range(rep):
                    first = block * rows * rows + (group * rep + k) * rows
                    if ratio == 1:
                        first = (group * rep + k) * rows
                    else:
                        first = pl.multiple_of(first, rows)
                    flat_scr[quad, pl.ds(first, rows), :] = found[k].astype(BF16)
    flat = jnp.concatenate([flat_scr[quad] for quad in range(flat_scr.shape[0])], axis=1)
    outer_mean = dot(flat, proj_ref[...]) * inverse_ref[...]
    one = (base_ref[...] + outer_mean).astype(BF16).astype(F32)
    one_scr[...] = one
    norm = layer_norm(one).astype(BF16)
    for side, weight in enumerate((tl_ref, tr_ref)):
        both = dot(norm, weight[...])
        factor = jax.nn.sigmoid(both[:, :channels]) * both[:, channels:] * live_ref[...]
        both_ref[side] = factor.astype(BF16)
        if side == 0:
            left_ref[...] = factor.astype(BF16)
    cols = pairs // rows
    for row in range(rows):
        one_ref[row * cols : (row + 1) * cols, :] = one_scr[pl.ds(row, cols, stride=rows), :].astype(BF16)


def pair_update(hidden, zlt, zrs, seen, base, inverse, live, proj, triangle_left, triangle_right):
    pairs, channels = base.shape
    ratio = len(zrs) // PARTS
    shape = jax.ShapeDtypeStruct((pairs, channels), BF16)
    return pl.pallas_call(
        functools.partial(pair_kernel, ratio, hidden),
        out_shape=(jax.ShapeDtypeStruct((2, pairs, channels), BF16), shape, shape),
        in_specs=[vmem()] * (8 + len(zrs)),
        out_specs=[vmem()] * 3,
        scratch_shapes=[
            pltpu.VMEM((zrs[0].shape[0] * PARTS, zlt.shape[1], LANES), F32),
            pltpu.VMEM((proj.shape[0] // LANES, pairs, LANES), BF16),
            pltpu.VMEM((pairs, channels), F32),
        ],
        compiler_params=pltpu.CompilerParams(vmem_limit_bytes=32 << 20),
        cost_estimate=pl.CostEstimate(
            flops=2 * pairs * 1024 * 512, bytes_accessed=2 << 20, transcendentals=pairs * 256
        ),
    )(zlt, *zrs, seen, base, inverse, live, proj, triangle_left, triangle_right)


def other(sub):
    return sub + 1 - 2 * (sub % 2)


SENDERS = ((0, 2, 3, 1), (2, 1, 0, 3), (0, 3, 2, 1), (2, 0, 1, 3))


def sender(a, b, subs, ratio):
    if (subs, ratio) == (4, 1):
        return SENDERS[b][a]
    return a // ratio


def sender_index(a, b, subs, ratio):
    if (subs, ratio) != (4, 1):
        return a // ratio
    found = 0
    for col, places in enumerate(SENDERS):
        for row, place in enumerate(places):
            found = jnp.where((a == row) & (b == col), place, found)
    return found


def add_terms(sums, start, lefts, rights, steps, ratio, cols, left_scr):
    subs = left_scr.shape[0]
    _, channels = sums.shape
    rows = left_scr.shape[1] // cols
    here, there = lax.axis_index("dap"), lax.axis_index("sub")
    first_sub = sender_index(here, there, subs, ratio)
    own, near, across, beyond = lefts
    left_scr[there] = own[0].astype(F32)
    left_scr[other(there)] = near[0].astype(F32)
    for step in range(1, subs // 2):
        sub = lax.rem(there + 2 * step, subs)
        left_scr[sub] = across[step - 1][...].astype(F32)
        left_scr[other(sub)] = beyond[step - 1][...].astype(F32)
    for turn in range(ratio):
        block = lax.rem(here + turn, ratio) if ratio > 1 else 0
        places = [i * cols + block * rows for i in range(rows)]
        if ratio > 1:
            places = [pl.multiple_of(place, rows) for place in places]
        if start is None:
            totals = tuple(jnp.zeros((rows, channels), F32) for _ in range(rows))
        else:
            totals = tuple(start[pl.ds(place, rows), :] for place in places)
        for index, step in enumerate(steps):
            sub = lax.rem(first_sub + 2 * step, subs)
            pair = rights[turn * len(steps) + index]
            for member, slot in enumerate((sub, other(sub))):

                def body(k, totals, slot=slot, member=member, pair=pair):
                    first = pl.multiple_of(k * rows, rows)
                    right = pair[member, pl.ds(first, rows), :].astype(F32)
                    return tuple(
                        totals[i] + left_scr[slot, pl.ds(first + i, 1), :] * right
                        for i in range(rows)
                    )

                totals = lax.fori_loop(0, cols, body, totals, unroll=4)
        for place, total in zip(places, totals):
            sums[pl.ds(place, rows), :] = total


def split_lefts(refs, twos):
    count = twos - 1
    lefts = (refs[0], refs[1], refs[2 : 2 + count], refs[2 + count : 2 + 2 * count])
    return lefts, refs[2 + 2 * count :]


def first_kernel(steps, twos, ratio, cols, *refs):
    lefts, refs = split_lefts(refs, twos)
    rights, refs = refs[: ratio * len(steps)], refs[ratio * len(steps) :]
    one_ref, weight_ref, sums_ref, gate_ref, left_scr = refs
    add_terms(sums_ref, None, lefts, rights, steps, ratio, cols, left_scr)
    norm = layer_norm(one_ref[...].astype(F32)).astype(BF16)
    gate_ref[...] = jax.nn.sigmoid(dot(norm, weight_ref[...]))


def last_kernel(steps, twos, ratio, cols, *refs):
    lefts, refs = split_lefts(refs, twos)
    rights, refs = refs[: ratio * len(steps)], refs[ratio * len(steps) :]
    (start_ref, one_ref, gate_ref, out_ref, up_ref, down_ref, result_ref, left_scr, sum_scr) = refs
    add_terms(sum_scr, start_ref, lefts, rights, steps, ratio, cols, left_scr)
    one = one_ref[...].astype(F32)
    hidden = layer_norm(sum_scr[...].astype(BF16).astype(F32)).astype(BF16)
    two = (one + gate_ref[...] * dot(hidden, out_ref[...])).astype(BF16).astype(F32)
    wide = jnp.maximum(dot(layer_norm(two).astype(BF16), up_ref[...]), 0.0).astype(BF16)
    result = (two + dot(wide, down_ref[...])).astype(BF16)
    result_ref[...] = result.reshape(result_ref.shape)


def triangle_update(lefts, rights, one, cols, gate_weight, out, up, down):
    pairs, channels = one.shape
    rows = pairs // cols
    twos = len(lefts) // 2
    subs = 2 * twos
    ratio = len(rights) // twos
    late, early = range(twos // 2), range(twos // 2, twos)
    limit = (12 << 20) if ratio == 1 else (50 << 20)
    left_scr = pltpu.VMEM((subs, pairs, channels), F32)
    shape = jax.ShapeDtypeStruct((pairs, channels), F32)

    def chosen(steps):
        return [rights[turn * twos + step] for turn in range(ratio) for step in steps]

    sums, gate = pl.pallas_call(
        functools.partial(first_kernel, early, twos, ratio, cols),
        out_shape=(shape, shape),
        in_specs=[vmem()] * (len(lefts) + ratio * len(early) + 2),
        out_specs=[vmem()] * 2,
        scratch_shapes=[left_scr],
        compiler_params=pltpu.CompilerParams(vmem_limit_bytes=limit),
        cost_estimate=pl.CostEstimate(
            flops=2 * pairs * channels * 1024, bytes_accessed=1 << 20, transcendentals=pairs * 128
        ),
    )(*lefts, *chosen(early), one, gate_weight)
    return pl.pallas_call(
        functools.partial(last_kernel, late, twos, ratio, cols),
        out_shape=jax.ShapeDtypeStruct((rows, cols, channels), BF16),
        in_specs=[vmem()] * (len(lefts) + ratio * len(late) + 6),
        out_specs=vmem(),
        scratch_shapes=[left_scr, pltpu.VMEM((pairs, channels), F32)],
        compiler_params=pltpu.CompilerParams(vmem_limit_bytes=limit),
        cost_estimate=pl.CostEstimate(
            flops=2 * pairs * channels * 2048, bytes_accessed=2 << 20, transcendentals=pairs * 128
        ),
    )(*lefts, *chosen(late), sums, one, gate, out, up, down)


def per_device(
    alignment,
    alignment_mask,
    pair_input,
    residue_mask,
    chain_index,
    outer_left,
    outer_right,
    outer_proj,
    triangle_left,
    triangle_right,
    triangle_gate,
    triangle_out,
    relative_table,
    transition_up,
    transition_down,
):
    daps, subs = lax.axis_size("dap"), lax.axis_size("sub")
    ratio = daps // subs
    cols = pair_input.shape[1]

    def fetch(values, source):
        perm = []
        for a in range(daps):
            for b in range(subs):
                dap, sub = source(a, b)
                perm.append((dap * subs + sub, a * subs + b))
        return lax.ppermute(values, ("dap", "sub"), perm)

    def owner(a, b, turn):
        return ratio * b + (a + turn) % ratio

    hidden = outer_left.shape[1]
    mask = alignment_mask.T
    zr = factor(alignment, repeat_weight(outer_right.T), hidden, PARTS)
    zrs = [
        fetch(
            zr[part],
            lambda a, b, t=turn, p=part: (
                owner(a, b, t), (sender(a, b, subs, ratio) + 2 * p) % subs
            ),
        )
        for turn in range(ratio)
        for part in range(PARTS)
    ]
    (zl,) = factor(alignment, repeat_weight(outer_left.T), hidden, 1, mask)
    zlt, base, inverse, live, proj, seen = prepare(
        zl, mask, pair_input, residue_mask, chain_index, relative_table, outer_proj
    )
    own, left, one = pair_update(
        hidden, zlt, zrs, seen, base, inverse, live, proj, triangle_left, triangle_right
    )
    near = fetch(own, lambda a, b: (a, other(b)))
    across = [
        fetch(left, lambda a, b, m=step: (a, (b + 2 * m) % subs)) for step in range(1, subs // 2)
    ]
    beyond = [fetch(block, lambda a, b: (a, other(b))) for block in across]
    right = jnp.stack([own[1], near[1]])
    rights = [
        fetch(
            right,
            lambda a, b, t=turn, m=step: (
                owner(a, b, t), (sender(a, b, subs, ratio) + 2 * m) % subs
            ),
        )
        for turn in range(ratio)
        for step in range(subs // 2)
    ]
    return triangle_update(
        [own, near, *across, *beyond],
        rights,
        one,
        cols,
        triangle_gate,
        triangle_out,
        transition_up,
        transition_down,
    )


def solution(mesh):
    in_specs = (
        P("parts", "dap", None),
        P("parts", None),
        P(("parts", "dap"), "sub", None),
        P("parts"),
        P("parts"),
        P(),
        P(),
        P(),
        P(),
        P(),
        P(),
        P(),
        P(),
        P(),
        P(),
    )
    out_specs = P(("parts", "dap"), "sub", None)
    return jax.shard_map(
        per_device, mesh=mesh, in_specs=in_specs, out_specs=out_specs, check_vma=False
    )
```

```python
import functools

import jax
import jax.numpy as jnp
from jax import lax
from jax.experimental import pallas as pl
from jax.experimental.pallas import tpu as pltpu
from jax.sharding import PartitionSpec as P

REL_CLIP = 32
LANES = 128
PARTS = 2
EPSILON = 1e-05
BF16 = jnp.bfloat16
F32 = jnp.float32
NT = (((1,), (1,)), ((), ()))
TN = (((0,), (0,)), ((), ()))


def layer_norm(values):
    average = jnp.mean(values, axis=-1, keepdims=True)
    centered = values - average
    spread = jnp.mean(centered * centered, axis=-1, keepdims=True)
    return centered * lax.rsqrt(spread + EPSILON)


def dot(left, right):
    return jnp.dot(left, right, preferred_element_type=F32)


def dot_nt(left, right):
    return lax.dot_general(left, right, NT, preferred_element_type=F32)


def dot_tn(left, right):
    return lax.dot_general(left, right, TN, preferred_element_type=F32)


def iota(shape, dim):
    return lax.broadcasted_iota(jnp.int32, shape, dim)


def vmem():
    return pl.BlockSpec(memory_space=pltpu.VMEM)


def over(index, size):
    return lax.shift_right_logical(index, size.bit_length() - 1)


def within(index, size):
    return lax.bitwise_and(index, size - 1)


def factor_kernel(masked, x_any, weight_any, *refs):
    mask_ref = refs[0] if masked else None
    z_refs, (x_scr, y_scr, weight_scr, sems) = refs[masked:-4], refs[-4:]
    each, seqs, _ = z_refs[0].shape
    groups = each * len(z_refs)
    steps, step, rows, channels = x_scr.shape
    hidden = weight_scr.shape[0]
    rep = rows // groups
    width = rows * hidden
    fetches = [pltpu.make_async_copy(weight_any, weight_scr, sems.at[steps])]
    for turn in range(steps):
        part = x_any.at[pl.ds(turn * step, step)]
        fetches.append(pltpu.make_async_copy(part, x_scr.at[turn], sems.at[turn]))
    for fetch in fetches:
        fetch.start()
    ones = jnp.full((LANES, LANES), 1.0 / channels, BF16)
    block = over(iota((step, LANES), 1), hidden)
    if masked:
        residues = mask_ref.shape[0]
        column = lax.axis_index("dap") * rows + over(iota((residues, width), 1), hidden)
        lanes_of = (iota((residues, width), 0) == column).astype(BF16)
        live = dot_tn(mask_ref[...].astype(BF16), lanes_of)
    fetches[0].wait()
    weight = jnp.concatenate([weight_scr[...]] * rep, axis=0).T
    w = jnp.concatenate([weight, jnp.full((channels, LANES), 1.0 / channels, BF16)], axis=1)
    sums = dot(jnp.ones((8, channels), BF16), weight)[:1]
    for turn in range(steps):
        fetches[turn + 1].wait()
        x = x_scr[turn].reshape(step * rows, channels)
        y = dot(x, w)
        mean = y[:, LANES:]
        square = jnp.zeros_like(mean)
        for half in range(channels // LANES):
            centered = x[:, half * LANES : (half + 1) * LANES].astype(F32) - mean
            square = square + centered * centered
        scale = lax.rsqrt(dot(square.astype(BF16), ones) + EPSILON)
        y_scr[turn] = (y[:, :LANES] - mean * sums) * scale
        here = slice(turn * step, (turn + 1) * step)
        for group in range(groups):
            z = y_scr[turn, pl.ds(group * rep, step, stride=rows), :]
            for k in range(1, rep):
                next_z = y_scr[turn, pl.ds(group * rep + k, step, stride=rows), :]
                z = jnp.where(block == k, next_z, z)
            if masked:
                z = z * live[here, group * LANES : (group + 1) * LANES]
            z_refs[group // each][group % each, here, :] = z.astype(BF16)


def factor(alignment, weight, parts, mask=None):
    seqs, rows, channels = alignment.shape
    hidden = weight.shape[0]
    steps = 4
    operands = (alignment, weight) if mask is None else (alignment, weight, mask)
    away = pl.BlockSpec(memory_space=pl.ANY)
    shape = jax.ShapeDtypeStruct((rows * hidden // LANES // parts, seqs, LANES), BF16)
    return pl.pallas_call(
        functools.partial(factor_kernel, mask is not None),
        out_shape=(shape,) * parts,
        in_specs=[away, away, vmem()][: len(operands)],
        out_specs=[vmem()] * parts,
        scratch_shapes=[
            pltpu.VMEM((steps, seqs // steps, rows, channels), BF16),
            pltpu.VMEM((steps, seqs // steps * rows, LANES), F32),
            pltpu.VMEM(weight.shape, BF16),
            pltpu.SemaphoreType.DMA((steps + 1,)),
        ],
        compiler_params=pltpu.CompilerParams(vmem_limit_bytes=119 << 19),
        cost_estimate=pl.CostEstimate(
            flops=2 * seqs * rows * channels * 512, bytes_accessed=seqs << 14, transcendentals=0
        ),
    )(*operands)


def prepare_kernel(
    zl_ref, mask_ref, pair_ref, live_ref, chain_ref, table_ref, proj_ref,
    zlt_ref, base_ref, inverse_ref, live_out_ref, proj_out_ref, seen_ref, pair_scr, table_scr,
):
    rows, cols, _ = pair_ref.shape
    pairs = rows * cols
    residues = mask_ref.shape[0]
    classes = table_ref.shape[0]
    row_start = lax.axis_index("dap") * rows
    col_start = lax.axis_index("sub") * cols
    for group in range(zl_ref.shape[0]):
        turned = zl_ref[group].T
        for half in range(zlt_ref.shape[0]):
            lanes = slice(half * LANES, (half + 1) * LANES)
            zlt_ref[half, group * LANES : (group + 1) * LANES, :] = turned[:, lanes]
    proj_out_ref[...] = proj_ref[...].reshape(proj_out_ref.shape).astype(BF16)
    groups = zl_ref.shape[0]
    width = groups * LANES
    hidden = width // rows
    for block in range(cols // rows):
        column = col_start + block * rows + over(iota((residues, width), 1), hidden)
        spread = (iota((residues, width), 0) == column).astype(BF16)
        seen = dot_tn(mask_ref[...].astype(BF16), spread).astype(BF16)
        for group in range(groups):
            seen_ref[block * groups + group] = seen[:, group * LANES : (group + 1) * LANES]
    which = iota((pairs, residues), 0)
    place = iota((pairs, residues), 1)
    pick_row = (place == row_start + within(which, rows)).astype(BF16)
    pick_col = (place == col_start + over(which, rows)).astype(BF16)
    mask = mask_ref[...].astype(BF16)
    both = (dot(pick_row, mask) * dot(pick_col, mask)).astype(BF16)
    counts = dot(both, jnp.ones((mask.shape[1], LANES), BF16))
    inverse_ref[...] = 1.0 / jnp.maximum(counts, 1.0)
    live = jnp.broadcast_to(live_ref[...].astype(F32), (LANES, residues)).astype(BF16)
    chain = jnp.broadcast_to(chain_ref[...].astype(F32), (LANES, residues)).astype(BF16)
    live_out_ref[...] = dot_nt(pick_row, live) * dot_nt(pick_col, live)
    same = dot_nt(pick_row, chain) == dot_nt(pick_col, chain)
    pair = iota((pairs, LANES), 0)
    offset = (row_start + within(pair, rows)) - (col_start + over(pair, rows)) + REL_CLIP
    bucket = jnp.where(same, jnp.clip(offset, 0, 2 * REL_CLIP), 2 * REL_CLIP + 1)
    table_scr[...] = jnp.zeros_like(table_scr)
    table_scr[pl.ds(0, classes), :] = table_ref[...].astype(F32)
    onehot = (bucket == iota((pairs, LANES), 1)).astype(BF16)
    relative = dot(onehot, table_scr[...].astype(BF16))
    pair_scr[...] = pair_ref[...].reshape(pairs, LANES).astype(F32)
    for col in range(cols):
        here = slice(col * rows, (col + 1) * rows)
        base_ref[here, :] = relative[here] + pair_scr[pl.ds(col, rows, stride=cols), :]


def prepare(zl, mask, pair_input, residue_mask, chain_index, table, proj):
    rows, cols, channels = pair_input.shape
    pairs = rows * cols
    shape = jax.ShapeDtypeStruct((pairs, channels), F32)
    depth = proj.shape[0] * proj.shape[1]
    return pl.pallas_call(
        prepare_kernel,
        out_shape=(
            jax.ShapeDtypeStruct((zl.shape[1] // LANES, zl.shape[0] * LANES, LANES), BF16),
            shape,
            shape,
            shape,
            jax.ShapeDtypeStruct((depth, channels), BF16),
            jax.ShapeDtypeStruct((cols // rows * zl.shape[0], *zl.shape[1:]), BF16),
        ),
        in_specs=[vmem()] * 7,
        out_specs=[vmem()] * 6,
        scratch_shapes=[pltpu.VMEM((pairs, channels), F32), pltpu.VMEM((LANES, channels), F32)],
        compiler_params=pltpu.CompilerParams(vmem_limit_bytes=24 << 20),
        cost_estimate=pl.CostEstimate(
            flops=2 * pairs * 256 * 1024, bytes_accessed=2 << 20, transcendentals=0
        ),
    )(zl, mask, pair_input, residue_mask[None, :], chain_index[None, :], table, proj)


def pair_kernel(ratio, hidden, zlt_ref, *refs):
    zr_refs, refs = refs[: ratio * PARTS], refs[ratio * PARTS :]
    (seen_ref, base_ref, inverse_ref, live_ref, proj_ref, tl_ref, tr_ref,
     both_ref, left_ref, one_ref, outer_scr, flat_scr, one_scr) = refs
    pairs, channels = base_ref.shape
    rows = zlt_ref.shape[1] // hidden
    rep = LANES // hidden
    me = lax.axis_index("dap")
    lane = iota((rows, LANES), 1)
    odd = (lane // hidden) % 2 == 1
    upper = lane // (2 * hidden) == 1
    half = 2 * hidden
    left = jnp.concatenate([zlt_ref[part] for part in range(zlt_ref.shape[0])], axis=1)
    for step in range(ratio):
        block = lax.rem(me + step, ratio)
        right = []
        for group in range(rows // rep):
            each = rows // rep // PARTS
            factor = zr_refs[step * PARTS + group // each][group % each]
            right.append(factor * seen_ref[block * (rows // rep) + group])
        outer = dot(left, jnp.concatenate(right, axis=1))
        for group in range(rows // rep):
            outer_scr[group] = outer[:, group * LANES : (group + 1) * LANES]
        for group in range(rows // rep):
            for quad in range(hidden // rep):
                s0, s1, s2, s3 = (
                    outer_scr[group, pl.ds(quad * rep + k, rows, stride=hidden), :] for k in range(rep)
                )
                t0 = jnp.where(upper, pltpu.roll(s2, half, 1), s0)
                t1 = jnp.where(upper, pltpu.roll(s3, half, 1), s1)
                t2 = jnp.where(upper, s2, pltpu.roll(s0, half, 1))
                t3 = jnp.where(upper, s3, pltpu.roll(s1, half, 1))
                back = LANES - hidden
                found = (
                    jnp.where(odd, pltpu.roll(t1, hidden, 1), t0),
                    jnp.where(odd, t1, pltpu.roll(t0, back, 1)),
                    jnp.where(odd, pltpu.roll(t3, hidden, 1), t2),
                    jnp.where(odd, t3, pltpu.roll(t2, back, 1)),
                )
                for k in range(rep):
                    first = block * rows * rows + (group * rep + k) * rows
                    if ratio == 1:
                        first = (group * rep + k) * rows
                    else:
                        first = pl.multiple_of(first, rows)
                    flat_scr[quad, pl.ds(first, rows), :] = found[k].astype(BF16)
    flat = jnp.concatenate([flat_scr[quad] for quad in range(flat_scr.shape[0])], axis=1)
    outer_mean = dot(flat, proj_ref[...]) * inverse_ref[...]
    one = (base_ref[...] + outer_mean).astype(BF16).astype(F32)
    one_scr[...] = one
    norm = layer_norm(one).astype(BF16)
    for side, weight in enumerate((tl_ref, tr_ref)):
        both = dot(norm, weight[...])
        factor = jax.nn.sigmoid(both[:, :channels]) * both[:, channels:] * live_ref[...]
        both_ref[side] = factor.astype(BF16)
        if side == 0:
            left_ref[...] = factor.astype(BF16)
    cols = pairs // rows
    for row in range(rows):
        one_ref[row * cols : (row + 1) * cols, :] = one_scr[pl.ds(row, cols, stride=rows), :].astype(BF16)


def pair_update(hidden, zlt, zrs, seen, base, inverse, live, proj, triangle_left, triangle_right):
    pairs, channels = base.shape
    ratio = len(zrs) // PARTS
    shape = jax.ShapeDtypeStruct((pairs, channels), BF16)
    return pl.pallas_call(
        functools.partial(pair_kernel, ratio, hidden),
        out_shape=(jax.ShapeDtypeStruct((2, pairs, channels), BF16), shape, shape),
        in_specs=[vmem()] * (8 + len(zrs)),
        out_specs=[vmem()] * 3,
        scratch_shapes=[
            pltpu.VMEM((zrs[0].shape[0] * PARTS, zlt.shape[1], LANES), F32),
            pltpu.VMEM((proj.shape[0] // LANES, pairs, LANES), BF16),
            pltpu.VMEM((pairs, channels), F32),
        ],
        compiler_params=pltpu.CompilerParams(vmem_limit_bytes=32 << 20),
        cost_estimate=pl.CostEstimate(
            flops=2 * pairs * 1024 * 512, bytes_accessed=2 << 20, transcendentals=pairs * 256
        ),
    )(zlt, *zrs, seen, base, inverse, live, proj, triangle_left, triangle_right)


def other(sub):
    return sub + 1 - 2 * (sub % 2)


SENDERS = ((0, 2, 3, 1), (2, 1, 0, 3), (0, 3, 2, 1), (2, 0, 1, 3))


def sender(a, b, subs, ratio):
    if (subs, ratio) == (4, 1):
        return SENDERS[b][a]
    return a // ratio


def sender_index(a, b, subs, ratio):
    if (subs, ratio) != (4, 1):
        return a // ratio
    found = 0
    for col, places in enumerate(SENDERS):
        for row, place in enumerate(places):
            found = jnp.where((a == row) & (b == col), place, found)
    return found


def add_terms(sums, start, lefts, rights, steps, ratio, cols, left_scr):
    subs = left_scr.shape[0]
    _, channels = sums.shape
    rows = left_scr.shape[1] // cols
    here, there = lax.axis_index("dap"), lax.axis_index("sub")
    first_sub = sender_index(here, there, subs, ratio)
    own, near, across, beyond = lefts
    left_scr[there] = own[0].astype(F32)
    left_scr[other(there)] = near[0].astype(F32)
    for step in range(1, subs // 2):
        sub = lax.rem(there + 2 * step, subs)
        left_scr[sub] = across[step - 1][...].astype(F32)
        left_scr[other(sub)] = beyond[step - 1][...].astype(F32)
    for turn in range(ratio):
        block = lax.rem(here + turn, ratio) if ratio > 1 else 0
        places = [i * cols + block * rows for i in range(rows)]
        if ratio > 1:
            places = [pl.multiple_of(place, rows) for place in places]
        if start is None:
            totals = tuple(jnp.zeros((rows, channels), F32) for _ in range(rows))
        else:
            totals = tuple(start[pl.ds(place, rows), :] for place in places)
        for index, step in enumerate(steps):
            sub = lax.rem(first_sub + 2 * step, subs)
            pair = rights[turn * len(steps) + index]
            for member, slot in enumerate((sub, other(sub))):

                def body(k, totals, slot=slot, member=member, pair=pair):
                    first = pl.multiple_of(k * rows, rows)
                    right = pair[member, pl.ds(first, rows), :].astype(F32)
                    return tuple(
                        totals[i] + left_scr[slot, pl.ds(first + i, 1), :] * right
                        for i in range(rows)
                    )

                totals = lax.fori_loop(0, cols, body, totals, unroll=4)
        for place, total in zip(places, totals):
            sums[pl.ds(place, rows), :] = total


def split_lefts(refs, twos):
    count = twos - 1
    lefts = (refs[0], refs[1], refs[2 : 2 + count], refs[2 + count : 2 + 2 * count])
    return lefts, refs[2 + 2 * count :]


def first_kernel(steps, twos, ratio, cols, *refs):
    lefts, refs = split_lefts(refs, twos)
    rights, refs = refs[: ratio * len(steps)], refs[ratio * len(steps) :]
    one_ref, weight_ref, sums_ref, gate_ref, left_scr = refs
    add_terms(sums_ref, None, lefts, rights, steps, ratio, cols, left_scr)
    norm = layer_norm(one_ref[...].astype(F32)).astype(BF16)
    gate_ref[...] = jax.nn.sigmoid(dot(norm, weight_ref[...]))


def last_kernel(steps, twos, ratio, cols, *refs):
    lefts, refs = split_lefts(refs, twos)
    rights, refs = refs[: ratio * len(steps)], refs[ratio * len(steps) :]
    (start_ref, one_ref, gate_ref, out_ref, up_ref, down_ref, result_ref, left_scr, sum_scr) = refs
    add_terms(sum_scr, start_ref, lefts, rights, steps, ratio, cols, left_scr)
    one = one_ref[...].astype(F32)
    hidden = layer_norm(sum_scr[...].astype(BF16).astype(F32)).astype(BF16)
    two = (one + gate_ref[...] * dot(hidden, out_ref[...])).astype(BF16).astype(F32)
    wide = jnp.maximum(dot(layer_norm(two).astype(BF16), up_ref[...]), 0.0).astype(BF16)
    result = (two + dot(wide, down_ref[...])).astype(BF16)
    result_ref[...] = result.reshape(result_ref.shape)


def triangle_update(lefts, rights, one, cols, gate_weight, out, up, down):
    pairs, channels = one.shape
    rows = pairs // cols
    twos = len(lefts) // 2
    subs = 2 * twos
    ratio = len(rights) // twos
    late, early = range(twos // 2), range(twos // 2, twos)
    limit = (12 << 20) if ratio == 1 else (50 << 20)
    left_scr = pltpu.VMEM((subs, pairs, channels), F32)
    shape = jax.ShapeDtypeStruct((pairs, channels), F32)

    def chosen(steps):
        return [rights[turn * twos + step] for turn in range(ratio) for step in steps]

    sums, gate = pl.pallas_call(
        functools.partial(first_kernel, early, twos, ratio, cols),
        out_shape=(shape, shape),
        in_specs=[vmem()] * (len(lefts) + ratio * len(early) + 2),
        out_specs=[vmem()] * 2,
        scratch_shapes=[left_scr],
        compiler_params=pltpu.CompilerParams(vmem_limit_bytes=limit),
        cost_estimate=pl.CostEstimate(
            flops=2 * pairs * channels * 1024, bytes_accessed=1 << 20, transcendentals=pairs * 128
        ),
    )(*lefts, *chosen(early), one, gate_weight)
    return pl.pallas_call(
        functools.partial(last_kernel, late, twos, ratio, cols),
        out_shape=jax.ShapeDtypeStruct((rows, cols, channels), BF16),
        in_specs=[vmem()] * (len(lefts) + ratio * len(late) + 6),
        out_specs=vmem(),
        scratch_shapes=[left_scr, pltpu.VMEM((pairs, channels), F32)],
        compiler_params=pltpu.CompilerParams(vmem_limit_bytes=limit),
        cost_estimate=pl.CostEstimate(
            flops=2 * pairs * channels * 2048, bytes_accessed=2 << 20, transcendentals=pairs * 128
        ),
    )(*lefts, *chosen(late), sums, one, gate, out, up, down)


def per_device(
    alignment,
    alignment_mask,
    pair_input,
    residue_mask,
    chain_index,
    outer_left,
    outer_right,
    outer_proj,
    triangle_left,
    triangle_right,
    triangle_gate,
    triangle_out,
    relative_table,
    transition_up,
    transition_down,
):
    daps, subs = lax.axis_size("dap"), lax.axis_size("sub")
    ratio = daps // subs
    cols = pair_input.shape[1]

    def fetch(values, source):
        perm = []
        for a in range(daps):
            for b in range(subs):
                dap, sub = source(a, b)
                perm.append((dap * subs + sub, a * subs + b))
        return lax.ppermute(values, ("dap", "sub"), perm)

    def owner(a, b, turn):
        return ratio * b + (a + turn) % ratio

    hidden = outer_left.shape[1]
    mask = alignment_mask.T
    zr = factor(alignment, outer_right.T, PARTS)
    zrs = [
        fetch(
            zr[part],
            lambda a, b, t=turn, p=part: (
                owner(a, b, t), (sender(a, b, subs, ratio) + 2 * p) % subs
            ),
        )
        for turn in range(ratio)
        for part in range(PARTS)
    ]
    (zl,) = factor(alignment, outer_left.T, 1, mask)
    zlt, base, inverse, live, proj, seen = prepare(
        zl, mask, pair_input, residue_mask, chain_index, relative_table, outer_proj
    )
    own, left, one = pair_update(
        hidden, zlt, zrs, seen, base, inverse, live, proj, triangle_left, triangle_right
    )
    near = fetch(own, lambda a, b: (a, other(b)))
    across = [
        fetch(left, lambda a, b, m=step: (a, (b + 2 * m) % subs)) for step in range(1, subs // 2)
    ]
    beyond = [fetch(block, lambda a, b: (a, other(b))) for block in across]
    right = jnp.stack([own[1], near[1]])
    rights = [
        fetch(
            right,
            lambda a, b, t=turn, m=step: (
                owner(a, b, t), (sender(a, b, subs, ratio) + 2 * m) % subs
            ),
        )
        for turn in range(ratio)
        for step in range(subs // 2)
    ]
    return triangle_update(
        [own, near, *across, *beyond],
        rights,
        one,
        cols,
        triangle_gate,
        triangle_out,
        transition_up,
        transition_down,
    )


def solution(mesh):
    in_specs = (
        P("parts", "dap", None),
        P("parts", None),
        P(("parts", "dap"), "sub", None),
        P("parts"),
        P("parts"),
        P(),
        P(),
        P(),
        P(),
        P(),
        P(),
        P(),
        P(),
        P(),
        P(),
    )
    out_specs = P(("parts", "dap"), "sub", None)
    return jax.shard_map(
        per_device, mesh=mesh, in_specs=in_specs, out_specs=out_specs, check_vma=False
    )
```

```python
import functools

import jax
import jax.numpy as jnp
from jax import lax
from jax.experimental import pallas as pl
from jax.experimental.pallas import tpu as pltpu
from jax.sharding import PartitionSpec as P

REL_CLIP = 32
LANES = 128
PARTS = 2
EPSILON = 1e-05
BF16 = jnp.bfloat16
F32 = jnp.float32
NT = (((1,), (1,)), ((), ()))
TN = (((0,), (0,)), ((), ()))


def layer_norm(values):
    average = jnp.mean(values, axis=-1, keepdims=True)
    centered = values - average
    spread = jnp.mean(centered * centered, axis=-1, keepdims=True)
    return centered * lax.rsqrt(spread + EPSILON)


def dot(left, right):
    return jnp.dot(left, right, preferred_element_type=F32)


def dot_nt(left, right):
    return lax.dot_general(left, right, NT, preferred_element_type=F32)


def dot_tn(left, right):
    return lax.dot_general(left, right, TN, preferred_element_type=F32)


def iota(shape, dim):
    return lax.broadcasted_iota(jnp.int32, shape, dim)


def vmem():
    return pl.BlockSpec(memory_space=pltpu.VMEM)


def over(index, size):
    return lax.shift_right_logical(index, size.bit_length() - 1)


def within(index, size):
    return lax.bitwise_and(index, size - 1)


def repeat_kernel(weight_ref, out_ref):
    rep = LANES // weight_ref.shape[0]
    out_ref[...] = jnp.concatenate([weight_ref[...]] * rep, axis=0).T


def repeat_weight(weight):
    return pl.pallas_call(
        repeat_kernel,
        out_shape=jax.ShapeDtypeStruct((weight.shape[1], LANES), BF16),
        in_specs=[vmem()],
        out_specs=vmem(),
        compiler_params=pltpu.CompilerParams(vmem_limit_bytes=2 << 20),
        cost_estimate=pl.CostEstimate(flops=1 << 30, bytes_accessed=1 << 17, transcendentals=0),
    )(weight)


def factor_kernel(masked, hidden, x_ref, weight_ref, *refs):
    mask_ref = refs[0] if masked else None
    z_refs, y_scr = refs[masked:-1], refs[-1]
    each, seqs, _ = z_refs[0].shape
    groups = each * len(z_refs)
    _, rows, channels = x_ref.shape
    rep = rows // groups
    width = rows * hidden
    step = y_scr.shape[1] // rows
    share = jnp.full((channels, LANES), 1.0 / channels, BF16)
    w = jnp.concatenate([weight_ref[...], share], axis=1)
    sums = dot(jnp.ones((8, channels), BF16), weight_ref[...])[:1]
    block = over(iota((step, LANES), 1), hidden)
    if mask_ref is not None:
        residues = mask_ref.shape[0]
        column = lax.axis_index("dap") * rows + over(iota((residues, width), 1), hidden)
        lanes_of = (iota((residues, width), 0) == column).astype(BF16)
        live = dot_tn(mask_ref[...].astype(BF16), lanes_of)
    for turn in range(seqs // step):
        x = x_ref[turn * step : (turn + 1) * step].reshape(step * rows, channels)
        y = dot(x, w)
        mean = y[:, LANES:]
        square = jnp.zeros_like(mean)
        for half in range(channels // LANES):
            centered = x[:, half * LANES : (half + 1) * LANES].astype(F32) - mean
            square = square + centered * centered
        scale = lax.rsqrt(dot(square.astype(BF16), share[:LANES]) + EPSILON)
        y_scr[turn] = (y[:, :LANES] - mean * sums) * scale
        here = slice(turn * step, (turn + 1) * step)
        for group in range(groups):
            z = y_scr[turn, pl.ds(group * rep, step, stride=rows), :]
            for k in range(1, rep):
                next_z = y_scr[turn, pl.ds(group * rep + k, step, stride=rows), :]
                z = jnp.where(block == k, next_z, z)
            if mask_ref is not None:
                z = z * live[here, group * LANES : (group + 1) * LANES]
            z_refs[group // each][group % each, here, :] = z.astype(BF16)


def factor(alignment, weight, hidden, parts, mask=None):
    seqs, rows, channels = alignment.shape
    step = seqs // 2
    operands = (alignment, weight) if mask is None else (alignment, weight, mask)
    shape = jax.ShapeDtypeStruct((rows * hidden // LANES // parts, seqs, LANES), BF16)
    return pl.pallas_call(
        functools.partial(factor_kernel, mask is not None, hidden),
        out_shape=(shape,) * parts,
        in_specs=[vmem()] * len(operands),
        out_specs=[vmem()] * parts,
        scratch_shapes=[pltpu.VMEM((seqs // step, step * rows, LANES), F32)],
        compiler_params=pltpu.CompilerParams(vmem_limit_bytes=24 << 20),
        cost_estimate=pl.CostEstimate(
            flops=2 * seqs * rows * channels * 512, bytes_accessed=seqs << 14, transcendentals=0
        ),
    )(*operands)


def prepare_kernel(
    zl_ref, mask_ref, pair_ref, live_ref, chain_ref, table_ref, proj_ref,
    zlt_ref, base_ref, inverse_ref, live_out_ref, proj_out_ref, seen_ref, pair_scr, table_scr,
):
    rows, cols, _ = pair_ref.shape
    pairs = rows * cols
    residues = mask_ref.shape[0]
    classes = table_ref.shape[0]
    row_start = lax.axis_index("dap") * rows
    col_start = lax.axis_index("sub") * cols
    for group in range(zl_ref.shape[0]):
        turned = zl_ref[group].T
        for half in range(zlt_ref.shape[0]):
            lanes = slice(half * LANES, (half + 1) * LANES)
            zlt_ref[half, group * LANES : (group + 1) * LANES, :] = turned[:, lanes]
    proj_out_ref[...] = proj_ref[...].reshape(proj_out_ref.shape).astype(BF16)
    groups = zl_ref.shape[0]
    width = groups * LANES
    hidden = width // rows
    for block in range(cols // rows):
        column = col_start + block * rows + over(iota((residues, width), 1), hidden)
        spread = (iota((residues, width), 0) == column).astype(BF16)
        seen = dot_tn(mask_ref[...].astype(BF16), spread).astype(BF16)
        for group in range(groups):
            seen_ref[block * groups + group] = seen[:, group * LANES : (group + 1) * LANES]
    which = iota((pairs, residues), 0)
    place = iota((pairs, residues), 1)
    pick_row = (place == row_start + within(which, rows)).astype(BF16)
    pick_col = (place == col_start + over(which, rows)).astype(BF16)
    mask = mask_ref[...].astype(BF16)
    both = (dot(pick_row, mask) * dot(pick_col, mask)).astype(BF16)
    counts = dot(both, jnp.ones((mask.shape[1], LANES), BF16))
    inverse_ref[...] = 1.0 / jnp.maximum(counts, 1.0)
    live = jnp.broadcast_to(live_ref[...].astype(F32), (LANES, residues)).astype(BF16)
    chain = jnp.broadcast_to(chain_ref[...].astype(F32), (LANES, residues)).astype(BF16)
    live_out_ref[...] = dot_nt(pick_row, live) * dot_nt(pick_col, live)
    same = dot_nt(pick_row, chain) == dot_nt(pick_col, chain)
    pair = iota((pairs, LANES), 0)
    offset = (row_start + within(pair, rows)) - (col_start + over(pair, rows)) + REL_CLIP
    bucket = jnp.where(same, jnp.clip(offset, 0, 2 * REL_CLIP), 2 * REL_CLIP + 1)
    table_scr[...] = jnp.zeros_like(table_scr)
    table_scr[pl.ds(0, classes), :] = table_ref[...].astype(F32)
    onehot = (bucket == iota((pairs, LANES), 1)).astype(BF16)
    relative = dot(onehot, table_scr[...].astype(BF16))
    pair_scr[...] = pair_ref[...].reshape(pairs, LANES).astype(F32)
    for col in range(cols):
        here = slice(col * rows, (col + 1) * rows)
        base_ref[here, :] = relative[here] + pair_scr[pl.ds(col, rows, stride=cols), :]


def prepare(zl, mask, pair_input, residue_mask, chain_index, table, proj):
    rows, cols, channels = pair_input.shape
    pairs = rows * cols
    shape = jax.ShapeDtypeStruct((pairs, channels), F32)
    depth = proj.shape[0] * proj.shape[1]
    return pl.pallas_call(
        prepare_kernel,
        out_shape=(
            jax.ShapeDtypeStruct((zl.shape[1] // LANES, zl.shape[0] * LANES, LANES), BF16),
            shape,
            shape,
            shape,
            jax.ShapeDtypeStruct((depth, channels), BF16),
            jax.ShapeDtypeStruct((cols // rows * zl.shape[0], *zl.shape[1:]), BF16),
        ),
        in_specs=[vmem()] * 7,
        out_specs=[vmem()] * 6,
        scratch_shapes=[pltpu.VMEM((pairs, channels), F32), pltpu.VMEM((LANES, channels), F32)],
        compiler_params=pltpu.CompilerParams(vmem_limit_bytes=24 << 20),
        cost_estimate=pl.CostEstimate(
            flops=2 * pairs * 256 * 1024, bytes_accessed=2 << 20, transcendentals=0
        ),
    )(zl, mask, pair_input, residue_mask[None, :], chain_index[None, :], table, proj)


def pair_kernel(ratio, hidden, zlt_ref, *refs):
    zr_refs, refs = refs[: ratio * PARTS], refs[ratio * PARTS :]
    (seen_ref, base_ref, inverse_ref, live_ref, proj_ref, weight_ref,
     right_ref, one_ref, outer_scr, flat_scr) = refs
    pairs, channels = base_ref.shape
    rows = zlt_ref.shape[1] // hidden
    rep = LANES // hidden
    me = lax.axis_index("dap")
    lane = iota((rows, LANES), 1)
    odd = (lane // hidden) % 2 == 1
    upper = lane // (2 * hidden) == 1
    half = 2 * hidden
    left = jnp.concatenate([zlt_ref[part] for part in range(zlt_ref.shape[0])], axis=1)
    for step in range(ratio):
        block = lax.rem(me + step, ratio)
        right = []
        for group in range(rows // rep):
            each = rows // rep // PARTS
            factor = zr_refs[step * PARTS + group // each][group % each]
            right.append(factor * seen_ref[block * (rows // rep) + group])
        outer = dot(left, jnp.concatenate(right, axis=1))
        for group in range(rows // rep):
            outer_scr[group] = outer[:, group * LANES : (group + 1) * LANES]
        for group in range(rows // rep):
            for quad in range(hidden // rep):
                s0, s1, s2, s3 = (
                    outer_scr[group, pl.ds(quad * rep + k, rows, stride=hidden), :] for k in range(rep)
                )
                t0 = jnp.where(upper, pltpu.roll(s2, half, 1), s0)
                t1 = jnp.where(upper, pltpu.roll(s3, half, 1), s1)
                t2 = jnp.where(upper, s2, pltpu.roll(s0, half, 1))
                t3 = jnp.where(upper, s3, pltpu.roll(s1, half, 1))
                back = LANES - hidden
                found = (
                    jnp.where(odd, pltpu.roll(t1, hidden, 1), t0),
                    jnp.where(odd, t1, pltpu.roll(t0, back, 1)),
                    jnp.where(odd, pltpu.roll(t3, hidden, 1), t2),
                    jnp.where(odd, t3, pltpu.roll(t2, back, 1)),
                )
                for k in range(rep):
                    first = block * rows * rows + (group * rep + k) * rows
                    if ratio == 1:
                        first = (group * rep + k) * rows
                    else:
                        first = pl.multiple_of(first, rows)
                    flat_scr[quad, pl.ds(first, rows), :] = found[k].astype(BF16)
    flat = jnp.concatenate([flat_scr[quad] for quad in range(flat_scr.shape[0])], axis=1)
    outer_mean = dot(flat, proj_ref[...]) * inverse_ref[...]
    one = (base_ref[...] + outer_mean).astype(BF16).astype(F32)
    one_ref[...] = one
    right_ref[...] = gated(layer_norm(one).astype(BF16), weight_ref, live_ref)


def gated(norm, weight_ref, live_ref):
    both = dot(norm, weight_ref[...])
    channels = both.shape[1] // 2
    return (jax.nn.sigmoid(both[:, :channels]) * both[:, channels:] * live_ref[...]).astype(BF16)


def side_kernel(one_ref, live_ref, left_weight, gate_weight, left_ref, gate_ref, pair_ref, norm_scr):
    pairs, _ = one_ref.shape
    rows, cols = pair_ref.shape[:2]
    norm = layer_norm(one_ref[...]).astype(BF16)
    left_ref[...] = gated(norm, left_weight, live_ref)
    norm_scr[...] = jax.nn.sigmoid(dot(norm, gate_weight[...]))
    for row in range(rows):
        pair_ref[row] = one_ref[pl.ds(row, cols, stride=rows), :]
        gate_ref[row] = norm_scr[pl.ds(row, cols, stride=rows), :]


def side_update(one, live, left_weight, gate_weight, rows):
    pairs, channels = one.shape
    by_row = jax.ShapeDtypeStruct((rows, pairs // rows, channels), F32)
    return pl.pallas_call(
        side_kernel,
        out_shape=(jax.ShapeDtypeStruct((pairs, channels), BF16), by_row, by_row),
        in_specs=[vmem()] * 4,
        out_specs=[vmem()] * 3,
        scratch_shapes=[pltpu.VMEM((pairs, channels), F32)],
        compiler_params=pltpu.CompilerParams(vmem_limit_bytes=8 << 20),
        cost_estimate=pl.CostEstimate(
            flops=2 * pairs * channels * 384, bytes_accessed=1 << 19, transcendentals=pairs * 256
        ),
    )(one, live, left_weight, gate_weight)


def pair_update(hidden, zlt, zrs, seen, base, inverse, live, proj, weight):
    pairs, channels = base.shape
    ratio = len(zrs) // PARTS
    return pl.pallas_call(
        functools.partial(pair_kernel, ratio, hidden),
        out_shape=(
            jax.ShapeDtypeStruct((pairs, channels), BF16),
            jax.ShapeDtypeStruct((pairs, channels), F32),
        ),
        in_specs=[vmem()] * (7 + len(zrs)),
        out_specs=[vmem()] * 2,
        scratch_shapes=[
            pltpu.VMEM((zrs[0].shape[0] * PARTS, zlt.shape[1], LANES), F32),
            pltpu.VMEM((proj.shape[0] // LANES, pairs, LANES), BF16),
        ],
        compiler_params=pltpu.CompilerParams(vmem_limit_bytes=32 << 20),
        cost_estimate=pl.CostEstimate(
            flops=2 * pairs * 1024 * 512, bytes_accessed=2 << 20, transcendentals=pairs * 256
        ),
    )(zlt, *zrs, seen, base, inverse, live, proj, weight)


def other(sub):
    return sub + 1 - 2 * (sub % 2)


SENDERS = ((0, 2, 3, 1), (2, 1, 0, 3), (0, 3, 2, 1), (2, 0, 1, 3))


def sender(a, b, subs, ratio):
    if (subs, ratio) == (4, 1):
        return SENDERS[b][a]
    return a // ratio


def sender_index(a, b, subs, ratio):
    if (subs, ratio) != (4, 1):
        return a // ratio
    found = 0
    for col, places in enumerate(SENDERS):
        for row, place in enumerate(places):
            found = jnp.where((a == row) & (b == col), place, found)
    return found


def add_terms(sums, start, lefts, rights, steps, ratio, cols, left_scr):
    subs = left_scr.shape[0]
    _, channels = sums.shape
    rows = left_scr.shape[1] // cols
    here, there = lax.axis_index("dap"), lax.axis_index("sub")
    first_sub = sender_index(here, there, subs, ratio)
    own, near = lefts
    for step in range(subs // 2):
        sub = lax.rem(there + 2 * step, subs)
        left_scr[sub] = own[step].astype(F32)
        left_scr[other(sub)] = near[step].astype(F32)
    for turn in range(ratio):
        block = lax.rem(here + turn, ratio) if ratio > 1 else 0
        places = [i * cols + block * rows for i in range(rows)]
        if ratio > 1:
            places = [pl.multiple_of(place, rows) for place in places]
        if start is None:
            totals = tuple(jnp.zeros((rows, channels), F32) for _ in range(rows))
        else:
            totals = tuple(start[pl.ds(place, rows), :] for place in places)
        for index, step in enumerate(steps):
            sub = lax.rem(first_sub + 2 * step, subs)
            pair = rights[turn * len(steps) + index]
            for member, slot in enumerate((sub, other(sub))):

                def body(k, totals, slot=slot, member=member, pair=pair):
                    first = pl.multiple_of(k * rows, rows)
                    right = pair[member, pl.ds(first, rows), :].astype(F32)
                    return tuple(
                        totals[i] + left_scr[slot, pl.ds(first + i, 1), :] * right
                        for i in range(rows)
                    )

                totals = lax.fori_loop(0, cols, body, totals, unroll=4)
        for place, total in zip(places, totals):
            sums[pl.ds(place, rows), :] = total


def first_kernel(steps, ratio, cols, *refs):
    lefts, (sums_ref, left_scr) = refs[:2], refs[-2:]
    add_terms(sums_ref, None, lefts, refs[2:-2], steps, ratio, cols, left_scr)


def last_kernel(steps, ratio, cols, *refs):
    lefts, refs = refs[:2], refs[2:]
    rights, refs = refs[: ratio * len(steps)], refs[ratio * len(steps) :]
    (start_ref, one_ref, gate_ref, out_ref, up_ref, down_ref, result_ref, left_scr, sum_scr) = refs
    add_terms(sum_scr, start_ref, lefts, rights, steps, ratio, cols, left_scr)
    one, gate = (ref[...].reshape(sum_scr.shape) for ref in (one_ref, gate_ref))
    hidden = layer_norm(sum_scr[...].astype(BF16).astype(F32)).astype(BF16)
    two = (one + gate * dot(hidden, out_ref[...])).astype(BF16).astype(F32)
    wide = jnp.maximum(dot(layer_norm(two).astype(BF16), up_ref[...]), 0.0).astype(BF16)
    result = (two + dot(wide, down_ref[...])).astype(BF16)
    result_ref[...] = result.reshape(result_ref.shape)


def triangle_update(lefts, rights, one, gate, out, up, down):
    rows, cols, channels = one.shape
    pairs = rows * cols
    twos = lefts[0].shape[0]
    subs = 2 * twos
    ratio = len(rights) // twos
    late, early = range(twos // 2), range(twos // 2, twos)
    limit = (12 << 20) if ratio == 1 else (50 << 20)
    left_scr = pltpu.VMEM((subs, pairs, channels), F32)
    shape = jax.ShapeDtypeStruct((pairs, channels), F32)

    def chosen(steps):
        return [rights[turn * twos + step] for turn in range(ratio) for step in steps]

    sums = pl.pallas_call(
        functools.partial(first_kernel, early, ratio, cols),
        out_shape=shape,
        in_specs=[vmem()] * (2 + ratio * len(early)),
        out_specs=vmem(),
        scratch_shapes=[left_scr],
        compiler_params=pltpu.CompilerParams(vmem_limit_bytes=limit),
        cost_estimate=pl.CostEstimate(
            flops=2 * pairs * channels * 1024, bytes_accessed=1 << 20, transcendentals=0
        ),
    )(*lefts, *chosen(early))
    return pl.pallas_call(
        functools.partial(last_kernel, late, ratio, cols),
        out_shape=jax.ShapeDtypeStruct((rows, cols, channels), BF16),
        in_specs=[vmem()] * (2 + ratio * len(late) + 6),
        out_specs=vmem(),
        scratch_shapes=[left_scr, pltpu.VMEM((pairs, channels), F32)],
        compiler_params=pltpu.CompilerParams(vmem_limit_bytes=limit),
        cost_estimate=pl.CostEstimate(
            flops=2 * pairs * channels * 2048, bytes_accessed=2 << 20, transcendentals=pairs * 128
        ),
    )(*lefts, *chosen(late), sums, one, gate, out, up, down)


def per_device(
    alignment,
    alignment_mask,
    pair_input,
    residue_mask,
    chain_index,
    outer_left,
    outer_right,
    outer_proj,
    triangle_left,
    triangle_right,
    triangle_gate,
    triangle_out,
    relative_table,
    transition_up,
    transition_down,
):
    daps, subs = lax.axis_size("dap"), lax.axis_size("sub")
    ratio = daps // subs

    def fetch(values, source):
        perm = []
        for a in range(daps):
            for b in range(subs):
                dap, sub = source(a, b)
                perm.append((dap * subs + sub, a * subs + b))
        return lax.ppermute(values, ("dap", "sub"), perm)

    def owner(a, b, turn):
        return ratio * b + (a + turn) % ratio

    hidden = outer_left.shape[1]
    mask = alignment_mask.T
    zr = factor(alignment, repeat_weight(outer_right.T), hidden, PARTS)
    zrs = [
        fetch(
            zr[part],
            lambda a, b, t=turn, p=part: (
                owner(a, b, t), (sender(a, b, subs, ratio) + 2 * p) % subs
            ),
        )
        for turn in range(ratio)
        for part in range(PARTS)
    ]
    (zl,) = factor(alignment, repeat_weight(outer_left.T), hidden, 1, mask)
    zlt, base, inverse, live, proj, seen = prepare(
        zl, mask, pair_input, residue_mask, chain_index, relative_table, outer_proj
    )
    right, one = pair_update(
        hidden, zlt, zrs, seen, base, inverse, live, proj, triangle_right
    )
    near_right = fetch(right, lambda a, b: (a, other(b)))
    left, gate, pair = side_update(one, live, triangle_left, triangle_gate, pair_input.shape[0])
    across = [
        fetch(left, lambda a, b, m=step: (a, (b + 2 * m) % subs)) for step in range(1, subs // 2)
    ]
    left_pair = jnp.stack([left, *across])
    near_left = fetch(left_pair, lambda a, b: (a, other(b)))
    right = jnp.stack([right, near_right])
    rights = [
        fetch(
            right,
            lambda a, b, t=turn, m=step: (
                owner(a, b, t), (sender(a, b, subs, ratio) + 2 * m) % subs
            ),
        )
        for turn in range(ratio)
        for step in range(subs // 2)
    ]
    return triangle_update(
        [left_pair, near_left], rights, pair, gate, triangle_out, transition_up, transition_down
    )


def solution(mesh):
    in_specs = (
        P("parts", "dap", None),
        P("parts", None),
        P(("parts", "dap"), "sub", None),
        P("parts"),
        P("parts"),
        P(),
        P(),
        P(),
        P(),
        P(),
        P(),
        P(),
        P(),
        P(),
        P(),
    )
    out_specs = P(("parts", "dap"), "sub", None)
    return jax.shard_map(
        per_device, mesh=mesh, in_specs=in_specs, out_specs=out_specs, check_vma=False
    )
```

```python
import functools

import jax
import jax.numpy as jnp
from jax import lax
from jax.experimental import pallas as pl
from jax.experimental.pallas import tpu as pltpu
from jax.sharding import PartitionSpec as P

REL_CLIP = 32
LANES = 128
PARTS = 2
EPSILON = 1e-05
BF16 = jnp.bfloat16
F32 = jnp.float32
NT = (((1,), (1,)), ((), ()))
TN = (((0,), (0,)), ((), ()))


def layer_norm(values):
    average = jnp.mean(values, axis=-1, keepdims=True)
    centered = values - average
    spread = jnp.mean(centered * centered, axis=-1, keepdims=True)
    return centered * lax.rsqrt(spread + EPSILON)


def dot(left, right):
    return jnp.dot(left, right, preferred_element_type=F32)


def dot_nt(left, right):
    return lax.dot_general(left, right, NT, preferred_element_type=F32)


def dot_tn(left, right):
    return lax.dot_general(left, right, TN, preferred_element_type=F32)


def iota(shape, dim):
    return lax.broadcasted_iota(jnp.int32, shape, dim)


def vmem():
    return pl.BlockSpec(memory_space=pltpu.VMEM)


def over(index, size):
    return lax.shift_right_logical(index, size.bit_length() - 1)


def within(index, size):
    return lax.bitwise_and(index, size - 1)


def repeat_kernel(weight_ref, out_ref):
    rep = LANES // weight_ref.shape[0]
    out_ref[...] = jnp.concatenate([weight_ref[...]] * rep, axis=0).T


def repeat_weight(weight):
    return pl.pallas_call(
        repeat_kernel,
        out_shape=jax.ShapeDtypeStruct((weight.shape[1], LANES), BF16),
        in_specs=[vmem()],
        out_specs=vmem(),
        compiler_params=pltpu.CompilerParams(vmem_limit_bytes=2 << 20),
        cost_estimate=pl.CostEstimate(flops=1 << 30, bytes_accessed=1 << 17, transcendentals=0),
    )(weight)


def factor_kernel(masked, hidden, x_ref, weight_ref, *refs):
    mask_ref = refs[0] if masked else None
    z_refs, y_scr = refs[masked:-1], refs[-1]
    each, seqs, _ = z_refs[0].shape
    groups = each * len(z_refs)
    _, rows, channels = x_ref.shape
    rep = rows // groups
    width = rows * hidden
    step = y_scr.shape[1] // rows
    share = jnp.full((channels, LANES), 1.0 / channels, BF16)
    w = jnp.concatenate([weight_ref[...], share], axis=1)
    sums = dot(jnp.ones((8, channels), BF16), weight_ref[...])[:1]
    block = over(iota((step, LANES), 1), hidden)
    if mask_ref is not None:
        residues = mask_ref.shape[0]
        column = lax.axis_index("dap") * rows + over(iota((residues, width), 1), hidden)
        lanes_of = (iota((residues, width), 0) == column).astype(BF16)
        live = dot_tn(mask_ref[...].astype(BF16), lanes_of)
    for turn in range(seqs // step):
        x = x_ref[turn * step : (turn + 1) * step].reshape(step * rows, channels)
        y = dot(x, w)
        mean = y[:, LANES:]
        square = jnp.zeros_like(mean)
        for half in range(channels // LANES):
            centered = x[:, half * LANES : (half + 1) * LANES].astype(F32) - mean
            square = square + centered * centered
        scale = lax.rsqrt(dot(square.astype(BF16), share[:LANES]) + EPSILON)
        y_scr[turn] = (y[:, :LANES] - mean * sums) * scale
        here = slice(turn * step, (turn + 1) * step)
        for group in range(groups):
            z = y_scr[turn, pl.ds(group * rep, step, stride=rows), :]
            for k in range(1, rep):
                next_z = y_scr[turn, pl.ds(group * rep + k, step, stride=rows), :]
                z = jnp.where(block == k, next_z, z)
            if mask_ref is not None:
                z = z * live[here, group * LANES : (group + 1) * LANES]
            z_refs[group // each][group % each, here, :] = z.astype(BF16)


def factor(alignment, weight, hidden, parts, mask=None):
    seqs, rows, channels = alignment.shape
    step = seqs // 2
    operands = (alignment, weight) if mask is None else (alignment, weight, mask)
    shape = jax.ShapeDtypeStruct((rows * hidden // LANES // parts, seqs, LANES), BF16)
    return pl.pallas_call(
        functools.partial(factor_kernel, mask is not None, hidden),
        out_shape=(shape,) * parts,
        in_specs=[vmem()] * len(operands),
        out_specs=[vmem()] * parts,
        scratch_shapes=[pltpu.VMEM((seqs // step, step * rows, LANES), F32)],
        compiler_params=pltpu.CompilerParams(vmem_limit_bytes=24 << 20),
        cost_estimate=pl.CostEstimate(
            flops=2 * seqs * rows * channels * 512, bytes_accessed=seqs << 14, transcendentals=0
        ),
    )(*operands)


def prepare_kernel(
    zl_ref, mask_ref, pair_ref, live_ref, chain_ref, table_ref, proj_ref,
    zlt_ref, base_ref, inverse_ref, live_out_ref, proj_out_ref, seen_ref, pair_scr, table_scr, turn_scr,
):
    rows, cols, _ = pair_ref.shape
    pairs = rows * cols
    residues = mask_ref.shape[0]
    classes = table_ref.shape[0]
    row_start = lax.axis_index("dap") * rows
    col_start = lax.axis_index("sub") * cols
    groups = zl_ref.shape[0]
    hidden = groups * LANES // rows
    for group in range(groups):
        turned = zl_ref[group].astype(F32).T
        for half in range(zlt_ref.shape[0]):
            lanes = slice(half * LANES, (half + 1) * LANES)
            turn_scr[half, group * LANES : (group + 1) * LANES, :] = turned[:, lanes]
    for half in range(zlt_ref.shape[0]):
        for channel in range(hidden):
            here = slice(channel * rows, (channel + 1) * rows)
            picked = turn_scr[half, pl.ds(channel, rows, stride=hidden), :]
            zlt_ref[half, here, :] = picked.astype(BF16)
    proj_out_ref[...] = proj_ref[...].reshape(proj_out_ref.shape).astype(BF16)
    width = groups * LANES
    for block in range(cols // rows):
        column = col_start + block * rows + over(iota((residues, width), 1), hidden)
        spread = (iota((residues, width), 0) == column).astype(BF16)
        seen = dot_tn(mask_ref[...].astype(BF16), spread).astype(BF16)
        for group in range(groups):
            seen_ref[block * groups + group] = seen[:, group * LANES : (group + 1) * LANES]
    which = iota((pairs, residues), 0)
    place = iota((pairs, residues), 1)
    pick_row = (place == row_start + within(which, rows)).astype(BF16)
    pick_col = (place == col_start + over(which, rows)).astype(BF16)
    mask = mask_ref[...].astype(BF16)
    both = (dot(pick_row, mask) * dot(pick_col, mask)).astype(BF16)
    counts = dot(both, jnp.ones((mask.shape[1], LANES), BF16))
    inverse_ref[...] = 1.0 / jnp.maximum(counts, 1.0)
    live = jnp.broadcast_to(live_ref[...].astype(F32), (LANES, residues)).astype(BF16)
    chain = jnp.broadcast_to(chain_ref[...].astype(F32), (LANES, residues)).astype(BF16)
    live_out_ref[...] = dot_nt(pick_row, live) * dot_nt(pick_col, live)
    same = dot_nt(pick_row, chain) == dot_nt(pick_col, chain)
    pair = iota((pairs, LANES), 0)
    offset = (row_start + within(pair, rows)) - (col_start + over(pair, rows)) + REL_CLIP
    bucket = jnp.where(same, jnp.clip(offset, 0, 2 * REL_CLIP), 2 * REL_CLIP + 1)
    table_scr[...] = jnp.zeros_like(table_scr)
    table_scr[pl.ds(0, classes), :] = table_ref[...].astype(F32)
    onehot = (bucket == iota((pairs, LANES), 1)).astype(BF16)
    relative = dot(onehot, table_scr[...].astype(BF16))
    pair_scr[...] = pair_ref[...].reshape(pairs, LANES).astype(F32)
    for col in range(cols):
        here = slice(col * rows, (col + 1) * rows)
        base_ref[here, :] = relative[here] + pair_scr[pl.ds(col, rows, stride=cols), :]


def prepare(zl, mask, pair_input, residue_mask, chain_index, table, proj):
    rows, cols, channels = pair_input.shape
    pairs = rows * cols
    shape = jax.ShapeDtypeStruct((pairs, channels), F32)
    depth = proj.shape[0] * proj.shape[1]
    return pl.pallas_call(
        prepare_kernel,
        out_shape=(
            jax.ShapeDtypeStruct((zl.shape[1] // LANES, zl.shape[0] * LANES, LANES), BF16),
            shape,
            shape,
            shape,
            jax.ShapeDtypeStruct((depth, channels), BF16),
            jax.ShapeDtypeStruct((cols // rows * zl.shape[0], *zl.shape[1:]), BF16),
        ),
        in_specs=[vmem()] * 7,
        out_specs=[vmem()] * 6,
        scratch_shapes=[
            pltpu.VMEM((pairs, channels), F32),
            pltpu.VMEM((LANES, channels), F32),
            pltpu.VMEM((zl.shape[1] // LANES, zl.shape[0] * LANES, LANES), F32),
        ],
        compiler_params=pltpu.CompilerParams(vmem_limit_bytes=24 << 20),
        cost_estimate=pl.CostEstimate(
            flops=2 * pairs * 256 * 1024, bytes_accessed=2 << 20, transcendentals=0
        ),
    )(zl, mask, pair_input, residue_mask[None, :], chain_index[None, :], table, proj)


def pair_kernel(ratio, hidden, zlt_ref, *refs):
    zr_refs, refs = refs[: ratio * PARTS], refs[ratio * PARTS :]
    (seen_ref, base_ref, inverse_ref, live_ref, proj_ref, tl_ref, tr_ref,
     both_ref, left_ref, one_ref, flat_scr, one_scr) = refs
    pairs, channels = base_ref.shape
    rows = zlt_ref.shape[1] // hidden
    rep = LANES // hidden
    me = lax.axis_index("dap")
    lane = iota((rows, LANES), 1)
    odd = (lane // hidden) % 2 == 1
    upper = lane // (2 * hidden) == 1
    half = 2 * hidden
    left = jnp.concatenate([zlt_ref[part] for part in range(zlt_ref.shape[0])], axis=1)
    for step in range(ratio):
        block = lax.rem(me + step, ratio)
        right = []
        for group in range(rows // rep):
            each = rows // rep // PARTS
            factor = zr_refs[step * PARTS + group // each][group % each]
            right.append(factor * seen_ref[block * (rows // rep) + group])
        outer = dot(left, jnp.concatenate(right, axis=1))
        for group in range(rows // rep):
            lanes = slice(group * LANES, (group + 1) * LANES)
            for quad in range(hidden // rep):
                s0, s1, s2, s3 = (
                    outer[(quad * rep + k) * rows : (quad * rep + k + 1) * rows, lanes]
                    for k in range(rep)
                )
                t0 = jnp.where(upper, pltpu.roll(s2, half, 1), s0)
                t1 = jnp.where(upper, pltpu.roll(s3, half, 1), s1)
                t2 = jnp.where(upper, s2, pltpu.roll(s0, half, 1))
                t3 = jnp.where(upper, s3, pltpu.roll(s1, half, 1))
                back = LANES - hidden
                found = (
                    jnp.where(odd, pltpu.roll(t1, hidden, 1), t0),
                    jnp.where(odd, t1, pltpu.roll(t0, back, 1)),
                    jnp.where(odd, pltpu.roll(t3, hidden, 1), t2),
                    jnp.where(odd, t3, pltpu.roll(t2, back, 1)),
                )
                for k in range(rep):
                    first = block * rows * rows + (group * rep + k) * rows
                    if ratio == 1:
                        first = (group * rep + k) * rows
                    else:
                        first = pl.multiple_of(first, rows)
                    flat_scr[quad, pl.ds(first, rows), :] = found[k].astype(BF16)
    flat = jnp.concatenate([flat_scr[quad] for quad in range(flat_scr.shape[0])], axis=1)
    outer_mean = dot(flat, proj_ref[...]) * inverse_ref[...]
    one = (base_ref[...] + outer_mean).astype(BF16).astype(F32)
    one_scr[...] = one
    norm = layer_norm(one).astype(BF16)
    for side, weight in enumerate((tl_ref, tr_ref)):
        both = dot(norm, weight[...])
        factor = jax.nn.sigmoid(both[:, :channels]) * both[:, channels:] * live_ref[...]
        both_ref[side] = factor.astype(BF16)
        if side == 0:
            left_ref[...] = factor.astype(BF16)
    cols = pairs // rows
    for row in range(rows):
        one_ref[row * cols : (row + 1) * cols, :] = one_scr[pl.ds(row, cols, stride=rows), :].astype(BF16)


def pair_update(hidden, zlt, zrs, seen, base, inverse, live, proj, triangle_left, triangle_right):
    pairs, channels = base.shape
    ratio = len(zrs) // PARTS
    shape = jax.ShapeDtypeStruct((pairs, channels), BF16)
    return pl.pallas_call(
        functools.partial(pair_kernel, ratio, hidden),
        out_shape=(jax.ShapeDtypeStruct((2, pairs, channels), BF16), shape, shape),
        in_specs=[vmem()] * (8 + len(zrs)),
        out_specs=[vmem()] * 3,
        scratch_shapes=[
            pltpu.VMEM((proj.shape[0] // LANES, pairs, LANES), BF16),
            pltpu.VMEM((pairs, channels), F32),
        ],
        compiler_params=pltpu.CompilerParams(vmem_limit_bytes=32 << 20),
        cost_estimate=pl.CostEstimate(
            flops=2 * pairs * 1024 * 512, bytes_accessed=2 << 20, transcendentals=pairs * 256
        ),
    )(zlt, *zrs, seen, base, inverse, live, proj, triangle_left, triangle_right)


def other(sub):
    return sub + 1 - 2 * (sub % 2)


SENDERS = ((0, 2, 3, 1), (2, 1, 0, 3), (0, 3, 2, 1), (2, 0, 1, 3))


def sender(a, b, subs, ratio):
    if (subs, ratio) == (4, 1):
        return SENDERS[b][a]
    return a // ratio


def sender_index(a, b, subs, ratio):
    if (subs, ratio) != (4, 1):
        return a // ratio
    found = 0
    for col, places in enumerate(SENDERS):
        for row, place in enumerate(places):
            found = jnp.where((a == row) & (b == col), place, found)
    return found


def add_terms(sums, start, lefts, rights, steps, ratio, cols, left_scr):
    subs = left_scr.shape[0]
    _, channels = sums.shape
    rows = left_scr.shape[1] // cols
    here, there = lax.axis_index("dap"), lax.axis_index("sub")
    first_sub = sender_index(here, there, subs, ratio)
    own, near, across, beyond = lefts
    left_scr[there] = own[0].astype(F32)
    left_scr[other(there)] = near[0].astype(F32)
    for step in range(1, subs // 2):
        sub = lax.rem(there + 2 * step, subs)
        left_scr[sub] = across[step - 1][...].astype(F32)
        left_scr[other(sub)] = beyond[step - 1][...].astype(F32)
    for turn in range(ratio):
        block = lax.rem(here + turn, ratio) if ratio > 1 else 0
        places = [i * cols + block * rows for i in range(rows)]
        if ratio > 1:
            places = [pl.multiple_of(place, rows) for place in places]
        if start is None:
            totals = tuple(jnp.zeros((rows, channels), F32) for _ in range(rows))
        else:
            totals = tuple(start[pl.ds(place, rows), :] for place in places)
        for index, step in enumerate(steps):
            sub = lax.rem(first_sub + 2 * step, subs)
            pair = rights[turn * len(steps) + index]
            for member, slot in enumerate((sub, other(sub))):

                def body(k, totals, slot=slot, member=member, pair=pair):
                    first = pl.multiple_of(k * rows, rows)
                    right = pair[member, pl.ds(first, rows), :].astype(F32)
                    return tuple(
                        totals[i] + left_scr[slot, pl.ds(first + i, 1), :] * right
                        for i in range(rows)
                    )

                totals = lax.fori_loop(0, cols, body, totals, unroll=4)
        for place, total in zip(places, totals):
            sums[pl.ds(place, rows), :] = total


def split_lefts(refs, twos):
    count = twos - 1
    lefts = (refs[0], refs[1], refs[2 : 2 + count], refs[2 + count : 2 + 2 * count])
    return lefts, refs[2 + 2 * count :]


def first_kernel(steps, twos, ratio, cols, *refs):
    lefts, refs = split_lefts(refs, twos)
    rights, refs = refs[: ratio * len(steps)], refs[ratio * len(steps) :]
    one_ref, weight_ref, sums_ref, gate_ref, left_scr = refs
    add_terms(sums_ref, None, lefts, rights, steps, ratio, cols, left_scr)
    norm = layer_norm(one_ref[...].astype(F32)).astype(BF16)
    gate_ref[...] = jax.nn.sigmoid(dot(norm, weight_ref[...]))


def last_kernel(steps, twos, ratio, cols, *refs):
    lefts, refs = split_lefts(refs, twos)
    rights, refs = refs[: ratio * len(steps)], refs[ratio * len(steps) :]
    (start_ref, one_ref, gate_ref, out_ref, up_ref, down_ref, result_ref, left_scr, sum_scr) = refs
    add_terms(sum_scr, start_ref, lefts, rights, steps, ratio, cols, left_scr)
    one = one_ref[...].astype(F32)
    hidden = layer_norm(sum_scr[...].astype(BF16).astype(F32)).astype(BF16)
    two = (one + gate_ref[...] * dot(hidden, out_ref[...])).astype(BF16).astype(F32)
    wide = jnp.maximum(dot(layer_norm(two).astype(BF16), up_ref[...]), 0.0).astype(BF16)
    result = (two + dot(wide, down_ref[...])).astype(BF16)
    result_ref[...] = result.reshape(result_ref.shape)


def triangle_update(lefts, rights, one, cols, gate_weight, out, up, down):
    pairs, channels = one.shape
    rows = pairs // cols
    twos = len(lefts) // 2
    subs = 2 * twos
    ratio = len(rights) // twos
    late, early = range(twos // 2), range(twos // 2, twos)
    limit = (12 << 20) if ratio == 1 else (50 << 20)
    left_scr = pltpu.VMEM((subs, pairs, channels), F32)
    shape = jax.ShapeDtypeStruct((pairs, channels), F32)

    def chosen(steps):
        return [rights[turn * twos + step] for turn in range(ratio) for step in steps]

    sums, gate = pl.pallas_call(
        functools.partial(first_kernel, early, twos, ratio, cols),
        out_shape=(shape, shape),
        in_specs=[vmem()] * (len(lefts) + ratio * len(early) + 2),
        out_specs=[vmem()] * 2,
        scratch_shapes=[left_scr],
        compiler_params=pltpu.CompilerParams(vmem_limit_bytes=limit),
        cost_estimate=pl.CostEstimate(
            flops=2 * pairs * channels * 1024, bytes_accessed=1 << 20, transcendentals=pairs * 128
        ),
    )(*lefts, *chosen(early), one, gate_weight)
    return pl.pallas_call(
        functools.partial(last_kernel, late, twos, ratio, cols),
        out_shape=jax.ShapeDtypeStruct((rows, cols, channels), BF16),
        in_specs=[vmem()] * (len(lefts) + ratio * len(late) + 6),
        out_specs=vmem(),
        scratch_shapes=[left_scr, pltpu.VMEM((pairs, channels), F32)],
        compiler_params=pltpu.CompilerParams(vmem_limit_bytes=limit),
        cost_estimate=pl.CostEstimate(
            flops=2 * pairs * channels * 2048, bytes_accessed=2 << 20, transcendentals=pairs * 128
        ),
    )(*lefts, *chosen(late), sums, one, gate, out, up, down)


def per_device(
    alignment,
    alignment_mask,
    pair_input,
    residue_mask,
    chain_index,
    outer_left,
    outer_right,
    outer_proj,
    triangle_left,
    triangle_right,
    triangle_gate,
    triangle_out,
    relative_table,
    transition_up,
    transition_down,
):
    daps, subs = lax.axis_size("dap"), lax.axis_size("sub")
    ratio = daps // subs
    cols = pair_input.shape[1]

    def fetch(values, source):
        perm = []
        for a in range(daps):
            for b in range(subs):
                dap, sub = source(a, b)
                perm.append((dap * subs + sub, a * subs + b))
        return lax.ppermute(values, ("dap", "sub"), perm)

    def owner(a, b, turn):
        return ratio * b + (a + turn) % ratio

    hidden = outer_left.shape[1]
    mask = alignment_mask.T
    zr = factor(alignment, repeat_weight(outer_right.T), hidden, PARTS)
    zrs = [
        fetch(
            zr[part],
            lambda a, b, t=turn, p=part: (
                owner(a, b, t), (sender(a, b, subs, ratio) + 2 * p) % subs
            ),
        )
        for turn in range(ratio)
        for part in range(PARTS)
    ]
    (zl,) = factor(alignment, repeat_weight(outer_left.T), hidden, 1, mask)
    zlt, base, inverse, live, proj, seen = prepare(
        zl, mask, pair_input, residue_mask, chain_index, relative_table, outer_proj
    )
    own, left, one = pair_update(
        hidden, zlt, zrs, seen, base, inverse, live, proj, triangle_left, triangle_right
    )
    near = fetch(own, lambda a, b: (a, other(b)))
    across = [
        fetch(left, lambda a, b, m=step: (a, (b + 2 * m) % subs)) for step in range(1, subs // 2)
    ]
    beyond = [fetch(block, lambda a, b: (a, other(b))) for block in across]
    right = jnp.stack([own[1], near[1]])
    rights = [
        fetch(
            right,
            lambda a, b, t=turn, m=step: (
                owner(a, b, t), (sender(a, b, subs, ratio) + 2 * m) % subs
            ),
        )
        for turn in range(ratio)
        for step in range(subs // 2)
    ]
    return triangle_update(
        [own, near, *across, *beyond],
        rights,
        one,
        cols,
        triangle_gate,
        triangle_out,
        transition_up,
        transition_down,
    )


def solution(mesh):
    in_specs = (
        P("parts", "dap", None),
        P("parts", None),
        P(("parts", "dap"), "sub", None),
        P("parts"),
        P("parts"),
        P(),
        P(),
        P(),
        P(),
        P(),
        P(),
        P(),
        P(),
        P(),
        P(),
    )
    out_specs = P(("parts", "dap"), "sub", None)
    return jax.shard_map(
        per_device, mesh=mesh, in_specs=in_specs, out_specs=out_specs, check_vma=False
    )
```

```python
import functools

import jax
import jax.numpy as jnp
from jax import lax
from jax.experimental import pallas as pl
from jax.experimental.pallas import tpu as pltpu
from jax.sharding import PartitionSpec as P

REL_CLIP = 32
LANES = 128
PARTS = 2
EPSILON = 1e-05
BF16 = jnp.bfloat16
F32 = jnp.float32
NT = (((1,), (1,)), ((), ()))
TN = (((0,), (0,)), ((), ()))


def layer_norm(values):
    average = jnp.mean(values, axis=-1, keepdims=True)
    centered = values - average
    spread = jnp.mean(centered * centered, axis=-1, keepdims=True)
    return centered * lax.rsqrt(spread + EPSILON)


def dot(left, right):
    return jnp.dot(left, right, preferred_element_type=F32)


def dot_nt(left, right):
    return lax.dot_general(left, right, NT, preferred_element_type=F32)


def dot_tn(left, right):
    return lax.dot_general(left, right, TN, preferred_element_type=F32)


def iota(shape, dim):
    return lax.broadcasted_iota(jnp.int32, shape, dim)


def vmem():
    return pl.BlockSpec(memory_space=pltpu.VMEM)


def over(index, size):
    return lax.shift_right_logical(index, size.bit_length() - 1)


def within(index, size):
    return lax.bitwise_and(index, size - 1)


def repeat_kernel(weight_ref, out_ref):
    rep = LANES // weight_ref.shape[0]
    out_ref[...] = jnp.concatenate([weight_ref[...]] * rep, axis=0).T


def repeat_weight(weight):
    return pl.pallas_call(
        repeat_kernel,
        out_shape=jax.ShapeDtypeStruct((weight.shape[1], LANES), BF16),
        in_specs=[vmem()],
        out_specs=vmem(),
        compiler_params=pltpu.CompilerParams(vmem_limit_bytes=2 << 20),
        cost_estimate=pl.CostEstimate(flops=1 << 30, bytes_accessed=1 << 17, transcendentals=0),
    )(weight)


def factor_kernel(masked, hidden, x_ref, weight_ref, *refs):
    mask_ref = refs[0] if masked else None
    z_refs, y_scr = refs[masked:-1], refs[-1]
    each, seqs, _ = z_refs[0].shape
    groups = each * len(z_refs)
    _, rows, channels = x_ref.shape
    rep = rows // groups
    width = rows * hidden
    step = y_scr.shape[1] // rows
    share = jnp.full((channels, LANES), 1.0 / channels, BF16)
    w = jnp.concatenate([weight_ref[...], share], axis=1)
    sums = dot(jnp.ones((8, channels), BF16), weight_ref[...])[:1]
    block = over(iota((step, LANES), 1), hidden)
    if mask_ref is not None:
        residues = mask_ref.shape[0]
        column = lax.axis_index("dap") * rows + over(iota((residues, width), 1), hidden)
        lanes_of = (iota((residues, width), 0) == column).astype(BF16)
        live = dot_tn(mask_ref[...].astype(BF16), lanes_of)
    for turn in range(seqs // step):
        x = x_ref[turn * step : (turn + 1) * step].reshape(step * rows, channels)
        y = dot(x, w)
        mean = y[:, LANES:]
        square = jnp.zeros_like(mean)
        for half in range(channels // LANES):
            centered = x[:, half * LANES : (half + 1) * LANES].astype(F32) - mean
            square = square + centered * centered
        scale = lax.rsqrt(dot(square.astype(BF16), share[:LANES]) + EPSILON)
        y_scr[turn] = (y[:, :LANES] - mean * sums) * scale
        here = slice(turn * step, (turn + 1) * step)
        for group in range(groups):
            z = y_scr[turn, pl.ds(group * rep, step, stride=rows), :]
            for k in range(1, rep):
                next_z = y_scr[turn, pl.ds(group * rep + k, step, stride=rows), :]
                z = jnp.where(block == k, next_z, z)
            if mask_ref is not None:
                z = z * live[here, group * LANES : (group + 1) * LANES]
            z_refs[group // each][group % each, here, :] = z.astype(BF16)


def factor(alignment, weight, hidden, parts, mask=None):
    seqs, rows, channels = alignment.shape
    step = seqs // 2
    operands = (alignment, weight) if mask is None else (alignment, weight, mask)
    shape = jax.ShapeDtypeStruct((rows * hidden // LANES // parts, seqs, LANES), BF16)
    return pl.pallas_call(
        functools.partial(factor_kernel, mask is not None, hidden),
        out_shape=(shape,) * parts,
        in_specs=[vmem()] * len(operands),
        out_specs=[vmem()] * parts,
        scratch_shapes=[pltpu.VMEM((seqs // step, step * rows, LANES), F32)],
        compiler_params=pltpu.CompilerParams(vmem_limit_bytes=24 << 20),
        cost_estimate=pl.CostEstimate(
            flops=2 * seqs * rows * channels * 512, bytes_accessed=seqs << 14, transcendentals=0
        ),
    )(*operands)


def prepare_kernel(
    zl_ref, mask_ref, pair_ref, live_ref, chain_ref, table_ref, proj_ref,
    zlt_ref, base_ref, inverse_ref, live_out_ref, proj_out_ref, seen_ref, pair_scr, table_scr, turn_scr,
):
    rows, cols, _ = pair_ref.shape
    pairs = rows * cols
    residues = mask_ref.shape[0]
    classes = table_ref.shape[0]
    row_start = lax.axis_index("dap") * rows
    col_start = lax.axis_index("sub") * cols
    groups = zl_ref.shape[0]
    hidden = groups * LANES // rows
    for group in range(groups):
        turned = zl_ref[group].astype(F32).T
        for half in range(zlt_ref.shape[0]):
            lanes = slice(half * LANES, (half + 1) * LANES)
            turn_scr[half, group * LANES : (group + 1) * LANES, :] = turned[:, lanes]
    for half in range(zlt_ref.shape[0]):
        for channel in range(hidden):
            here = slice(channel * rows, (channel + 1) * rows)
            picked = turn_scr[half, pl.ds(channel, rows, stride=hidden), :]
            zlt_ref[half, here, :] = picked.astype(BF16)
    proj_out_ref[...] = proj_ref[...].reshape(proj_out_ref.shape).astype(BF16)
    width = groups * LANES
    for block in range(cols // rows):
        column = col_start + block * rows + over(iota((residues, width), 1), hidden)
        spread = (iota((residues, width), 0) == column).astype(BF16)
        seen = dot_tn(mask_ref[...].astype(BF16), spread).astype(BF16)
        for group in range(groups):
            seen_ref[block * groups + group] = seen[:, group * LANES : (group + 1) * LANES]
    which = iota((pairs, residues), 0)
    place = iota((pairs, residues), 1)
    pick_row = (place == row_start + within(which, rows)).astype(BF16)
    pick_col = (place == col_start + over(which, rows)).astype(BF16)
    mask = mask_ref[...].astype(BF16)
    both = (dot(pick_row, mask) * dot(pick_col, mask)).astype(BF16)
    counts = dot(both, jnp.ones((mask.shape[1], LANES), BF16))
    inverse_ref[...] = 1.0 / jnp.maximum(counts, 1.0)
    live = jnp.broadcast_to(live_ref[...].astype(F32), (LANES, residues)).astype(BF16)
    chain = jnp.broadcast_to(chain_ref[...].astype(F32), (LANES, residues)).astype(BF16)
    live_out_ref[...] = dot_nt(pick_row, live) * dot_nt(pick_col, live)
    same = dot_nt(pick_row, chain) == dot_nt(pick_col, chain)
    pair = iota((pairs, LANES), 0)
    offset = (row_start + within(pair, rows)) - (col_start + over(pair, rows)) + REL_CLIP
    bucket = jnp.where(same, jnp.clip(offset, 0, 2 * REL_CLIP), 2 * REL_CLIP + 1)
    table_scr[...] = jnp.zeros_like(table_scr)
    table_scr[pl.ds(0, classes), :] = table_ref[...].astype(F32)
    onehot = (bucket == iota((pairs, LANES), 1)).astype(BF16)
    relative = dot(onehot, table_scr[...].astype(BF16))
    pair_scr[...] = pair_ref[...].reshape(pairs, LANES).astype(F32)
    for col in range(cols):
        here = slice(col * rows, (col + 1) * rows)
        base_ref[here, :] = relative[here] + pair_scr[pl.ds(col, rows, stride=cols), :]


def prepare(zl, mask, pair_input, residue_mask, chain_index, table, proj):
    rows, cols, channels = pair_input.shape
    pairs = rows * cols
    shape = jax.ShapeDtypeStruct((pairs, channels), F32)
    depth = proj.shape[0] * proj.shape[1]
    return pl.pallas_call(
        prepare_kernel,
        out_shape=(
            jax.ShapeDtypeStruct((zl.shape[1] // LANES, zl.shape[0] * LANES, LANES), BF16),
            shape,
            shape,
            shape,
            jax.ShapeDtypeStruct((depth, channels), BF16),
            jax.ShapeDtypeStruct((cols // rows * zl.shape[0], *zl.shape[1:]), BF16),
        ),
        in_specs=[vmem()] * 7,
        out_specs=[vmem()] * 6,
        scratch_shapes=[
            pltpu.VMEM((pairs, channels), F32),
            pltpu.VMEM((LANES, channels), F32),
            pltpu.VMEM((zl.shape[1] // LANES, zl.shape[0] * LANES, LANES), F32),
        ],
        compiler_params=pltpu.CompilerParams(vmem_limit_bytes=24 << 20),
        cost_estimate=pl.CostEstimate(
            flops=2 * pairs * 256 * 1024, bytes_accessed=2 << 20, transcendentals=0
        ),
    )(zl, mask, pair_input, residue_mask[None, :], chain_index[None, :], table, proj)


def pair_kernel(ratio, hidden, zlt_ref, *refs):
    zr_refs, refs = refs[: ratio * PARTS], refs[ratio * PARTS :]
    (seen_ref, base_ref, inverse_ref, live_ref, proj_ref, tl_ref, tr_ref,
     both_ref, left_ref, one_ref, flat_scr, one_scr) = refs
    pairs, channels = base_ref.shape
    rows = zlt_ref.shape[1] // hidden
    rep = LANES // hidden
    me = lax.axis_index("dap")
    lane = iota((rows, LANES), 1)
    odd = (lane // hidden) % 2 == 1
    upper = lane // (2 * hidden) == 1
    half = 2 * hidden
    left = jnp.concatenate([zlt_ref[part] for part in range(zlt_ref.shape[0])], axis=1)
    for step in range(ratio):
        block = lax.rem(me + step, ratio)
        right = []
        for group in range(rows // rep):
            each = rows // rep // PARTS
            factor = zr_refs[step * PARTS + group // each][group % each]
            right.append(factor * seen_ref[block * (rows // rep) + group])
        outer = dot(left, jnp.concatenate(right, axis=1))
        for group in range(rows // rep):
            lanes = slice(group * LANES, (group + 1) * LANES)
            for quad in range(hidden // rep):
                s0, s1, s2, s3 = (
                    outer[(quad * rep + k) * rows : (quad * rep + k + 1) * rows, lanes]
                    for k in range(rep)
                )
                t0 = jnp.where(upper, pltpu.roll(s2, half, 1), s0)
                t1 = jnp.where(upper, pltpu.roll(s3, half, 1), s1)
                t2 = jnp.where(upper, s2, pltpu.roll(s0, half, 1))
                t3 = jnp.where(upper, s3, pltpu.roll(s1, half, 1))
                back = LANES - hidden
                found = (
                    jnp.where(odd, pltpu.roll(t1, hidden, 1), t0),
                    jnp.where(odd, t1, pltpu.roll(t0, back, 1)),
                    jnp.where(odd, pltpu.roll(t3, hidden, 1), t2),
                    jnp.where(odd, t3, pltpu.roll(t2, back, 1)),
                )
                for k in range(rep):
                    first = block * rows * rows + (group * rep + k) * rows
                    if ratio == 1:
                        first = (group * rep + k) * rows
                    else:
                        first = pl.multiple_of(first, rows)
                    flat_scr[quad, pl.ds(first, rows), :] = found[k].astype(BF16)
    flat = jnp.concatenate([flat_scr[quad] for quad in range(flat_scr.shape[0])], axis=1)
    outer_mean = dot(flat, proj_ref[...]) * inverse_ref[...]
    one = (base_ref[...] + outer_mean).astype(BF16).astype(F32)
    one_scr[...] = one
    norm = layer_norm(one).astype(BF16)
    for side, weight in enumerate((tl_ref, tr_ref)):
        both = dot(norm, weight[...])
        factor = jax.nn.sigmoid(both[:, :channels]) * both[:, channels:] * live_ref[...]
        both_ref[side] = factor.astype(BF16)
        if side == 0:
            left_ref[...] = factor.astype(BF16)
    cols = pairs // rows
    for row in range(rows):
        one_ref[row * cols : (row + 1) * cols, :] = one_scr[pl.ds(row, cols, stride=rows), :].astype(BF16)


def pair_update(hidden, zlt, zrs, seen, base, inverse, live, proj, triangle_left, triangle_right):
    pairs, channels = base.shape
    ratio = len(zrs) // PARTS
    shape = jax.ShapeDtypeStruct((pairs, channels), BF16)
    return pl.pallas_call(
        functools.partial(pair_kernel, ratio, hidden),
        out_shape=(jax.ShapeDtypeStruct((2, pairs, channels), BF16), shape, shape),
        in_specs=[vmem()] * (8 + len(zrs)),
        out_specs=[vmem()] * 3,
        scratch_shapes=[
            pltpu.VMEM((proj.shape[0] // LANES, pairs, LANES), BF16),
            pltpu.VMEM((pairs, channels), F32),
        ],
        compiler_params=pltpu.CompilerParams(vmem_limit_bytes=32 << 20),
        cost_estimate=pl.CostEstimate(
            flops=2 * pairs * 1024 * 512, bytes_accessed=2 << 20, transcendentals=pairs * 256
        ),
    )(zlt, *zrs, seen, base, inverse, live, proj, triangle_left, triangle_right)


def other(sub):
    return sub + 1 - 2 * (sub % 2)


SENDERS = ((0, 2, 3, 1), (2, 1, 0, 3), (0, 3, 2, 1), (2, 0, 1, 3))


def sender(a, b, subs, ratio):
    if (subs, ratio) == (4, 1):
        return SENDERS[b][a]
    return a // ratio


def sender_index(a, b, subs, ratio):
    if (subs, ratio) != (4, 1):
        return a // ratio
    found = 0
    for col, places in enumerate(SENDERS):
        for row, place in enumerate(places):
            found = jnp.where((a == row) & (b == col), place, found)
    return found


def add_terms(sums, start, lefts, rights, steps, ratio, cols, left_scr):
    subs = left_scr.shape[0]
    _, channels = sums.shape
    rows = left_scr.shape[1] // cols
    here, there = lax.axis_index("dap"), lax.axis_index("sub")
    first_sub = sender_index(here, there, subs, ratio)
    own, near, across, beyond = lefts
    left_scr[there] = own[0].astype(F32)
    left_scr[other(there)] = near[0].astype(F32)
    for step in range(1, subs // 2):
        sub = lax.rem(there + 2 * step, subs)
        left_scr[sub] = across[step - 1][...].astype(F32)
        left_scr[other(sub)] = beyond[step - 1][...].astype(F32)
    for turn in range(ratio):
        block = lax.rem(here + turn, ratio) if ratio > 1 else 0
        places = [i * cols + block * rows for i in range(rows)]
        if ratio > 1:
            places = [pl.multiple_of(place, rows) for place in places]
        if start is None:
            totals = tuple(jnp.zeros((rows, channels), F32) for _ in range(rows))
        else:
            totals = tuple(start[pl.ds(place, rows), :] for place in places)
        for index, step in enumerate(steps):
            sub = lax.rem(first_sub + 2 * step + 2, subs)
            pair = rights[turn * len(steps) + index]
            for member, slot in enumerate((sub, other(sub))):

                def body(k, totals, slot=slot, member=member, pair=pair):
                    first = pl.multiple_of(k * rows, rows)
                    right = pair[member, pl.ds(first, rows), :].astype(F32)
                    return tuple(
                        totals[i] + left_scr[slot, pl.ds(first + i, 1), :] * right
                        for i in range(rows)
                    )

                totals = lax.fori_loop(0, cols, body, totals, unroll=4)
        for place, total in zip(places, totals):
            sums[pl.ds(place, rows), :] = total


def split_lefts(refs, twos):
    count = twos - 1
    lefts = (refs[0], refs[1], refs[2 : 2 + count], refs[2 + count : 2 + 2 * count])
    return lefts, refs[2 + 2 * count :]


def first_kernel(steps, twos, ratio, cols, *refs):
    lefts, refs = split_lefts(refs, twos)
    rights, refs = refs[: ratio * len(steps)], refs[ratio * len(steps) :]
    one_ref, weight_ref, sums_ref, gate_ref, left_scr = refs
    add_terms(sums_ref, None, lefts, rights, steps, ratio, cols, left_scr)
    norm = layer_norm(one_ref[...].astype(F32)).astype(BF16)
    gate_ref[...] = jax.nn.sigmoid(dot(norm, weight_ref[...]))


def last_kernel(steps, twos, ratio, cols, *refs):
    lefts, refs = split_lefts(refs, twos)
    rights, refs = refs[: ratio * len(steps)], refs[ratio * len(steps) :]
    (start_ref, one_ref, gate_ref, out_ref, up_ref, down_ref, result_ref, left_scr, sum_scr) = refs
    add_terms(sum_scr, start_ref, lefts, rights, steps, ratio, cols, left_scr)
    one = one_ref[...].astype(F32)
    hidden = layer_norm(sum_scr[...].astype(BF16).astype(F32)).astype(BF16)
    two = (one + gate_ref[...] * dot(hidden, out_ref[...])).astype(BF16).astype(F32)
    wide = jnp.maximum(dot(layer_norm(two).astype(BF16), up_ref[...]), 0.0).astype(BF16)
    result = (two + dot(wide, down_ref[...])).astype(BF16)
    result_ref[...] = result.reshape(result_ref.shape)


def triangle_update(lefts, rights, one, cols, gate_weight, out, up, down):
    pairs, channels = one.shape
    rows = pairs // cols
    twos = len(lefts) // 2
    subs = 2 * twos
    ratio = len(rights) // twos
    late, early = range(twos // 2), range(twos // 2, twos)
    limit = (12 << 20) if ratio == 1 else (50 << 20)
    left_scr = pltpu.VMEM((subs, pairs, channels), F32)
    shape = jax.ShapeDtypeStruct((pairs, channels), F32)

    def chosen(steps):
        return [rights[turn * twos + step] for turn in range(ratio) for step in steps]

    sums, gate = pl.pallas_call(
        functools.partial(first_kernel, early, twos, ratio, cols),
        out_shape=(shape, shape),
        in_specs=[vmem()] * (len(lefts) + ratio * len(early) + 2),
        out_specs=[vmem()] * 2,
        scratch_shapes=[left_scr],
        compiler_params=pltpu.CompilerParams(vmem_limit_bytes=limit),
        cost_estimate=pl.CostEstimate(
            flops=2 * pairs * channels * 1024, bytes_accessed=1 << 20, transcendentals=pairs * 128
        ),
    )(*lefts, *chosen(early), one, gate_weight)
    return pl.pallas_call(
        functools.partial(last_kernel, late, twos, ratio, cols),
        out_shape=jax.ShapeDtypeStruct((rows, cols, channels), BF16),
        in_specs=[vmem()] * (len(lefts) + ratio * len(late) + 6),
        out_specs=vmem(),
        scratch_shapes=[left_scr, pltpu.VMEM((pairs, channels), F32)],
        compiler_params=pltpu.CompilerParams(vmem_limit_bytes=limit),
        cost_estimate=pl.CostEstimate(
            flops=2 * pairs * channels * 2048, bytes_accessed=2 << 20, transcendentals=pairs * 128
        ),
    )(*lefts, *chosen(late), sums, one, gate, out, up, down)


def per_device(
    alignment,
    alignment_mask,
    pair_input,
    residue_mask,
    chain_index,
    outer_left,
    outer_right,
    outer_proj,
    triangle_left,
    triangle_right,
    triangle_gate,
    triangle_out,
    relative_table,
    transition_up,
    transition_down,
):
    daps, subs = lax.axis_size("dap"), lax.axis_size("sub")
    ratio = daps // subs
    cols = pair_input.shape[1]

    def fetch(values, source):
        perm = []
        for a in range(daps):
            for b in range(subs):
                dap, sub = source(a, b)
                perm.append((dap * subs + sub, a * subs + b))
        return lax.ppermute(values, ("dap", "sub"), perm)

    def owner(a, b, turn):
        return ratio * b + (a + turn) % ratio

    hidden = outer_left.shape[1]
    mask = alignment_mask.T
    zr = factor(alignment, repeat_weight(outer_right.T), hidden, PARTS)
    zrs = [
        fetch(
            zr[part],
            lambda a, b, t=turn, p=part: (
                owner(a, b, t), (sender(a, b, subs, ratio) + 2 * p) % subs
            ),
        )
        for turn in range(ratio)
        for part in range(PARTS)
    ]
    (zl,) = factor(alignment, repeat_weight(outer_left.T), hidden, 1, mask)
    zlt, base, inverse, live, proj, seen = prepare(
        zl, mask, pair_input, residue_mask, chain_index, relative_table, outer_proj
    )
    own, left, one = pair_update(
        hidden, zlt, zrs, seen, base, inverse, live, proj, triangle_left, triangle_right
    )
    near = fetch(own, lambda a, b: (a, other(b)))
    across = [
        fetch(left, lambda a, b, m=step: (a, (b + 2 * m) % subs)) for step in range(1, subs // 2)
    ]
    beyond = [fetch(block, lambda a, b: (a, other(b))) for block in across]
    right = jnp.stack([own[1], near[1]])
    rights = [
        fetch(
            right,
            lambda a, b, t=turn, m=step: (
                owner(a, b, t), (sender(a, b, subs, ratio) + 2 * m + 2) % subs
            ),
        )
        for turn in range(ratio)
        for step in range(subs // 2)
    ]
    return triangle_update(
        [own, near, *across, *beyond],
        rights,
        one,
        cols,
        triangle_gate,
        triangle_out,
        transition_up,
        transition_down,
    )


def solution(mesh):
    in_specs = (
        P("parts", "dap", None),
        P("parts", None),
        P(("parts", "dap"), "sub", None),
        P("parts"),
        P("parts"),
        P(),
        P(),
        P(),
        P(),
        P(),
        P(),
        P(),
        P(),
        P(),
        P(),
    )
    out_specs = P(("parts", "dap"), "sub", None)
    return jax.shard_map(
        per_device, mesh=mesh, in_specs=in_specs, out_specs=out_specs, check_vma=False
    )
```

```python
import functools

import jax
import jax.numpy as jnp
from jax import lax
from jax.experimental import pallas as pl
from jax.experimental.pallas import tpu as pltpu
from jax.sharding import PartitionSpec as P

REL_CLIP = 32
LANES = 128
PARTS = 1
EPSILON = 1e-05
BF16 = jnp.bfloat16
F32 = jnp.float32
NT = (((1,), (1,)), ((), ()))
TN = (((0,), (0,)), ((), ()))


def layer_norm(values):
    average = jnp.mean(values, axis=-1, keepdims=True)
    centered = values - average
    spread = jnp.mean(centered * centered, axis=-1, keepdims=True)
    return centered * lax.rsqrt(spread + EPSILON)


def matmul_norm(values):
    channels = values.shape[-1]
    share = jnp.full((channels, LANES), 1.0 / channels, BF16)
    wide = values.astype(F32)
    centered = wide - dot(values, share)
    spread = dot((centered * centered).astype(BF16), share)
    return (centered * lax.rsqrt(spread + EPSILON)).astype(BF16)


def dot(left, right):
    return jnp.dot(left, right, preferred_element_type=F32)


def dot_nt(left, right):
    return lax.dot_general(left, right, NT, preferred_element_type=F32)


def dot_tn(left, right):
    return lax.dot_general(left, right, TN, preferred_element_type=F32)


def iota(shape, dim):
    return lax.broadcasted_iota(jnp.int32, shape, dim)


def vmem():
    return pl.BlockSpec(memory_space=pltpu.VMEM)


def over(index, size):
    return lax.shift_right_logical(index, size.bit_length() - 1)


def within(index, size):
    return lax.bitwise_and(index, size - 1)


def repeat_kernel(weight_ref, out_ref):
    rep = LANES // weight_ref.shape[0]
    out_ref[...] = jnp.concatenate([weight_ref[...]] * rep, axis=0).T


def repeat_weight(weight):
    return pl.pallas_call(
        repeat_kernel,
        out_shape=jax.ShapeDtypeStruct((weight.shape[1], LANES), BF16),
        in_specs=[vmem()],
        out_specs=vmem(),
        compiler_params=pltpu.CompilerParams(vmem_limit_bytes=2 << 20),
        cost_estimate=pl.CostEstimate(flops=1 << 30, bytes_accessed=1 << 17, transcendentals=0),
    )(weight)


def factor_kernel(masked, hidden, x_ref, weight_ref, *refs):
    mask_ref = refs[0] if masked else None
    z_refs, y_scr = refs[masked:-1], refs[-1]
    each, seqs, _ = z_refs[0].shape
    groups = each * len(z_refs)
    _, rows, channels = x_ref.shape
    rep = rows // groups
    width = rows * hidden
    step = y_scr.shape[1] // rows
    share = jnp.full((channels, LANES), 1.0 / channels, BF16)
    w = jnp.concatenate([weight_ref[...], share], axis=1)
    sums = dot(jnp.ones((8, channels), BF16), weight_ref[...])[:1]
    block = over(iota((step, LANES), 1), hidden)
    if mask_ref is not None:
        residues = mask_ref.shape[0]
        column = lax.axis_index("dap") * rows + over(iota((residues, width), 1), hidden)
        lanes_of = (iota((residues, width), 0) == column).astype(BF16)
        live = dot_tn(mask_ref[...].astype(BF16), lanes_of)
    for turn in range(seqs // step):
        x = x_ref[turn * step : (turn + 1) * step].reshape(step * rows, channels)
        y = dot(x, w)
        mean = y[:, LANES:]
        square = jnp.zeros_like(mean)
        for half in range(channels // LANES):
            centered = x[:, half * LANES : (half + 1) * LANES].astype(F32) - mean
            square = square + centered * centered
        scale = lax.rsqrt(dot(square.astype(BF16), share[:LANES]) + EPSILON)
        y_scr[turn] = (y[:, :LANES] - mean * sums) * scale
        here = slice(turn * step, (turn + 1) * step)
        for group in range(groups):
            z = y_scr[turn, pl.ds(group * rep, step, stride=rows), :]
            for k in range(1, rep):
                next_z = y_scr[turn, pl.ds(group * rep + k, step, stride=rows), :]
                z = jnp.where(block == k, next_z, z)
            if mask_ref is not None:
                z = z * live[here, group * LANES : (group + 1) * LANES]
            z_refs[group // each][group % each, here, :] = z.astype(BF16)


def factor(alignment, weight, hidden, parts, mask=None):
    seqs, rows, channels = alignment.shape
    step = seqs // 2
    operands = (alignment, weight) if mask is None else (alignment, weight, mask)
    shape = jax.ShapeDtypeStruct((rows * hidden // LANES // parts, seqs, LANES), BF16)
    return pl.pallas_call(
        functools.partial(factor_kernel, mask is not None, hidden),
        out_shape=(shape,) * parts,
        in_specs=[vmem()] * len(operands),
        out_specs=[vmem()] * parts,
        scratch_shapes=[pltpu.VMEM((seqs // step, step * rows, LANES), F32)],
        compiler_params=pltpu.CompilerParams(vmem_limit_bytes=24 << 20),
        cost_estimate=pl.CostEstimate(
            flops=2 * seqs * rows * channels * 512, bytes_accessed=seqs << 14, transcendentals=0
        ),
    )(*operands)


def prepare_kernel(
    zl_ref, mask_ref, pair_ref, live_ref, chain_ref, table_ref, proj_ref,
    zlt_ref, base_ref, inverse_ref, live_out_ref, proj_out_ref, seen_ref, pair_scr, table_scr, turn_scr,
):
    rows, cols, _ = pair_ref.shape
    pairs = rows * cols
    residues = mask_ref.shape[0]
    classes = table_ref.shape[0]
    row_start = lax.axis_index("dap") * rows
    col_start = lax.axis_index("sub") * cols
    groups = zl_ref.shape[0]
    hidden = groups * LANES // rows
    for group in range(groups):
        turned = zl_ref[group].astype(F32).T
        for half in range(zlt_ref.shape[0]):
            lanes = slice(half * LANES, (half + 1) * LANES)
            turn_scr[half, group * LANES : (group + 1) * LANES, :] = turned[:, lanes]
    for half in range(zlt_ref.shape[0]):
        for channel in range(hidden):
            here = slice(channel * rows, (channel + 1) * rows)
            picked = turn_scr[half, pl.ds(channel, rows, stride=hidden), :]
            zlt_ref[half, here, :] = picked.astype(BF16)
    proj_out_ref[...] = proj_ref[...].reshape(proj_out_ref.shape).astype(BF16)
    width = groups * LANES
    for block in range(cols // rows):
        column = col_start + block * rows + over(iota((residues, width), 1), hidden)
        spread = (iota((residues, width), 0) == column).astype(BF16)
        seen = dot_tn(mask_ref[...].astype(BF16), spread).astype(BF16)
        for group in range(groups):
            seen_ref[block * groups + group] = seen[:, group * LANES : (group + 1) * LANES]
    which = iota((pairs, residues), 0)
    place = iota((pairs, residues), 1)
    pick_row = (place == row_start + within(which, rows)).astype(BF16)
    pick_col = (place == col_start + over(which, rows)).astype(BF16)
    mask = mask_ref[...].astype(BF16)
    both = (dot(pick_row, mask) * dot(pick_col, mask)).astype(BF16)
    counts = dot(both, jnp.ones((mask.shape[1], LANES), BF16))
    inverse_ref[...] = 1.0 / jnp.maximum(counts, 1.0)
    live = jnp.broadcast_to(live_ref[...].astype(F32), (LANES, residues)).astype(BF16)
    chain = jnp.broadcast_to(chain_ref[...].astype(F32), (LANES, residues)).astype(BF16)
    live_out_ref[...] = dot_nt(pick_row, live) * dot_nt(pick_col, live)
    same = dot_nt(pick_row, chain) == dot_nt(pick_col, chain)
    pair = iota((pairs, LANES), 0)
    offset = (row_start + within(pair, rows)) - (col_start + over(pair, rows)) + REL_CLIP
    bucket = jnp.where(same, jnp.clip(offset, 0, 2 * REL_CLIP), 2 * REL_CLIP + 1)
    table_scr[...] = jnp.zeros_like(table_scr)
    table_scr[pl.ds(0, classes), :] = table_ref[...].astype(F32)
    onehot = (bucket == iota((pairs, LANES), 1)).astype(BF16)
    relative = dot(onehot, table_scr[...].astype(BF16))
    pair_scr[...] = pair_ref[...].reshape(pairs, LANES).astype(F32)
    for col in range(cols):
        here = slice(col * rows, (col + 1) * rows)
        base_ref[here, :] = relative[here] + pair_scr[pl.ds(col, rows, stride=cols), :]


def prepare(zl, mask, pair_input, residue_mask, chain_index, table, proj):
    rows, cols, channels = pair_input.shape
    pairs = rows * cols
    shape = jax.ShapeDtypeStruct((pairs, channels), F32)
    depth = proj.shape[0] * proj.shape[1]
    return pl.pallas_call(
        prepare_kernel,
        out_shape=(
            jax.ShapeDtypeStruct((zl.shape[1] // LANES, zl.shape[0] * LANES, LANES), BF16),
            shape,
            shape,
            shape,
            jax.ShapeDtypeStruct((depth, channels), BF16),
            jax.ShapeDtypeStruct((cols // rows * zl.shape[0], *zl.shape[1:]), BF16),
        ),
        in_specs=[vmem()] * 7,
        out_specs=[vmem()] * 6,
        scratch_shapes=[
            pltpu.VMEM((pairs, channels), F32),
            pltpu.VMEM((LANES, channels), F32),
            pltpu.VMEM((zl.shape[1] // LANES, zl.shape[0] * LANES, LANES), F32),
        ],
        compiler_params=pltpu.CompilerParams(vmem_limit_bytes=24 << 20),
        cost_estimate=pl.CostEstimate(
            flops=2 * pairs * 256 * 1024, bytes_accessed=2 << 20, transcendentals=0
        ),
    )(zl, mask, pair_input, residue_mask[None, :], chain_index[None, :], table, proj)


def pair_kernel(ratio, hidden, zlt_ref, *refs):
    zr_refs, refs = refs[: ratio * PARTS], refs[ratio * PARTS :]
    (seen_ref, base_ref, inverse_ref, live_ref, proj_ref, tl_ref, tr_ref,
     both_ref, left_ref, one_ref, flat_scr, one_scr) = refs
    pairs, channels = base_ref.shape
    rows = zlt_ref.shape[1] // hidden
    rep = LANES // hidden
    me = lax.axis_index("dap")
    lane = iota((rows, LANES), 1)
    odd = (lane // hidden) % 2 == 1
    upper = lane // (2 * hidden) == 1
    half = 2 * hidden
    left = jnp.concatenate([zlt_ref[part] for part in range(zlt_ref.shape[0])], axis=1)
    for step in range(ratio):
        block = lax.rem(me + step, ratio)
        right = []
        for group in range(rows // rep):
            each = rows // rep // PARTS
            factor = zr_refs[step * PARTS + group // each][group % each]
            right.append(factor * seen_ref[block * (rows // rep) + group])
        outer = dot(left, jnp.concatenate(right, axis=1))
        for group in range(rows // rep):
            lanes = slice(group * LANES, (group + 1) * LANES)
            for quad in range(hidden // rep):
                s0, s1, s2, s3 = (
                    outer[(quad * rep + k) * rows : (quad * rep + k + 1) * rows, lanes]
                    for k in range(rep)
                )
                t0 = jnp.where(upper, pltpu.roll(s2, half, 1), s0)
                t1 = jnp.where(upper, pltpu.roll(s3, half, 1), s1)
                t2 = jnp.where(upper, s2, pltpu.roll(s0, half, 1))
                t3 = jnp.where(upper, s3, pltpu.roll(s1, half, 1))
                back = LANES - hidden
                found = (
                    jnp.where(odd, pltpu.roll(t1, hidden, 1), t0),
                    jnp.where(odd, t1, pltpu.roll(t0, back, 1)),
                    jnp.where(odd, pltpu.roll(t3, hidden, 1), t2),
                    jnp.where(odd, t3, pltpu.roll(t2, back, 1)),
                )
                for k in range(rep):
                    first = block * rows * rows + (group * rep + k) * rows
                    if ratio == 1:
                        first = (group * rep + k) * rows
                    else:
                        first = pl.multiple_of(first, rows)
                    flat_scr[quad, pl.ds(first, rows), :] = found[k].astype(BF16)
    flat = jnp.concatenate([flat_scr[quad] for quad in range(flat_scr.shape[0])], axis=1)
    outer_mean = dot(flat, proj_ref[...]) * inverse_ref[...]
    one = (base_ref[...] + outer_mean).astype(BF16).astype(F32)
    one_scr[...] = one
    norm = layer_norm(one).astype(BF16)
    for side, weight in enumerate((tl_ref, tr_ref)):
        both = dot(norm, weight[...])
        factor = jax.nn.sigmoid(both[:, :channels]) * both[:, channels:] * live_ref[...]
        both_ref[side] = factor.astype(BF16)
        if side == 0:
            left_ref[...] = factor.astype(BF16)
    cols = pairs // rows
    for row in range(rows):
        one_ref[row * cols : (row + 1) * cols, :] = one_scr[pl.ds(row, cols, stride=rows), :].astype(BF16)


def pair_update(hidden, zlt, zrs, seen, base, inverse, live, proj, triangle_left, triangle_right):
    pairs, channels = base.shape
    ratio = len(zrs) // PARTS
    shape = jax.ShapeDtypeStruct((pairs, channels), BF16)
    return pl.pallas_call(
        functools.partial(pair_kernel, ratio, hidden),
        out_shape=(jax.ShapeDtypeStruct((2, pairs, channels), BF16), shape, shape),
        in_specs=[vmem()] * (8 + len(zrs)),
        out_specs=[vmem()] * 3,
        scratch_shapes=[
            pltpu.VMEM((proj.shape[0] // LANES, pairs, LANES), BF16),
            pltpu.VMEM((pairs, channels), F32),
        ],
        compiler_params=pltpu.CompilerParams(vmem_limit_bytes=32 << 20),
        cost_estimate=pl.CostEstimate(
            flops=2 * pairs * 1024 * 512, bytes_accessed=2 << 20, transcendentals=pairs * 256
        ),
    )(zlt, *zrs, seen, base, inverse, live, proj, triangle_left, triangle_right)


def other(sub):
    return sub + 1 - 2 * (sub % 2)


SENDERS = ((0, 2, 3, 1), (2, 1, 0, 3), (0, 3, 2, 1), (2, 0, 1, 3))


def sender(a, b, subs, ratio):
    if (subs, ratio) == (4, 1):
        return SENDERS[b][a]
    return a // ratio


def sender_index(a, b, subs, ratio):
    if (subs, ratio) != (4, 1):
        return a // ratio
    found = 0
    for col, places in enumerate(SENDERS):
        for row, place in enumerate(places):
            found = jnp.where((a == row) & (b == col), place, found)
    return found


def add_terms(sums, start, lefts, rights, steps, ratio, cols, left_scr):
    subs = left_scr.shape[0]
    _, channels = sums.shape
    rows = left_scr.shape[1] // cols
    here, there = lax.axis_index("dap"), lax.axis_index("sub")
    first_sub = sender_index(here, there, subs, ratio)
    own, near, across, beyond = lefts
    left_scr[there] = own[0].astype(F32)
    left_scr[other(there)] = near[0].astype(F32)
    for step in range(1, subs // 2):
        sub = lax.rem(there + 2 * step, subs)
        left_scr[sub] = across[step - 1][...].astype(F32)
        left_scr[other(sub)] = beyond[step - 1][...].astype(F32)
    for turn in range(ratio):
        block = lax.rem(here + turn, ratio) if ratio > 1 else 0
        places = [i * cols + block * rows for i in range(rows)]
        if ratio > 1:
            places = [pl.multiple_of(place, rows) for place in places]
        if start is None:
            totals = tuple(jnp.zeros((rows, channels), F32) for _ in range(rows))
        else:
            totals = tuple(start[pl.ds(place, rows), :] for place in places)
        for index, step in enumerate(steps):
            sub = lax.rem(first_sub + 2 * step, subs)
            pair = rights[turn * len(steps) + index]
            for member, slot in enumerate((sub, other(sub))):

                def body(k, totals, slot=slot, member=member, pair=pair):
                    first = pl.multiple_of(k * rows, rows)
                    right = pair[member, pl.ds(first, rows), :].astype(F32)
                    return tuple(
                        totals[i] + left_scr[slot, pl.ds(first + i, 1), :] * right
                        for i in range(rows)
                    )

                totals = lax.fori_loop(0, cols, body, totals, unroll=4)
        for place, total in zip(places, totals):
            sums[pl.ds(place, rows), :] = total


def split_lefts(refs, twos):
    count = twos - 1
    lefts = (refs[0], refs[1], refs[2 : 2 + count], refs[2 + count : 2 + 2 * count])
    return lefts, refs[2 + 2 * count :]


def first_kernel(steps, twos, ratio, cols, *refs):
    lefts, refs = split_lefts(refs, twos)
    rights, refs = refs[: ratio * len(steps)], refs[ratio * len(steps) :]
    one_ref, weight_ref, sums_ref, gate_ref, left_scr = refs
    add_terms(sums_ref, None, lefts, rights, steps, ratio, cols, left_scr)
    norm = layer_norm(one_ref[...].astype(F32)).astype(BF16)
    gate_ref[...] = jax.nn.sigmoid(dot(norm, weight_ref[...]))


def last_kernel(steps, twos, ratio, cols, *refs):
    lefts, refs = split_lefts(refs, twos)
    rights, refs = refs[: ratio * len(steps)], refs[ratio * len(steps) :]
    (start_ref, one_ref, gate_ref, out_ref, up_ref, down_ref, result_ref, left_scr, sum_scr) = refs
    add_terms(sum_scr, start_ref, lefts, rights, steps, ratio, cols, left_scr)
    one = one_ref[...].astype(F32)
    hidden = matmul_norm(sum_scr[...].astype(BF16))
    two = (one + gate_ref[...] * dot(hidden, out_ref[...])).astype(BF16)
    wide = jnp.maximum(dot(matmul_norm(two), up_ref[...]), 0.0).astype(BF16)
    result = (two.astype(F32) + dot(wide, down_ref[...])).astype(BF16)
    result_ref[...] = result.reshape(result_ref.shape)


def triangle_update(lefts, rights, one, cols, gate_weight, out, up, down):
    pairs, channels = one.shape
    rows = pairs // cols
    twos = len(lefts) // 2
    subs = 2 * twos
    ratio = len(rights) // twos
    late, early = range(twos // 2), range(twos // 2, twos)
    limit = (12 << 20) if ratio == 1 else (50 << 20)
    left_scr = pltpu.VMEM((subs, pairs, channels), F32)
    shape = jax.ShapeDtypeStruct((pairs, channels), F32)

    def chosen(steps):
        return [rights[turn * twos + step] for turn in range(ratio) for step in steps]

    sums, gate = pl.pallas_call(
        functools.partial(first_kernel, early, twos, ratio, cols),
        out_shape=(shape, shape),
        in_specs=[vmem()] * (len(lefts) + ratio * len(early) + 2),
        out_specs=[vmem()] * 2,
        scratch_shapes=[left_scr],
        compiler_params=pltpu.CompilerParams(vmem_limit_bytes=limit),
        cost_estimate=pl.CostEstimate(
            flops=2 * pairs * channels * 1024, bytes_accessed=1 << 20, transcendentals=pairs * 128
        ),
    )(*lefts, *chosen(early), one, gate_weight)
    return pl.pallas_call(
        functools.partial(last_kernel, late, twos, ratio, cols),
        out_shape=jax.ShapeDtypeStruct((rows, cols, channels), BF16),
        in_specs=[vmem()] * (len(lefts) + ratio * len(late) + 6),
        out_specs=vmem(),
        scratch_shapes=[left_scr, pltpu.VMEM((pairs, channels), F32)],
        compiler_params=pltpu.CompilerParams(vmem_limit_bytes=limit),
        cost_estimate=pl.CostEstimate(
            flops=2 * pairs * channels * 2048, bytes_accessed=2 << 20, transcendentals=pairs * 128
        ),
    )(*lefts, *chosen(late), sums, one, gate, out, up, down)


def per_device(
    alignment,
    alignment_mask,
    pair_input,
    residue_mask,
    chain_index,
    outer_left,
    outer_right,
    outer_proj,
    triangle_left,
    triangle_right,
    triangle_gate,
    triangle_out,
    relative_table,
    transition_up,
    transition_down,
):
    daps, subs = lax.axis_size("dap"), lax.axis_size("sub")
    ratio = daps // subs
    cols = pair_input.shape[1]

    def fetch(values, source):
        perm = []
        for a in range(daps):
            for b in range(subs):
                dap, sub = source(a, b)
                perm.append((dap * subs + sub, a * subs + b))
        return lax.ppermute(values, ("dap", "sub"), perm)

    def owner(a, b, turn):
        return ratio * b + (a + turn) % ratio

    hidden = outer_left.shape[1]
    mask = alignment_mask.T
    zr = factor(alignment, repeat_weight(outer_right.T), hidden, PARTS)
    zrs = [
        fetch(
            zr[part],
            lambda a, b, t=turn, p=part: (
                owner(a, b, t), (sender(a, b, subs, ratio) + 2 * p) % subs
            ),
        )
        for turn in range(ratio)
        for part in range(PARTS)
    ]
    (zl,) = factor(alignment, repeat_weight(outer_left.T), hidden, 1, mask)
    zlt, base, inverse, live, proj, seen = prepare(
        zl, mask, pair_input, residue_mask, chain_index, relative_table, outer_proj
    )
    own, left, one = pair_update(
        hidden, zlt, zrs, seen, base, inverse, live, proj, triangle_left, triangle_right
    )
    near = fetch(own, lambda a, b: (a, other(b)))
    across = [
        fetch(left, lambda a, b, m=step: (a, (b + 2 * m) % subs)) for step in range(1, subs // 2)
    ]
    beyond = [fetch(block, lambda a, b: (a, other(b))) for block in across]
    right = jnp.stack([own[1], near[1]])
    rights = [
        fetch(
            right,
            lambda a, b, t=turn, m=step: (
                owner(a, b, t), (sender(a, b, subs, ratio) + 2 * m) % subs
            ),
        )
        for turn in range(ratio)
        for step in range(subs // 2)
    ]
    return triangle_update(
        [own, near, *across, *beyond],
        rights,
        one,
        cols,
        triangle_gate,
        triangle_out,
        transition_up,
        transition_down,
    )


def solution(mesh):
    in_specs = (
        P("parts", "dap", None),
        P("parts", None),
        P(("parts", "dap"), "sub", None),
        P("parts"),
        P("parts"),
        P(),
        P(),
        P(),
        P(),
        P(),
        P(),
        P(),
        P(),
        P(),
        P(),
    )
    out_specs = P(("parts", "dap"), "sub", None)
    return jax.shard_map(
        per_device, mesh=mesh, in_specs=in_specs, out_specs=out_specs, check_vma=False
    )
```

```python
import functools

import jax
import jax.numpy as jnp
from jax import lax
from jax.experimental import pallas as pl
from jax.experimental.pallas import tpu as pltpu
from jax.sharding import PartitionSpec as P

REL_CLIP = 32
LANES = 128
PARTS = 1
EPSILON = 1e-05
BF16 = jnp.bfloat16
F32 = jnp.float32
NT = (((1,), (1,)), ((), ()))
TN = (((0,), (0,)), ((), ()))


def layer_norm(values):
    average = jnp.mean(values, axis=-1, keepdims=True)
    centered = values - average
    spread = jnp.mean(centered * centered, axis=-1, keepdims=True)
    return centered * lax.rsqrt(spread + EPSILON)


def dot(left, right):
    return jnp.dot(left, right, preferred_element_type=F32)


def dot_nt(left, right):
    return lax.dot_general(left, right, NT, preferred_element_type=F32)


def dot_tn(left, right):
    return lax.dot_general(left, right, TN, preferred_element_type=F32)


def iota(shape, dim):
    return lax.broadcasted_iota(jnp.int32, shape, dim)


def vmem():
    return pl.BlockSpec(memory_space=pltpu.VMEM)


def over(index, size):
    return lax.shift_right_logical(index, size.bit_length() - 1)


def within(index, size):
    return lax.bitwise_and(index, size - 1)


def repeat_kernel(weight_ref, out_ref):
    hidden, channels = weight_ref.shape
    rep = LANES // hidden
    wide = jnp.concatenate([weight_ref[...]] * rep, axis=0).T
    block = over(iota((channels, LANES), 1), hidden)
    for k in range(rep):
        out_ref[k * channels : (k + 1) * channels, :] = jnp.where(block == k, wide, 0)


def repeat_weight(weight):
    hidden, channels = weight.shape
    return pl.pallas_call(
        repeat_kernel,
        out_shape=jax.ShapeDtypeStruct((channels * LANES // hidden, LANES), BF16),
        in_specs=[vmem()],
        out_specs=vmem(),
        compiler_params=pltpu.CompilerParams(vmem_limit_bytes=2 << 20),
        cost_estimate=pl.CostEstimate(flops=1 << 30, bytes_accessed=1 << 17, transcendentals=0),
    )(weight)


def exchange(s0, s1, s2, s3):
    lane = iota(s0.shape, 1)
    block = LANES // 4
    odd = within(over(lane, block), 2) == 1
    upper = over(lane, 2 * block) == 1
    t0 = jnp.where(upper, pltpu.roll(s2, 2 * block, 1), s0)
    t1 = jnp.where(upper, pltpu.roll(s3, 2 * block, 1), s1)
    t2 = jnp.where(upper, s2, pltpu.roll(s0, 2 * block, 1))
    t3 = jnp.where(upper, s3, pltpu.roll(s1, 2 * block, 1))
    return (
        jnp.where(odd, pltpu.roll(t1, block, 1), t0),
        jnp.where(odd, t1, pltpu.roll(t0, 3 * block, 1)),
        jnp.where(odd, pltpu.roll(t3, block, 1), t2),
        jnp.where(odd, t3, pltpu.roll(t2, 3 * block, 1)),
    )


def factor_kernel(masked, hidden, x_ref, weight_ref, *refs):
    mask_ref = refs[0] if masked else None
    z_refs, y_scr = refs[masked:-1], refs[-1]
    each, seqs, _ = z_refs[0].shape
    groups = each * len(z_refs)
    _, rows, channels = x_ref.shape
    rep = rows // groups
    width = rows * hidden
    steps, step = y_scr.shape[0], y_scr.shape[1] // rows
    quarter = seqs // rep
    weight = weight_ref[...]
    sums = dot(jnp.ones((8, channels * rep), BF16), weight)[:1]
    share = jnp.full((channels, LANES), 1.0 / channels, BF16)
    side = (rep * LANES, LANES)
    own = over(iota(side, 0), LANES) == over(iota(side, 1), hidden)
    own = jnp.where(own, 1.0 / channels, 0.0).astype(BF16)
    block = over(iota((step * rows, LANES), 1), hidden)
    if masked:
        residues = mask_ref.shape[0]
        column = lax.axis_index("dap") * rows + over(iota((residues, width), 1), hidden)
        lanes_of = (iota((residues, width), 0) == column).astype(BF16)
        live = dot_tn(mask_ref[...].astype(BF16), lanes_of)
    for turn in range(steps):
        inputs, squares, mean = [], [], None
        for part in range(rep):
            first = part * quarter + turn * step
            x = x_ref[first : first + step].reshape(step * rows, channels)
            inputs.append(x)
            average = dot(x, share)
            mean = average if mean is None else jnp.where(block == part, average, mean)
            square = jnp.zeros_like(average)
            for half in range(channels // LANES):
                centered = x[:, half * LANES : (half + 1) * LANES].astype(F32) - average
                square = square + centered * centered
            squares.append(square.astype(BF16))
        y = dot(jnp.concatenate(inputs, axis=1), weight)
        scale = lax.rsqrt(dot(jnp.concatenate(squares, axis=1), own) + EPSILON)
        y_scr[turn] = (y - mean * sums) * scale
        for group in range(groups):
            taken = [
                y_scr[turn, pl.ds(group * rep + k, step, stride=rows), :] for k in range(rep)
            ]
            for part, z in enumerate(exchange(*taken)):
                first = part * quarter + turn * step
                here = slice(first, first + step)
                if masked:
                    z = z * live[here, group * LANES : (group + 1) * LANES]
                z_refs[group // each][group % each, here, :] = z.astype(BF16)


def factor(alignment, weight, hidden, parts, mask=None):
    seqs, rows, channels = alignment.shape
    steps = 2
    operands = (alignment, weight) if mask is None else (alignment, weight, mask)
    shape = jax.ShapeDtypeStruct((rows * hidden // LANES // parts, seqs, LANES), BF16)
    packed = seqs * rows * hidden // LANES
    return pl.pallas_call(
        functools.partial(factor_kernel, mask is not None, hidden),
        out_shape=(shape,) * parts,
        in_specs=[vmem()] * len(operands),
        out_specs=[vmem()] * parts,
        scratch_shapes=[pltpu.VMEM((steps, packed // steps, LANES), F32)],
        compiler_params=pltpu.CompilerParams(vmem_limit_bytes=24 << 20),
        cost_estimate=pl.CostEstimate(
            flops=2 * seqs * rows * channels * 512, bytes_accessed=seqs << 14, transcendentals=0
        ),
    )(*operands)


def prepare_kernel(
    zl_ref, mask_ref, pair_ref, live_ref, chain_ref, table_ref, proj_ref,
    zlt_ref, base_ref, inverse_ref, live_out_ref, proj_out_ref, seen_ref, pair_scr, table_scr, turn_scr,
):
    rows, cols, _ = pair_ref.shape
    pairs = rows * cols
    residues = mask_ref.shape[0]
    classes = table_ref.shape[0]
    row_start = lax.axis_index("dap") * rows
    col_start = lax.axis_index("sub") * cols
    groups = zl_ref.shape[0]
    hidden = groups * LANES // rows
    for group in range(groups):
        turned = zl_ref[group].astype(F32).T
        for half in range(zlt_ref.shape[0]):
            lanes = slice(half * LANES, (half + 1) * LANES)
            turn_scr[half, group * LANES : (group + 1) * LANES, :] = turned[:, lanes]
    for half in range(zlt_ref.shape[0]):
        for channel in range(hidden):
            here = slice(channel * rows, (channel + 1) * rows)
            picked = turn_scr[half, pl.ds(channel, rows, stride=hidden), :]
            zlt_ref[half, here, :] = picked.astype(BF16)
    proj_out_ref[...] = proj_ref[...].reshape(proj_out_ref.shape).astype(BF16)
    width = groups * LANES
    for block in range(cols // rows):
        column = col_start + block * rows + over(iota((residues, width), 1), hidden)
        spread = (iota((residues, width), 0) == column).astype(BF16)
        seen = dot_tn(mask_ref[...].astype(BF16), spread).astype(BF16)
        for group in range(groups):
            seen_ref[block * groups + group] = seen[:, group * LANES : (group + 1) * LANES]
    which = iota((pairs, residues), 0)
    place = iota((pairs, residues), 1)
    pick_row = (place == row_start + within(which, rows)).astype(BF16)
    pick_col = (place == col_start + over(which, rows)).astype(BF16)
    mask = mask_ref[...].astype(BF16)
    both = (dot(pick_row, mask) * dot(pick_col, mask)).astype(BF16)
    counts = dot(both, jnp.ones((mask.shape[1], LANES), BF16))
    inverse_ref[...] = 1.0 / jnp.maximum(counts, 1.0)
    live = jnp.broadcast_to(live_ref[...].astype(F32), (LANES, residues)).astype(BF16)
    chain = jnp.broadcast_to(chain_ref[...].astype(F32), (LANES, residues)).astype(BF16)
    live_out_ref[...] = dot_nt(pick_row, live) * dot_nt(pick_col, live)
    same = dot_nt(pick_row, chain) == dot_nt(pick_col, chain)
    pair = iota((pairs, LANES), 0)
    offset = (row_start + within(pair, rows)) - (col_start + over(pair, rows)) + REL_CLIP
    bucket = jnp.where(same, jnp.clip(offset, 0, 2 * REL_CLIP), 2 * REL_CLIP + 1)
    table_scr[...] = jnp.zeros_like(table_scr)
    table_scr[pl.ds(0, classes), :] = table_ref[...].astype(F32)
    onehot = (bucket == iota((pairs, LANES), 1)).astype(BF16)
    relative = dot(onehot, table_scr[...].astype(BF16))
    pair_scr[...] = pair_ref[...].reshape(pairs, LANES).astype(F32)
    for col in range(cols):
        here = slice(col * rows, (col + 1) * rows)
        base_ref[here, :] = relative[here] + pair_scr[pl.ds(col, rows, stride=cols), :]


def prepare(zl, mask, pair_input, residue_mask, chain_index, table, proj):
    rows, cols, channels = pair_input.shape
    pairs = rows * cols
    shape = jax.ShapeDtypeStruct((pairs, channels), F32)
    depth = proj.shape[0] * proj.shape[1]
    return pl.pallas_call(
        prepare_kernel,
        out_shape=(
            jax.ShapeDtypeStruct((zl.shape[1] // LANES, zl.shape[0] * LANES, LANES), BF16),
            shape,
            shape,
            shape,
            jax.ShapeDtypeStruct((depth, channels), BF16),
            jax.ShapeDtypeStruct((cols // rows * zl.shape[0], *zl.shape[1:]), BF16),
        ),
        in_specs=[vmem()] * 7,
        out_specs=[vmem()] * 6,
        scratch_shapes=[
            pltpu.VMEM((pairs, channels), F32),
            pltpu.VMEM((LANES, channels), F32),
            pltpu.VMEM((zl.shape[1] // LANES, zl.shape[0] * LANES, LANES), F32),
        ],
        compiler_params=pltpu.CompilerParams(vmem_limit_bytes=24 << 20),
        cost_estimate=pl.CostEstimate(
            flops=2 * pairs * 256 * 1024, bytes_accessed=2 << 20, transcendentals=0
        ),
    )(zl, mask, pair_input, residue_mask[None, :], chain_index[None, :], table, proj)


def pair_kernel(ratio, hidden, zlt_ref, *refs):
    zr_refs, refs = refs[: ratio * PARTS], refs[ratio * PARTS :]
    (seen_ref, base_ref, inverse_ref, live_ref, proj_ref, tl_ref, tr_ref,
     both_ref, left_ref, one_ref, flat_scr, one_scr) = refs
    pairs, channels = base_ref.shape
    rows = zlt_ref.shape[1] // hidden
    rep = LANES // hidden
    me = lax.axis_index("dap")
    left = jnp.concatenate([zlt_ref[part] for part in range(zlt_ref.shape[0])], axis=1)
    for step in range(ratio):
        block = lax.rem(me + step, ratio)
        right = []
        for group in range(rows // rep):
            each = rows // rep // PARTS
            factor = zr_refs[step * PARTS + group // each][group % each]
            right.append(factor * seen_ref[block * (rows // rep) + group])
        outer = dot(left, jnp.concatenate(right, axis=1))
        for group in range(rows // rep):
            lanes = slice(group * LANES, (group + 1) * LANES)
            for quad in range(hidden // rep):
                s0, s1, s2, s3 = (
                    outer[(quad * rep + k) * rows : (quad * rep + k + 1) * rows, lanes]
                    for k in range(rep)
                )
                found = exchange(s0, s1, s2, s3)
                for k in range(rep):
                    first = block * rows * rows + (group * rep + k) * rows
                    if ratio == 1:
                        first = (group * rep + k) * rows
                    else:
                        first = pl.multiple_of(first, rows)
                    flat_scr[quad, pl.ds(first, rows), :] = found[k].astype(BF16)
    flat = jnp.concatenate([flat_scr[quad] for quad in range(flat_scr.shape[0])], axis=1)
    outer_mean = dot(flat, proj_ref[...]) * inverse_ref[...]
    one = (base_ref[...] + outer_mean).astype(BF16).astype(F32)
    one_scr[...] = one
    norm = layer_norm(one).astype(BF16)
    for side, weight in enumerate((tl_ref, tr_ref)):
        both = dot(norm, weight[...])
        factor = jax.nn.sigmoid(both[:, :channels]) * both[:, channels:] * live_ref[...]
        both_ref[side] = factor.astype(BF16)
        if side == 0:
            left_ref[...] = factor.astype(BF16)
    cols = pairs // rows
    for row in range(rows):
        one_ref[row * cols : (row + 1) * cols, :] = one_scr[pl.ds(row, cols, stride=rows), :].astype(BF16)


def pair_update(hidden, zlt, zrs, seen, base, inverse, live, proj, triangle_left, triangle_right):
    pairs, channels = base.shape
    ratio = len(zrs) // PARTS
    shape = jax.ShapeDtypeStruct((pairs, channels), BF16)
    return pl.pallas_call(
        functools.partial(pair_kernel, ratio, hidden),
        out_shape=(jax.ShapeDtypeStruct((2, pairs, channels), BF16), shape, shape),
        in_specs=[vmem()] * (8 + len(zrs)),
        out_specs=[vmem()] * 3,
        scratch_shapes=[
            pltpu.VMEM((proj.shape[0] // LANES, pairs, LANES), BF16),
            pltpu.VMEM((pairs, channels), F32),
        ],
        compiler_params=pltpu.CompilerParams(vmem_limit_bytes=32 << 20),
        cost_estimate=pl.CostEstimate(
            flops=2 * pairs * 1024 * 512, bytes_accessed=2 << 20, transcendentals=pairs * 256
        ),
    )(zlt, *zrs, seen, base, inverse, live, proj, triangle_left, triangle_right)


def other(sub):
    return sub + 1 - 2 * (sub % 2)


SENDERS = ((0, 2, 3, 1), (2, 1, 0, 3), (0, 3, 2, 1), (2, 0, 1, 3))


def sender(a, b, subs, ratio):
    if (subs, ratio) == (4, 1):
        return SENDERS[b][a]
    return a // ratio


def sender_index(a, b, subs, ratio):
    if (subs, ratio) != (4, 1):
        return a // ratio
    found = 0
    for col, places in enumerate(SENDERS):
        for row, place in enumerate(places):
            found = jnp.where((a == row) & (b == col), place, found)
    return found


def add_terms(sums, start, lefts, rights, steps, ratio, cols, left_scr):
    subs = left_scr.shape[0]
    _, channels = sums.shape
    rows = left_scr.shape[1] // cols
    here, there = lax.axis_index("dap"), lax.axis_index("sub")
    first_sub = sender_index(here, there, subs, ratio)
    own, near, across, beyond = lefts
    left_scr[there] = own[0].astype(F32)
    left_scr[other(there)] = near[0].astype(F32)
    for step in range(1, subs // 2):
        sub = lax.rem(there + 2 * step, subs)
        left_scr[sub] = across[step - 1][...].astype(F32)
        left_scr[other(sub)] = beyond[step - 1][...].astype(F32)
    for turn in range(ratio):
        block = lax.rem(here + turn, ratio) if ratio > 1 else 0
        places = [i * cols + block * rows for i in range(rows)]
        if ratio > 1:
            places = [pl.multiple_of(place, rows) for place in places]
        if start is None:
            totals = tuple(jnp.zeros((rows, channels), F32) for _ in range(rows))
        else:
            totals = tuple(start[pl.ds(place, rows), :] for place in places)
        for index, step in enumerate(steps):
            sub = lax.rem(first_sub + 2 * step, subs)
            pair = rights[turn * len(steps) + index]
            for member, slot in enumerate((sub, other(sub))):

                def body(k, totals, slot=slot, member=member, pair=pair):
                    first = pl.multiple_of(k * rows, rows)
                    right = pair[member, pl.ds(first, rows), :].astype(F32)
                    return tuple(
                        totals[i] + left_scr[slot, pl.ds(first + i, 1), :] * right
                        for i in range(rows)
                    )

                totals = lax.fori_loop(0, cols, body, totals, unroll=4)
        for place, total in zip(places, totals):
            sums[pl.ds(place, rows), :] = total


def split_lefts(refs, twos):
    count = twos - 1
    lefts = (refs[0], refs[1], refs[2 : 2 + count], refs[2 + count : 2 + 2 * count])
    return lefts, refs[2 + 2 * count :]


def first_kernel(steps, twos, ratio, cols, *refs):
    lefts, refs = split_lefts(refs, twos)
    rights, refs = refs[: ratio * len(steps)], refs[ratio * len(steps) :]
    one_ref, weight_ref, sums_ref, gate_ref, left_scr = refs
    add_terms(sums_ref, None, lefts, rights, steps, ratio, cols, left_scr)
    norm = layer_norm(one_ref[...].astype(F32)).astype(BF16)
    gate_ref[...] = jax.nn.sigmoid(dot(norm, weight_ref[...]))


def last_kernel(steps, twos, ratio, cols, *refs):
    lefts, refs = split_lefts(refs, twos)
    rights, refs = refs[: ratio * len(steps)], refs[ratio * len(steps) :]
    (start_ref, one_ref, gate_ref, out_ref, up_ref, down_ref, result_ref, left_scr, sum_scr) = refs
    add_terms(sum_scr, start_ref, lefts, rights, steps, ratio, cols, left_scr)
    one = one_ref[...].astype(F32)
    hidden = layer_norm(sum_scr[...].astype(BF16).astype(F32)).astype(BF16)
    two = (one + gate_ref[...] * dot(hidden, out_ref[...])).astype(BF16).astype(F32)
    wide = jnp.maximum(dot(layer_norm(two).astype(BF16), up_ref[...]), 0.0).astype(BF16)
    result = (two + dot(wide, down_ref[...])).astype(BF16)
    result_ref[...] = result.reshape(result_ref.shape)


def triangle_update(lefts, rights, one, cols, gate_weight, out, up, down):
    pairs, channels = one.shape
    rows = pairs // cols
    twos = len(lefts) // 2
    subs = 2 * twos
    ratio = len(rights) // twos
    late, early = range(twos // 2), range(twos // 2, twos)
    limit = (12 << 20) if ratio == 1 else (50 << 20)
    left_scr = pltpu.VMEM((subs, pairs, channels), F32)
    shape = jax.ShapeDtypeStruct((pairs, channels), F32)

    def chosen(steps):
        return [rights[turn * twos + step] for turn in range(ratio) for step in steps]

    sums, gate = pl.pallas_call(
        functools.partial(first_kernel, early, twos, ratio, cols),
        out_shape=(shape, shape),
        in_specs=[vmem()] * (len(lefts) + ratio * len(early) + 2),
        out_specs=[vmem()] * 2,
        scratch_shapes=[left_scr],
        compiler_params=pltpu.CompilerParams(vmem_limit_bytes=limit),
        cost_estimate=pl.CostEstimate(
            flops=2 * pairs * channels * 1024, bytes_accessed=1 << 20, transcendentals=pairs * 128
        ),
    )(*lefts, *chosen(early), one, gate_weight)
    return pl.pallas_call(
        functools.partial(last_kernel, late, twos, ratio, cols),
        out_shape=jax.ShapeDtypeStruct((rows, cols, channels), BF16),
        in_specs=[vmem()] * (len(lefts) + ratio * len(late) + 6),
        out_specs=vmem(),
        scratch_shapes=[left_scr, pltpu.VMEM((pairs, channels), F32)],
        compiler_params=pltpu.CompilerParams(vmem_limit_bytes=limit),
        cost_estimate=pl.CostEstimate(
            flops=2 * pairs * channels * 2048, bytes_accessed=2 << 20, transcendentals=pairs * 128
        ),
    )(*lefts, *chosen(late), sums, one, gate, out, up, down)


def per_device(
    alignment,
    alignment_mask,
    pair_input,
    residue_mask,
    chain_index,
    outer_left,
    outer_right,
    outer_proj,
    triangle_left,
    triangle_right,
    triangle_gate,
    triangle_out,
    relative_table,
    transition_up,
    transition_down,
):
    daps, subs = lax.axis_size("dap"), lax.axis_size("sub")
    ratio = daps // subs
    cols = pair_input.shape[1]

    def fetch(values, source):
        perm = []
        for a in range(daps):
            for b in range(subs):
                dap, sub = source(a, b)
                perm.append((dap * subs + sub, a * subs + b))
        return lax.ppermute(values, ("dap", "sub"), perm)

    def owner(a, b, turn):
        return ratio * b + (a + turn) % ratio

    hidden = outer_left.shape[1]
    mask = alignment_mask.T
    zr = factor(alignment, repeat_weight(outer_right.T), hidden, PARTS)
    zrs = [
        fetch(
            zr[part],
            lambda a, b, t=turn, p=part: (
                owner(a, b, t), (sender(a, b, subs, ratio) + 2 * p) % subs
            ),
        )
        for turn in range(ratio)
        for part in range(PARTS)
    ]
    (zl,) = factor(alignment, repeat_weight(outer_left.T), hidden, 1, mask)
    zlt, base, inverse, live, proj, seen = prepare(
        zl, mask, pair_input, residue_mask, chain_index, relative_table, outer_proj
    )
    own, left, one = pair_update(
        hidden, zlt, zrs, seen, base, inverse, live, proj, triangle_left, triangle_right
    )
    near = fetch(own, lambda a, b: (a, other(b)))
    across = [
        fetch(left, lambda a, b, m=step: (a, (b + 2 * m) % subs)) for step in range(1, subs // 2)
    ]
    beyond = [fetch(block, lambda a, b: (a, other(b))) for block in across]
    right = jnp.stack([own[1], near[1]])
    rights = [
        fetch(
            right,
            lambda a, b, t=turn, m=step: (
                owner(a, b, t), (sender(a, b, subs, ratio) + 2 * m) % subs
            ),
        )
        for turn in range(ratio)
        for step in range(subs // 2)
    ]
    return triangle_update(
        [own, near, *across, *beyond],
        rights,
        one,
        cols,
        triangle_gate,
        triangle_out,
        transition_up,
        transition_down,
    )


def solution(mesh):
    in_specs = (
        P("parts", "dap", None),
        P("parts", None),
        P(("parts", "dap"), "sub", None),
        P("parts"),
        P("parts"),
        P(),
        P(),
        P(),
        P(),
        P(),
        P(),
        P(),
        P(),
        P(),
        P(),
    )
    out_specs = P(("parts", "dap"), "sub", None)
    return jax.shard_map(
        per_device, mesh=mesh, in_specs=in_specs, out_specs=out_specs, check_vma=False
    )
```

```python
import functools

import jax
import jax.numpy as jnp
from jax import lax
from jax.experimental import pallas as pl
from jax.experimental.pallas import tpu as pltpu
from jax.sharding import PartitionSpec as P

REL_CLIP = 32
LANES = 128
PARTS = 1
EPSILON = 1e-05
BF16 = jnp.bfloat16
F32 = jnp.float32
NT = (((1,), (1,)), ((), ()))
TN = (((0,), (0,)), ((), ()))


def layer_norm(values):
    average = jnp.mean(values, axis=-1, keepdims=True)
    centered = values - average
    spread = jnp.mean(centered * centered, axis=-1, keepdims=True)
    return centered * lax.rsqrt(spread + EPSILON)


def dot(left, right):
    return jnp.dot(left, right, preferred_element_type=F32)


def dot_nt(left, right):
    return lax.dot_general(left, right, NT, preferred_element_type=F32)


def dot_tn(left, right):
    return lax.dot_general(left, right, TN, preferred_element_type=F32)


def iota(shape, dim):
    return lax.broadcasted_iota(jnp.int32, shape, dim)


def vmem():
    return pl.BlockSpec(memory_space=pltpu.VMEM)


def over(index, size):
    return lax.shift_right_logical(index, size.bit_length() - 1)


def within(index, size):
    return lax.bitwise_and(index, size - 1)


def repeat_kernel(weight_ref, out_ref):
    rep = LANES // weight_ref.shape[0]
    out_ref[...] = jnp.concatenate([weight_ref[...]] * rep, axis=0).T


def repeat_weight(weight):
    return pl.pallas_call(
        repeat_kernel,
        out_shape=jax.ShapeDtypeStruct((weight.shape[1], LANES), BF16),
        in_specs=[vmem()],
        out_specs=vmem(),
        compiler_params=pltpu.CompilerParams(vmem_limit_bytes=2 << 20),
        cost_estimate=pl.CostEstimate(flops=1 << 30, bytes_accessed=1 << 17, transcendentals=0),
    )(weight)


def exchange(s0, s1, s2, s3):
    lane = iota(s0.shape, 1)
    block = LANES // 4
    odd = within(over(lane, block), 2) == 1
    upper = over(lane, 2 * block) == 1
    t0 = jnp.where(upper, pltpu.roll(s2, 2 * block, 1), s0)
    t1 = jnp.where(upper, pltpu.roll(s3, 2 * block, 1), s1)
    t2 = jnp.where(upper, s2, pltpu.roll(s0, 2 * block, 1))
    t3 = jnp.where(upper, s3, pltpu.roll(s1, 2 * block, 1))
    return (
        jnp.where(odd, pltpu.roll(t1, block, 1), t0),
        jnp.where(odd, t1, pltpu.roll(t0, 3 * block, 1)),
        jnp.where(odd, pltpu.roll(t3, block, 1), t2),
        jnp.where(odd, t3, pltpu.roll(t2, 3 * block, 1)),
    )


def factor_kernel(masked, hidden, x_ref, weight_ref, *refs):
    mask_ref = refs[0] if masked else None
    z_refs, y_scr = refs[masked:-1], refs[-1]
    each, seqs, _ = z_refs[0].shape
    groups = each * len(z_refs)
    _, rows, channels = x_ref.shape
    rep = rows // groups
    width = rows * hidden
    steps, step = y_scr.shape[0], y_scr.shape[1] // rows
    quarter = seqs // rep
    share = jnp.full((channels, LANES), 1.0 / channels, BF16)
    weight = jnp.concatenate([weight_ref[...], share], axis=1)
    sums = dot(jnp.ones((8, channels), BF16), weight_ref[...])[:1]
    side = (rep * LANES, LANES)
    own = over(iota(side, 0), LANES) == over(iota(side, 1), hidden)
    own = jnp.where(own, 1.0 / channels, 0.0).astype(BF16)
    block = over(iota((step * rows, LANES), 1), hidden)
    if masked:
        residues = mask_ref.shape[0]
        column = lax.axis_index("dap") * rows + over(iota((residues, width), 1), hidden)
        lanes_of = (iota((residues, width), 0) == column).astype(BF16)
        live = dot_tn(mask_ref[...].astype(BF16), lanes_of)
    for turn in range(steps):
        squares, y, mean = [], None, None
        for part in range(rep):
            first = part * quarter + turn * step
            x = x_ref[first : first + step].reshape(step * rows, channels)
            both = dot(x, weight)
            product, average = both[:, :LANES], both[:, LANES:]
            y = product if part == 0 else jnp.where(block == part, product, y)
            mean = average if part == 0 else jnp.where(block == part, average, mean)
            square = jnp.zeros_like(average)
            for half in range(channels // LANES):
                centered = x[:, half * LANES : (half + 1) * LANES].astype(F32) - average
                square = square + centered * centered
            squares.append(square.astype(BF16))
        scale = lax.rsqrt(dot(jnp.concatenate(squares, axis=1), own) + EPSILON)
        y_scr[turn] = (y - mean * sums) * scale
        for group in range(groups):
            taken = [
                y_scr[turn, pl.ds(group * rep + k, step, stride=rows), :] for k in range(rep)
            ]
            for part, z in enumerate(exchange(*taken)):
                first = part * quarter + turn * step
                here = slice(first, first + step)
                if masked:
                    z = z * live[here, group * LANES : (group + 1) * LANES]
                z_refs[group // each][group % each, here, :] = z.astype(BF16)


def factor(alignment, weight, hidden, parts, mask=None):
    seqs, rows, channels = alignment.shape
    steps = 2
    operands = (alignment, weight) if mask is None else (alignment, weight, mask)
    shape = jax.ShapeDtypeStruct((rows * hidden // LANES // parts, seqs, LANES), BF16)
    packed = seqs * rows * hidden // LANES
    return pl.pallas_call(
        functools.partial(factor_kernel, mask is not None, hidden),
        out_shape=(shape,) * parts,
        in_specs=[vmem()] * len(operands),
        out_specs=[vmem()] * parts,
        scratch_shapes=[pltpu.VMEM((steps, packed // steps, LANES), F32)],
        compiler_params=pltpu.CompilerParams(vmem_limit_bytes=24 << 20),
        cost_estimate=pl.CostEstimate(
            flops=2 * seqs * rows * channels * 512, bytes_accessed=seqs << 14, transcendentals=0
        ),
    )(*operands)


def prepare_kernel(
    zl_ref, mask_ref, pair_ref, live_ref, chain_ref, table_ref, proj_ref,
    zlt_ref, base_ref, inverse_ref, live_out_ref, proj_out_ref, seen_ref, pair_scr, table_scr, turn_scr,
):
    rows, cols, _ = pair_ref.shape
    pairs = rows * cols
    residues = mask_ref.shape[0]
    classes = table_ref.shape[0]
    row_start = lax.axis_index("dap") * rows
    col_start = lax.axis_index("sub") * cols
    groups = zl_ref.shape[0]
    hidden = groups * LANES // rows
    for group in range(groups):
        turned = zl_ref[group].astype(F32).T
        for half in range(zlt_ref.shape[0]):
            lanes = slice(half * LANES, (half + 1) * LANES)
            turn_scr[half, group * LANES : (group + 1) * LANES, :] = turned[:, lanes]
    for half in range(zlt_ref.shape[0]):
        for channel in range(hidden):
            here = slice(channel * rows, (channel + 1) * rows)
            picked = turn_scr[half, pl.ds(channel, rows, stride=hidden), :]
            zlt_ref[half, here, :] = picked.astype(BF16)
    proj_out_ref[...] = proj_ref[...].reshape(proj_out_ref.shape).astype(BF16)
    width = groups * LANES
    for block in range(cols // rows):
        column = col_start + block * rows + over(iota((residues, width), 1), hidden)
        spread = (iota((residues, width), 0) == column).astype(BF16)
        seen = dot_tn(mask_ref[...].astype(BF16), spread).astype(BF16)
        for group in range(groups):
            seen_ref[block * groups + group] = seen[:, group * LANES : (group + 1) * LANES]
    which = iota((pairs, residues), 0)
    place = iota((pairs, residues), 1)
    pick_row = (place == row_start + within(which, rows)).astype(BF16)
    pick_col = (place == col_start + over(which, rows)).astype(BF16)
    mask = mask_ref[...].astype(BF16)
    both = (dot(pick_row, mask) * dot(pick_col, mask)).astype(BF16)
    counts = dot(both, jnp.ones((mask.shape[1], LANES), BF16))
    inverse_ref[...] = 1.0 / jnp.maximum(counts, 1.0)
    live = jnp.broadcast_to(live_ref[...].astype(F32), (LANES, residues)).astype(BF16)
    chain = jnp.broadcast_to(chain_ref[...].astype(F32), (LANES, residues)).astype(BF16)
    live_out_ref[...] = dot_nt(pick_row, live) * dot_nt(pick_col, live)
    same = dot_nt(pick_row, chain) == dot_nt(pick_col, chain)
    pair = iota((pairs, LANES), 0)
    offset = (row_start + within(pair, rows)) - (col_start + over(pair, rows)) + REL_CLIP
    bucket = jnp.where(same, jnp.clip(offset, 0, 2 * REL_CLIP), 2 * REL_CLIP + 1)
    table_scr[...] = jnp.zeros_like(table_scr)
    table_scr[pl.ds(0, classes), :] = table_ref[...].astype(F32)
    onehot = (bucket == iota((pairs, LANES), 1)).astype(BF16)
    relative = dot(onehot, table_scr[...].astype(BF16))
    pair_scr[...] = pair_ref[...].reshape(pairs, LANES).astype(F32)
    for col in range(cols):
        here = slice(col * rows, (col + 1) * rows)
        base_ref[here, :] = relative[here] + pair_scr[pl.ds(col, rows, stride=cols), :]


def prepare(zl, mask, pair_input, residue_mask, chain_index, table, proj):
    rows, cols, channels = pair_input.shape
    pairs = rows * cols
    shape = jax.ShapeDtypeStruct((pairs, channels), F32)
    depth = proj.shape[0] * proj.shape[1]
    return pl.pallas_call(
        prepare_kernel,
        out_shape=(
            jax.ShapeDtypeStruct((zl.shape[1] // LANES, zl.shape[0] * LANES, LANES), BF16),
            shape,
            shape,
            shape,
            jax.ShapeDtypeStruct((depth, channels), BF16),
            jax.ShapeDtypeStruct((cols // rows * zl.shape[0], *zl.shape[1:]), BF16),
        ),
        in_specs=[vmem()] * 7,
        out_specs=[vmem()] * 6,
        scratch_shapes=[
            pltpu.VMEM((pairs, channels), F32),
            pltpu.VMEM((LANES, channels), F32),
            pltpu.VMEM((zl.shape[1] // LANES, zl.shape[0] * LANES, LANES), F32),
        ],
        compiler_params=pltpu.CompilerParams(vmem_limit_bytes=24 << 20),
        cost_estimate=pl.CostEstimate(
            flops=2 * pairs * 256 * 1024, bytes_accessed=2 << 20, transcendentals=0
        ),
    )(zl, mask, pair_input, residue_mask[None, :], chain_index[None, :], table, proj)


def pair_kernel(ratio, hidden, zlt_ref, *refs):
    zr_refs, refs = refs[: ratio * PARTS], refs[ratio * PARTS :]
    (seen_ref, base_ref, inverse_ref, live_ref, proj_ref, tl_ref, tr_ref,
     both_ref, left_ref, one_ref, flat_scr, one_scr) = refs
    pairs, channels = base_ref.shape
    rows = zlt_ref.shape[1] // hidden
    rep = LANES // hidden
    me = lax.axis_index("dap")
    left = jnp.concatenate([zlt_ref[part] for part in range(zlt_ref.shape[0])], axis=1)
    for step in range(ratio):
        block = lax.rem(me + step, ratio)
        right = []
        for group in range(rows // rep):
            each = rows // rep // PARTS
            factor = zr_refs[step * PARTS + group // each][group % each]
            right.append(factor * seen_ref[block * (rows // rep) + group])
        outer = dot(left, jnp.concatenate(right, axis=1))
        for group in range(rows // rep):
            lanes = slice(group * LANES, (group + 1) * LANES)
            for quad in range(hidden // rep):
                s0, s1, s2, s3 = (
                    outer[(quad * rep + k) * rows : (quad * rep + k + 1) * rows, lanes]
                    for k in range(rep)
                )
                found = exchange(s0, s1, s2, s3)
                for k in range(rep):
                    first = block * rows * rows + (group * rep + k) * rows
                    if ratio == 1:
                        first = (group * rep + k) * rows
                    else:
                        first = pl.multiple_of(first, rows)
                    flat_scr[quad, pl.ds(first, rows), :] = found[k].astype(BF16)
    flat = jnp.concatenate([flat_scr[quad] for quad in range(flat_scr.shape[0])], axis=1)
    outer_mean = dot(flat, proj_ref[...]) * inverse_ref[...]
    one = (base_ref[...] + outer_mean).astype(BF16).astype(F32)
    one_scr[...] = one
    norm = layer_norm(one).astype(BF16)
    for side, weight in enumerate((tl_ref, tr_ref)):
        both = dot(norm, weight[...])
        factor = jax.nn.sigmoid(both[:, :channels]) * both[:, channels:] * live_ref[...]
        both_ref[side] = factor.astype(BF16)
        if side == 0:
            left_ref[...] = factor.astype(BF16)
    cols = pairs // rows
    for row in range(rows):
        one_ref[row * cols : (row + 1) * cols, :] = one_scr[pl.ds(row, cols, stride=rows), :].astype(BF16)


def pair_update(hidden, zlt, zrs, seen, base, inverse, live, proj, triangle_left, triangle_right):
    pairs, channels = base.shape
    ratio = len(zrs) // PARTS
    shape = jax.ShapeDtypeStruct((pairs, channels), BF16)
    return pl.pallas_call(
        functools.partial(pair_kernel, ratio, hidden),
        out_shape=(jax.ShapeDtypeStruct((2, pairs, channels), BF16), shape, shape),
        in_specs=[vmem()] * (8 + len(zrs)),
        out_specs=[vmem()] * 3,
        scratch_shapes=[
            pltpu.VMEM((proj.shape[0] // LANES, pairs, LANES), BF16),
            pltpu.VMEM((pairs, channels), F32),
        ],
        compiler_params=pltpu.CompilerParams(vmem_limit_bytes=32 << 20),
        cost_estimate=pl.CostEstimate(
            flops=2 * pairs * 1024 * 512, bytes_accessed=2 << 20, transcendentals=pairs * 256
        ),
    )(zlt, *zrs, seen, base, inverse, live, proj, triangle_left, triangle_right)


def other(sub):
    return sub + 1 - 2 * (sub % 2)


SENDERS = ((0, 2, 3, 1), (2, 1, 0, 3), (0, 3, 2, 1), (2, 0, 1, 3))


def sender(a, b, subs, ratio):
    if (subs, ratio) == (4, 1):
        return SENDERS[b][a]
    return a // ratio


def sender_index(a, b, subs, ratio):
    if (subs, ratio) != (4, 1):
        return a // ratio
    found = 0
    for col, places in enumerate(SENDERS):
        for row, place in enumerate(places):
            found = jnp.where((a == row) & (b == col), place, found)
    return found


def add_terms(sums, start, lefts, rights, steps, ratio, cols, left_scr):
    subs = left_scr.shape[0]
    _, channels = sums.shape
    rows = left_scr.shape[1] // cols
    here, there = lax.axis_index("dap"), lax.axis_index("sub")
    first_sub = sender_index(here, there, subs, ratio)
    own, near, across, beyond = lefts
    left_scr[there] = own[0].astype(F32)
    left_scr[other(there)] = near[0].astype(F32)
    for step in range(1, subs // 2):
        sub = lax.rem(there + 2 * step, subs)
        left_scr[sub] = across[step - 1][...].astype(F32)
        left_scr[other(sub)] = beyond[step - 1][...].astype(F32)
    for turn in range(ratio):
        block = lax.rem(here + turn, ratio) if ratio > 1 else 0
        places = [i * cols + block * rows for i in range(rows)]
        if ratio > 1:
            places = [pl.multiple_of(place, rows) for place in places]
        if start is None:
            totals = tuple(jnp.zeros((rows, channels), F32) for _ in range(rows))
        else:
            totals = tuple(start[pl.ds(place, rows), :] for place in places)
        for index, step in enumerate(steps):
            sub = lax.rem(first_sub + 2 * step, subs)
            pair = rights[turn * len(steps) + index]
            for member, slot in enumerate((sub, other(sub))):

                def body(k, totals, slot=slot, member=member, pair=pair):
                    first = pl.multiple_of(k * rows, rows)
                    right = pair[member, pl.ds(first, rows), :].astype(F32)
                    return tuple(
                        totals[i] + left_scr[slot, pl.ds(first + i, 1), :] * right
                        for i in range(rows)
                    )

                totals = lax.fori_loop(0, cols, body, totals, unroll=4)
        for place, total in zip(places, totals):
            sums[pl.ds(place, rows), :] = total


def split_lefts(refs, twos):
    count = twos - 1
    lefts = (refs[0], refs[1], refs[2 : 2 + count], refs[2 + count : 2 + 2 * count])
    return lefts, refs[2 + 2 * count :]


def first_kernel(steps, twos, ratio, cols, *refs):
    lefts, refs = split_lefts(refs, twos)
    rights, refs = refs[: ratio * len(steps)], refs[ratio * len(steps) :]
    one_ref, weight_ref, sums_ref, gate_ref, left_scr = refs
    add_terms(sums_ref, None, lefts, rights, steps, ratio, cols, left_scr)
    norm = layer_norm(one_ref[...].astype(F32)).astype(BF16)
    gate_ref[...] = jax.nn.sigmoid(dot(norm, weight_ref[...]))


def last_kernel(steps, twos, ratio, cols, *refs):
    lefts, refs = split_lefts(refs, twos)
    rights, refs = refs[: ratio * len(steps)], refs[ratio * len(steps) :]
    (start_ref, one_ref, gate_ref, out_ref, up_ref, down_ref, result_ref, left_scr, sum_scr) = refs
    add_terms(sum_scr, start_ref, lefts, rights, steps, ratio, cols, left_scr)
    one = one_ref[...].astype(F32)
    hidden = layer_norm(sum_scr[...].astype(BF16).astype(F32)).astype(BF16)
    two = (one + gate_ref[...] * dot(hidden, out_ref[...])).astype(BF16).astype(F32)
    wide = jnp.maximum(dot(layer_norm(two).astype(BF16), up_ref[...]), 0.0).astype(BF16)
    result = (two + dot(wide, down_ref[...])).astype(BF16)
    result_ref[...] = result.reshape(result_ref.shape)


def triangle_update(lefts, rights, one, cols, gate_weight, out, up, down):
    pairs, channels = one.shape
    rows = pairs // cols
    twos = len(lefts) // 2
    subs = 2 * twos
    ratio = len(rights) // twos
    late, early = range(twos // 2), range(twos // 2, twos)
    limit = (12 << 20) if ratio == 1 else (50 << 20)
    left_scr = pltpu.VMEM((subs, pairs, channels), F32)
    shape = jax.ShapeDtypeStruct((pairs, channels), F32)

    def chosen(steps):
        return [rights[turn * twos + step] for turn in range(ratio) for step in steps]

    sums, gate = pl.pallas_call(
        functools.partial(first_kernel, early, twos, ratio, cols),
        out_shape=(shape, shape),
        in_specs=[vmem()] * (len(lefts) + ratio * len(early) + 2),
        out_specs=[vmem()] * 2,
        scratch_shapes=[left_scr],
        compiler_params=pltpu.CompilerParams(vmem_limit_bytes=limit),
        cost_estimate=pl.CostEstimate(
            flops=2 * pairs * channels * 1024, bytes_accessed=1 << 20, transcendentals=pairs * 128
        ),
    )(*lefts, *chosen(early), one, gate_weight)
    return pl.pallas_call(
        functools.partial(last_kernel, late, twos, ratio, cols),
        out_shape=jax.ShapeDtypeStruct((rows, cols, channels), BF16),
        in_specs=[vmem()] * (len(lefts) + ratio * len(late) + 6),
        out_specs=vmem(),
        scratch_shapes=[left_scr, pltpu.VMEM((pairs, channels), F32)],
        compiler_params=pltpu.CompilerParams(vmem_limit_bytes=limit),
        cost_estimate=pl.CostEstimate(
            flops=2 * pairs * channels * 2048, bytes_accessed=2 << 20, transcendentals=pairs * 128
        ),
    )(*lefts, *chosen(late), sums, one, gate, out, up, down)


def per_device(
    alignment,
    alignment_mask,
    pair_input,
    residue_mask,
    chain_index,
    outer_left,
    outer_right,
    outer_proj,
    triangle_left,
    triangle_right,
    triangle_gate,
    triangle_out,
    relative_table,
    transition_up,
    transition_down,
):
    daps, subs = lax.axis_size("dap"), lax.axis_size("sub")
    ratio = daps // subs
    cols = pair_input.shape[1]

    def fetch(values, source):
        perm = []
        for a in range(daps):
            for b in range(subs):
                dap, sub = source(a, b)
                perm.append((dap * subs + sub, a * subs + b))
        return lax.ppermute(values, ("dap", "sub"), perm)

    def owner(a, b, turn):
        return ratio * b + (a + turn) % ratio

    hidden = outer_left.shape[1]
    mask = alignment_mask.T
    zr = factor(alignment, repeat_weight(outer_right.T), hidden, PARTS)
    zrs = [
        fetch(
            zr[part],
            lambda a, b, t=turn, p=part: (
                owner(a, b, t), (sender(a, b, subs, ratio) + 2 * p) % subs
            ),
        )
        for turn in range(ratio)
        for part in range(PARTS)
    ]
    (zl,) = factor(alignment, repeat_weight(outer_left.T), hidden, 1, mask)
    zlt, base, inverse, live, proj, seen = prepare(
        zl, mask, pair_input, residue_mask, chain_index, relative_table, outer_proj
    )
    own, left, one = pair_update(
        hidden, zlt, zrs, seen, base, inverse, live, proj, triangle_left, triangle_right
    )
    near = fetch(own, lambda a, b: (a, other(b)))
    across = [
        fetch(left, lambda a, b, m=step: (a, (b + 2 * m) % subs)) for step in range(1, subs // 2)
    ]
    beyond = [fetch(block, lambda a, b: (a, other(b))) for block in across]
    right = jnp.stack([own[1], near[1]])
    rights = [
        fetch(
            right,
            lambda a, b, t=turn, m=step: (
                owner(a, b, t), (sender(a, b, subs, ratio) + 2 * m) % subs
            ),
        )
        for turn in range(ratio)
        for step in range(subs // 2)
    ]
    return triangle_update(
        [own, near, *across, *beyond],
        rights,
        one,
        cols,
        triangle_gate,
        triangle_out,
        transition_up,
        transition_down,
    )


def solution(mesh):
    in_specs = (
        P("parts", "dap", None),
        P("parts", None),
        P(("parts", "dap"), "sub", None),
        P("parts"),
        P("parts"),
        P(),
        P(),
        P(),
        P(),
        P(),
        P(),
        P(),
        P(),
        P(),
        P(),
    )
    out_specs = P(("parts", "dap"), "sub", None)
    return jax.shard_map(
        per_device, mesh=mesh, in_specs=in_specs, out_specs=out_specs, check_vma=False
    )
```

```python
import functools

import jax
import jax.numpy as jnp
from jax import lax
from jax.experimental import pallas as pl
from jax.experimental.pallas import tpu as pltpu
from jax.sharding import PartitionSpec as P

REL_CLIP = 32
LANES = 128
PARTS = 1
EPSILON = 1e-05
BF16 = jnp.bfloat16
F32 = jnp.float32
NT = (((1,), (1,)), ((), ()))
TN = (((0,), (0,)), ((), ()))


def layer_norm(values):
    average = jnp.mean(values, axis=-1, keepdims=True)
    centered = values - average
    spread = jnp.mean(centered * centered, axis=-1, keepdims=True)
    return centered * lax.rsqrt(spread + EPSILON)


def dot(left, right):
    return jnp.dot(left, right, preferred_element_type=F32)


def dot_nt(left, right):
    return lax.dot_general(left, right, NT, preferred_element_type=F32)


def dot_tn(left, right):
    return lax.dot_general(left, right, TN, preferred_element_type=F32)


def iota(shape, dim):
    return lax.broadcasted_iota(jnp.int32, shape, dim)


def vmem():
    return pl.BlockSpec(memory_space=pltpu.VMEM)


def over(index, size):
    return lax.shift_right_logical(index, size.bit_length() - 1)


def within(index, size):
    return lax.bitwise_and(index, size - 1)


def repeat_kernel(weight_ref, out_ref):
    rep = LANES // weight_ref.shape[0]
    out_ref[...] = jnp.concatenate([weight_ref[...]] * rep, axis=0).T


def repeat_weight(weight):
    return pl.pallas_call(
        repeat_kernel,
        out_shape=jax.ShapeDtypeStruct((weight.shape[1], LANES), BF16),
        in_specs=[vmem()],
        out_specs=vmem(),
        compiler_params=pltpu.CompilerParams(vmem_limit_bytes=2 << 20),
        cost_estimate=pl.CostEstimate(flops=1 << 30, bytes_accessed=1 << 17, transcendentals=0),
    )(weight)


def exchange(s0, s1, s2, s3):
    lane = iota(s0.shape, 1)
    block = LANES // 4
    odd = within(over(lane, block), 2) == 1
    upper = over(lane, 2 * block) == 1
    t0 = jnp.where(upper, pltpu.roll(s2, 2 * block, 1), s0)
    t1 = jnp.where(upper, pltpu.roll(s3, 2 * block, 1), s1)
    t2 = jnp.where(upper, s2, pltpu.roll(s0, 2 * block, 1))
    t3 = jnp.where(upper, s3, pltpu.roll(s1, 2 * block, 1))
    return (
        jnp.where(odd, pltpu.roll(t1, block, 1), t0),
        jnp.where(odd, t1, pltpu.roll(t0, 3 * block, 1)),
        jnp.where(odd, pltpu.roll(t3, block, 1), t2),
        jnp.where(odd, t3, pltpu.roll(t2, 3 * block, 1)),
    )


def factor_kernel(masked, hidden, x_ref, weight_ref, *refs):
    mask_ref = refs[0] if masked else None
    z_refs, y_scr = refs[masked:-1], refs[-1]
    each, seqs, _ = z_refs[0].shape
    groups = each * len(z_refs)
    _, rows, channels = x_ref.shape
    rep = rows // groups
    width = rows * hidden
    steps, step = y_scr.shape[0], y_scr.shape[1] // rows
    quarter = seqs // rep
    share = jnp.full((channels, LANES), 1.0 / channels, BF16)
    weight = jnp.concatenate([weight_ref[...], share], axis=1)
    sums = dot(jnp.ones((8, channels), BF16), weight_ref[...])[:1]
    side = (rep * LANES, LANES)
    own = over(iota(side, 0), LANES) == over(iota(side, 1), hidden)
    own = jnp.where(own, 1.0 / channels, 0.0).astype(BF16)
    block = over(iota((step * rows, LANES), 1), hidden)
    if masked:
        residues = mask_ref.shape[0]
        column = lax.axis_index("dap") * rows + over(iota((residues, width), 1), hidden)
        lanes_of = (iota((residues, width), 0) == column).astype(BF16)
        live = dot_tn(mask_ref[...].astype(BF16), lanes_of)
    for turn in range(steps):
        squares, y, mean = [], None, None
        for part in range(rep):
            first = part * quarter + turn * step
            x = x_ref[first : first + step].reshape(step * rows, channels)
            both = dot(x, weight)
            product, average = both[:, :LANES], both[:, LANES:]
            y = product if part == 0 else jnp.where(block == part, product, y)
            mean = average if part == 0 else jnp.where(block == part, average, mean)
            square = jnp.zeros_like(average)
            for half in range(channels // LANES):
                centered = x[:, half * LANES : (half + 1) * LANES].astype(F32) - average
                square = square + centered * centered
            squares.append(square.astype(BF16))
        scale = lax.rsqrt(dot(jnp.concatenate(squares, axis=1), own) + EPSILON)
        y_scr[turn] = (y - mean * sums) * scale
        for group in range(groups):
            taken = [
                y_scr[turn, pl.ds(group * rep + k, step, stride=rows), :] for k in range(rep)
            ]
            for part, z in enumerate(exchange(*taken)):
                first = part * quarter + turn * step
                here = slice(first, first + step)
                if masked:
                    z = z * live[here, group * LANES : (group + 1) * LANES]
                z_refs[group // each][group % each, here, :] = z.astype(BF16)


def factor(alignment, weight, hidden, parts, mask=None):
    seqs, rows, channels = alignment.shape
    steps = 2
    operands = (alignment, weight) if mask is None else (alignment, weight, mask)
    shape = jax.ShapeDtypeStruct((rows * hidden // LANES // parts, seqs, LANES), BF16)
    packed = seqs * rows * hidden // LANES
    return pl.pallas_call(
        functools.partial(factor_kernel, mask is not None, hidden),
        out_shape=(shape,) * parts,
        in_specs=[vmem()] * len(operands),
        out_specs=[vmem()] * parts,
        scratch_shapes=[pltpu.VMEM((steps, packed // steps, LANES), F32)],
        compiler_params=pltpu.CompilerParams(vmem_limit_bytes=24 << 20),
        cost_estimate=pl.CostEstimate(
            flops=2 * seqs * rows * channels * 512, bytes_accessed=seqs << 14, transcendentals=0
        ),
    )(*operands)


def prepare_kernel(
    zl_ref, mask_ref, pair_ref, live_ref, chain_ref, table_ref, proj_ref,
    zlt_ref, base_ref, inverse_ref, live_out_ref, proj_out_ref, seen_ref, pair_scr, table_scr, turn_scr,
):
    rows, cols, _ = pair_ref.shape
    pairs = rows * cols
    residues = mask_ref.shape[0]
    classes = table_ref.shape[0]
    row_start = lax.axis_index("dap") * rows
    col_start = lax.axis_index("sub") * cols
    groups = zl_ref.shape[0]
    hidden = groups * LANES // rows
    for group in range(groups):
        turned = zl_ref[group].astype(F32).T
        for half in range(zlt_ref.shape[0]):
            lanes = slice(half * LANES, (half + 1) * LANES)
            turn_scr[half, group * LANES : (group + 1) * LANES, :] = turned[:, lanes]
    for half in range(zlt_ref.shape[0]):
        for channel in range(hidden):
            here = slice(channel * rows, (channel + 1) * rows)
            picked = turn_scr[half, pl.ds(channel, rows, stride=hidden), :]
            zlt_ref[half, here, :] = picked.astype(BF16)
    proj_out_ref[...] = proj_ref[...].reshape(proj_out_ref.shape).astype(BF16)
    width = groups * LANES
    for block in range(cols // rows):
        column = col_start + block * rows + over(iota((residues, width), 1), hidden)
        spread = (iota((residues, width), 0) == column).astype(BF16)
        seen = dot_tn(mask_ref[...].astype(BF16), spread).astype(BF16)
        for group in range(groups):
            seen_ref[block * groups + group] = seen[:, group * LANES : (group + 1) * LANES]
    which = iota((pairs, residues), 0)
    place = iota((pairs, residues), 1)
    pick_row = (place == row_start + within(which, rows)).astype(BF16)
    pick_col = (place == col_start + over(which, rows)).astype(BF16)
    mask = mask_ref[...].astype(BF16)
    both = (dot(pick_row, mask) * dot(pick_col, mask)).astype(BF16)
    counts = dot(both, jnp.ones((mask.shape[1], LANES), BF16))
    inverse_ref[...] = 1.0 / jnp.maximum(counts, 1.0)
    live = jnp.broadcast_to(live_ref[...].astype(F32), (LANES, residues)).astype(BF16)
    chain = jnp.broadcast_to(chain_ref[...].astype(F32), (LANES, residues)).astype(BF16)
    live_out_ref[...] = dot_nt(pick_row, live) * dot_nt(pick_col, live)
    same = dot_nt(pick_row, chain) == dot_nt(pick_col, chain)
    pair = iota((pairs, LANES), 0)
    offset = (row_start + within(pair, rows)) - (col_start + over(pair, rows)) + REL_CLIP
    bucket = jnp.where(same, jnp.clip(offset, 0, 2 * REL_CLIP), 2 * REL_CLIP + 1)
    table_scr[...] = jnp.zeros_like(table_scr)
    table_scr[pl.ds(0, classes), :] = table_ref[...].astype(F32)
    onehot = (bucket == iota((pairs, LANES), 1)).astype(BF16)
    relative = dot(onehot, table_scr[...].astype(BF16))
    pair_scr[...] = pair_ref[...].reshape(pairs, LANES).astype(F32)
    for col in range(cols):
        here = slice(col * rows, (col + 1) * rows)
        base_ref[here, :] = relative[here] + pair_scr[pl.ds(col, rows, stride=cols), :]


def prepare(zl, mask, pair_input, residue_mask, chain_index, table, proj):
    rows, cols, channels = pair_input.shape
    pairs = rows * cols
    shape = jax.ShapeDtypeStruct((pairs, channels), F32)
    depth = proj.shape[0] * proj.shape[1]
    return pl.pallas_call(
        prepare_kernel,
        out_shape=(
            jax.ShapeDtypeStruct((zl.shape[1] // LANES, zl.shape[0] * LANES, LANES), BF16),
            shape,
            shape,
            shape,
            jax.ShapeDtypeStruct((depth, channels), BF16),
            jax.ShapeDtypeStruct((cols // rows * zl.shape[0], *zl.shape[1:]), BF16),
        ),
        in_specs=[vmem()] * 7,
        out_specs=[vmem()] * 6,
        scratch_shapes=[
            pltpu.VMEM((pairs, channels), F32),
            pltpu.VMEM((LANES, channels), F32),
            pltpu.VMEM((zl.shape[1] // LANES, zl.shape[0] * LANES, LANES), F32),
        ],
        compiler_params=pltpu.CompilerParams(vmem_limit_bytes=24 << 20),
        cost_estimate=pl.CostEstimate(
            flops=2 * pairs * 256 * 1024, bytes_accessed=2 << 20, transcendentals=0
        ),
    )(zl, mask, pair_input, residue_mask[None, :], chain_index[None, :], table, proj)


def pair_kernel(ratio, hidden, zlt_ref, *refs):
    zr_refs, refs = refs[: ratio * PARTS], refs[ratio * PARTS :]
    (seen_ref, base_ref, inverse_ref, live_ref, proj_ref, tl_ref, tr_ref,
     both_ref, left_ref, one_ref, flat_scr, one_scr) = refs
    pairs, channels = base_ref.shape
    rows = zlt_ref.shape[1] // hidden
    rep = LANES // hidden
    me = lax.axis_index("dap")
    left = jnp.concatenate([zlt_ref[part] for part in range(zlt_ref.shape[0])], axis=1)
    for step in range(ratio):
        block = lax.rem(me + step, ratio)
        right = []
        for group in range(rows // rep):
            each = rows // rep // PARTS
            factor = zr_refs[step * PARTS + group // each][group % each]
            right.append(factor * seen_ref[block * (rows // rep) + group])
        outer = dot(left, jnp.concatenate(right, axis=1))
        for group in range(rows // rep):
            lanes = slice(group * LANES, (group + 1) * LANES)
            for quad in range(hidden // rep):
                s0, s1, s2, s3 = (
                    outer[(quad * rep + k) * rows : (quad * rep + k + 1) * rows, lanes]
                    for k in range(rep)
                )
                found = exchange(s0, s1, s2, s3)
                for k in range(rep):
                    first = block * rows * rows + (group * rep + k) * rows
                    if ratio == 1:
                        first = (group * rep + k) * rows
                    else:
                        first = pl.multiple_of(first, rows)
                    flat_scr[quad, pl.ds(first, rows), :] = found[k].astype(BF16)
    flat = jnp.concatenate([flat_scr[quad] for quad in range(flat_scr.shape[0])], axis=1)
    outer_mean = dot(flat, proj_ref[...]) * inverse_ref[...]
    one = (base_ref[...] + outer_mean).astype(BF16).astype(F32)
    one_scr[...] = one
    norm = layer_norm(one).astype(BF16)
    for side, weight in enumerate((tl_ref, tr_ref)):
        both = dot(norm, weight[...])
        factor = jax.nn.sigmoid(both[:, :channels]) * both[:, channels:] * live_ref[...]
        both_ref[side] = factor.astype(BF16)
        if side == 0:
            left_ref[...] = factor.astype(BF16)
    cols = pairs // rows
    for row in range(rows):
        one_ref[row * cols : (row + 1) * cols, :] = one_scr[pl.ds(row, cols, stride=rows), :].astype(BF16)


def pair_update(hidden, zlt, zrs, seen, base, inverse, live, proj, triangle_left, triangle_right):
    pairs, channels = base.shape
    ratio = len(zrs) // PARTS
    shape = jax.ShapeDtypeStruct((pairs, channels), BF16)
    return pl.pallas_call(
        functools.partial(pair_kernel, ratio, hidden),
        out_shape=(jax.ShapeDtypeStruct((2, pairs, channels), BF16), shape, shape),
        in_specs=[vmem()] * (8 + len(zrs)),
        out_specs=[vmem()] * 3,
        scratch_shapes=[
            pltpu.VMEM((proj.shape[0] // LANES, pairs, LANES), BF16),
            pltpu.VMEM((pairs, channels), F32),
        ],
        compiler_params=pltpu.CompilerParams(vmem_limit_bytes=32 << 20),
        cost_estimate=pl.CostEstimate(
            flops=2 * pairs * 1024 * 512, bytes_accessed=2 << 20, transcendentals=pairs * 256
        ),
    )(zlt, *zrs, seen, base, inverse, live, proj, triangle_left, triangle_right)


def other(sub):
    return sub + 1 - 2 * (sub % 2)


SENDERS = ((3, 0, 2, 1), (0, 3, 2, 1), (2, 0, 1, 3), (2, 0, 3, 1))


def sender(a, b, subs, ratio):
    if (subs, ratio) == (4, 1):
        return SENDERS[b][a]
    return a // ratio


def sender_index(a, b, subs, ratio):
    if (subs, ratio) != (4, 1):
        return a // ratio
    found = 0
    for col, places in enumerate(SENDERS):
        for row, place in enumerate(places):
            found = jnp.where((a == row) & (b == col), place, found)
    return found


def add_terms(sums, start, lefts, rights, steps, ratio, cols, left_scr):
    subs = left_scr.shape[0]
    _, channels = sums.shape
    rows = left_scr.shape[1] // cols
    here, there = lax.axis_index("dap"), lax.axis_index("sub")
    first_sub = sender_index(here, there, subs, ratio)
    own, near, across, beyond = lefts
    left_scr[there] = own[0].astype(F32)
    left_scr[other(there)] = near[0].astype(F32)
    for step in range(1, subs // 2):
        sub = lax.rem(there + 2 * step, subs)
        left_scr[sub] = across[step - 1][...].astype(F32)
        left_scr[other(sub)] = beyond[step - 1][...].astype(F32)
    for turn in range(ratio):
        block = lax.rem(here + turn, ratio) if ratio > 1 else 0
        places = [i * cols + block * rows for i in range(rows)]
        if ratio > 1:
            places = [pl.multiple_of(place, rows) for place in places]
        if start is None:
            totals = tuple(jnp.zeros((rows, channels), F32) for _ in range(rows))
        else:
            totals = tuple(start[pl.ds(place, rows), :] for place in places)
        for index, step in enumerate(steps):
            sub = lax.rem(first_sub + 2 * step, subs)
            pair = rights[turn * len(steps) + index]
            for member, slot in enumerate((sub, other(sub))):

                def body(k, totals, slot=slot, member=member, pair=pair):
                    first = pl.multiple_of(k * rows, rows)
                    right = pair[member, pl.ds(first, rows), :].astype(F32)
                    return tuple(
                        totals[i] + left_scr[slot, pl.ds(first + i, 1), :] * right
                        for i in range(rows)
                    )

                totals = lax.fori_loop(0, cols, body, totals, unroll=4)
        for place, total in zip(places, totals):
            sums[pl.ds(place, rows), :] = total


def split_lefts(refs, twos):
    count = twos - 1
    lefts = (refs[0], refs[1], refs[2 : 2 + count], refs[2 + count : 2 + 2 * count])
    return lefts, refs[2 + 2 * count :]


def first_kernel(steps, twos, ratio, cols, *refs):
    lefts, refs = split_lefts(refs, twos)
    rights, refs = refs[: ratio * len(steps)], refs[ratio * len(steps) :]
    one_ref, weight_ref, sums_ref, gate_ref, left_scr = refs
    add_terms(sums_ref, None, lefts, rights, steps, ratio, cols, left_scr)
    norm = layer_norm(one_ref[...].astype(F32)).astype(BF16)
    gate_ref[...] = jax.nn.sigmoid(dot(norm, weight_ref[...]))


def last_kernel(steps, twos, ratio, cols, *refs):
    lefts, refs = split_lefts(refs, twos)
    rights, refs = refs[: ratio * len(steps)], refs[ratio * len(steps) :]
    (start_ref, one_ref, gate_ref, out_ref, up_ref, down_ref, result_ref, left_scr, sum_scr) = refs
    add_terms(sum_scr, start_ref, lefts, rights, steps, ratio, cols, left_scr)
    one = one_ref[...].astype(F32)
    hidden = layer_norm(sum_scr[...].astype(BF16).astype(F32)).astype(BF16)
    two = (one + gate_ref[...] * dot(hidden, out_ref[...])).astype(BF16).astype(F32)
    wide = jnp.maximum(dot(layer_norm(two).astype(BF16), up_ref[...]), 0.0).astype(BF16)
    result = (two + dot(wide, down_ref[...])).astype(BF16)
    result_ref[...] = result.reshape(result_ref.shape)


def triangle_update(lefts, rights, one, cols, gate_weight, out, up, down):
    pairs, channels = one.shape
    rows = pairs // cols
    twos = len(lefts) // 2
    subs = 2 * twos
    ratio = len(rights) // twos
    late, early = range(twos // 2), range(twos // 2, twos)
    limit = (12 << 20) if ratio == 1 else (50 << 20)
    left_scr = pltpu.VMEM((subs, pairs, channels), F32)
    shape = jax.ShapeDtypeStruct((pairs, channels), F32)

    def chosen(steps):
        return [rights[turn * twos + step] for turn in range(ratio) for step in steps]

    sums, gate = pl.pallas_call(
        functools.partial(first_kernel, early, twos, ratio, cols),
        out_shape=(shape, shape),
        in_specs=[vmem()] * (len(lefts) + ratio * len(early) + 2),
        out_specs=[vmem()] * 2,
        scratch_shapes=[left_scr],
        compiler_params=pltpu.CompilerParams(vmem_limit_bytes=limit),
        cost_estimate=pl.CostEstimate(
            flops=2 * pairs * channels * 1024, bytes_accessed=1 << 20, transcendentals=pairs * 128
        ),
    )(*lefts, *chosen(early), one, gate_weight)
    return pl.pallas_call(
        functools.partial(last_kernel, late, twos, ratio, cols),
        out_shape=jax.ShapeDtypeStruct((rows, cols, channels), BF16),
        in_specs=[vmem()] * (len(lefts) + ratio * len(late) + 6),
        out_specs=vmem(),
        scratch_shapes=[left_scr, pltpu.VMEM((pairs, channels), F32)],
        compiler_params=pltpu.CompilerParams(vmem_limit_bytes=limit),
        cost_estimate=pl.CostEstimate(
            flops=2 * pairs * channels * 2048, bytes_accessed=2 << 20, transcendentals=pairs * 128
        ),
    )(*lefts, *chosen(late), sums, one, gate, out, up, down)


def per_device(
    alignment,
    alignment_mask,
    pair_input,
    residue_mask,
    chain_index,
    outer_left,
    outer_right,
    outer_proj,
    triangle_left,
    triangle_right,
    triangle_gate,
    triangle_out,
    relative_table,
    transition_up,
    transition_down,
):
    daps, subs = lax.axis_size("dap"), lax.axis_size("sub")
    ratio = daps // subs
    cols = pair_input.shape[1]

    def fetch(values, source):
        perm = []
        for a in range(daps):
            for b in range(subs):
                dap, sub = source(a, b)
                perm.append((dap * subs + sub, a * subs + b))
        return lax.ppermute(values, ("dap", "sub"), perm)

    def owner(a, b, turn):
        return ratio * b + (a + turn) % ratio

    hidden = outer_left.shape[1]
    mask = alignment_mask.T
    zr = factor(alignment, repeat_weight(outer_right.T), hidden, PARTS)
    zrs = [
        fetch(
            zr[part],
            lambda a, b, t=turn, p=part: (
                owner(a, b, t), (sender(a, b, subs, ratio) + 2 * p) % subs
            ),
        )
        for turn in range(ratio)
        for part in range(PARTS)
    ]
    (zl,) = factor(alignment, repeat_weight(outer_left.T), hidden, 1, mask)
    zlt, base, inverse, live, proj, seen = prepare(
        zl, mask, pair_input, residue_mask, chain_index, relative_table, outer_proj
    )
    own, left, one = pair_update(
        hidden, zlt, zrs, seen, base, inverse, live, proj, triangle_left, triangle_right
    )
    near = fetch(own, lambda a, b: (a, other(b)))
    across = [
        fetch(left, lambda a, b, m=step: (a, (b + 2 * m) % subs)) for step in range(1, subs // 2)
    ]
    beyond = [fetch(block, lambda a, b: (a, other(b))) for block in across]
    right = jnp.stack([own[1], near[1]])
    rights = [
        fetch(
            right,
            lambda a, b, t=turn, m=step: (
                owner(a, b, t), (sender(a, b, subs, ratio) + 2 * m) % subs
            ),
        )
        for turn in range(ratio)
        for step in range(subs // 2)
    ]
    return triangle_update(
        [own, near, *across, *beyond],
        rights,
        one,
        cols,
        triangle_gate,
        triangle_out,
        transition_up,
        transition_down,
    )


def solution(mesh):
    in_specs = (
        P("parts", "dap", None),
        P("parts", None),
        P(("parts", "dap"), "sub", None),
        P("parts"),
        P("parts"),
        P(),
        P(),
        P(),
        P(),
        P(),
        P(),
        P(),
        P(),
        P(),
        P(),
    )
    out_specs = P(("parts", "dap"), "sub", None)
    return jax.shard_map(
        per_device, mesh=mesh, in_specs=in_specs, out_specs=out_specs, check_vma=False
    )
```

```python
import functools

import jax
import jax.numpy as jnp
from jax import lax
from jax.experimental import pallas as pl
from jax.experimental.pallas import tpu as pltpu
from jax.sharding import PartitionSpec as P

REL_CLIP = 32
LANES = 128
PARTS = 1
EPSILON = 1e-05
BF16 = jnp.bfloat16
F32 = jnp.float32
NT = (((1,), (1,)), ((), ()))
TN = (((0,), (0,)), ((), ()))


def layer_norm(values):
    average = jnp.mean(values, axis=-1, keepdims=True)
    centered = values - average
    spread = jnp.mean(centered * centered, axis=-1, keepdims=True)
    return centered * lax.rsqrt(spread + EPSILON)


def dot(left, right):
    return jnp.dot(left, right, preferred_element_type=F32)


def dot_nt(left, right):
    return lax.dot_general(left, right, NT, preferred_element_type=F32)


def dot_tn(left, right):
    return lax.dot_general(left, right, TN, preferred_element_type=F32)


def iota(shape, dim):
    return lax.broadcasted_iota(jnp.int32, shape, dim)


def vmem():
    return pl.BlockSpec(memory_space=pltpu.VMEM)


def over(index, size):
    return lax.shift_right_logical(index, size.bit_length() - 1)


def within(index, size):
    return lax.bitwise_and(index, size - 1)


def repeat_kernel(weight_ref, out_ref):
    rep = LANES // weight_ref.shape[0]
    out_ref[...] = jnp.concatenate([weight_ref[...]] * rep, axis=0).T


def repeat_weight(weight):
    return pl.pallas_call(
        repeat_kernel,
        out_shape=jax.ShapeDtypeStruct((weight.shape[1], LANES), BF16),
        in_specs=[vmem()],
        out_specs=vmem(),
        compiler_params=pltpu.CompilerParams(vmem_limit_bytes=2 << 20),
        cost_estimate=pl.CostEstimate(flops=1 << 30, bytes_accessed=1 << 17, transcendentals=0),
    )(weight)


def exchange(s0, s1, s2, s3):
    lane = iota(s0.shape, 1)
    block = LANES // 4
    odd = within(over(lane, block), 2) == 1
    upper = over(lane, 2 * block) == 1
    t0 = jnp.where(upper, pltpu.roll(s2, 2 * block, 1), s0)
    t1 = jnp.where(upper, pltpu.roll(s3, 2 * block, 1), s1)
    t2 = jnp.where(upper, s2, pltpu.roll(s0, 2 * block, 1))
    t3 = jnp.where(upper, s3, pltpu.roll(s1, 2 * block, 1))
    return (
        jnp.where(odd, pltpu.roll(t1, block, 1), t0),
        jnp.where(odd, t1, pltpu.roll(t0, 3 * block, 1)),
        jnp.where(odd, pltpu.roll(t3, block, 1), t2),
        jnp.where(odd, t3, pltpu.roll(t2, 3 * block, 1)),
    )


def factor_kernel(masked, hidden, x_ref, weight_ref, *refs):
    mask_ref = refs[0] if masked else None
    z_refs, y_scr = refs[masked:-1], refs[-1]
    each, seqs, _ = z_refs[0].shape
    groups = each * len(z_refs)
    _, rows, channels = x_ref.shape
    rep = rows // groups
    width = rows * hidden
    steps, step = y_scr.shape[0], y_scr.shape[1] // rows
    quarter = seqs // rep
    share = jnp.full((channels, LANES), 1.0 / channels, BF16)
    weight = jnp.concatenate([weight_ref[...], share], axis=1)
    sums = dot(jnp.ones((8, channels), BF16), weight_ref[...])[:1]
    side = (rep * LANES, LANES)
    own = over(iota(side, 0), LANES) == over(iota(side, 1), hidden)
    own = jnp.where(own, 1.0 / channels, 0.0).astype(BF16)
    block = over(iota((step * rows, LANES), 1), hidden)
    if masked:
        residues = mask_ref.shape[0]
        column = lax.axis_index("dap") * rows + over(iota((residues, width), 1), hidden)
        lanes_of = (iota((residues, width), 0) == column).astype(BF16)
        live = dot_tn(mask_ref[...].astype(BF16), lanes_of)
    for turn in range(steps):
        squares, y, mean = [], None, None
        for part in range(rep):
            first = part * quarter + turn * step
            x = x_ref[first : first + step].reshape(step * rows, channels)
            both = dot(x, weight)
            product, average = both[:, :LANES], both[:, LANES:]
            y = product if part == 0 else jnp.where(block == part, product, y)
            mean = average if part == 0 else jnp.where(block == part, average, mean)
            square = jnp.zeros_like(average)
            for half in range(channels // LANES):
                centered = x[:, half * LANES : (half + 1) * LANES].astype(F32) - average
                square = square + centered * centered
            squares.append(square.astype(BF16))
        scale = lax.rsqrt(dot(jnp.concatenate(squares, axis=1), own) + EPSILON)
        y_scr[turn] = (y - mean * sums) * scale
        for group in range(groups):
            taken = [
                y_scr[turn, pl.ds(group * rep + k, step, stride=rows), :] for k in range(rep)
            ]
            for part, z in enumerate(exchange(*taken)):
                first = part * quarter + turn * step
                here = slice(first, first + step)
                if masked:
                    z = z * live[here, group * LANES : (group + 1) * LANES]
                z_refs[group // each][group % each, here, :] = z.astype(BF16)


def factor(alignment, weight, hidden, parts, mask=None):
    seqs, rows, channels = alignment.shape
    steps = 2
    operands = (alignment, weight) if mask is None else (alignment, weight, mask)
    shape = jax.ShapeDtypeStruct((rows * hidden // LANES // parts, seqs, LANES), BF16)
    packed = seqs * rows * hidden // LANES
    return pl.pallas_call(
        functools.partial(factor_kernel, mask is not None, hidden),
        out_shape=(shape,) * parts,
        in_specs=[vmem()] * len(operands),
        out_specs=[vmem()] * parts,
        scratch_shapes=[pltpu.VMEM((steps, packed // steps, LANES), F32)],
        compiler_params=pltpu.CompilerParams(vmem_limit_bytes=24 << 20),
        cost_estimate=pl.CostEstimate(
            flops=2 * seqs * rows * channels * 512, bytes_accessed=seqs << 14, transcendentals=0
        ),
    )(*operands)


def prepare_kernel(
    zl_ref, mask_ref, pair_ref, live_ref, chain_ref, table_ref, proj_ref,
    zlt_ref, base_ref, inverse_ref, live_out_ref, proj_out_ref, seen_ref, pair_scr, table_scr, turn_scr,
):
    rows, cols, _ = pair_ref.shape
    pairs = rows * cols
    residues = mask_ref.shape[0]
    classes = table_ref.shape[0]
    row_start = lax.axis_index("dap") * rows
    col_start = lax.axis_index("sub") * cols
    groups = zl_ref.shape[0]
    hidden = groups * LANES // rows
    for group in range(groups):
        turned = zl_ref[group].astype(F32).T
        for half in range(zlt_ref.shape[0]):
            lanes = slice(half * LANES, (half + 1) * LANES)
            turn_scr[half, group * LANES : (group + 1) * LANES, :] = turned[:, lanes]
    for half in range(zlt_ref.shape[0]):
        for channel in range(hidden):
            here = slice(channel * rows, (channel + 1) * rows)
            picked = turn_scr[half, pl.ds(channel, rows, stride=hidden), :]
            zlt_ref[half, here, :] = picked.astype(BF16)
    proj_out_ref[...] = proj_ref[...].reshape(proj_out_ref.shape).astype(BF16)
    width = groups * LANES
    for block in range(cols // rows):
        column = col_start + block * rows + over(iota((residues, width), 1), hidden)
        spread = (iota((residues, width), 0) == column).astype(BF16)
        seen = dot_tn(mask_ref[...].astype(BF16), spread).astype(BF16)
        for group in range(groups):
            seen_ref[block * groups + group] = seen[:, group * LANES : (group + 1) * LANES]
    which = iota((pairs, residues), 0)
    place = iota((pairs, residues), 1)
    pick_row = (place == row_start + within(which, rows)).astype(BF16)
    pick_col = (place == col_start + over(which, rows)).astype(BF16)
    mask = mask_ref[...].astype(BF16)
    both = (dot(pick_row, mask) * dot(pick_col, mask)).astype(BF16)
    counts = dot(both, jnp.ones((mask.shape[1], LANES), BF16))
    inverse_ref[...] = 1.0 / jnp.maximum(counts, 1.0)
    live = jnp.broadcast_to(live_ref[...].astype(F32), (LANES, residues)).astype(BF16)
    chain = jnp.broadcast_to(chain_ref[...].astype(F32), (LANES, residues)).astype(BF16)
    live_out_ref[...] = dot_nt(pick_row, live) * dot_nt(pick_col, live)
    same = dot_nt(pick_row, chain) == dot_nt(pick_col, chain)
    pair = iota((pairs, LANES), 0)
    offset = (row_start + within(pair, rows)) - (col_start + over(pair, rows)) + REL_CLIP
    bucket = jnp.where(same, jnp.clip(offset, 0, 2 * REL_CLIP), 2 * REL_CLIP + 1)
    table_scr[...] = jnp.zeros_like(table_scr)
    table_scr[pl.ds(0, classes), :] = table_ref[...].astype(F32)
    onehot = (bucket == iota((pairs, LANES), 1)).astype(BF16)
    relative = dot(onehot, table_scr[...].astype(BF16))
    pair_scr[...] = pair_ref[...].reshape(pairs, LANES).astype(F32)
    for col in range(cols):
        here = slice(col * rows, (col + 1) * rows)
        base_ref[here, :] = relative[here] + pair_scr[pl.ds(col, rows, stride=cols), :]


def prepare(zl, mask, pair_input, residue_mask, chain_index, table, proj):
    rows, cols, channels = pair_input.shape
    pairs = rows * cols
    shape = jax.ShapeDtypeStruct((pairs, channels), F32)
    depth = proj.shape[0] * proj.shape[1]
    return pl.pallas_call(
        prepare_kernel,
        out_shape=(
            jax.ShapeDtypeStruct((zl.shape[1] // LANES, zl.shape[0] * LANES, LANES), BF16),
            shape,
            shape,
            shape,
            jax.ShapeDtypeStruct((depth, channels), BF16),
            jax.ShapeDtypeStruct((cols // rows * zl.shape[0], *zl.shape[1:]), BF16),
        ),
        in_specs=[vmem()] * 7,
        out_specs=[vmem()] * 6,
        scratch_shapes=[
            pltpu.VMEM((pairs, channels), F32),
            pltpu.VMEM((LANES, channels), F32),
            pltpu.VMEM((zl.shape[1] // LANES, zl.shape[0] * LANES, LANES), F32),
        ],
        compiler_params=pltpu.CompilerParams(vmem_limit_bytes=24 << 20),
        cost_estimate=pl.CostEstimate(
            flops=2 * pairs * 256 * 1024, bytes_accessed=2 << 20, transcendentals=0
        ),
    )(zl, mask, pair_input, residue_mask[None, :], chain_index[None, :], table, proj)


def pair_kernel(ratio, hidden, zlt_ref, *refs):
    zr_refs, refs = refs[: ratio * PARTS], refs[ratio * PARTS :]
    (seen_ref, base_ref, inverse_ref, live_ref, proj_ref, tl_ref, tr_ref,
     both_ref, left_ref, one_ref, flat_scr, one_scr) = refs
    pairs, channels = base_ref.shape
    rows = zlt_ref.shape[1] // hidden
    rep = LANES // hidden
    me = lax.axis_index("dap")
    left = jnp.concatenate([zlt_ref[part] for part in range(zlt_ref.shape[0])], axis=1)
    for step in range(ratio):
        block = lax.rem(me + step, ratio)
        right = []
        for group in range(rows // rep):
            each = rows // rep // PARTS
            factor = zr_refs[step * PARTS + group // each][group % each]
            right.append(factor * seen_ref[block * (rows // rep) + group])
        outer = dot(left, jnp.concatenate(right, axis=1))
        for group in range(rows // rep):
            lanes = slice(group * LANES, (group + 1) * LANES)
            for quad in range(hidden // rep):
                s0, s1, s2, s3 = (
                    outer[(quad * rep + k) * rows : (quad * rep + k + 1) * rows, lanes]
                    for k in range(rep)
                )
                found = exchange(s0, s1, s2, s3)
                for k in range(rep):
                    first = block * rows * rows + (group * rep + k) * rows
                    if ratio == 1:
                        first = (group * rep + k) * rows
                    else:
                        first = pl.multiple_of(first, rows)
                    flat_scr[quad, pl.ds(first, rows), :] = found[k].astype(BF16)
    flat = jnp.concatenate([flat_scr[quad] for quad in range(flat_scr.shape[0])], axis=1)
    outer_mean = dot(flat, proj_ref[...]) * inverse_ref[...]
    one = (base_ref[...] + outer_mean).astype(BF16).astype(F32)
    one_scr[...] = one
    norm = layer_norm(one).astype(BF16)
    for side, weight in enumerate((tl_ref, tr_ref)):
        both = dot(norm, weight[...])
        factor = jax.nn.sigmoid(both[:, :channels]) * both[:, channels:] * live_ref[...]
        both_ref[side] = factor.astype(BF16)
        if side == 0:
            left_ref[...] = factor.astype(BF16)
    cols = pairs // rows
    for row in range(rows):
        one_ref[row * cols : (row + 1) * cols, :] = one_scr[pl.ds(row, cols, stride=rows), :].astype(BF16)


def pair_update(hidden, zlt, zrs, seen, base, inverse, live, proj, triangle_left, triangle_right):
    pairs, channels = base.shape
    ratio = len(zrs) // PARTS
    shape = jax.ShapeDtypeStruct((pairs, channels), BF16)
    return pl.pallas_call(
        functools.partial(pair_kernel, ratio, hidden),
        out_shape=(jax.ShapeDtypeStruct((2, pairs, channels), BF16), shape, shape),
        in_specs=[vmem()] * (8 + len(zrs)),
        out_specs=[vmem()] * 3,
        scratch_shapes=[
            pltpu.VMEM((proj.shape[0] // LANES, pairs, LANES), BF16),
            pltpu.VMEM((pairs, channels), F32),
        ],
        compiler_params=pltpu.CompilerParams(vmem_limit_bytes=32 << 20),
        cost_estimate=pl.CostEstimate(
            flops=2 * pairs * 1024 * 512, bytes_accessed=2 << 20, transcendentals=pairs * 256
        ),
    )(zlt, *zrs, seen, base, inverse, live, proj, triangle_left, triangle_right)


def other(sub):
    return sub + 1 - 2 * (sub % 2)


SENDERS = ((3, 0, 2, 1), (0, 3, 2, 1), (2, 0, 1, 3), (2, 0, 3, 1))


def sender(a, b, subs, ratio):
    if (subs, ratio) == (4, 1):
        return SENDERS[b][a]
    return a // ratio


def sender_index(a, b, subs, ratio):
    if (subs, ratio) != (4, 1):
        return a // ratio
    found = 0
    for col, places in enumerate(SENDERS):
        for row, place in enumerate(places):
            found = jnp.where((a == row) & (b == col), place, found)
    return found


def add_terms(sums, start, lefts, rights, steps, ratio, cols, left_scr):
    subs = left_scr.shape[0]
    _, channels = sums.shape
    rows = left_scr.shape[1] // cols
    here, there = lax.axis_index("dap"), lax.axis_index("sub")
    first_sub = sender_index(here, there, subs, ratio)
    own, near, across, beyond = lefts
    left_scr[there] = own[0].astype(F32)
    left_scr[other(there)] = near[0].astype(F32)
    for step in range(1, subs // 2):
        sub = lax.rem(there + 2 * step, subs)
        left_scr[sub] = across[step - 1][...].astype(F32)
        left_scr[other(sub)] = beyond[step - 1][...].astype(F32)
    for turn in range(ratio):
        block = lax.rem(here + turn, ratio) if ratio > 1 else 0
        places = [i * cols + block * rows for i in range(rows)]
        if ratio > 1:
            places = [pl.multiple_of(place, rows) for place in places]
        if start is None:
            totals = tuple(jnp.zeros((rows, channels), F32) for _ in range(rows))
        else:
            totals = tuple(start[pl.ds(place, rows), :] for place in places)
        for index, step in enumerate(steps):
            sub = lax.rem(first_sub + 2 * step + 2, subs)
            pair = rights[turn * len(steps) + index]
            for member, slot in enumerate((sub, other(sub))):

                def body(k, totals, slot=slot, member=member, pair=pair):
                    first = pl.multiple_of(k * rows, rows)
                    right = pair[member, pl.ds(first, rows), :].astype(F32)
                    return tuple(
                        totals[i] + left_scr[slot, pl.ds(first + i, 1), :] * right
                        for i in range(rows)
                    )

                totals = lax.fori_loop(0, cols, body, totals, unroll=4)
        for place, total in zip(places, totals):
            sums[pl.ds(place, rows), :] = total


def split_lefts(refs, twos):
    count = twos - 1
    lefts = (refs[0], refs[1], refs[2 : 2 + count], refs[2 + count : 2 + 2 * count])
    return lefts, refs[2 + 2 * count :]


def first_kernel(steps, twos, ratio, cols, *refs):
    lefts, refs = split_lefts(refs, twos)
    rights, refs = refs[: ratio * len(steps)], refs[ratio * len(steps) :]
    one_ref, weight_ref, sums_ref, gate_ref, left_scr = refs
    add_terms(sums_ref, None, lefts, rights, steps, ratio, cols, left_scr)
    norm = layer_norm(one_ref[...].astype(F32)).astype(BF16)
    gate_ref[...] = jax.nn.sigmoid(dot(norm, weight_ref[...]))


def last_kernel(steps, twos, ratio, cols, *refs):
    lefts, refs = split_lefts(refs, twos)
    rights, refs = refs[: ratio * len(steps)], refs[ratio * len(steps) :]
    (start_ref, one_ref, gate_ref, out_ref, up_ref, down_ref, result_ref, left_scr, sum_scr) = refs
    add_terms(sum_scr, start_ref, lefts, rights, steps, ratio, cols, left_scr)
    one = one_ref[...].astype(F32)
    hidden = layer_norm(sum_scr[...].astype(BF16).astype(F32)).astype(BF16)
    two = (one + gate_ref[...] * dot(hidden, out_ref[...])).astype(BF16).astype(F32)
    wide = jnp.maximum(dot(layer_norm(two).astype(BF16), up_ref[...]), 0.0).astype(BF16)
    result = (two + dot(wide, down_ref[...])).astype(BF16)
    result_ref[...] = result.reshape(result_ref.shape)


def triangle_update(lefts, rights, one, cols, gate_weight, out, up, down):
    pairs, channels = one.shape
    rows = pairs // cols
    twos = len(lefts) // 2
    subs = 2 * twos
    ratio = len(rights) // twos
    late, early = range(twos // 2), range(twos // 2, twos)
    limit = (12 << 20) if ratio == 1 else (50 << 20)
    left_scr = pltpu.VMEM((subs, pairs, channels), F32)
    shape = jax.ShapeDtypeStruct((pairs, channels), F32)

    def chosen(steps):
        return [rights[turn * twos + step] for turn in range(ratio) for step in steps]

    sums, gate = pl.pallas_call(
        functools.partial(first_kernel, early, twos, ratio, cols),
        out_shape=(shape, shape),
        in_specs=[vmem()] * (len(lefts) + ratio * len(early) + 2),
        out_specs=[vmem()] * 2,
        scratch_shapes=[left_scr],
        compiler_params=pltpu.CompilerParams(vmem_limit_bytes=limit),
        cost_estimate=pl.CostEstimate(
            flops=2 * pairs * channels * 1024, bytes_accessed=1 << 20, transcendentals=pairs * 128
        ),
    )(*lefts, *chosen(early), one, gate_weight)
    return pl.pallas_call(
        functools.partial(last_kernel, late, twos, ratio, cols),
        out_shape=jax.ShapeDtypeStruct((rows, cols, channels), BF16),
        in_specs=[vmem()] * (len(lefts) + ratio * len(late) + 6),
        out_specs=vmem(),
        scratch_shapes=[left_scr, pltpu.VMEM((pairs, channels), F32)],
        compiler_params=pltpu.CompilerParams(vmem_limit_bytes=limit),
        cost_estimate=pl.CostEstimate(
            flops=2 * pairs * channels * 2048, bytes_accessed=2 << 20, transcendentals=pairs * 128
        ),
    )(*lefts, *chosen(late), sums, one, gate, out, up, down)


def per_device(
    alignment,
    alignment_mask,
    pair_input,
    residue_mask,
    chain_index,
    outer_left,
    outer_right,
    outer_proj,
    triangle_left,
    triangle_right,
    triangle_gate,
    triangle_out,
    relative_table,
    transition_up,
    transition_down,
):
    daps, subs = lax.axis_size("dap"), lax.axis_size("sub")
    ratio = daps // subs
    cols = pair_input.shape[1]

    def fetch(values, source):
        perm = []
        for a in range(daps):
            for b in range(subs):
                dap, sub = source(a, b)
                perm.append((dap * subs + sub, a * subs + b))
        return lax.ppermute(values, ("dap", "sub"), perm)

    def owner(a, b, turn):
        return ratio * b + (a + turn) % ratio

    hidden = outer_left.shape[1]
    mask = alignment_mask.T
    zr = factor(alignment, repeat_weight(outer_right.T), hidden, PARTS)
    zrs = [
        fetch(
            zr[part],
            lambda a, b, t=turn, p=part: (
                owner(a, b, t), (sender(a, b, subs, ratio) + 2 * p) % subs
            ),
        )
        for turn in range(ratio)
        for part in range(PARTS)
    ]
    (zl,) = factor(alignment, repeat_weight(outer_left.T), hidden, 1, mask)
    zlt, base, inverse, live, proj, seen = prepare(
        zl, mask, pair_input, residue_mask, chain_index, relative_table, outer_proj
    )
    own, left, one = pair_update(
        hidden, zlt, zrs, seen, base, inverse, live, proj, triangle_left, triangle_right
    )
    near = fetch(own, lambda a, b: (a, other(b)))
    across = [
        fetch(left, lambda a, b, m=step: (a, (b + 2 * m) % subs)) for step in range(1, subs // 2)
    ]
    beyond = [fetch(block, lambda a, b: (a, other(b))) for block in across]
    right = jnp.stack([own[1], near[1]])
    rights = [
        fetch(
            right,
            lambda a, b, t=turn, m=step: (
                owner(a, b, t), (sender(a, b, subs, ratio) + 2 * m + 2) % subs
            ),
        )
        for turn in range(ratio)
        for step in range(subs // 2)
    ]
    return triangle_update(
        [own, near, *across, *beyond],
        rights,
        one,
        cols,
        triangle_gate,
        triangle_out,
        transition_up,
        transition_down,
    )


def solution(mesh):
    in_specs = (
        P("parts", "dap", None),
        P("parts", None),
        P(("parts", "dap"), "sub", None),
        P("parts"),
        P("parts"),
        P(),
        P(),
        P(),
        P(),
        P(),
        P(),
        P(),
        P(),
        P(),
        P(),
    )
    out_specs = P(("parts", "dap"), "sub", None)
    return jax.shard_map(
        per_device, mesh=mesh, in_specs=in_specs, out_specs=out_specs, check_vma=False
    )
```

```python
import functools

import jax
import jax.numpy as jnp
from jax import lax
from jax.experimental import pallas as pl
from jax.experimental.pallas import tpu as pltpu
from jax.sharding import PartitionSpec as P

REL_CLIP = 32
LANES = 128
PARTS = 1
EPSILON = 1e-05
BF16 = jnp.bfloat16
F32 = jnp.float32
NT = (((1,), (1,)), ((), ()))
TN = (((0,), (0,)), ((), ()))


def layer_norm(values):
    average = jnp.mean(values, axis=-1, keepdims=True)
    centered = values - average
    spread = jnp.mean(centered * centered, axis=-1, keepdims=True)
    return centered * lax.rsqrt(spread + EPSILON)


def dot(left, right):
    return jnp.dot(left, right, preferred_element_type=F32)


def dot_nt(left, right):
    return lax.dot_general(left, right, NT, preferred_element_type=F32)


def dot_tn(left, right):
    return lax.dot_general(left, right, TN, preferred_element_type=F32)


def iota(shape, dim):
    return lax.broadcasted_iota(jnp.int32, shape, dim)


def vmem():
    return pl.BlockSpec(memory_space=pltpu.VMEM)


def over(index, size):
    return lax.shift_right_logical(index, size.bit_length() - 1)


def within(index, size):
    return lax.bitwise_and(index, size - 1)


def repeat_kernel(weight_ref, out_ref):
    rep = LANES // weight_ref.shape[0]
    out_ref[...] = jnp.concatenate([weight_ref[...]] * rep, axis=0).T


def repeat_weight(weight):
    return pl.pallas_call(
        repeat_kernel,
        out_shape=jax.ShapeDtypeStruct((weight.shape[1], LANES), BF16),
        in_specs=[vmem()],
        out_specs=vmem(),
        compiler_params=pltpu.CompilerParams(vmem_limit_bytes=2 << 20),
        cost_estimate=pl.CostEstimate(flops=1 << 30, bytes_accessed=1 << 17, transcendentals=0),
    )(weight)


def exchange(s0, s1, s2, s3):
    lane = iota(s0.shape, 1)
    block = LANES // 4
    odd = within(over(lane, block), 2) == 1
    upper = over(lane, 2 * block) == 1
    t0 = jnp.where(upper, pltpu.roll(s2, 2 * block, 1), s0)
    t1 = jnp.where(upper, pltpu.roll(s3, 2 * block, 1), s1)
    t2 = jnp.where(upper, s2, pltpu.roll(s0, 2 * block, 1))
    t3 = jnp.where(upper, s3, pltpu.roll(s1, 2 * block, 1))
    return (
        jnp.where(odd, pltpu.roll(t1, block, 1), t0),
        jnp.where(odd, t1, pltpu.roll(t0, 3 * block, 1)),
        jnp.where(odd, pltpu.roll(t3, block, 1), t2),
        jnp.where(odd, t3, pltpu.roll(t2, 3 * block, 1)),
    )


def factor_kernel(masked, hidden, x_ref, weight_ref, *refs):
    mask_ref = refs[0] if masked else None
    z_refs, y_scr = refs[masked:-1], refs[-1]
    each, seqs, _ = z_refs[0].shape
    groups = each * len(z_refs)
    _, rows, channels = x_ref.shape
    rep = rows // groups
    width = rows * hidden
    steps, step = y_scr.shape[0], y_scr.shape[1] // rows
    quarter = seqs // rep
    share = jnp.full((channels, LANES), 1.0 / channels, BF16)
    weight = jnp.concatenate([weight_ref[...], share], axis=1)
    sums = dot(jnp.ones((8, channels), BF16), weight_ref[...])[:1]
    side = (rep * LANES, LANES)
    own = over(iota(side, 0), LANES) == over(iota(side, 1), hidden)
    own = jnp.where(own, 1.0 / channels, 0.0).astype(BF16)
    block = over(iota((step * rows, LANES), 1), hidden)
    if masked:
        residues = mask_ref.shape[0]
        column = lax.axis_index("dap") * rows + over(iota((residues, width), 1), hidden)
        lanes_of = (iota((residues, width), 0) == column).astype(BF16)
        live = dot_tn(mask_ref[...].astype(BF16), lanes_of)
    for turn in range(steps):
        squares, y, mean = [], None, None
        for part in range(rep):
            first = part * quarter + turn * step
            x = x_ref[first : first + step].reshape(step * rows, channels)
            both = dot(x, weight)
            product, average = both[:, :LANES], both[:, LANES:]
            y = product if part == 0 else jnp.where(block == part, product, y)
            mean = average if part == 0 else jnp.where(block == part, average, mean)
            square = jnp.zeros_like(average)
            for half in range(channels // LANES):
                centered = x[:, half * LANES : (half + 1) * LANES].astype(F32) - average
                square = square + centered * centered
            squares.append(square.astype(BF16))
        scale = lax.rsqrt(dot(jnp.concatenate(squares, axis=1), own) + EPSILON)
        y_scr[turn] = (y - mean * sums) * scale
        for group in range(groups):
            taken = [
                y_scr[turn, pl.ds(group * rep + k, step, stride=rows), :] for k in range(rep)
            ]
            for part, z in enumerate(exchange(*taken)):
                first = part * quarter + turn * step
                here = slice(first, first + step)
                if masked:
                    z = z * live[here, group * LANES : (group + 1) * LANES]
                z_refs[group // each][group % each, here, :] = z.astype(BF16)


def factor(alignment, weight, hidden, parts, mask=None):
    seqs, rows, channels = alignment.shape
    steps = 2
    operands = (alignment, weight) if mask is None else (alignment, weight, mask)
    shape = jax.ShapeDtypeStruct((rows * hidden // LANES // parts, seqs, LANES), BF16)
    packed = seqs * rows * hidden // LANES
    return pl.pallas_call(
        functools.partial(factor_kernel, mask is not None, hidden),
        out_shape=(shape,) * parts,
        in_specs=[vmem()] * len(operands),
        out_specs=[vmem()] * parts,
        scratch_shapes=[pltpu.VMEM((steps, packed // steps, LANES), F32)],
        compiler_params=pltpu.CompilerParams(vmem_limit_bytes=24 << 20),
        cost_estimate=pl.CostEstimate(
            flops=2 * seqs * rows * channels * 512, bytes_accessed=seqs << 14, transcendentals=0
        ),
    )(*operands)


def prepare_kernel(
    zl_ref, mask_ref, pair_ref, live_ref, chain_ref, table_ref, proj_ref,
    zlt_ref, base_ref, inverse_ref, live_out_ref, proj_out_ref, seen_ref, pair_scr, table_scr, turn_scr,
):
    rows, cols, _ = pair_ref.shape
    pairs = rows * cols
    residues = mask_ref.shape[0]
    classes = table_ref.shape[0]
    row_start = lax.axis_index("dap") * rows
    col_start = lax.axis_index("sub") * cols
    groups = zl_ref.shape[0]
    hidden = groups * LANES // rows
    for group in range(groups):
        turned = zl_ref[group].astype(F32).T
        for half in range(zlt_ref.shape[0]):
            lanes = slice(half * LANES, (half + 1) * LANES)
            turn_scr[half, group * LANES : (group + 1) * LANES, :] = turned[:, lanes]
    for half in range(zlt_ref.shape[0]):
        for channel in range(hidden):
            here = slice(channel * rows, (channel + 1) * rows)
            picked = turn_scr[half, pl.ds(channel, rows, stride=hidden), :]
            zlt_ref[half, here, :] = picked.astype(BF16)
    proj_out_ref[...] = proj_ref[...].reshape(proj_out_ref.shape).astype(BF16)
    width = groups * LANES
    for block in range(cols // rows):
        column = col_start + block * rows + over(iota((residues, width), 1), hidden)
        spread = (iota((residues, width), 0) == column).astype(BF16)
        seen = dot_tn(mask_ref[...].astype(BF16), spread).astype(BF16)
        for group in range(groups):
            seen_ref[block * groups + group] = seen[:, group * LANES : (group + 1) * LANES]
    which = iota((pairs, residues), 0)
    place = iota((pairs, residues), 1)
    pick_row = (place == row_start + within(which, rows)).astype(BF16)
    pick_col = (place == col_start + over(which, rows)).astype(BF16)
    mask = mask_ref[...].astype(BF16)
    both = (dot(pick_row, mask) * dot(pick_col, mask)).astype(BF16)
    counts = dot(both, jnp.ones((mask.shape[1], LANES), BF16))
    inverse_ref[...] = 1.0 / jnp.maximum(counts, 1.0)
    live = jnp.broadcast_to(live_ref[...].astype(F32), (LANES, residues)).astype(BF16)
    chain = jnp.broadcast_to(chain_ref[...].astype(F32), (LANES, residues)).astype(BF16)
    live_out_ref[...] = dot_nt(pick_row, live) * dot_nt(pick_col, live)
    same = dot_nt(pick_row, chain) == dot_nt(pick_col, chain)
    pair = iota((pairs, LANES), 0)
    offset = (row_start + within(pair, rows)) - (col_start + over(pair, rows)) + REL_CLIP
    bucket = jnp.where(same, jnp.clip(offset, 0, 2 * REL_CLIP), 2 * REL_CLIP + 1)
    table_scr[...] = jnp.zeros_like(table_scr)
    table_scr[pl.ds(0, classes), :] = table_ref[...].astype(F32)
    onehot = (bucket == iota((pairs, LANES), 1)).astype(BF16)
    relative = dot(onehot, table_scr[...].astype(BF16))
    pair_scr[...] = pair_ref[...].reshape(pairs, LANES).astype(F32)
    for col in range(cols):
        here = slice(col * rows, (col + 1) * rows)
        base_ref[here, :] = relative[here] + pair_scr[pl.ds(col, rows, stride=cols), :]


def prepare(zl, mask, pair_input, residue_mask, chain_index, table, proj):
    rows, cols, channels = pair_input.shape
    pairs = rows * cols
    shape = jax.ShapeDtypeStruct((pairs, channels), F32)
    depth = proj.shape[0] * proj.shape[1]
    return pl.pallas_call(
        prepare_kernel,
        out_shape=(
            jax.ShapeDtypeStruct((zl.shape[1] // LANES, zl.shape[0] * LANES, LANES), BF16),
            shape,
            shape,
            shape,
            jax.ShapeDtypeStruct((depth, channels), BF16),
            jax.ShapeDtypeStruct((cols // rows * zl.shape[0], *zl.shape[1:]), BF16),
        ),
        in_specs=[vmem()] * 7,
        out_specs=[vmem()] * 6,
        scratch_shapes=[
            pltpu.VMEM((pairs, channels), F32),
            pltpu.VMEM((LANES, channels), F32),
            pltpu.VMEM((zl.shape[1] // LANES, zl.shape[0] * LANES, LANES), F32),
        ],
        compiler_params=pltpu.CompilerParams(vmem_limit_bytes=24 << 20),
        cost_estimate=pl.CostEstimate(
            flops=2 * pairs * 256 * 1024, bytes_accessed=2 << 20, transcendentals=0
        ),
    )(zl, mask, pair_input, residue_mask[None, :], chain_index[None, :], table, proj)


def pair_kernel(ratio, hidden, zlt_ref, *refs):
    zr_refs, refs = refs[: ratio * PARTS], refs[ratio * PARTS :]
    (seen_ref, base_ref, inverse_ref, live_ref, proj_ref, tl_ref, tr_ref,
     both_ref, left_ref, one_ref, flat_scr, one_scr) = refs
    pairs, channels = base_ref.shape
    rows = zlt_ref.shape[1] // hidden
    rep = LANES // hidden
    me = lax.axis_index("dap")
    left = jnp.concatenate([zlt_ref[part] for part in range(zlt_ref.shape[0])], axis=1)
    for step in range(ratio):
        block = lax.rem(me + step, ratio)
        right = []
        for group in range(rows // rep):
            each = rows // rep // PARTS
            factor = zr_refs[step * PARTS + group // each][group % each]
            right.append(factor * seen_ref[block * (rows // rep) + group])
        outer = dot(left, jnp.concatenate(right, axis=1))
        for group in range(rows // rep):
            lanes = slice(group * LANES, (group + 1) * LANES)
            for quad in range(hidden // rep):
                s0, s1, s2, s3 = (
                    outer[(quad * rep + k) * rows : (quad * rep + k + 1) * rows, lanes]
                    for k in range(rep)
                )
                found = exchange(s0, s1, s2, s3)
                for k in range(rep):
                    first = block * rows * rows + (group * rep + k) * rows
                    if ratio == 1:
                        first = (group * rep + k) * rows
                    else:
                        first = pl.multiple_of(first, rows)
                    flat_scr[quad, pl.ds(first, rows), :] = found[k].astype(BF16)
    flat = jnp.concatenate([flat_scr[quad] for quad in range(flat_scr.shape[0])], axis=1)
    outer_mean = dot(flat, proj_ref[...]) * inverse_ref[...]
    one = (base_ref[...] + outer_mean).astype(BF16).astype(F32)
    one_scr[...] = one
    norm = layer_norm(one).astype(BF16)
    for side, weight in enumerate((tl_ref, tr_ref)):
        both = dot(norm, weight[...])
        factor = jax.nn.sigmoid(both[:, :channels]) * both[:, channels:] * live_ref[...]
        both_ref[side] = factor.astype(BF16)
        if side == 0:
            left_ref[...] = factor.astype(BF16)
    cols = pairs // rows
    for row in range(rows):
        one_ref[row * cols : (row + 1) * cols, :] = one_scr[pl.ds(row, cols, stride=rows), :].astype(BF16)


def pair_update(hidden, zlt, zrs, seen, base, inverse, live, proj, triangle_left, triangle_right):
    pairs, channels = base.shape
    ratio = len(zrs) // PARTS
    shape = jax.ShapeDtypeStruct((pairs, channels), BF16)
    return pl.pallas_call(
        functools.partial(pair_kernel, ratio, hidden),
        out_shape=(jax.ShapeDtypeStruct((2, pairs, channels), BF16), shape, shape),
        in_specs=[vmem()] * (8 + len(zrs)),
        out_specs=[vmem()] * 3,
        scratch_shapes=[
            pltpu.VMEM((proj.shape[0] // LANES, pairs, LANES), BF16),
            pltpu.VMEM((pairs, channels), F32),
        ],
        compiler_params=pltpu.CompilerParams(vmem_limit_bytes=32 << 20),
        cost_estimate=pl.CostEstimate(
            flops=2 * pairs * 1024 * 512, bytes_accessed=2 << 20, transcendentals=pairs * 256
        ),
    )(zlt, *zrs, seen, base, inverse, live, proj, triangle_left, triangle_right)


def other(sub):
    return sub + 1 - 2 * (sub % 2)


SENDERS = ((3, 0, 2, 1), (0, 3, 2, 1), (2, 0, 1, 3), (2, 0, 3, 1))
PAIR_SENDERS = ((3, 0, 2, 1), (0, 3, 1, 2), (0, 2, 1, 3), (2, 0, 3, 1))


def sender(a, b, subs, ratio, table):
    if (subs, ratio) == (4, 1):
        return table[b][a]
    return a // ratio


def sender_index(a, b, subs, ratio):
    if (subs, ratio) != (4, 1):
        return a // ratio
    found = 0
    for col, places in enumerate(PAIR_SENDERS):
        for row, place in enumerate(places):
            found = jnp.where((a == row) & (b == col), place, found)
    return found


def add_terms(sums, start, lefts, rights, steps, ratio, cols, left_scr):
    subs = left_scr.shape[0]
    _, channels = sums.shape
    rows = left_scr.shape[1] // cols
    here, there = lax.axis_index("dap"), lax.axis_index("sub")
    first_sub = sender_index(here, there, subs, ratio)
    own, near, across, beyond = lefts
    left_scr[there] = own[0].astype(F32)
    left_scr[other(there)] = near[0].astype(F32)
    for step in range(1, subs // 2):
        sub = lax.rem(there + 2 * step, subs)
        left_scr[sub] = across[step - 1][...].astype(F32)
        left_scr[other(sub)] = beyond[step - 1][...].astype(F32)
    for turn in range(ratio):
        block = lax.rem(here + turn, ratio) if ratio > 1 else 0
        places = [i * cols + block * rows for i in range(rows)]
        if ratio > 1:
            places = [pl.multiple_of(place, rows) for place in places]
        if start is None:
            totals = tuple(jnp.zeros((rows, channels), F32) for _ in range(rows))
        else:
            totals = tuple(start[pl.ds(place, rows), :] for place in places)
        for index, step in enumerate(steps):
            sub = lax.rem(first_sub + 2 * step + 2, subs)
            pair = rights[turn * len(steps) + index]
            for member, slot in enumerate((sub, other(sub))):

                def body(k, totals, slot=slot, member=member, pair=pair):
                    first = pl.multiple_of(k * rows, rows)
                    right = pair[member, pl.ds(first, rows), :].astype(F32)
                    return tuple(
                        totals[i] + left_scr[slot, pl.ds(first + i, 1), :] * right
                        for i in range(rows)
                    )

                totals = lax.fori_loop(0, cols, body, totals, unroll=4)
        for place, total in zip(places, totals):
            sums[pl.ds(place, rows), :] = total


def split_lefts(refs, twos):
    count = twos - 1
    lefts = (refs[0], refs[1], refs[2 : 2 + count], refs[2 + count : 2 + 2 * count])
    return lefts, refs[2 + 2 * count :]


def first_kernel(steps, twos, ratio, cols, *refs):
    lefts, refs = split_lefts(refs, twos)
    rights, refs = refs[: ratio * len(steps)], refs[ratio * len(steps) :]
    one_ref, weight_ref, sums_ref, gate_ref, left_scr = refs
    add_terms(sums_ref, None, lefts, rights, steps, ratio, cols, left_scr)
    norm = layer_norm(one_ref[...].astype(F32)).astype(BF16)
    gate_ref[...] = jax.nn.sigmoid(dot(norm, weight_ref[...]))


def last_kernel(steps, twos, ratio, cols, *refs):
    lefts, refs = split_lefts(refs, twos)
    rights, refs = refs[: ratio * len(steps)], refs[ratio * len(steps) :]
    (start_ref, one_ref, gate_ref, out_ref, up_ref, down_ref, result_ref, left_scr, sum_scr) = refs
    add_terms(sum_scr, start_ref, lefts, rights, steps, ratio, cols, left_scr)
    one = one_ref[...].astype(F32)
    hidden = layer_norm(sum_scr[...].astype(BF16).astype(F32)).astype(BF16)
    two = (one + gate_ref[...] * dot(hidden, out_ref[...])).astype(BF16).astype(F32)
    wide = jnp.maximum(dot(layer_norm(two).astype(BF16), up_ref[...]), 0.0).astype(BF16)
    result = (two + dot(wide, down_ref[...])).astype(BF16)
    result_ref[...] = result.reshape(result_ref.shape)


def triangle_update(lefts, rights, one, cols, gate_weight, out, up, down):
    pairs, channels = one.shape
    rows = pairs // cols
    twos = len(lefts) // 2
    subs = 2 * twos
    ratio = len(rights) // twos
    late, early = range(twos // 2), range(twos // 2, twos)
    limit = (12 << 20) if ratio == 1 else (50 << 20)
    left_scr = pltpu.VMEM((subs, pairs, channels), F32)
    shape = jax.ShapeDtypeStruct((pairs, channels), F32)

    def chosen(steps):
        return [rights[turn * twos + step] for turn in range(ratio) for step in steps]

    sums, gate = pl.pallas_call(
        functools.partial(first_kernel, early, twos, ratio, cols),
        out_shape=(shape, shape),
        in_specs=[vmem()] * (len(lefts) + ratio * len(early) + 2),
        out_specs=[vmem()] * 2,
        scratch_shapes=[left_scr],
        compiler_params=pltpu.CompilerParams(vmem_limit_bytes=limit),
        cost_estimate=pl.CostEstimate(
            flops=2 * pairs * channels * 1024, bytes_accessed=1 << 20, transcendentals=pairs * 128
        ),
    )(*lefts, *chosen(early), one, gate_weight)
    return pl.pallas_call(
        functools.partial(last_kernel, late, twos, ratio, cols),
        out_shape=jax.ShapeDtypeStruct((rows, cols, channels), BF16),
        in_specs=[vmem()] * (len(lefts) + ratio * len(late) + 6),
        out_specs=vmem(),
        scratch_shapes=[left_scr, pltpu.VMEM((pairs, channels), F32)],
        compiler_params=pltpu.CompilerParams(vmem_limit_bytes=limit),
        cost_estimate=pl.CostEstimate(
            flops=2 * pairs * channels * 2048, bytes_accessed=2 << 20, transcendentals=pairs * 128
        ),
    )(*lefts, *chosen(late), sums, one, gate, out, up, down)


def per_device(
    alignment,
    alignment_mask,
    pair_input,
    residue_mask,
    chain_index,
    outer_left,
    outer_right,
    outer_proj,
    triangle_left,
    triangle_right,
    triangle_gate,
    triangle_out,
    relative_table,
    transition_up,
    transition_down,
):
    daps, subs = lax.axis_size("dap"), lax.axis_size("sub")
    ratio = daps // subs
    cols = pair_input.shape[1]

    def fetch(values, source):
        perm = []
        for a in range(daps):
            for b in range(subs):
                dap, sub = source(a, b)
                perm.append((dap * subs + sub, a * subs + b))
        return lax.ppermute(values, ("dap", "sub"), perm)

    def owner(a, b, turn):
        return ratio * b + (a + turn) % ratio

    hidden = outer_left.shape[1]
    mask = alignment_mask.T
    zr = factor(alignment, repeat_weight(outer_right.T), hidden, PARTS)
    zrs = [
        fetch(
            zr[part],
            lambda a, b, t=turn, p=part: (
                owner(a, b, t), (sender(a, b, subs, ratio, SENDERS) + 2 * p) % subs
            ),
        )
        for turn in range(ratio)
        for part in range(PARTS)
    ]
    (zl,) = factor(alignment, repeat_weight(outer_left.T), hidden, 1, mask)
    zlt, base, inverse, live, proj, seen = prepare(
        zl, mask, pair_input, residue_mask, chain_index, relative_table, outer_proj
    )
    own, left, one = pair_update(
        hidden, zlt, zrs, seen, base, inverse, live, proj, triangle_left, triangle_right
    )
    near = fetch(own, lambda a, b: (a, other(b)))
    across = [
        fetch(left, lambda a, b, m=step: (a, (b + 2 * m) % subs)) for step in range(1, subs // 2)
    ]
    beyond = [fetch(block, lambda a, b: (a, other(b))) for block in across]
    right = jnp.stack([own[1], near[1]])
    rights = [
        fetch(
            right,
            lambda a, b, t=turn, m=step: (
                owner(a, b, t),
                (sender(a, b, subs, ratio, PAIR_SENDERS) + 2 * m + 2) % subs,
            ),
        )
        for turn in range(ratio)
        for step in range(subs // 2)
    ]
    return triangle_update(
        [own, near, *across, *beyond],
        rights,
        one,
        cols,
        triangle_gate,
        triangle_out,
        transition_up,
        transition_down,
    )


def solution(mesh):
    in_specs = (
        P("parts", "dap", None),
        P("parts", None),
        P(("parts", "dap"), "sub", None),
        P("parts"),
        P("parts"),
        P(),
        P(),
        P(),
        P(),
        P(),
        P(),
        P(),
        P(),
        P(),
        P(),
    )
    out_specs = P(("parts", "dap"), "sub", None)
    return jax.shard_map(
        per_device, mesh=mesh, in_specs=in_specs, out_specs=out_specs, check_vma=False
    )
```

```python
import functools

import jax
import jax.numpy as jnp
from jax import lax
from jax.experimental import pallas as pl
from jax.experimental.pallas import tpu as pltpu
from jax.sharding import PartitionSpec as P

REL_CLIP = 32
LANES = 128
PARTS = 2
EPSILON = 1e-05
BF16 = jnp.bfloat16
F32 = jnp.float32
NT = (((1,), (1,)), ((), ()))
TN = (((0,), (0,)), ((), ()))


def layer_norm(values):
    average = jnp.mean(values, axis=-1, keepdims=True)
    centered = values - average
    spread = jnp.mean(centered * centered, axis=-1, keepdims=True)
    return centered * lax.rsqrt(spread + EPSILON)


def dot(left, right):
    return jnp.dot(left, right, preferred_element_type=F32)


def dot_nt(left, right):
    return lax.dot_general(left, right, NT, preferred_element_type=F32)


def dot_tn(left, right):
    return lax.dot_general(left, right, TN, preferred_element_type=F32)


def iota(shape, dim):
    return lax.broadcasted_iota(jnp.int32, shape, dim)


def vmem():
    return pl.BlockSpec(memory_space=pltpu.VMEM)


def over(index, size):
    return lax.shift_right_logical(index, size.bit_length() - 1)


def within(index, size):
    return lax.bitwise_and(index, size - 1)


def repeat_kernel(weight_ref, out_ref):
    rep = LANES // weight_ref.shape[0]
    out_ref[...] = jnp.concatenate([weight_ref[...]] * rep, axis=0).T


def repeat_weight(weight):
    return pl.pallas_call(
        repeat_kernel,
        out_shape=jax.ShapeDtypeStruct((weight.shape[1], LANES), BF16),
        in_specs=[vmem()],
        out_specs=vmem(),
        compiler_params=pltpu.CompilerParams(vmem_limit_bytes=2 << 20),
        cost_estimate=pl.CostEstimate(flops=1 << 30, bytes_accessed=1 << 17, transcendentals=0),
    )(weight)


def exchange(s0, s1, s2, s3):
    lane = iota(s0.shape, 1)
    block = LANES // 4
    odd = within(over(lane, block), 2) == 1
    upper = over(lane, 2 * block) == 1
    t0 = jnp.where(upper, pltpu.roll(s2, 2 * block, 1), s0)
    t1 = jnp.where(upper, pltpu.roll(s3, 2 * block, 1), s1)
    t2 = jnp.where(upper, s2, pltpu.roll(s0, 2 * block, 1))
    t3 = jnp.where(upper, s3, pltpu.roll(s1, 2 * block, 1))
    return (
        jnp.where(odd, pltpu.roll(t1, block, 1), t0),
        jnp.where(odd, t1, pltpu.roll(t0, 3 * block, 1)),
        jnp.where(odd, pltpu.roll(t3, block, 1), t2),
        jnp.where(odd, t3, pltpu.roll(t2, 3 * block, 1)),
    )


def factor_kernel(masked, hidden, x_ref, weight_ref, *refs):
    mask_ref = refs[0] if masked else None
    z_refs, y_scr = refs[masked:-1], refs[-1]
    each, seqs, _ = z_refs[0].shape
    groups = each * len(z_refs)
    _, rows, channels = x_ref.shape
    rep = rows // groups
    width = rows * hidden
    steps, step = y_scr.shape[0], y_scr.shape[1] // rows
    quarter = seqs // rep
    share = jnp.full((channels, LANES), 1.0 / channels, BF16)
    weight = jnp.concatenate([weight_ref[...], share], axis=1)
    sums = dot(jnp.ones((8, channels), BF16), weight_ref[...])[:1]
    side = (rep * LANES, LANES)
    own = over(iota(side, 0), LANES) == over(iota(side, 1), hidden)
    own = jnp.where(own, 1.0 / channels, 0.0).astype(BF16)
    block = over(iota((step * rows, LANES), 1), hidden)
    if masked:
        residues = mask_ref.shape[0]
        column = lax.axis_index("dap") * rows + over(iota((residues, width), 1), hidden)
        lanes_of = (iota((residues, width), 0) == column).astype(BF16)
        live = dot_tn(mask_ref[...].astype(BF16), lanes_of)
    for turn in range(steps):
        squares, y, mean = [], None, None
        for part in range(rep):
            first = part * quarter + turn * step
            x = x_ref[first : first + step].reshape(step * rows, channels)
            both = dot(x, weight)
            product, average = both[:, :LANES], both[:, LANES:]
            y = product if part == 0 else jnp.where(block == part, product, y)
            mean = average if part == 0 else jnp.where(block == part, average, mean)
            square = jnp.zeros_like(average)
            for half in range(channels // LANES):
                centered = x[:, half * LANES : (half + 1) * LANES].astype(F32) - average
                square = square + centered * centered
            squares.append(square.astype(BF16))
        scale = lax.rsqrt(dot(jnp.concatenate(squares, axis=1), own) + EPSILON)
        y_scr[turn] = (y - mean * sums) * scale
        for group in range(groups):
            taken = [
                y_scr[turn, pl.ds(group * rep + k, step, stride=rows), :] for k in range(rep)
            ]
            for part, z in enumerate(exchange(*taken)):
                first = part * quarter + turn * step
                here = slice(first, first + step)
                if masked:
                    z = z * live[here, group * LANES : (group + 1) * LANES]
                z_refs[group // each][group % each, here, :] = z.astype(BF16)


def factor(alignment, weight, hidden, parts, mask=None):
    seqs, rows, channels = alignment.shape
    steps = 2
    operands = (alignment, weight) if mask is None else (alignment, weight, mask)
    shape = jax.ShapeDtypeStruct((rows * hidden // LANES // parts, seqs, LANES), BF16)
    packed = seqs * rows * hidden // LANES
    return pl.pallas_call(
        functools.partial(factor_kernel, mask is not None, hidden),
        out_shape=(shape,) * parts,
        in_specs=[vmem()] * len(operands),
        out_specs=[vmem()] * parts,
        scratch_shapes=[pltpu.VMEM((steps, packed // steps, LANES), F32)],
        compiler_params=pltpu.CompilerParams(vmem_limit_bytes=24 << 20),
        cost_estimate=pl.CostEstimate(
            flops=2 * seqs * rows * channels * 512, bytes_accessed=seqs << 14, transcendentals=0
        ),
    )(*operands)


def prepare_kernel(
    zl_ref, mask_ref, pair_ref, live_ref, chain_ref, table_ref, proj_ref,
    zlt_ref, base_ref, inverse_ref, live_out_ref, proj_out_ref, seen_ref, pair_scr, table_scr, turn_scr,
):
    rows, cols, _ = pair_ref.shape
    pairs = rows * cols
    residues = mask_ref.shape[0]
    classes = table_ref.shape[0]
    row_start = lax.axis_index("dap") * rows
    col_start = lax.axis_index("sub") * cols
    groups = zl_ref.shape[0]
    hidden = groups * LANES // rows
    for group in range(groups):
        turned = zl_ref[group].astype(F32).T
        for half in range(zlt_ref.shape[0]):
            lanes = slice(half * LANES, (half + 1) * LANES)
            turn_scr[half, group * LANES : (group + 1) * LANES, :] = turned[:, lanes]
    for half in range(zlt_ref.shape[0]):
        for channel in range(hidden):
            here = slice(channel * rows, (channel + 1) * rows)
            picked = turn_scr[half, pl.ds(channel, rows, stride=hidden), :]
            zlt_ref[half, here, :] = picked.astype(BF16)
    proj_out_ref[...] = proj_ref[...].reshape(proj_out_ref.shape).astype(BF16)
    width = groups * LANES
    for block in range(cols // rows):
        column = col_start + block * rows + over(iota((residues, width), 1), hidden)
        spread = (iota((residues, width), 0) == column).astype(BF16)
        seen = dot_tn(mask_ref[...].astype(BF16), spread).astype(BF16)
        for group in range(groups):
            seen_ref[block * groups + group] = seen[:, group * LANES : (group + 1) * LANES]
    which = iota((pairs, residues), 0)
    place = iota((pairs, residues), 1)
    pick_row = (place == row_start + within(which, rows)).astype(BF16)
    pick_col = (place == col_start + over(which, rows)).astype(BF16)
    mask = mask_ref[...].astype(BF16)
    both = (dot(pick_row, mask) * dot(pick_col, mask)).astype(BF16)
    counts = dot(both, jnp.ones((mask.shape[1], LANES), BF16))
    inverse_ref[...] = 1.0 / jnp.maximum(counts, 1.0)
    live = jnp.broadcast_to(live_ref[...].astype(F32), (LANES, residues)).astype(BF16)
    chain = jnp.broadcast_to(chain_ref[...].astype(F32), (LANES, residues)).astype(BF16)
    live_out_ref[...] = dot_nt(pick_row, live) * dot_nt(pick_col, live)
    same = dot_nt(pick_row, chain) == dot_nt(pick_col, chain)
    pair = iota((pairs, LANES), 0)
    offset = (row_start + within(pair, rows)) - (col_start + over(pair, rows)) + REL_CLIP
    bucket = jnp.where(same, jnp.clip(offset, 0, 2 * REL_CLIP), 2 * REL_CLIP + 1)
    table_scr[...] = jnp.zeros_like(table_scr)
    table_scr[pl.ds(0, classes), :] = table_ref[...].astype(F32)
    onehot = (bucket == iota((pairs, LANES), 1)).astype(BF16)
    relative = dot(onehot, table_scr[...].astype(BF16))
    pair_scr[...] = pair_ref[...].reshape(pairs, LANES).astype(F32)
    for col in range(cols):
        here = slice(col * rows, (col + 1) * rows)
        base_ref[here, :] = relative[here] + pair_scr[pl.ds(col, rows, stride=cols), :]


def prepare(zl, mask, pair_input, residue_mask, chain_index, table, proj):
    rows, cols, channels = pair_input.shape
    pairs = rows * cols
    shape = jax.ShapeDtypeStruct((pairs, channels), F32)
    depth = proj.shape[0] * proj.shape[1]
    return pl.pallas_call(
        prepare_kernel,
        out_shape=(
            jax.ShapeDtypeStruct((zl.shape[1] // LANES, zl.shape[0] * LANES, LANES), BF16),
            shape,
            shape,
            shape,
            jax.ShapeDtypeStruct((depth, channels), BF16),
            jax.ShapeDtypeStruct((cols // rows * zl.shape[0], *zl.shape[1:]), BF16),
        ),
        in_specs=[vmem()] * 7,
        out_specs=[vmem()] * 6,
        scratch_shapes=[
            pltpu.VMEM((pairs, channels), F32),
            pltpu.VMEM((LANES, channels), F32),
            pltpu.VMEM((zl.shape[1] // LANES, zl.shape[0] * LANES, LANES), F32),
        ],
        compiler_params=pltpu.CompilerParams(vmem_limit_bytes=24 << 20),
        cost_estimate=pl.CostEstimate(
            flops=2 * pairs * 256 * 1024, bytes_accessed=2 << 20, transcendentals=0
        ),
    )(zl, mask, pair_input, residue_mask[None, :], chain_index[None, :], table, proj)


def pair_kernel(ratio, hidden, zlt_ref, *refs):
    zr_refs, refs = refs[: ratio * PARTS], refs[ratio * PARTS :]
    (seen_ref, base_ref, inverse_ref, live_ref, proj_ref, tl_ref, tr_ref,
     both_ref, left_ref, one_ref, flat_scr, one_scr) = refs
    pairs, channels = base_ref.shape
    rows = zlt_ref.shape[1] // hidden
    rep = LANES // hidden
    me = lax.axis_index("dap")
    left = jnp.concatenate([zlt_ref[part] for part in range(zlt_ref.shape[0])], axis=1)
    for step in range(ratio):
        block = lax.rem(me + step, ratio)
        right = []
        for group in range(rows // rep):
            each = rows // rep // PARTS
            factor = zr_refs[step * PARTS + group // each][group % each]
            right.append(factor * seen_ref[block * (rows // rep) + group])
        outer = dot(left, jnp.concatenate(right, axis=1))
        for group in range(rows // rep):
            lanes = slice(group * LANES, (group + 1) * LANES)
            for quad in range(hidden // rep):
                s0, s1, s2, s3 = (
                    outer[(quad * rep + k) * rows : (quad * rep + k + 1) * rows, lanes]
                    for k in range(rep)
                )
                found = exchange(s0, s1, s2, s3)
                for k in range(rep):
                    first = block * rows * rows + (group * rep + k) * rows
                    if ratio == 1:
                        first = (group * rep + k) * rows
                    else:
                        first = pl.multiple_of(first, rows)
                    flat_scr[quad, pl.ds(first, rows), :] = found[k].astype(BF16)
    flat = jnp.concatenate([flat_scr[quad] for quad in range(flat_scr.shape[0])], axis=1)
    outer_mean = dot(flat, proj_ref[...]) * inverse_ref[...]
    one = (base_ref[...] + outer_mean).astype(BF16).astype(F32)
    one_scr[...] = one
    norm = layer_norm(one).astype(BF16)
    for side, weight in enumerate((tl_ref, tr_ref)):
        both = dot(norm, weight[...])
        factor = jax.nn.sigmoid(both[:, :channels]) * both[:, channels:] * live_ref[...]
        both_ref[side] = factor.astype(BF16)
        if side == 0:
            left_ref[...] = factor.astype(BF16)
    cols = pairs // rows
    for row in range(rows):
        one_ref[row * cols : (row + 1) * cols, :] = one_scr[pl.ds(row, cols, stride=rows), :].astype(BF16)


def pair_update(hidden, zlt, zrs, seen, base, inverse, live, proj, triangle_left, triangle_right):
    pairs, channels = base.shape
    ratio = len(zrs) // PARTS
    shape = jax.ShapeDtypeStruct((pairs, channels), BF16)
    return pl.pallas_call(
        functools.partial(pair_kernel, ratio, hidden),
        out_shape=(jax.ShapeDtypeStruct((2, pairs, channels), BF16), shape, shape),
        in_specs=[vmem()] * (8 + len(zrs)),
        out_specs=[vmem()] * 3,
        scratch_shapes=[
            pltpu.VMEM((proj.shape[0] // LANES, pairs, LANES), BF16),
            pltpu.VMEM((pairs, channels), F32),
        ],
        compiler_params=pltpu.CompilerParams(vmem_limit_bytes=32 << 20),
        cost_estimate=pl.CostEstimate(
            flops=2 * pairs * 1024 * 512, bytes_accessed=2 << 20, transcendentals=pairs * 256
        ),
    )(zlt, *zrs, seen, base, inverse, live, proj, triangle_left, triangle_right)


def other(sub):
    return sub + 1 - 2 * (sub % 2)


SENDERS = ((3, 0, 2, 1), (0, 3, 2, 1), (2, 0, 1, 3), (2, 0, 3, 1))
PAIR_SENDERS = ((3, 0, 2, 1), (0, 3, 1, 2), (0, 2, 1, 3), (2, 0, 3, 1))


def sender(a, b, subs, ratio, table):
    if (subs, ratio) == (4, 1):
        return table[b][a]
    return a // ratio


def sender_index(a, b, subs, ratio):
    if (subs, ratio) != (4, 1):
        return a // ratio
    found = 0
    for col, places in enumerate(PAIR_SENDERS):
        for row, place in enumerate(places):
            found = jnp.where((a == row) & (b == col), place, found)
    return found


def add_terms(sums, start, lefts, rights, steps, ratio, cols, left_scr):
    subs = left_scr.shape[0]
    _, channels = sums.shape
    rows = left_scr.shape[1] // cols
    here, there = lax.axis_index("dap"), lax.axis_index("sub")
    first_sub = sender_index(here, there, subs, ratio)
    own, near, across, beyond = lefts
    left_scr[there] = own[0].astype(F32)
    left_scr[other(there)] = near[0].astype(F32)
    for step in range(1, subs // 2):
        sub = lax.rem(there + 2 * step, subs)
        left_scr[sub] = across[step - 1][...].astype(F32)
        left_scr[other(sub)] = beyond[step - 1][...].astype(F32)
    for turn in range(ratio):
        block = lax.rem(here + turn, ratio) if ratio > 1 else 0
        places = [i * cols + block * rows for i in range(rows)]
        if ratio > 1:
            places = [pl.multiple_of(place, rows) for place in places]
        if start is None:
            totals = tuple(jnp.zeros((rows, channels), F32) for _ in range(rows))
        else:
            totals = tuple(start[pl.ds(place, rows), :] for place in places)
        for index, step in enumerate(steps):
            sub = lax.rem(first_sub + 2 * step + 2, subs)
            pair = rights[turn * len(steps) + index]
            for member, slot in enumerate((sub, other(sub))):

                def body(k, totals, slot=slot, member=member, pair=pair):
                    first = pl.multiple_of(k * rows, rows)
                    right = pair[member, pl.ds(first, rows), :].astype(F32)
                    return tuple(
                        totals[i] + left_scr[slot, pl.ds(first + i, 1), :] * right
                        for i in range(rows)
                    )

                totals = lax.fori_loop(0, cols, body, totals, unroll=4)
        for place, total in zip(places, totals):
            sums[pl.ds(place, rows), :] = total


def split_lefts(refs, twos):
    count = twos - 1
    lefts = (refs[0], refs[1], refs[2 : 2 + count], refs[2 + count : 2 + 2 * count])
    return lefts, refs[2 + 2 * count :]


def first_kernel(steps, twos, ratio, cols, *refs):
    lefts, refs = split_lefts(refs, twos)
    rights, refs = refs[: ratio * len(steps)], refs[ratio * len(steps) :]
    one_ref, weight_ref, sums_ref, gate_ref, left_scr = refs
    add_terms(sums_ref, None, lefts, rights, steps, ratio, cols, left_scr)
    norm = layer_norm(one_ref[...].astype(F32)).astype(BF16)
    gate_ref[...] = jax.nn.sigmoid(dot(norm, weight_ref[...]))


def last_kernel(steps, twos, ratio, cols, *refs):
    lefts, refs = split_lefts(refs, twos)
    rights, refs = refs[: ratio * len(steps)], refs[ratio * len(steps) :]
    (start_ref, one_ref, gate_ref, out_ref, up_ref, down_ref, result_ref, left_scr, sum_scr) = refs
    add_terms(sum_scr, start_ref, lefts, rights, steps, ratio, cols, left_scr)
    one = one_ref[...].astype(F32)
    hidden = layer_norm(sum_scr[...].astype(BF16).astype(F32)).astype(BF16)
    two = (one + gate_ref[...] * dot(hidden, out_ref[...])).astype(BF16).astype(F32)
    wide = jnp.maximum(dot(layer_norm(two).astype(BF16), up_ref[...]), 0.0).astype(BF16)
    result = (two + dot(wide, down_ref[...])).astype(BF16)
    result_ref[...] = result.reshape(result_ref.shape)


def triangle_update(lefts, rights, one, cols, gate_weight, out, up, down):
    pairs, channels = one.shape
    rows = pairs // cols
    twos = len(lefts) // 2
    subs = 2 * twos
    ratio = len(rights) // twos
    late, early = range(twos // 2), range(twos // 2, twos)
    limit = (12 << 20) if ratio == 1 else (50 << 20)
    left_scr = pltpu.VMEM((subs, pairs, channels), F32)
    shape = jax.ShapeDtypeStruct((pairs, channels), F32)

    def chosen(steps):
        return [rights[turn * twos + step] for turn in range(ratio) for step in steps]

    sums, gate = pl.pallas_call(
        functools.partial(first_kernel, early, twos, ratio, cols),
        out_shape=(shape, shape),
        in_specs=[vmem()] * (len(lefts) + ratio * len(early) + 2),
        out_specs=[vmem()] * 2,
        scratch_shapes=[left_scr],
        compiler_params=pltpu.CompilerParams(vmem_limit_bytes=limit),
        cost_estimate=pl.CostEstimate(
            flops=2 * pairs * channels * 1024, bytes_accessed=1 << 20, transcendentals=pairs * 128
        ),
    )(*lefts, *chosen(early), one, gate_weight)
    return pl.pallas_call(
        functools.partial(last_kernel, late, twos, ratio, cols),
        out_shape=jax.ShapeDtypeStruct((rows, cols, channels), BF16),
        in_specs=[vmem()] * (len(lefts) + ratio * len(late) + 6),
        out_specs=vmem(),
        scratch_shapes=[left_scr, pltpu.VMEM((pairs, channels), F32)],
        compiler_params=pltpu.CompilerParams(vmem_limit_bytes=limit),
        cost_estimate=pl.CostEstimate(
            flops=2 * pairs * channels * 2048, bytes_accessed=2 << 20, transcendentals=pairs * 128
        ),
    )(*lefts, *chosen(late), sums, one, gate, out, up, down)


def per_device(
    alignment,
    alignment_mask,
    pair_input,
    residue_mask,
    chain_index,
    outer_left,
    outer_right,
    outer_proj,
    triangle_left,
    triangle_right,
    triangle_gate,
    triangle_out,
    relative_table,
    transition_up,
    transition_down,
):
    daps, subs = lax.axis_size("dap"), lax.axis_size("sub")
    ratio = daps // subs
    cols = pair_input.shape[1]

    def fetch(values, source):
        perm = []
        for a in range(daps):
            for b in range(subs):
                dap, sub = source(a, b)
                perm.append((dap * subs + sub, a * subs + b))
        return lax.ppermute(values, ("dap", "sub"), perm)

    def owner(a, b, turn):
        return ratio * b + (a + turn) % ratio

    hidden = outer_left.shape[1]
    mask = alignment_mask.T
    zr = factor(alignment, repeat_weight(outer_right.T), hidden, PARTS)
    zrs = [
        fetch(
            zr[part],
            lambda a, b, t=turn, p=part: (
                owner(a, b, t), (sender(a, b, subs, ratio, SENDERS) + 2 * p) % subs
            ),
        )
        for turn in range(ratio)
        for part in range(PARTS)
    ]
    (zl,) = factor(alignment, repeat_weight(outer_left.T), hidden, 1, mask)
    zlt, base, inverse, live, proj, seen = prepare(
        zl, mask, pair_input, residue_mask, chain_index, relative_table, outer_proj
    )
    own, left, one = pair_update(
        hidden, zlt, zrs, seen, base, inverse, live, proj, triangle_left, triangle_right
    )
    near = fetch(own, lambda a, b: (a, other(b)))
    across = [
        fetch(left, lambda a, b, m=step: (a, (b + 2 * m) % subs)) for step in range(1, subs // 2)
    ]
    beyond = [fetch(block, lambda a, b: (a, other(b))) for block in across]
    right = jnp.stack([own[1], near[1]])
    rights = [
        fetch(
            right,
            lambda a, b, t=turn, m=step: (
                owner(a, b, t),
                (sender(a, b, subs, ratio, PAIR_SENDERS) + 2 * m + 2) % subs,
            ),
        )
        for turn in range(ratio)
        for step in range(subs // 2)
    ]
    return triangle_update(
        [own, near, *across, *beyond],
        rights,
        one,
        cols,
        triangle_gate,
        triangle_out,
        transition_up,
        transition_down,
    )


def solution(mesh):
    in_specs = (
        P("parts", "dap", None),
        P("parts", None),
        P(("parts", "dap"), "sub", None),
        P("parts"),
        P("parts"),
        P(),
        P(),
        P(),
        P(),
        P(),
        P(),
        P(),
        P(),
        P(),
        P(),
    )
    out_specs = P(("parts", "dap"), "sub", None)
    return jax.shard_map(
        per_device, mesh=mesh, in_specs=in_specs, out_specs=out_specs, check_vma=False
    )
```

```python
import functools

import jax
import jax.numpy as jnp
from jax import lax
from jax.experimental import pallas as pl
from jax.experimental.pallas import tpu as pltpu
from jax.sharding import PartitionSpec as P

REL_CLIP = 32
LANES = 128
PARTS = 1
EPSILON = 1e-05
BF16 = jnp.bfloat16
F32 = jnp.float32
NT = (((1,), (1,)), ((), ()))
TN = (((0,), (0,)), ((), ()))


def layer_norm(values):
    average = jnp.mean(values, axis=-1, keepdims=True)
    centered = values - average
    spread = jnp.mean(centered * centered, axis=-1, keepdims=True)
    return centered * lax.rsqrt(spread + EPSILON)


def dot(left, right):
    return jnp.dot(left, right, preferred_element_type=F32)


def dot_nt(left, right):
    return lax.dot_general(left, right, NT, preferred_element_type=F32)


def dot_tn(left, right):
    return lax.dot_general(left, right, TN, preferred_element_type=F32)


def iota(shape, dim):
    return lax.broadcasted_iota(jnp.int32, shape, dim)


def vmem():
    return pl.BlockSpec(memory_space=pltpu.VMEM)


def over(index, size):
    return lax.shift_right_logical(index, size.bit_length() - 1)


def within(index, size):
    return lax.bitwise_and(index, size - 1)


def repeat_kernel(weight_ref, out_ref):
    rep = LANES // weight_ref.shape[0]
    out_ref[...] = jnp.concatenate([weight_ref[...]] * rep, axis=0).T


def repeat_weight(weight):
    return pl.pallas_call(
        repeat_kernel,
        out_shape=jax.ShapeDtypeStruct((weight.shape[1], LANES), BF16),
        in_specs=[vmem()],
        out_specs=vmem(),
        compiler_params=pltpu.CompilerParams(vmem_limit_bytes=2 << 20),
        cost_estimate=pl.CostEstimate(flops=1 << 30, bytes_accessed=1 << 17, transcendentals=0),
    )(weight)


def exchange(s0, s1, s2, s3):
    lane = iota(s0.shape, 1)
    block = LANES // 4
    odd = within(over(lane, block), 2) == 1
    upper = over(lane, 2 * block) == 1
    t0 = jnp.where(upper, pltpu.roll(s2, 2 * block, 1), s0)
    t1 = jnp.where(upper, pltpu.roll(s3, 2 * block, 1), s1)
    t2 = jnp.where(upper, s2, pltpu.roll(s0, 2 * block, 1))
    t3 = jnp.where(upper, s3, pltpu.roll(s1, 2 * block, 1))
    return (
        jnp.where(odd, pltpu.roll(t1, block, 1), t0),
        jnp.where(odd, t1, pltpu.roll(t0, 3 * block, 1)),
        jnp.where(odd, pltpu.roll(t3, block, 1), t2),
        jnp.where(odd, t3, pltpu.roll(t2, 3 * block, 1)),
    )


def factor_kernel(masked, hidden, x_ref, weight_ref, *refs):
    mask_ref = refs[0] if masked else None
    z_refs, y_scr = refs[masked:-1], refs[-1]
    each, seqs, _ = z_refs[0].shape
    groups = each * len(z_refs)
    _, rows, channels = x_ref.shape
    rep = rows // groups
    width = rows * hidden
    steps, step = y_scr.shape[0], y_scr.shape[1] // rows
    quarter = seqs // rep
    share = jnp.full((channels, LANES), 1.0 / channels, BF16)
    weight = jnp.concatenate([weight_ref[...], share], axis=1)
    sums = dot(jnp.ones((8, channels), BF16), weight_ref[...])[:1]
    side = (rep * LANES, LANES)
    own = over(iota(side, 0), LANES) == over(iota(side, 1), hidden)
    own = jnp.where(own, 1.0 / channels, 0.0).astype(BF16)
    block = over(iota((step * rows, LANES), 1), hidden)
    if masked:
        residues = mask_ref.shape[0]
        column = lax.axis_index("dap") * rows + over(iota((residues, width), 1), hidden)
        lanes_of = (iota((residues, width), 0) == column).astype(BF16)
        live = dot_tn(mask_ref[...].astype(BF16), lanes_of)
    for turn in range(steps):
        squares, y, mean = [], None, None
        for part in range(rep):
            first = part * quarter + turn * step
            x = x_ref[first : first + step].reshape(step * rows, channels)
            both = dot(x, weight)
            product, average = both[:, :LANES], both[:, LANES:]
            y = product if part == 0 else jnp.where(block == part, product, y)
            mean = average if part == 0 else jnp.where(block == part, average, mean)
            square = jnp.zeros_like(average)
            for half in range(channels // LANES):
                centered = x[:, half * LANES : (half + 1) * LANES].astype(F32) - average
                square = square + centered * centered
            squares.append(square.astype(BF16))
        scale = lax.rsqrt(dot(jnp.concatenate(squares, axis=1), own) + EPSILON)
        y_scr[turn] = (y - mean * sums) * scale
        for group in range(groups):
            taken = [
                y_scr[turn, pl.ds(group * rep + k, step, stride=rows), :] for k in range(rep)
            ]
            for part, z in enumerate(exchange(*taken)):
                first = part * quarter + turn * step
                here = slice(first, first + step)
                if masked:
                    z = z * live[here, group * LANES : (group + 1) * LANES]
                z_refs[group // each][group % each, here, :] = z.astype(BF16)


def factor(alignment, weight, hidden, parts, mask=None):
    seqs, rows, channels = alignment.shape
    steps = 2
    operands = (alignment, weight) if mask is None else (alignment, weight, mask)
    shape = jax.ShapeDtypeStruct((rows * hidden // LANES // parts, seqs, LANES), BF16)
    packed = seqs * rows * hidden // LANES
    return pl.pallas_call(
        functools.partial(factor_kernel, mask is not None, hidden),
        out_shape=(shape,) * parts,
        in_specs=[vmem()] * len(operands),
        out_specs=[vmem()] * parts,
        scratch_shapes=[pltpu.VMEM((steps, packed // steps, LANES), F32)],
        compiler_params=pltpu.CompilerParams(vmem_limit_bytes=24 << 20),
        cost_estimate=pl.CostEstimate(
            flops=2 * seqs * rows * channels * 512, bytes_accessed=seqs << 14, transcendentals=0
        ),
    )(*operands)


def prepare_kernel(
    zl_ref, mask_ref, pair_ref, live_ref, chain_ref, table_ref, proj_ref,
    zlt_ref, base_ref, inverse_ref, live_out_ref, proj_out_ref, seen_ref, pair_scr, table_scr, turn_scr,
):
    rows, cols, _ = pair_ref.shape
    pairs = rows * cols
    residues = mask_ref.shape[0]
    classes = table_ref.shape[0]
    row_start = lax.axis_index("dap") * rows
    col_start = lax.axis_index("sub") * cols
    groups = zl_ref.shape[0]
    hidden = groups * LANES // rows
    for group in range(groups):
        turned = zl_ref[group].astype(F32).T
        for half in range(zlt_ref.shape[0]):
            lanes = slice(half * LANES, (half + 1) * LANES)
            turn_scr[half, group * LANES : (group + 1) * LANES, :] = turned[:, lanes]
    for half in range(zlt_ref.shape[0]):
        for channel in range(hidden):
            here = slice(channel * rows, (channel + 1) * rows)
            picked = turn_scr[half, pl.ds(channel, rows, stride=hidden), :]
            zlt_ref[half, here, :] = picked.astype(BF16)
    proj_out_ref[...] = proj_ref[...].reshape(proj_out_ref.shape).astype(BF16)
    width = groups * LANES
    for block in range(cols // rows):
        column = col_start + block * rows + over(iota((residues, width), 1), hidden)
        spread = (iota((residues, width), 0) == column).astype(BF16)
        seen = dot_tn(mask_ref[...].astype(BF16), spread).astype(BF16)
        for group in range(groups):
            seen_ref[block * groups + group] = seen[:, group * LANES : (group + 1) * LANES]
    which = iota((pairs, residues), 0)
    place = iota((pairs, residues), 1)
    pick_row = (place == row_start + within(which, rows)).astype(BF16)
    pick_col = (place == col_start + over(which, rows)).astype(BF16)
    mask = mask_ref[...].astype(BF16)
    both = (dot(pick_row, mask) * dot(pick_col, mask)).astype(BF16)
    counts = dot(both, jnp.ones((mask.shape[1], LANES), BF16))
    inverse_ref[...] = 1.0 / jnp.maximum(counts, 1.0)
    live = jnp.broadcast_to(live_ref[...].astype(F32), (LANES, residues)).astype(BF16)
    chain = jnp.broadcast_to(chain_ref[...].astype(F32), (LANES, residues)).astype(BF16)
    live_out_ref[...] = dot_nt(pick_row, live) * dot_nt(pick_col, live)
    same = dot_nt(pick_row, chain) == dot_nt(pick_col, chain)
    pair = iota((pairs, LANES), 0)
    offset = (row_start + within(pair, rows)) - (col_start + over(pair, rows)) + REL_CLIP
    bucket = jnp.where(same, jnp.clip(offset, 0, 2 * REL_CLIP), 2 * REL_CLIP + 1)
    table_scr[...] = jnp.zeros_like(table_scr)
    table_scr[pl.ds(0, classes), :] = table_ref[...].astype(F32)
    onehot = (bucket == iota((pairs, LANES), 1)).astype(BF16)
    relative = dot(onehot, table_scr[...].astype(BF16))
    pair_scr[...] = pair_ref[...].reshape(pairs, LANES).astype(F32)
    for col in range(cols):
        here = slice(col * rows, (col + 1) * rows)
        base_ref[here, :] = relative[here] + pair_scr[pl.ds(col, rows, stride=cols), :]


def prepare(zl, mask, pair_input, residue_mask, chain_index, table, proj):
    rows, cols, channels = pair_input.shape
    pairs = rows * cols
    shape = jax.ShapeDtypeStruct((pairs, channels), F32)
    depth = proj.shape[0] * proj.shape[1]
    return pl.pallas_call(
        prepare_kernel,
        out_shape=(
            jax.ShapeDtypeStruct((zl.shape[1] // LANES, zl.shape[0] * LANES, LANES), BF16),
            shape,
            shape,
            shape,
            jax.ShapeDtypeStruct((depth, channels), BF16),
            jax.ShapeDtypeStruct((cols // rows * zl.shape[0], *zl.shape[1:]), BF16),
        ),
        in_specs=[vmem()] * 7,
        out_specs=[vmem()] * 6,
        scratch_shapes=[
            pltpu.VMEM((pairs, channels), F32),
            pltpu.VMEM((LANES, channels), F32),
            pltpu.VMEM((zl.shape[1] // LANES, zl.shape[0] * LANES, LANES), F32),
        ],
        compiler_params=pltpu.CompilerParams(vmem_limit_bytes=24 << 20),
        cost_estimate=pl.CostEstimate(
            flops=2 * pairs * 256 * 1024, bytes_accessed=2 << 20, transcendentals=0
        ),
    )(zl, mask, pair_input, residue_mask[None, :], chain_index[None, :], table, proj)


def pair_kernel(ratio, hidden, zlt_ref, *refs):
    zr_refs, refs = refs[: ratio * PARTS], refs[ratio * PARTS :]
    (seen_ref, base_ref, inverse_ref, live_ref, proj_ref, tl_ref, tr_ref,
     both_ref, left_ref, one_ref, flat_scr, one_scr) = refs
    pairs, channels = base_ref.shape
    rows = zlt_ref.shape[1] // hidden
    rep = LANES // hidden
    me = lax.axis_index("dap")
    left = jnp.concatenate([zlt_ref[part] for part in range(zlt_ref.shape[0])], axis=1)
    for step in range(ratio):
        block = lax.rem(me + step, ratio)
        right = []
        for group in range(rows // rep):
            each = rows // rep // PARTS
            factor = zr_refs[step * PARTS + group // each][group % each]
            right.append(factor * seen_ref[block * (rows // rep) + group])
        outer = dot(left, jnp.concatenate(right, axis=1))
        for group in range(rows // rep):
            lanes = slice(group * LANES, (group + 1) * LANES)
            for quad in range(hidden // rep):
                s0, s1, s2, s3 = (
                    outer[(quad * rep + k) * rows : (quad * rep + k + 1) * rows, lanes]
                    for k in range(rep)
                )
                found = exchange(s0, s1, s2, s3)
                for k in range(rep):
                    first = block * rows * rows + (group * rep + k) * rows
                    if ratio == 1:
                        first = (group * rep + k) * rows
                    else:
                        first = pl.multiple_of(first, rows)
                    flat_scr[quad, pl.ds(first, rows), :] = found[k].astype(BF16)
    flat = jnp.concatenate([flat_scr[quad] for quad in range(flat_scr.shape[0])], axis=1)
    outer_mean = dot(flat, proj_ref[...]) * inverse_ref[...]
    one = (base_ref[...] + outer_mean).astype(BF16).astype(F32)
    one_scr[...] = one
    norm = layer_norm(one).astype(BF16)
    for side, weight in enumerate((tl_ref, tr_ref)):
        both = dot(norm, weight[...])
        factor = jax.nn.sigmoid(both[:, :channels]) * both[:, channels:] * live_ref[...]
        both_ref[side] = factor.astype(BF16)
        if side == 0:
            left_ref[...] = factor.astype(BF16)
    cols = pairs // rows
    for row in range(rows):
        one_ref[row * cols : (row + 1) * cols, :] = one_scr[pl.ds(row, cols, stride=rows), :].astype(BF16)


def pair_update(hidden, zlt, zrs, seen, base, inverse, live, proj, triangle_left, triangle_right):
    pairs, channels = base.shape
    ratio = len(zrs) // PARTS
    shape = jax.ShapeDtypeStruct((pairs, channels), BF16)
    return pl.pallas_call(
        functools.partial(pair_kernel, ratio, hidden),
        out_shape=(jax.ShapeDtypeStruct((2, pairs, channels), BF16), shape, shape),
        in_specs=[vmem()] * (8 + len(zrs)),
        out_specs=[vmem()] * 3,
        scratch_shapes=[
            pltpu.VMEM((proj.shape[0] // LANES, pairs, LANES), BF16),
            pltpu.VMEM((pairs, channels), F32),
        ],
        compiler_params=pltpu.CompilerParams(vmem_limit_bytes=32 << 20),
        cost_estimate=pl.CostEstimate(
            flops=2 * pairs * 1024 * 512, bytes_accessed=2 << 20, transcendentals=pairs * 256
        ),
    )(zlt, *zrs, seen, base, inverse, live, proj, triangle_left, triangle_right)


def other(sub):
    return sub + 1 - 2 * (sub % 2)


SENDERS = ((3, 0, 2, 1), (0, 3, 1, 2), (0, 2, 1, 3), (2, 0, 3, 1))


def sender(a, b, subs, ratio, table):
    if (subs, ratio) == (4, 1):
        return table[b][a]
    return a // ratio


def sender_index(a, b, subs, ratio):
    if (subs, ratio) != (4, 1):
        return a // ratio
    found = 0
    for col, places in enumerate(SENDERS):
        for row, place in enumerate(places):
            found = jnp.where((a == row) & (b == col), place, found)
    return found


def add_terms(sums, start, lefts, rights, steps, ratio, cols, left_scr):
    subs = left_scr.shape[0]
    _, channels = sums.shape
    rows = left_scr.shape[1] // cols
    here, there = lax.axis_index("dap"), lax.axis_index("sub")
    first_sub = sender_index(here, there, subs, ratio)
    own, near, across, beyond = lefts
    left_scr[there] = own[0].astype(F32)
    left_scr[other(there)] = near[0].astype(F32)
    for step in range(1, subs // 2):
        sub = lax.rem(there + 2 * step, subs)
        left_scr[sub] = across[step - 1][...].astype(F32)
        left_scr[other(sub)] = beyond[step - 1][...].astype(F32)
    for turn in range(ratio):
        block = lax.rem(here + turn, ratio) if ratio > 1 else 0
        places = [i * cols + block * rows for i in range(rows)]
        if ratio > 1:
            places = [pl.multiple_of(place, rows) for place in places]
        if start is None:
            totals = tuple(jnp.zeros((rows, channels), F32) for _ in range(rows))
        else:
            totals = tuple(start[pl.ds(place, rows), :] for place in places)
        for index, step in enumerate(steps):
            sub = lax.rem(first_sub + 2 * step + 2, subs)
            pair = rights[turn * len(steps) + index]
            for member, slot in enumerate((sub, other(sub))):

                def body(k, totals, slot=slot, member=member, pair=pair):
                    first = pl.multiple_of(k * rows, rows)
                    right = pair[member, pl.ds(first, rows), :].astype(F32)
                    return tuple(
                        totals[i] + left_scr[slot, pl.ds(first + i, 1), :] * right
                        for i in range(rows)
                    )

                totals = lax.fori_loop(0, cols, body, totals, unroll=4)
        for place, total in zip(places, totals):
            sums[pl.ds(place, rows), :] = total


def split_lefts(refs, twos):
    count = twos - 1
    lefts = (refs[0], refs[1], refs[2 : 2 + count], refs[2 + count : 2 + 2 * count])
    return lefts, refs[2 + 2 * count :]


def first_kernel(steps, twos, ratio, cols, *refs):
    lefts, refs = split_lefts(refs, twos)
    rights, refs = refs[: ratio * len(steps)], refs[ratio * len(steps) :]
    one_ref, weight_ref, sums_ref, gate_ref, left_scr = refs
    add_terms(sums_ref, None, lefts, rights, steps, ratio, cols, left_scr)
    norm = layer_norm(one_ref[...].astype(F32)).astype(BF16)
    gate_ref[...] = jax.nn.sigmoid(dot(norm, weight_ref[...]))


def last_kernel(steps, twos, ratio, cols, *refs):
    lefts, refs = split_lefts(refs, twos)
    rights, refs = refs[: ratio * len(steps)], refs[ratio * len(steps) :]
    (start_ref, one_ref, gate_ref, out_ref, up_ref, down_ref, result_ref, left_scr, sum_scr) = refs
    add_terms(sum_scr, start_ref, lefts, rights, steps, ratio, cols, left_scr)
    one = one_ref[...].astype(F32)
    hidden = layer_norm(sum_scr[...].astype(BF16).astype(F32)).astype(BF16)
    two = (one + gate_ref[...] * dot(hidden, out_ref[...])).astype(BF16).astype(F32)
    wide = jnp.maximum(dot(layer_norm(two).astype(BF16), up_ref[...]), 0.0).astype(BF16)
    result = (two + dot(wide, down_ref[...])).astype(BF16)
    result_ref[...] = result.reshape(result_ref.shape)


def triangle_update(lefts, rights, one, cols, gate_weight, out, up, down):
    pairs, channels = one.shape
    rows = pairs // cols
    twos = len(lefts) // 2
    subs = 2 * twos
    ratio = len(rights) // twos
    late, early = range(twos // 2), range(twos // 2, twos)
    limit = (12 << 20) if ratio == 1 else (50 << 20)
    left_scr = pltpu.VMEM((subs, pairs, channels), F32)
    shape = jax.ShapeDtypeStruct((pairs, channels), F32)

    def chosen(steps):
        return [rights[turn * twos + step] for turn in range(ratio) for step in steps]

    sums, gate = pl.pallas_call(
        functools.partial(first_kernel, early, twos, ratio, cols),
        out_shape=(shape, shape),
        in_specs=[vmem()] * (len(lefts) + ratio * len(early) + 2),
        out_specs=[vmem()] * 2,
        scratch_shapes=[left_scr],
        compiler_params=pltpu.CompilerParams(vmem_limit_bytes=limit),
        cost_estimate=pl.CostEstimate(
            flops=2 * pairs * channels * 1024, bytes_accessed=1 << 20, transcendentals=pairs * 128
        ),
    )(*lefts, *chosen(early), one, gate_weight)
    return pl.pallas_call(
        functools.partial(last_kernel, late, twos, ratio, cols),
        out_shape=jax.ShapeDtypeStruct((rows, cols, channels), BF16),
        in_specs=[vmem()] * (len(lefts) + ratio * len(late) + 6),
        out_specs=vmem(),
        scratch_shapes=[left_scr, pltpu.VMEM((pairs, channels), F32)],
        compiler_params=pltpu.CompilerParams(vmem_limit_bytes=limit),
        cost_estimate=pl.CostEstimate(
            flops=2 * pairs * channels * 2048, bytes_accessed=2 << 20, transcendentals=pairs * 128
        ),
    )(*lefts, *chosen(late), sums, one, gate, out, up, down)


def per_device(
    alignment,
    alignment_mask,
    pair_input,
    residue_mask,
    chain_index,
    outer_left,
    outer_right,
    outer_proj,
    triangle_left,
    triangle_right,
    triangle_gate,
    triangle_out,
    relative_table,
    transition_up,
    transition_down,
):
    daps, subs = lax.axis_size("dap"), lax.axis_size("sub")
    ratio = daps // subs
    cols = pair_input.shape[1]

    def fetch(values, source):
        perm = []
        for a in range(daps):
            for b in range(subs):
                dap, sub = source(a, b)
                perm.append((dap * subs + sub, a * subs + b))
        return lax.ppermute(values, ("dap", "sub"), perm)

    def owner(a, b, turn):
        return ratio * b + (a + turn) % ratio

    hidden = outer_left.shape[1]
    mask = alignment_mask.T
    zr = factor(alignment, repeat_weight(outer_right.T), hidden, PARTS)
    zrs = [
        fetch(
            zr[part],
            lambda a, b, t=turn, p=part: (
                owner(a, b, t), (sender(a, b, subs, ratio, SENDERS) + 2 * p) % subs
            ),
        )
        for turn in range(ratio)
        for part in range(PARTS)
    ]
    (zl,) = factor(alignment, repeat_weight(outer_left.T), hidden, 1, mask)
    zlt, base, inverse, live, proj, seen = prepare(
        zl, mask, pair_input, residue_mask, chain_index, relative_table, outer_proj
    )
    own, left, one = pair_update(
        hidden, zlt, zrs, seen, base, inverse, live, proj, triangle_left, triangle_right
    )
    near = fetch(own, lambda a, b: (a, other(b)))
    across = [
        fetch(left, lambda a, b, m=step: (a, (b + 2 * m) % subs)) for step in range(1, subs // 2)
    ]
    beyond = [fetch(block, lambda a, b: (a, other(b))) for block in across]
    right = jnp.stack([own[1], near[1]])
    rights = [
        fetch(
            right,
            lambda a, b, t=turn, m=step: (
                owner(a, b, t),
                (sender(a, b, subs, ratio, SENDERS) + 2 * m + 2) % subs,
            ),
        )
        for turn in range(ratio)
        for step in range(subs // 2)
    ]
    return triangle_update(
        [own, near, *across, *beyond],
        rights,
        one,
        cols,
        triangle_gate,
        triangle_out,
        transition_up,
        transition_down,
    )


def solution(mesh):
    in_specs = (
        P("parts", "dap", None),
        P("parts", None),
        P(("parts", "dap"), "sub", None),
        P("parts"),
        P("parts"),
        P(),
        P(),
        P(),
        P(),
        P(),
        P(),
        P(),
        P(),
        P(),
        P(),
    )
    out_specs = P(("parts", "dap"), "sub", None)
    return jax.shard_map(
        per_device, mesh=mesh, in_specs=in_specs, out_specs=out_specs, check_vma=False
    )
```
